32 devices in a mesh: batch: 4 (over z), row: 2 (over x), col: 4 (over y, core).
Axes of the slice: x: 2, y: 2, z: 4, core: 2. Of those that a mesh axis runs over, the one named last changes fastest.
Arguments:
- latents: bfloat16 [8, 4, 64, 64], P('batch', None, 'row', 'col'), may hold values from -6 to 6
- conditioning: bfloat16 [8, 1152], P('batch'), may hold values from -6 to 6
- kept_index: int32 [8, 1024], P('batch'), may hold values from 0 to 1023, each once within a row
- kept_count: int32 [8], P('batch'), may hold values from 256 to 768
- patch_weight: bfloat16 [16, 1152], P(None, 'batch'), may hold values from -1.5 to 1.5
- patch_bias: bfloat16 [1152], P('batch'), may hold values from -3 to 3
- adaptive_weight: bfloat16 [2, 1152, 6912], P(None, 'batch'), may hold values from -0.1875 to 0.1875
- adaptive_bias: bfloat16 [2, 6912], P(None, 'batch'), may hold values from -1.75 to 1.75
- project_weight: bfloat16 [2, 1152, 3456], P(None, 'batch'), may hold values from -0.1875 to 0.1875
- project_bias: bfloat16 [2, 2304], P(None, 'batch'), may hold values from -1.75 to 1.75
- attend_weight: bfloat16 [2, 1152, 1152], P(None, 'batch'), may hold values from -0.75 to 0.75
- attend_bias: bfloat16 [2, 1152], P(None, 'batch'), may hold values from -1.75 to 1.75
- expand_weight: bfloat16 [2, 1152, 4608], P(None, 'batch'), may hold values from -0.1875 to 0.1875
- expand_bias: bfloat16 [2, 4608], P(None, 'batch'), may hold values from -1.75 to 1.75
- shrink_weight: bfloat16 [2, 4608, 1152], P(None, None, 'batch'), may hold values from -0.125 to 0.125
- shrink_bias: bfloat16 [2, 1152], P(None, 'batch'), may hold values from -1.75 to 1.75
- final_adaptive: bfloat16 [1152, 2304], P('batch'), may hold values from -0.1875 to 0.1875
- final_offset: bfloat16 [2304], P('batch'), may hold values from -1.75 to 1.75
- final_weight: bfloat16 [1152, 32], P('batch'), may hold values from -0.1875 to 0.1875
- final_bias: bfloat16 [32], replicated, may hold values from -3 to 3
- cotangent: bfloat16 [8, 8, 64, 64], P('batch', None, 'row', 'col'), may hold values from -6 to 6
Outputs:
- prediction: float32 [8, 8, 64, 64], P('batch', None, 'row', 'col')
- latent_grad: float32 [8, 4, 64, 64], P('batch', None, 'row', 'col')
- conditioning_grad: float32 [8, 1152], P('batch')
- patch_weight_grad: float32 [16, 1152], P(None, 'batch')
- patch_bias_grad: float32 [1152], P('batch')
- adaptive_weight_grad: float32 [2, 1152, 6912], P(None, 'batch')
- adaptive_bias_grad: float32 [2, 6912], P(None, 'batch')
- project_weight_grad: float32 [2, 1152, 3456], P(None, 'batch')
- project_bias_grad: float32 [2, 2304], P(None, 'batch')
- attend_weight_grad: float32 [2, 1152, 1152], P(None, 'batch')
- attend_bias_grad: float32 [2, 1152], P(None, 'batch')
- expand_weight_grad: float32 [2, 1152, 4608], P(None, 'batch')
- expand_bias_grad: float32 [2, 4608], P(None, 'batch')
- shrink_weight_grad: float32 [2, 4608, 1152], P(None, None, 'batch')
- shrink_bias_grad: float32 [2, 1152], P(None, 'batch')
- final_adaptive_grad: float32 [1152, 2304], P('batch')
- final_offset_grad: float32 [2304], P('batch')
- final_weight_grad: float32 [1152, 32], P('batch')
- final_bias_grad: float32 [32], replicated
The draws below stay inside these ranges and needn't reach their ends.
Inputs may be any that keep to these rules, and one draw needn't show every extreme that they name: Each row lists all 1024 tokens of its image once; the tokens that the routed block keeps are kept_index[i, j] for j < kept_count[i]. Token t lies at grid row t // 32 and column t % 32.
All inputs are finite; a program needn't handle non-finite values.
Results may differ from the reference program's by a relative error of at most 0.018.
Values may be sent and summed in bfloat16 or wider, within the bound.
A program may use at most 384 MiB of HBM per device.

```python
import jax
import jax.numpy as jnp
from jax import lax

D = 1152
HEADS = 16
FF = 4608
LAYERS = 2
IMG = 2
GRID = 32
PATCH = 2
CIN = 4
COUT = 8
LAT = 64
PIN = 16
POUT = 32
SEQ = 1024
IMAGES = 8
N_BATCH = 4


def with_ends(entries, stream_key, low, top_value):
    spot = [jax.random.randint(jax.random.fold_in(stream_key, axis), (), 0, length) for axis, length in enumerate(entries.shape)]
    main_axis = entries.shape.index(max(entries.shape))
    next_to = spot[:main_axis] + [(spot[main_axis] + 1) % entries.shape[main_axis]] + spot[main_axis + 1:]
    return entries.at[tuple(spot)].set(low).at[tuple(next_to)].set(top_value)


def level_of(rng, shape, split, smallest, high):
    gain = 1.0
    for position, blocks in split:
        steps = jax.random.uniform(jax.random.fold_in(jax.random.fold_in(rng, 6), position), (blocks,), jnp.float32, smallest / len(split), high / len(split))
        gain = gain * jnp.repeat(jnp.exp(steps), shape[position] // blocks).reshape((-1,) + (1,) * (len(shape) - 1 - position))
    return gain


def gaussian(rng, extent, width, reach, cuts=(), kind=jnp.bfloat16):
    factor_of = level_of(rng, extent, cuts, -0.22, 0.18) if cuts else 1.0
    entries = jax.random.normal(rng, extent, jnp.float32) * width * factor_of
    return jnp.minimum(jnp.maximum(entries, -reach), reach).astype(kind)


def setup_inputs(seed: int = 0) -> dict:
    arg_keys = jax.random.split(jax.random.key(seed), 22)
    return {
        "latents": gaussian(arg_keys[0], (IMAGES, CIN, LAT, LAT), 1.0, 6.0, ((0, 4), (2, 2), (3, 4))),
        "conditioning": gaussian(arg_keys[1], (IMAGES, D), 1.0, 6.0, ((0, 4),)),
        "kept_index": jax.vmap(lambda own: jax.random.permutation(own, SEQ))(jax.random.split(arg_keys[2], IMAGES)).reshape((IMAGES, SEQ)).astype(jnp.int32),
        "kept_count": with_ends(jax.random.randint(arg_keys[3], (IMAGES,), SEQ // 4, 3 * SEQ // 4 + 1), jax.random.fold_in(arg_keys[3], 1), SEQ // 4, (3 * SEQ // 4 + 1) - 1).astype(jnp.int32),
        "patch_weight": gaussian(arg_keys[4], (PIN, D), PIN ** -0.5, 1.5, ((1, 4),)),
        "patch_bias": gaussian(arg_keys[5], (D,), 0.5, 3.0, ((0, 4),)),
        "adaptive_weight": gaussian(arg_keys[6], (LAYERS, D, 6 * D), D ** -0.5, 0.1875, ((1, 4),)),
        "adaptive_bias": gaussian(arg_keys[7], (LAYERS, 6 * D), 0.3, 1.75, ((1, 4),)),
        "project_weight": gaussian(arg_keys[8], (LAYERS, D, 3 * D), D ** -0.5, 0.1875, ((1, 4),)),
        "project_bias": gaussian(arg_keys[9], (LAYERS, 2 * D), 0.3, 1.75, ((1, 4),)),
        "attend_weight": gaussian(arg_keys[10], (LAYERS, D, D), (D // 16) ** -0.5, 0.75, ((1, 4),)),
        "attend_bias": gaussian(arg_keys[11], (LAYERS, D), 0.3, 1.75, ((1, 4),)),
        "expand_weight": gaussian(arg_keys[12], (LAYERS, D, FF), D ** -0.5, 0.1875, ((1, 4),)),
        "expand_bias": gaussian(arg_keys[13], (LAYERS, FF), 0.3, 1.75, ((1, 4),)),
        "shrink_weight": gaussian(arg_keys[14], (LAYERS, FF, D), (FF // 2) ** -0.5, 0.125, ((2, 4),)),
        "shrink_bias": gaussian(arg_keys[15], (LAYERS, D), 0.3, 1.75, ((1, 4),)),
        "final_adaptive": gaussian(arg_keys[16], (D, 2 * D), D ** -0.5, 0.1875, ((0, 4),)),
        "final_offset": gaussian(arg_keys[17], (2 * D,), 0.3, 1.75, ((0, 4),)),
        "final_weight": gaussian(arg_keys[18], (D, POUT), D ** -0.5, 0.1875, ((0, 4),)),
        "final_bias": gaussian(arg_keys[19], (POUT,), 0.5, 3.0),
        "cotangent": gaussian(arg_keys[20], (IMAGES, COUT, LAT, LAT), 1.0, 6.0, ((0, 4), (2, 2), (3, 4))),
    }


@jax.custom_vjp
def low(v):
    return lax.optimization_barrier(v.astype(jnp.bfloat16)).astype(jnp.float32)

@jax.custom_vjp
def low_back(v):
    return v

def low_keep(v):
    return (low(v), None)

def low_pass(kept, grad):
    return (grad,)

def back_keep(v):
    return (v, None)

def back_low(kept, grad):
    return (low(grad),)
low.defvjp(low_keep, low_pass)
low_back.defvjp(back_keep, back_low)
highest = lax.Precision.HIGHEST
masked_score = -1e+30

def dense(left, right):
    return jnp.einsum('...k,kn->...n', left, right, precision=highest)

def sincos_part(coords, count):
    omega = 1.0 / 10000.0 ** (jnp.arange(count, dtype=jnp.float32) / count)
    angles = coords[:, None] * omega[None, :]
    return jnp.concatenate([jnp.sin(angles), jnp.cos(angles)], axis=1)

def position_table(model_width):
    coords = jnp.arange(GRID, dtype=jnp.float32)
    along = sincos_part(coords, model_width // 4)
    half_width = model_width // 2
    rows_part = jnp.broadcast_to(along[:, None, :], (GRID, GRID, half_width))
    cols_part = jnp.broadcast_to(along[None, :, :], (GRID, GRID, half_width))
    return jnp.concatenate([rows_part, cols_part], axis=2).reshape(GRID * GRID, model_width)

def modulate(resid, shift_part, scale_part):
    centered = resid - lax.optimization_barrier(jnp.mean(resid, axis=-1, keepdims=True))
    variance = lax.optimization_barrier(jnp.mean(centered * centered, axis=-1, keepdims=True))
    return centered * lax.rsqrt(variance + 1e-06) * (1.0 + scale_part) + shift_part

def attention(queries, keys_in, values_in, key_kept):
    images, length, model_width = queries.shape
    head_size = model_width // HEADS
    query_heads = queries.reshape(images, length, HEADS, head_size)
    key_heads = keys_in.reshape(images, length, HEADS, head_size)
    value_heads = values_in.reshape(images, length, HEADS, head_size)
    scores = low_back(jnp.einsum('iqhe,ikhe->ihqk', query_heads, key_heads, precision=highest) * head_size ** (-0.5))
    scores = jnp.where(key_kept[:, None, None, :], scores, masked_score)
    weights = low(jax.nn.softmax(scores, axis=-1))
    mixed = jnp.einsum('ihqk,ikhe->iqhe', weights, value_heads, precision=highest)
    return mixed.reshape(images, length, model_width)

def block_forward(resid, silu_cond, layer_weights, kept_rows, key_kept):
    adaptive_full, adaptive_offset, project_full, project_offset, attend_full, attend_offset, expand_full, expand_offset, shrink_full, shrink_offset = layer_weights
    model_width = resid.shape[-1]
    modulation = low_back(dense(silu_cond, adaptive_full) + adaptive_offset)
    pieces = [modulation[:, None, slot_number * model_width:(slot_number + 1) * model_width] for slot_number in range(6)]
    normed = low(modulate(resid, pieces[0], pieces[1]))
    projected = dense(normed, project_full)
    queries = low(low_back(projected[..., :model_width] + project_offset[:model_width]))
    keys_in = low(low_back(projected[..., model_width:2 * model_width]))
    values_in = low(low_back(projected[..., 2 * model_width:] + project_offset[model_width:]))
    mixed = low(low_back(attention(queries, keys_in, values_in, key_kept)))
    attended = low_back(dense(mixed, attend_full) + attend_offset)
    resid_mid = resid + kept_rows * pieces[2] * attended
    normed_mid = low(modulate(resid_mid, pieces[3], pieces[4]))
    hidden = low_back(dense(normed_mid, expand_full) + expand_offset)
    active = low(jax.nn.gelu(hidden, approximate=True))
    expanded = low_back(dense(active, shrink_full) + shrink_offset)
    return resid_mid + kept_rows * pieces[5] * expanded

def group_forward(params, latent_group, cond_group, rows_group, keys_group):
    patch_full, patch_offset, adaptive_stack, adaptive_offsets, project_stack, project_offsets, attend_stack, attend_offsets, expand_stack, expand_offsets, shrink_stack, shrink_offsets, final_adaptive_full, final_offset_full, final_weight_full, final_bias_full = params
    images = latent_group.shape[0]
    model_width = patch_full.shape[1]
    patches = latent_group.reshape(images, CIN, GRID, PATCH, GRID, PATCH).transpose(0, 2, 4, 3, 5, 1).reshape(images, GRID * GRID, PIN)
    resid = low_back(dense(patches, patch_full)) + patch_offset + position_table(model_width)
    silu_cond = low(jax.nn.silu(cond_group))
    every_row = jnp.ones_like(rows_group)
    every_key = jnp.ones_like(keys_group)
    for block_number in range(LAYERS):
        layer_weights = (adaptive_stack[block_number], adaptive_offsets[block_number], project_stack[block_number], project_offsets[block_number], attend_stack[block_number], attend_offsets[block_number], expand_stack[block_number], expand_offsets[block_number], shrink_stack[block_number], shrink_offsets[block_number])
        if block_number == 0:
            resid = block_forward(resid, silu_cond, layer_weights, every_row, every_key)
        else:
            resid = block_forward(resid, silu_cond, layer_weights, rows_group, keys_group)
    final_mod = low_back(dense(silu_cond, final_adaptive_full) + final_offset_full)
    normed = low(modulate(resid, final_mod[:, None, :model_width], final_mod[:, None, model_width:]))
    outputs = dense(normed, final_weight_full) + final_bias_full
    return outputs.reshape(images, GRID, GRID, PATCH, PATCH, COUT).transpose(0, 5, 1, 3, 2, 4).reshape(images, COUT, LAT, LAT)

def reference(latents, conditioning, kept_index, kept_count, patch_weight, patch_bias, adaptive_weight, adaptive_bias, project_weight, project_bias, attend_weight, attend_bias, expand_weight, expand_bias, shrink_weight, shrink_bias, final_adaptive, final_offset, final_weight, final_bias, cotangent):
    token_ids = jnp.arange(SEQ, dtype=jnp.int32)
    listed = jnp.logical_and(kept_index[:, :, None] == token_ids[None, None, :], (token_ids[None, :] < kept_count[:, None])[:, :, None])
    kept_keys = jnp.any(listed, axis=1)
    kept_rows = kept_keys.astype(jnp.float32)[:, :, None]
    params = (patch_weight.astype(jnp.float32), patch_bias.astype(jnp.float32), adaptive_weight.astype(jnp.float32), adaptive_bias.astype(jnp.float32), project_weight.astype(jnp.float32), project_bias.astype(jnp.float32), attend_weight.astype(jnp.float32), attend_bias.astype(jnp.float32), expand_weight.astype(jnp.float32), expand_bias.astype(jnp.float32), shrink_weight.astype(jnp.float32), shrink_bias.astype(jnp.float32), final_adaptive.astype(jnp.float32), final_offset.astype(jnp.float32), final_weight.astype(jnp.float32), final_bias.astype(jnp.float32))

    def whole_model(model_params, latent_values, cond_values):

        def one_group(group_items):
            return group_forward(model_params, group_items[0], group_items[1], group_items[2], group_items[3])
        stacked = lax.map(jax.checkpoint(one_group), (latent_values.reshape(N_BATCH, IMG, CIN, LAT, LAT), cond_values.reshape(N_BATCH, IMG, D), kept_rows.reshape(N_BATCH, IMG, SEQ, 1), kept_keys.reshape(N_BATCH, IMG, SEQ)))
        return stacked.reshape(IMAGES, COUT, LAT, LAT)
    prediction, pullback = jax.vjp(whole_model, params, latents.astype(jnp.float32), conditioning.astype(jnp.float32))
    param_grads, latent_grad, conditioning_grad = pullback(cotangent.astype(jnp.float32))
    patch_weight_grad, patch_bias_grad, adaptive_weight_grad, adaptive_bias_grad, project_weight_grad, project_bias_grad, attend_weight_grad, attend_bias_grad, expand_weight_grad, expand_bias_grad, shrink_weight_grad, shrink_bias_grad, final_adaptive_grad, final_offset_grad, final_weight_grad, final_bias_grad = param_grads
    return (prediction, latent_grad, conditioning_grad, patch_weight_grad, patch_bias_grad, adaptive_weight_grad, adaptive_bias_grad, project_weight_grad, project_bias_grad, attend_weight_grad, attend_bias_grad, expand_weight_grad, expand_bias_grad, shrink_weight_grad, shrink_bias_grad, final_adaptive_grad, final_offset_grad, final_weight_grad, final_bias_grad)
```

```python
import jax
import jax.numpy as jnp
from jax import lax
from jax.sharding import PartitionSpec as P

HEADS = 16
PATCH = 2
LANES = 128
PLANE = ("row", "col")

norm_epsilon = 1e-06
masked_score = -1e30
f32 = jnp.float32
bf16 = jnp.bfloat16


def to_tokens(planes, patch_side):
    images, channels, height, breadth = planes.shape
    shaped = planes.reshape(
        images, channels, height // patch_side, patch_side, breadth // patch_side, patch_side
    )
    return shaped.transpose(0, 2, 4, 3, 5, 1).reshape(
        images, height // patch_side * (breadth // patch_side), patch_side * patch_side * channels
    )


def to_planes(token_rows, patch_side, channels, rows_tile, cols_tile):
    images = token_rows.shape[0]
    shaped = token_rows.reshape(images, rows_tile, cols_tile, patch_side, patch_side, channels)
    return shaped.transpose(0, 5, 1, 3, 2, 4).reshape(
        images, channels, rows_tile * patch_side, cols_tile * patch_side
    )


def dot(left, right, dims, precision=None):
    return lax.dot_general(left, right, (dims, ((), ())), precision=precision, preferred_element_type=f32)


def norm_parts(resid):
    centered = resid - jnp.mean(resid, axis=-1, keepdims=True)
    rstd = lax.rsqrt(jnp.mean(centered * centered, axis=-1, keepdims=True) + norm_epsilon)
    return centered * rstd, rstd


def modulate(resid, shift_part, scale_part):
    return norm_parts(resid)[0] * (1.0 + scale_part) + shift_part


def modulate_back(resid, scale_part, grad):
    unit, rstd = norm_parts(resid)
    inner = grad * (1.0 + scale_part)
    grad_in = rstd * (
        inner
        - jnp.mean(inner, axis=-1, keepdims=True)
        - unit * jnp.mean(inner * unit, axis=-1, keepdims=True)
    )
    return grad_in, jnp.sum(grad, axis=1), jnp.sum(grad * unit, axis=1)


def gather_tokens(local):
    full = lax.all_gather(local, PLANE, axis=1)
    return full.reshape(local.shape[0], -1, local.shape[-1])


def scatter_tokens(partial, length):
    low = partial.astype(bf16)
    return lax.psum_scatter(low, PLANE, scatter_dimension=1, tiled=True).astype(f32)


def attention_forward(normed, weights, key_mask):
    project, project_bias, attend = weights
    full = gather_tokens(normed)
    images, length, _ = full.shape
    width = project.shape[1] // 3
    heads = width // LANES
    projected = (jnp.einsum("isd,dn->isn", full, project, preferred_element_type=f32) + project_bias).astype(bf16)
    queries, keys, values = (
        projected[..., part * width : (part + 1) * width].reshape(images, length, heads, LANES)
        for part in range(3)
    )
    factor = HEAD_SIZE ** (-0.5)
    scores = jnp.einsum("ishe,iuhe->ihsu", queries, keys, preferred_element_type=f32) * factor
    if key_mask is not None:
        scores = jnp.where(key_mask[:, None, None, :], scores, masked_score)
    peak = jnp.max(scores, axis=-1, keepdims=True)
    log_total = peak + jnp.log(jnp.sum(jnp.exp(scores - peak), axis=-1, keepdims=True))
    probs = jnp.exp(scores - log_total).astype(bf16)
    mixed = jnp.einsum("ihsu,iuhe->ishe", probs, values, preferred_element_type=f32)
    mixed = mixed.astype(bf16).reshape(images, length, width)
    partial = jnp.einsum("isn,nd->isd", mixed, attend, preferred_element_type=f32)
    attended = scatter_tokens(partial, normed.shape[1])
    return attended, (full, queries, keys, values, mixed, log_total)


def attention_backward(grad_attended, weights, key_mask, saved):
    project, _, attend = weights
    normed, queries, keys, values, mixed, log_total = saved
    images, length, heads, _ = queries.shape
    full = gather_tokens(grad_attended)
    grad_attend = jnp.einsum("isn,isd->nd", mixed, full, preferred_element_type=f32)
    grad_attend_bias = jnp.sum(full.astype(f32), axis=(0, 1))
    grad_mixed = jnp.einsum("isd,nd->isn", full, attend, preferred_element_type=f32).astype(bf16)
    grad_heads = grad_mixed.reshape(queries.shape)
    factor = HEAD_SIZE ** (-0.5)
    scores = jnp.einsum("ishe,iuhe->ihsu", queries, keys, preferred_element_type=f32) * factor
    if key_mask is not None:
        scores = jnp.where(key_mask[:, None, None, :], scores, masked_score)
    probs = jnp.exp(scores - log_total)
    dprobs = jnp.einsum("ishe,iuhe->ihsu", grad_heads, values, preferred_element_type=f32)
    row_dot = jnp.sum(probs * dprobs, axis=-1, keepdims=True)
    grad_scores = (probs * (dprobs - row_dot)).astype(bf16)
    grad_queries = jnp.einsum("ihsu,iuhe->ishe", grad_scores, keys, preferred_element_type=f32) * factor
    grad_keys = jnp.einsum("ihsu,ishe->iuhe", grad_scores, queries, preferred_element_type=f32) * factor
    grad_values = jnp.einsum("ihsu,ishe->iuhe", probs.astype(bf16), grad_heads, preferred_element_type=f32)
    grad_projected = jnp.concatenate(
        [part.astype(bf16).reshape(images, length, -1) for part in (grad_queries, grad_keys, grad_values)], axis=-1
    )
    grad_project = jnp.einsum("isd,isn->dn", normed, grad_projected, preferred_element_type=f32)
    grad_project_bias = jnp.sum(grad_projected.astype(f32), axis=(0, 1))
    partial = jnp.einsum("isn,dn->isd", grad_projected, project, preferred_element_type=f32)
    grad_normed = scatter_tokens(partial, grad_attended.shape[1])
    return grad_normed, grad_project, grad_project_bias, grad_attend, grad_attend_bias


def mlp_forward(normed, weights):
    expand, expand_bias, shrink = weights
    full = gather_tokens(normed)
    hidden = jnp.einsum("isd,dn->isn", full, expand, preferred_element_type=f32) + expand_bias
    active = jax.nn.gelu(hidden, approximate=True).astype(bf16)
    partial = jnp.einsum("isn,nd->isd", active, shrink, preferred_element_type=f32)
    return scatter_tokens(partial, normed.shape[1]), (full, hidden)


def mlp_backward(grad_expanded, weights, saved):
    expand, _, shrink = weights
    normed, hidden = saved
    full = gather_tokens(grad_expanded)
    active, pull = jax.vjp(lambda h: jax.nn.gelu(h, approximate=True), hidden)
    grad_shrink = jnp.einsum("isn,isd->nd", active.astype(bf16), full, preferred_element_type=f32)
    grad_shrink_bias = jnp.sum(full.astype(f32), axis=(0, 1))
    grad_active = jnp.einsum("isd,nd->isn", full, shrink, preferred_element_type=f32)
    grad_hidden = pull(grad_active)[0].astype(bf16)
    grad_expand = jnp.einsum("isd,isn->dn", normed, grad_hidden, preferred_element_type=f32)
    grad_expand_bias = jnp.sum(grad_hidden.astype(f32), axis=(0, 1))
    partial = jnp.einsum("isn,dn->isd", grad_hidden, expand, preferred_element_type=f32)
    grad_normed = scatter_tokens(partial, grad_expanded.shape[1])
    return grad_normed, grad_expand, grad_expand_bias, grad_shrink, grad_shrink_bias


HEAD_SIZE = 72


def pad_heads(array, axis):
    shape = array.shape
    heads = shape[axis] // HEAD_SIZE
    split = array.reshape(shape[:axis] + (heads, HEAD_SIZE) + shape[axis + 1 :])
    widths = [(0, 0)] * split.ndim
    widths[axis + 1] = (0, LANES - HEAD_SIZE)
    return jnp.pad(split, widths).reshape(shape[:axis] + (heads * LANES,) + shape[axis + 1 :])


def unpad_heads(array, axis):
    shape = array.shape
    heads = shape[axis] // LANES
    split = array.reshape(shape[:axis] + (heads, LANES) + shape[axis + 1 :])
    kept = lax.slice_in_dim(split, 0, HEAD_SIZE, axis=axis + 1)
    return kept.reshape(shape[:axis] + (heads * HEAD_SIZE,) + shape[axis + 1 :])


def gather_small(arrays, dims):
    flat = jnp.concatenate([array.reshape(-1) for array in arrays])
    every = lax.all_gather(flat, "batch", axis=0)
    out = []
    start = 0
    for array, dim in zip(arrays, dims):
        piece = every[:, start : start + array.size].reshape((-1,) + array.shape)
        start += array.size
        piece = jnp.moveaxis(piece, 0, dim)
        shape = list(array.shape)
        shape[dim] = -1
        out.append(piece.reshape(shape))
    return out


def body(
    latents,
    conditioning,
    kept_index,
    kept_count,
    patch_weight,
    patch_bias,
    adaptive_weight,
    adaptive_bias,
    project_weight,
    project_bias,
    attend_weight,
    attend_bias,
    expand_weight,
    expand_bias,
    shrink_weight,
    shrink_bias,
    final_adaptive,
    final_offset,
    final_weight,
    final_bias,
    cotangent,
):
    rows, cols, ranks = lax.axis_size("row"), lax.axis_size("col"), lax.axis_size("batch")
    team = rows * cols
    place = lax.axis_index("row") * cols + lax.axis_index("col")
    rank = lax.axis_index("batch")
    images, channels_in = latents.shape[:2]
    channels_out = cotangent.shape[1]
    rows_tile, cols_tile = latents.shape[2] // PATCH, latents.shape[3] // PATCH
    tile_tokens = rows_tile * cols_tile
    sequence = tile_tokens * team
    width = conditioning.shape[1]
    depth = adaptive_weight.shape[0]
    shard = adaptive_weight.shape[1]
    kept_local = tile_tokens * 3 // 4
    highest = lax.Precision.HIGHEST

    head_cols = width // team
    hidden_cols = expand_weight.shape[2] // team

    def slice_of(array, axis, count):
        return lax.dynamic_slice_in_dim(array, place * count, count, axis=axis)

    blocks = []
    for b in range(depth):
        project_own = lax.dynamic_index_in_dim(
            project_weight[b].reshape(shard, 3, team, head_cols), place, axis=2, keepdims=False
        )
        project_full = lax.all_gather(project_own, "batch", axis=0, tiled=True)
        gap = jnp.zeros((head_cols, width), bf16)
        padded = jnp.concatenate([gap, attend_weight[b], gap], axis=0)
        start = jnp.clip(place * head_cols - rank * shard + head_cols, 0, shard + head_cols)
        attend_full = lax.psum(lax.dynamic_slice_in_dim(padded, start, head_cols, axis=0), "batch")
        expand_full = lax.all_gather(slice_of(expand_weight[b], 1, hidden_cols), "batch", axis=0, tiled=True)
        shrink_full = lax.all_gather(slice_of(shrink_weight[b], 0, hidden_cols), "batch", axis=1, tiled=True)
        blocks.append(
            (
                pad_heads(project_full, 2).reshape(width, -1),
                pad_heads(attend_full, 0),
                expand_full,
                shrink_full,
            )
        )

    (
        patch_full,
        patch_bias_full,
        adaptive_offset,
        project_offset,
        attend_offset,
        expand_offset,
        shrink_offset,
        final_offset_full,
        final_full,
        cond_all,
    ) = gather_small(
        [
            patch_weight,
            patch_bias,
            adaptive_bias,
            project_bias,
            attend_bias,
            expand_bias,
            shrink_bias,
            final_offset,
            final_weight,
            conditioning,
        ],
        [1, 0, 1, 1, 1, 1, 1, 0, 0, 0],
    )

    patch_tiles = to_tokens(latents, PATCH)
    grad_tiles = to_tokens(cotangent, PATCH)
    patch_in, patch_out = patch_tiles.shape[2], grad_tiles.shape[2]
    tiles = lax.all_gather(jnp.concatenate([patch_tiles, grad_tiles], axis=2), PLANE, axis=1)
    whole = tiles.reshape(images, rows, cols, rows_tile, cols_tile, -1).transpose(0, 1, 3, 2, 4, 5)
    whole = whole.reshape(images, sequence, patch_in + patch_out)
    grid_cols = cols * cols_tile
    own_ids = lax.dynamic_index_in_dim(
        kept_index.reshape(images, tile_tokens, team), place, axis=2, keepdims=False
    )
    pick = (own_ids[:, :, None] == jnp.arange(sequence, dtype=jnp.int32)).astype(bf16)
    own = jnp.einsum("ikt,itc->ikc", pick, whole, preferred_element_type=f32).astype(bf16)
    patches, grad_outputs = own[..., :patch_in], own[..., patch_in:]
    order = jnp.arange(kept_local, dtype=jnp.int32)[:, None] * team + jnp.arange(team, dtype=jnp.int32)
    kept_grid = order[None] < kept_count[:, None, None]
    key_mask = kept_grid.transpose(0, 2, 1).reshape(images, team * kept_local)
    kept_rows = lax.dynamic_index_in_dim(kept_grid, place, axis=2, keepdims=False).astype(f32)[:, :, None]

    count = width // 4
    omega = 1.0 / 10000.0 ** (jnp.arange(count, dtype=f32) / count)
    angles = jnp.arange(max(rows * rows_tile, grid_cols), dtype=f32)[:, None] * omega[None, :]
    along = jnp.concatenate([jnp.sin(angles), jnp.cos(angles)], axis=1)
    places = jnp.arange(along.shape[0], dtype=jnp.int32)

    def position_of(coords):
        chosen = (coords[..., None] == places).astype(f32)
        return jnp.einsum("ikt,tc->ikc", chosen, along, precision=highest)

    position = jnp.concatenate(
        [position_of(own_ids // grid_cols), position_of(own_ids % grid_cols)], axis=-1
    )
    resid = (
        jnp.einsum("ikc,cd->ikd", patches, patch_full, preferred_element_type=f32)
        + patch_bias_full.astype(f32)
        + position
    )

    silu_all = jax.nn.silu(cond_all.astype(f32)).astype(bf16)
    silu_rows = lax.dynamic_slice_in_dim(silu_all, rank * shard, shard, axis=1)
    mod_cols, final_cols = adaptive_weight.shape[2] // team, final_adaptive.shape[1] // team
    parts = [
        dot(silu_rows, slice_of(adaptive_weight[b], 1, mod_cols), ((1,), (0,))) for b in range(depth)
    ] + [dot(silu_rows, slice_of(final_adaptive, 1, final_cols), ((1,), (0,)))]
    mods = lax.psum_scatter(jnp.concatenate(parts, axis=1), "batch", scatter_dimension=0, tiled=True)
    mods = lax.all_gather(mods, PLANE, axis=1)
    pieces = []
    for b in range(depth):
        block_mod = mods[:, :, b * mod_cols : (b + 1) * mod_cols].reshape(images, -1)
        block_mod = (block_mod + adaptive_offset[b].astype(f32)).reshape(images, 6, 1, width)
        pieces.append([block_mod[:, s] for s in range(6)])
    final_mod = mods[:, :, depth * mod_cols :].reshape(images, -1) + final_offset_full.astype(f32)
    final_mod = final_mod.reshape(images, 2, 1, width)
    final_shift, final_scale = final_mod[:, 0], final_mod[:, 1]

    records = []
    for b in range(depth):
        project, attend, expand, shrink = blocks[b]
        shift1, scale1, gate1, shift2, scale2, gate2 = pieces[b]
        bias = project_offset[b].astype(f32).reshape(2, team, head_cols)
        bias = lax.dynamic_index_in_dim(bias, place, axis=1, keepdims=False)
        bias = pad_heads(jnp.stack([bias[0], jnp.zeros_like(bias[0]), bias[1]]), 1).reshape(-1)
        attention_weights = (project, bias, attend)
        mlp_weights = (expand, slice_of(expand_offset[b].astype(f32), 0, hidden_cols), shrink)
        routed = b > 0
        mask = key_mask if routed else None
        base = resid[:, :kept_local] if routed else resid
        gate_rows = kept_rows if routed else 1.0
        normed = modulate(base, shift1, scale1).astype(bf16)
        attended, attention_saved = attention_forward(normed, attention_weights, mask)
        attended = attended + attend_offset[b].astype(f32)
        mid = base + gate_rows * gate1 * attended
        normed_mid = modulate(mid, shift2, scale2).astype(bf16)
        expanded, mlp_saved = mlp_forward(normed_mid, mlp_weights)
        expanded = expanded + shrink_offset[b].astype(f32)
        after = mid + gate_rows * gate2 * expanded
        records.append((base, mid, attended, expanded, attention_weights, mlp_weights, mask, gate_rows, attention_saved, mlp_saved))
        resid = jnp.concatenate([after, resid[:, kept_local:]], axis=1) if routed else after

    final_normed = modulate(resid, final_shift, final_scale).astype(bf16)
    outputs = jnp.einsum("ikd,dc->ikc", final_normed, final_full, preferred_element_type=f32) + final_bias.astype(f32)
    final_bias_term = jnp.sum(grad_outputs.astype(f32), axis=(0, 1))
    final_weight_term = jnp.einsum("ikd,ikc->dc", final_normed, grad_outputs, preferred_element_type=f32)
    grad_final = jnp.einsum("ikc,dc->ikd", grad_outputs, final_full, preferred_element_type=f32)
    grad_resid, grad_final_shift, grad_final_scale = modulate_back(resid, final_scale, grad_final)
    final_mod_term = jnp.stack([grad_final_shift, grad_final_scale], axis=1)

    mod_terms = [None] * depth
    block_grads = [None] * depth
    for b in reversed(range(depth)):
        base, mid, attended, expanded, attention_weights, mlp_weights, mask, gate_rows, attention_saved, mlp_saved = records[b]
        shift1, scale1, gate1, shift2, scale2, gate2 = pieces[b]
        routed = b > 0
        grad_after = grad_resid[:, :kept_local] if routed else grad_resid
        gated = gate_rows * grad_after
        grad_gate2 = jnp.sum(gated * expanded, axis=1)
        grad_expanded = (gated * gate2).astype(bf16)
        grad_normed_mid, grad_expand, grad_expand_bias, grad_shrink, grad_shrink_bias = mlp_backward(
            grad_expanded, mlp_weights, mlp_saved
        )
        grad_mid, grad_shift2, grad_scale2 = modulate_back(mid, scale2, grad_normed_mid)
        grad_mid = grad_mid + grad_after
        gated = gate_rows * grad_mid
        grad_gate1 = jnp.sum(gated * attended, axis=1)
        grad_attended = (gated * gate1).astype(bf16)
        grad_normed, grad_project, grad_project_bias, grad_attend, grad_attend_bias = attention_backward(
            grad_attended, attention_weights, mask, attention_saved
        )
        grad_base, grad_shift1, grad_scale1 = modulate_back(base, scale1, grad_normed)
        grad_base = grad_base + grad_mid
        grad_resid = jnp.concatenate([grad_base, grad_resid[:, kept_local:]], axis=1) if routed else grad_base
        mod_terms[b] = jnp.stack(
            [grad_shift1, grad_scale1, grad_gate1, grad_shift2, grad_scale2, grad_gate2], axis=1
        )
        grad_project = unpad_heads(grad_project.reshape(width, 3, -1), 2).astype(bf16)
        grad_project = lax.psum_scatter(grad_project, "batch", scatter_dimension=0, tiled=True)
        grad_project = lax.all_gather(grad_project, PLANE, axis=2).reshape(shard, -1)
        grad_attend = lax.psum(unpad_heads(grad_attend, 0).astype(bf16), "batch")
        grad_attend = lax.all_gather(grad_attend, PLANE, axis=0, tiled=True)
        grad_attend = lax.dynamic_slice_in_dim(grad_attend, rank * shard, shard, axis=0)
        grad_expand = lax.psum_scatter(grad_expand.astype(bf16), "batch", scatter_dimension=0, tiled=True)
        grad_expand = lax.all_gather(grad_expand, PLANE, axis=1, tiled=True)
        grad_shrink = lax.psum_scatter(grad_shrink.astype(bf16), "batch", scatter_dimension=1, tiled=True)
        grad_shrink = lax.all_gather(grad_shrink, PLANE, axis=0, tiled=True)
        grad_bias = unpad_heads(grad_project_bias.reshape(3, -1), 1)
        grad_bias = jnp.stack([grad_bias[0], grad_bias[2]])
        block_grads[b] = (
            grad_project.astype(f32),
            grad_attend.astype(f32),
            grad_expand.astype(f32),
            grad_shrink.astype(f32),
            grad_bias,
            grad_attend_bias,
            grad_expand_bias,
            grad_shrink_bias,
        )

    mod_all = jnp.concatenate([jnp.stack(mod_terms, axis=1).reshape(images, -1), final_mod_term.reshape(images, -1)], axis=1)
    mod_low = lax.psum(mod_all, PLANE).astype(bf16)
    mod_every = lax.all_gather(mod_low, "batch", axis=0, tiled=True)
    mod_width = adaptive_weight.shape[2]
    block_mods = [mod_every[:, b * mod_width : (b + 1) * mod_width] for b in range(depth)]
    final_mods = mod_every[:, depth * mod_width :]
    adaptive_weight_grad = jnp.stack([dot(silu_rows, m, ((0,), (0,))) for m in block_mods])
    final_adaptive_grad = dot(silu_rows, final_mods, ((0,), (0,)))
    mod_sum = jnp.sum(mod_every.astype(f32), axis=0)
    offset_cols, final_offset_cols = adaptive_bias.shape[1], final_offset.shape[0]
    adaptive_bias_grad = lax.dynamic_slice_in_dim(
        mod_sum[: depth * mod_width].reshape(depth, mod_width), rank * offset_cols, offset_cols, axis=1
    )
    final_offset_grad = lax.dynamic_slice_in_dim(
        mod_sum[depth * mod_width :], rank * final_offset_cols, final_offset_cols
    )
    grad_silu = dot(final_mods, final_adaptive, ((1,), (1,)))
    for b in range(depth):
        grad_silu = grad_silu + dot(block_mods[b], adaptive_weight[b], ((1,), (1,)))
    grad_silu = lax.all_to_all(grad_silu.reshape(ranks, images, shard), "batch", 0, 0)
    grad_silu = grad_silu.transpose(1, 0, 2).reshape(images, width)
    conditioning_grad = jax.vjp(jax.nn.silu, conditioning.astype(f32))[1](grad_silu)[0]

    patch_bias_term = jnp.sum(grad_resid, axis=(0, 1))
    grad_embed = grad_resid.astype(bf16)
    patch_term = jnp.einsum("ikc,ikd->cd", patches, grad_embed, preferred_element_type=f32)
    grad_patches = jnp.einsum("ikd,cd->ikc", grad_embed, patch_full, preferred_element_type=f32)
    ordered = lax.all_gather(jnp.concatenate([outputs, grad_patches], axis=2), PLANE, axis=2)
    ordered = ordered.reshape(images, sequence, patch_out + patch_in)
    tile_rows = lax.axis_index("row") * rows_tile + jnp.arange(rows_tile, dtype=jnp.int32)
    tile_cols = lax.axis_index("col") * cols_tile + jnp.arange(cols_tile, dtype=jnp.int32)
    tile_ids = (tile_rows[:, None] * grid_cols + tile_cols).reshape(-1)
    back = (kept_index[:, None, :] == tile_ids[None, :, None]).astype(f32)
    tile_out = jnp.einsum("itj,ijc->itc", back, ordered, precision=highest)
    prediction = to_planes(tile_out[..., :patch_out], PATCH, channels_out, rows_tile, cols_tile)
    latent_grad = to_planes(tile_out[..., patch_out:], PATCH, channels_in, rows_tile, cols_tile)

    def scattered(full, axis, parted):
        return lax.psum_scatter(full, "batch", scatter_dimension=axis, tiled=True) if parted else full

    token_sums = lax.psum(
        (patch_term, patch_bias_term, final_weight_term, final_bias_term), ("batch", "row", "col")
    )
    patch_weight_grad = lax.dynamic_slice_in_dim(token_sums[0], rank * shard, shard, axis=1)
    patch_bias_grad = lax.dynamic_slice_in_dim(token_sums[1], rank * shard, shard)
    final_weight_grad = lax.dynamic_slice_in_dim(token_sums[2], rank * shard, shard, axis=0)
    final_bias_grad = token_sums[3]
    stacked = [jnp.stack([block_grads[b][n] for b in range(depth)]) for n in range(8)]
    bias_sums = lax.psum((stacked[4], stacked[5], stacked[6], stacked[7]), "batch")
    project_sum = lax.all_gather(bias_sums[0], PLANE, axis=2).reshape(depth, -1)
    expand_sum = lax.all_gather(bias_sums[2], PLANE, axis=1, tiled=True)

    def rank_part(full):
        part = full.shape[1] // ranks
        return lax.dynamic_slice_in_dim(full, rank * part, part, axis=1)

    return (
        prediction,
        latent_grad,
        conditioning_grad,
        patch_weight_grad,
        patch_bias_grad,
        adaptive_weight_grad,
        adaptive_bias_grad,
        stacked[0],
        rank_part(project_sum),
        stacked[1],
        rank_part(bias_sums[1]),
        stacked[2],
        rank_part(expand_sum),
        stacked[3],
        rank_part(bias_sums[3]),
        final_adaptive_grad,
        final_offset_grad,
        final_weight_grad,
        final_bias_grad,
    )


def solution(mesh):
    tokens = P("batch", None, "row", "col")
    placed = (
        tokens,
        P("batch", None),
        P("batch", None),
        P("batch"),
        P(None, "batch"),
        P("batch"),
        P(None, "batch", None),
        P(None, "batch"),
        P(None, "batch", None),
        P(None, "batch"),
        P(None, "batch", None),
        P(None, "batch"),
        P(None, "batch", None),
        P(None, "batch"),
        P(None, None, "batch"),
        P(None, "batch"),
        P("batch", None),
        P("batch"),
        P("batch", None),
        P(),
        tokens,
    )
    return jax.shard_map(
        body,
        mesh=mesh,
        in_specs=placed,
        out_specs=(tokens, tokens, P("batch", None)) + placed[4:16] + (placed[16], P("batch"), P("batch", None), P()),
        check_vma=False,
    )
```

```python
import jax
import jax.numpy as jnp
from jax import lax
from jax.experimental import pallas as pl
from jax.experimental.pallas import tpu as pltpu
from jax.sharding import PartitionSpec as P

HEADS = 16
PATCH = 2
LANES = 128
PLANE = ("row", "col")

norm_epsilon = 1e-06
masked_score = -1e30
f32 = jnp.float32
bf16 = jnp.bfloat16


def to_tokens(planes, patch_side):
    images, channels, height, breadth = planes.shape
    shaped = planes.reshape(
        images, channels, height // patch_side, patch_side, breadth // patch_side, patch_side
    )
    return shaped.transpose(0, 2, 4, 3, 5, 1).reshape(
        images, height // patch_side * (breadth // patch_side), patch_side * patch_side * channels
    )


def to_planes(token_rows, patch_side, channels, rows_tile, cols_tile):
    images = token_rows.shape[0]
    shaped = token_rows.reshape(images, rows_tile, cols_tile, patch_side, patch_side, channels)
    return shaped.transpose(0, 5, 1, 3, 2, 4).reshape(
        images, channels, rows_tile * patch_side, cols_tile * patch_side
    )


def dot(left, right, dims, precision=None):
    return lax.dot_general(left, right, (dims, ((), ())), precision=precision, preferred_element_type=f32)


def norm_parts(resid):
    centered = resid - jnp.mean(resid, axis=-1, keepdims=True)
    rstd = lax.rsqrt(jnp.mean(centered * centered, axis=-1, keepdims=True) + norm_epsilon)
    return centered * rstd, rstd


def modulate(resid, shift_part, scale_part):
    return norm_parts(resid)[0] * (1.0 + scale_part) + shift_part


def modulate_back(resid, scale_part, grad):
    unit, rstd = norm_parts(resid)
    inner = grad * (1.0 + scale_part)
    grad_in = rstd * (
        inner
        - jnp.mean(inner, axis=-1, keepdims=True)
        - unit * jnp.mean(inner * unit, axis=-1, keepdims=True)
    )
    return grad_in, jnp.sum(grad, axis=1), jnp.sum(grad * unit, axis=1)


def sides():
    row, col = lax.axis_index("row"), lax.axis_index("col")
    core = lax.rem(col, 2)
    across = col // 2
    chip = row * 2 + across
    chips = {
        "own": chip,
        "x": (1 - row) * 2 + across,
        "y": row * 2 + 1 - across,
        "far": (1 - row) * 2 + 1 - across,
    }
    address = {
        "x": {"row": 1 - row},
        "y": {"col": lax.rem(col + 2, 4)},
        "core": {"col": col + 1 - 2 * core},
    }
    return core, chips, address


def greet(address):
    barrier = pltpu.get_barrier_semaphore()
    for who in address.values():
        pl.semaphore_signal(barrier, inc=1, device_id=who, device_id_type=pl.DeviceIdType.MESH)
    pl.semaphore_wait(barrier, len(address))


class Copies:
    def __init__(self, send, recv, address):
        self.send, self.recv, self.address = send, recv, address
        self.started = {}

    def go(self, slot, source, target, who):
        copy = pltpu.make_async_remote_copy(
            src_ref=source,
            dst_ref=target,
            send_sem=self.send.at[slot],
            recv_sem=self.recv.at[slot],
            device_id=self.address[who],
            device_id_type=pl.DeviceIdType.MESH,
        )
        copy.start()
        self.started[slot] = copy

    def arrived(self, *slots):
        for slot in slots:
            self.started[slot].wait_recv()

    def drain(self):
        for copy in self.started.values():
            copy.wait_send()


class Gather(Copies):
    def __init__(self, full, send, recv, place):
        core, chips, address = place
        super().__init__(send, recv, address)
        self.full, self.half = full, full.shape[1] // 2
        self.at = {name: core * 4 + chip for name, chip in chips.items()}

    def whole(self, name):
        return self.full.at[self.at[name]]

    def part(self, name, second):
        return self.full.at[self.at[name], pl.ds(self.half * second, self.half)]

    def first(self):
        own = self.whole("own")
        self.go(0, own, own, "x")
        self.go(1, own, own, "y")
        self.go(2, own, own, "core")

    def second(self):
        self.arrived(0)
        self.go(3, self.part("x", 0), self.part("x", 0), "y")
        self.arrived(1)
        self.go(4, self.part("y", 1), self.part("y", 1), "x")
        self.go(5, self.whole("x"), self.whole("x"), "core")
        self.go(6, self.whole("y"), self.whole("y"), "core")

    def finish(self):
        self.arrived(3, 4)
        self.go(7, self.whole("far"), self.whole("far"), "core")
        self.arrived(2, 5, 6, 7)


class Scatter(Copies):
    def __init__(self, core_out, core_in, total, hop_out, hop_in, send, recv, place):
        _, self.chips, address = place
        super().__init__(send, recv, address)
        self.core_out, self.core_in, self.total = core_out, core_in, total
        self.hop_out, self.hop_in = hop_out, hop_in
        self.half = total.shape[1] // 2

    def cross(self):
        self.go(0, self.core_out, self.core_in, "core")

    def hop(self, slot, value, who):
        self.hop_out[slot] = value.astype(bf16)
        self.go(1 + slot, self.hop_out.at[slot], self.hop_in.at[slot], who)

    def first(self):
        self.arrived(0)
        half = self.half

        def summed(name):
            chip = self.chips[name]
            return self.total[chip] + self.core_in[chip].astype(f32)

        far = summed("far")
        self.hop(0, far[:half], "x")
        self.hop(2, far[half:], "y")
        x_sum = summed("x")
        self.hop(1, x_sum[:half], "x")
        self.total[self.chips["x"], half:] = x_sum[half:]
        y_sum = summed("y")
        self.hop(3, y_sum[half:], "y")
        self.total[self.chips["y"], :half] = y_sum[:half]

    def second(self):
        half = self.half
        self.arrived(1)
        self.hop(4, self.total[self.chips["y"], :half] + self.hop_in[0].astype(f32), "y")
        self.arrived(3)
        self.hop(5, self.total[self.chips["x"], half:] + self.hop_in[2].astype(f32), "x")

    def finish(self):
        self.arrived(2, 4, 5, 6)
        half, own = self.half, self.chips["own"]
        base = self.total[own] + self.core_in[own].astype(f32)
        low = base[:half] + self.hop_in[1].astype(f32) + self.hop_in[4].astype(f32)
        high = base[half:] + self.hop_in[3].astype(f32) + self.hop_in[5].astype(f32)
        return jnp.concatenate([low, high], axis=0)


def comm_scratch(images, length, width):
    half = length // 2
    return [
        pltpu.VMEM((images, 4, length, width), bf16),
        pltpu.VMEM((images, 4, length, width), bf16),
        pltpu.VMEM((images, 4, length, width), f32),
        pltpu.VMEM((images, 6, half, width), bf16),
        pltpu.VMEM((images, 6, half, width), bf16),
        pltpu.SemaphoreType.DMA((images, 8)),
        pltpu.SemaphoreType.DMA((images, 8)),
        pltpu.SemaphoreType.DMA((images, 7)),
        pltpu.SemaphoreType.DMA((images, 7)),
    ]


def exchanges(full, comm, place):
    core_out, core_in, total, hop_out, hop_in, gs, gr, ss, sr = comm
    images = full.shape[0]
    gathers = [Gather(full.at[i], gs.at[i], gr.at[i], place) for i in range(images)]
    scatters = [
        Scatter(
            core_out.at[i], core_in.at[i], total.at[i], hop_out.at[i], hop_in.at[i], ss.at[i], sr.at[i], place
        )
        for i in range(images)
    ]
    return gathers, scatters


def flat(value):
    return value.reshape(value.shape[0] * value.shape[1], value.shape[2])


def halves(core):
    return ((1 - core) * 4, True), (core * 4, False)


def keep_partial(partial, scatter, sibling):
    shape = scatter.total.shape
    if sibling:
        scatter.core_out[...] = partial.astype(bf16).reshape(shape)
        scatter.cross()
    else:
        scatter.total[...] = partial.reshape(shape)


def column_sum(value):
    return jnp.sum(value, axis=0, keepdims=True)


def row_sums(value):
    ones = jnp.ones((8, value.shape[0]), bf16)
    return dot(ones, value, ((1,), (0,)))


GELU_ROOT = 0.7978845608028654
GELU_CUBE = 0.044715
NN, NT, TN = ((1,), (0,)), ((1,), (1,)), ((0,), (0,))


def gelu(hidden):
    inner = GELU_ROOT * (hidden + GELU_CUBE * (hidden * hidden * hidden))
    return 0.5 * hidden * (1.0 + jnp.tanh(inner))


def gelu_with_slope(hidden):
    square = hidden * hidden
    bend = jnp.tanh(GELU_ROOT * hidden * (1.0 + GELU_CUBE * square))
    rise = 0.5 * (1.0 + bend)
    slope = rise + 0.5 * hidden * (1.0 - bend * bend) * (GELU_ROOT + 3.0 * GELU_ROOT * GELU_CUBE * square)
    return hidden * rise, slope


def modulate_back_rows(resid, scale_part, grad):
    unit, rstd = norm_parts(resid)
    inner = grad * (1.0 + scale_part)
    grad_in = rstd * (
        inner
        - jnp.mean(inner, axis=-1, keepdims=True)
        - unit * jnp.mean(inner * unit, axis=-1, keepdims=True)
    )
    return grad_in, column_sum(grad), column_sum(grad * unit)


def call(kernel, name, ident, outs, scratch, flops, *args):
    vmem = pl.BlockSpec(memory_space=pltpu.VMEM)
    moved = sum(a.size * a.dtype.itemsize for a in args) + sum(o.size * o.dtype.itemsize for o in outs)
    return pl.pallas_call(
        kernel,
        name=name,
        out_shape=outs,
        in_specs=[vmem] * len(args),
        out_specs=[vmem] * len(outs),
        scratch_shapes=scratch,
        compiler_params=pltpu.CompilerParams(
            collective_id=ident, has_side_effects=True, vmem_limit_bytes=60 * 2**20
        ),
        cost_estimate=pl.CostEstimate(flops=flops, bytes_accessed=moved, transcendentals=0),
    )(*args)


def shaped(shape, kind):
    return jax.ShapeDtypeStruct(shape, kind)


def mlp_forward_kernel(
    mid, gate_rows, vecs, expand, expand_bias, shrink, full, hidden, expanded, after, *comm
):
    place = sides()
    core, chips, address = place
    images = full.shape[0]
    gathers, scatters = exchanges(full, comm, place)
    greet(address)
    own = core * 4 + chips["own"]

    def begin(i):
        full[i, own] = modulate(mid[i], vecs[i, 0:1], vecs[i, 1:2]).astype(bf16)
        gathers[i].first()

    def compute(i, between):
        for step, (start, sibling) in enumerate(halves(core)):
            value = dot(flat(full[i, pl.ds(start, 4)]), expand[...], NN) + expand_bias[...]
            hidden[i, pl.ds(start, 4)] = value.reshape(4, -1, value.shape[1])
            partial = dot(gelu(value).astype(bf16), shrink[...], NN)
            keep_partial(partial, scatters[i], sibling)
            between[step]()

    def end(i):
        value = scatters[i].finish() + vecs[i, 3:4]
        expanded[i] = value
        after[i] = mid[i] + gate_rows[i] * vecs[i, 2:3] * value

    begin(0)
    gathers[0].second()
    begin(1)
    gathers[0].finish()
    compute(0, (gathers[1].second, scatters[0].first))
    gathers[1].finish()
    compute(1, (scatters[0].second, scatters[1].first))
    end(0)
    scatters[1].second()
    end(1)
    for part in gathers + scatters:
        part.drain()


def mlp_forward(mid, gate_rows, vecs, weights, ident):
    expand, expand_bias, shrink = weights
    images, length, width = mid.shape
    inner = expand.shape[1]
    return call(
        mlp_forward_kernel,
        "mlp_forward",
        ident,
        [
            shaped((images, 8, length, width), bf16),
            shaped((images, 8, length, inner), f32),
            shaped((images, length, width), f32),
            shaped((images, length, width), f32),
        ],
        comm_scratch(images, length, width),
        4 * images * 8 * length * width * inner * 6,
        mid,
        gate_rows,
        vecs,
        expand,
        expand_bias.reshape(1, -1),
        shrink,
    )


def mlp_backward_kernel(
    grad_after, mid, expanded, gate_rows, vecs, expand, shrink, normed, hidden,
    grad_mid, sums, grad_expand, grad_shrink, grad_bias,
    full, grad_hidden, active, sum_expand, sum_shrink, *comm
):
    place = sides()
    core, chips, address = place
    gathers, scatters = exchanges(full, comm, place)
    greet(address)
    own = core * 4 + chips["own"]

    def begin(i):
        gated = gate_rows[i] * grad_after[i]
        low = (gated * vecs[i, 1:2]).astype(bf16)
        full[i, own] = low
        gathers[i].first()
        sums[i, 2:3] = column_sum(gated * expanded[i])
        sums[i, 3:4] = column_sum(low.astype(f32))

    def compute(i, between):
        for step, (start, sibling) in enumerate(halves(core)):
            pull = dot(flat(full[i, pl.ds(start, 4)]), shrink[...], NT)
            value, slope = gelu_with_slope(flat(hidden[i, pl.ds(start, 4)]))
            active[i, pl.ds(start, 4)] = value.astype(bf16).reshape(4, -1, value.shape[1])
            low = (pull * slope).astype(bf16)
            grad_hidden[i, pl.ds(start, 4)] = low.reshape(4, -1, value.shape[1])
            keep_partial(dot(low, expand[...], NT), scatters[i], sibling)
            between[step]()

    def weigh_shrink(i):
        term = dot(flat(active[i]), flat(full[i]), TN)
        if i == 0:
            sum_shrink[...] = term
        else:
            grad_shrink[...] = (sum_shrink[...] + term).astype(bf16)

    def weigh_expand(i):
        low = flat(grad_hidden[i])
        term = dot(flat(normed[i]), low, TN)
        if i == 0:
            sum_expand[...] = term
            grad_bias[...] = row_sums(low)
        else:
            grad_expand[...] = (sum_expand[...] + term).astype(bf16)
            grad_bias[...] += row_sums(low)

    def end(i):
        grad, shift_sum, scale_sum = modulate_back_rows(mid[i], vecs[i, 0:1], scatters[i].finish())
        grad_mid[i] = grad + grad_after[i]
        sums[i, 0:1] = shift_sum
        sums[i, 1:2] = scale_sum

    begin(0)
    gathers[0].second()
    begin(1)
    gathers[0].finish()
    compute(0, (gathers[1].second, scatters[0].first))
    gathers[1].finish()
    compute(1, (scatters[0].second, scatters[1].first))
    weigh_shrink(0)
    end(0)
    scatters[1].second()
    weigh_expand(0)
    weigh_shrink(1)
    weigh_expand(1)
    end(1)
    for part in gathers + scatters:
        part.drain()


def mlp_backward(grad_after, mid, expanded, gate_rows, vecs, weights, saved, ident):
    expand, _, shrink = weights
    normed, hidden = saved
    images, length, width = mid.shape
    inner = expand.shape[1]
    return call(
        mlp_backward_kernel,
        "mlp_backward",
        ident,
        [
            shaped((images, length, width), f32),
            shaped((images, 8, width), f32),
            shaped((width, inner), bf16),
            shaped((inner, width), bf16),
            shaped((8, inner), f32),
        ],
        [
            pltpu.VMEM((images, 8, length, width), bf16),
            pltpu.VMEM((images, 8, length, inner), bf16),
            pltpu.VMEM((images, 8, length, inner), bf16),
            pltpu.VMEM((width, inner), f32),
            pltpu.VMEM((inner, width), f32),
        ]
        + comm_scratch(images, length, width),
        8 * images * 8 * length * width * inner * 6,
        grad_after,
        mid,
        expanded,
        gate_rows,
        vecs,
        expand,
        shrink,
        normed,
        hidden,
    )


LOG2E = 1.4426950408889634


def attention_forward_kernel(
    base, gate_rows, vecs, project, project_bias, attend, key_bias,
    full, packed, mixed, log_total, attended, mid, *comm
):
    place = sides()
    core, chips, address = place
    images, _, length, _ = full.shape
    gathers, scatters = exchanges(full, comm, place)
    greet(address)
    own = core * 4 + chips["own"]
    span = attend.shape[0]
    heads = span // LANES
    tile = 2 * length
    factor = HEAD_SIZE ** (-0.5) * LOG2E

    def begin(i):
        full[i, own] = modulate(base[i], vecs[i, 0:1], vecs[i, 1:2]).astype(bf16)
        gathers[i].first()

    def rows_of(start, count):
        return pl.ds(pl.multiple_of(start * length, length), count * length)

    def compute(i, between):
        for start, _ in halves(core):
            value = dot(flat(full[i, pl.ds(start, 4)]), project[...], NN) + project_bias[...]
            packed[i, rows_of(start, 4)] = value.astype(bf16)
        between[0]()
        for step, (start, sibling) in enumerate(halves(core)):

            def one(t, carry, start=start):
                rows = pl.ds(pl.multiple_of((start + 2 * t) * length, tile), tile)
                for h in range(heads):
                    q, k, v = (
                        pl.ds(part * span + h * LANES, LANES) for part in range(3)
                    )
                    scores = dot(packed[i, rows, q], packed[i, :, k], NT) * factor + key_bias[i]
                    peak = jnp.max(scores, axis=1, keepdims=True)
                    probs = jnp.exp2(scores - peak)
                    total = jnp.sum(probs, axis=1, keepdims=True)
                    out = dot(probs.astype(bf16), packed[i, :, v], NN) / total
                    mixed[i, rows, pl.ds(h * LANES, LANES)] = out.astype(bf16)
                    level = jnp.broadcast_to(peak + jnp.log2(total), (tile, LANES))
                    log_total[i, h, pl.ds(start // 2 + t, 1)] = level.T[0:1]
                return carry

            lax.fori_loop(0, 2, one, 0)
            partial = dot(mixed[i, rows_of(start, 4)], attend[...], NN)
            keep_partial(partial, scatters[i], sibling)
            between[1 + step]()

    def end(i):
        value = scatters[i].finish() + vecs[i, 3:4]
        attended[i] = value
        mid[i] = base[i] + gate_rows[i] * vecs[i, 2:3] * value

    def nothing():
        pass

    begin(0)
    gathers[0].second()
    begin(1)
    gathers[0].finish()
    compute(0, (gathers[1].second, nothing, scatters[0].first))
    gathers[1].finish()
    compute(1, (scatters[0].second, nothing, scatters[1].first))
    end(0)
    scatters[1].second()
    end(1)
    for part in gathers + scatters:
        part.drain()


def attention_forward(base, gate_rows, vecs, weights, key_bias, ident):
    project, project_bias, attend = weights
    images, length, width = base.shape
    span = attend.shape[0]
    return call(
        attention_forward_kernel,
        "attention_forward",
        ident,
        [
            shaped((images, 8, length, width), bf16),
            shaped((images, 8 * length, 3 * span), bf16),
            shaped((images, 8 * length, span), bf16),
            shaped((images, span // LANES, 4, 2 * length), f32),
            shaped((images, length, width), f32),
            shaped((images, length, width), f32),
        ],
        comm_scratch(images, length, width),
        8 * images * 8 * length * width * span * 6,
        base,
        gate_rows,
        vecs,
        project,
        project_bias.reshape(1, -1),
        attend,
        key_bias,
    )


def attention_backward_kernel(
    grad_mid, base, attended, gate_rows, vecs, project, attend, key_bias, normed, packed, mixed, log_total,
    grad_base, sums, grad_project, grad_attend, grad_bias,
    full, grad_mixed, grad_packed, grad_keys, grad_values, sum_project, sum_attend, *comm
):
    place = sides()
    core, chips, address = place
    images, _, length, _ = full.shape
    gathers, scatters = exchanges(full, comm, place)
    greet(address)
    own = core * 4 + chips["own"]
    span = attend.shape[0]
    heads = span // LANES
    tile = 2 * length
    factor = HEAD_SIZE ** (-0.5)

    def begin(i):
        gated = gate_rows[i] * grad_mid[i]
        low = (gated * vecs[i, 1:2]).astype(bf16)
        full[i, own] = low
        gathers[i].first()
        sums[i, 2:3] = column_sum(gated * attended[i])
        sums[i, 3:4] = column_sum(low.astype(f32))

    def rows_of(start, count):
        return pl.ds(pl.multiple_of(start * length, length), count * length)

    def compute(i, between):
        grad_mixed[...] = dot(flat(full[i]), attend[...], NT).astype(bf16)
        between[0]()
        for h in range(heads):
            lane = pl.ds(h * LANES, LANES)
            q, k, v = (pl.ds(part * span + h * LANES, LANES) for part in range(3))
            keys_turned = packed[i, :, k].T

            def one(t, carry):
                rows = pl.ds(pl.multiple_of(t * tile, tile), tile)
                queries, pulls = packed[i, rows, q], grad_mixed[rows, lane]
                scores = dot(packed[i, :, k], queries, NT) * (factor * LOG2E) + key_bias[i]
                probs = jnp.exp2(scores - log_total[i, h, pl.ds(t, 1)])
                dprobs = dot(packed[i, :, v], pulls, NT)
                row_dot = column_sum(probs * dprobs)
                grad_scores = (probs * (dprobs - row_dot)).astype(bf16)
                value_term = dot(probs.astype(bf16), pulls, NN)
                key_term = dot(grad_scores, queries, NN)

                @pl.when(t == 0)
                def _():
                    grad_values[...] = value_term
                    grad_keys[...] = key_term

                @pl.when(t > 0)
                def _():
                    grad_values[...] += value_term
                    grad_keys[...] += key_term

                query_term = dot(keys_turned, grad_scores, NN) * factor
                grad_packed[i, rows, q] = query_term.T.astype(bf16)
                return carry

            lax.fori_loop(0, 4, one, 0)
            grad_packed[i, :, k] = (grad_keys[...] * factor).astype(bf16)
            grad_packed[i, :, v] = grad_values[...].astype(bf16)
            between[1 + h]()
        for step, (start, sibling) in enumerate(halves(core)):
            keep_partial(dot(grad_packed[i, rows_of(start, 4)], project[...], NT), scatters[i], sibling)

    def weigh_attend(i):
        term = dot(mixed[i], flat(full[i]), TN)
        if i == 0:
            sum_attend[...] = term
        else:
            grad_attend[...] = (sum_attend[...] + term).astype(bf16)

    def weigh_project(i):
        low = grad_packed[i]
        term = dot(flat(normed[i]), low, TN)
        if i == 0:
            sum_project[...] = term
            grad_bias[...] = row_sums(low)
        else:
            grad_project[...] = (sum_project[...] + term).astype(bf16)
            grad_bias[...] += row_sums(low)

    def end(i):
        grad, shift_sum, scale_sum = modulate_back_rows(base[i], vecs[i, 0:1], scatters[i].finish())
        grad_base[i] = grad + grad_mid[i]
        sums[i, 0:1] = shift_sum
        sums[i, 1:2] = scale_sum

    def nothing():
        pass

    begin(0)
    gathers[0].second()
    begin(1)
    gathers[0].finish()
    compute(0, (gathers[1].second, nothing, gathers[1].finish))
    scatters[0].first()
    compute(1, (scatters[0].second, nothing, nothing))
    weigh_attend(0)
    scatters[1].first()
    weigh_project(0)
    end(0)
    scatters[1].second()
    weigh_attend(1)
    weigh_project(1)
    end(1)
    for part in gathers + scatters:
        part.drain()


def attention_backward(grad_mid, base, attended, gate_rows, vecs, weights, key_bias, saved, ident):
    project, _, attend = weights
    normed, packed, mixed, log_total = saved
    images, length, width = base.shape
    span = attend.shape[0]
    tokens = 8 * length
    return call(
        attention_backward_kernel,
        "attention_backward",
        ident,
        [
            shaped((images, length, width), f32),
            shaped((images, 8, width), f32),
            shaped((width, 3 * span), bf16),
            shaped((span, width), bf16),
            shaped((8, 3 * span), f32),
        ],
        [
            pltpu.VMEM((images, 8, length, width), bf16),
            pltpu.VMEM((tokens, span), bf16),
            pltpu.VMEM((images, tokens, 3 * span), bf16),
            pltpu.VMEM((tokens, LANES), f32),
            pltpu.VMEM((tokens, LANES), f32),
            pltpu.VMEM((width, 3 * span), f32),
            pltpu.VMEM((span, width), f32),
        ]
        + comm_scratch(images, length, width),
        16 * images * 8 * length * width * span * 6,
        grad_mid,
        base,
        attended,
        gate_rows,
        vecs,
        project,
        attend,
        key_bias,
        normed,
        packed,
        mixed,
        log_total,
    )


HEAD_SIZE = 72


def pad_heads(array, axis):
    shape = array.shape
    heads = shape[axis] // HEAD_SIZE
    split = array.reshape(shape[:axis] + (heads, HEAD_SIZE) + shape[axis + 1 :])
    widths = [(0, 0)] * split.ndim
    widths[axis + 1] = (0, LANES - HEAD_SIZE)
    return jnp.pad(split, widths).reshape(shape[:axis] + (heads * LANES,) + shape[axis + 1 :])


def unpad_heads(array, axis):
    shape = array.shape
    heads = shape[axis] // LANES
    split = array.reshape(shape[:axis] + (heads, LANES) + shape[axis + 1 :])
    kept = lax.slice_in_dim(split, 0, HEAD_SIZE, axis=axis + 1)
    return kept.reshape(shape[:axis] + (heads * HEAD_SIZE,) + shape[axis + 1 :])


def gather_small(arrays, dims):
    flat = jnp.concatenate([array.reshape(-1) for array in arrays])
    every = lax.all_gather(flat, "batch", axis=0)
    out = []
    start = 0
    for array, dim in zip(arrays, dims):
        piece = every[:, start : start + array.size].reshape((-1,) + array.shape)
        start += array.size
        piece = jnp.moveaxis(piece, 0, dim)
        shape = list(array.shape)
        shape[dim] = -1
        out.append(piece.reshape(shape))
    return out


def body(
    latents,
    conditioning,
    kept_index,
    kept_count,
    patch_weight,
    patch_bias,
    adaptive_weight,
    adaptive_bias,
    project_weight,
    project_bias,
    attend_weight,
    attend_bias,
    expand_weight,
    expand_bias,
    shrink_weight,
    shrink_bias,
    final_adaptive,
    final_offset,
    final_weight,
    final_bias,
    cotangent,
):
    rows, cols, ranks = lax.axis_size("row"), lax.axis_size("col"), lax.axis_size("batch")
    team = rows * cols
    place = lax.axis_index("row") * cols + lax.axis_index("col")
    rank = lax.axis_index("batch")
    images, channels_in = latents.shape[:2]
    channels_out = cotangent.shape[1]
    rows_tile, cols_tile = latents.shape[2] // PATCH, latents.shape[3] // PATCH
    tile_tokens = rows_tile * cols_tile
    sequence = tile_tokens * team
    width = conditioning.shape[1]
    depth = adaptive_weight.shape[0]
    shard = adaptive_weight.shape[1]
    kept_local = tile_tokens * 3 // 4
    highest = lax.Precision.HIGHEST

    head_cols = width // team
    hidden_cols = expand_weight.shape[2] // team

    def slice_of(array, axis, count):
        return lax.dynamic_slice_in_dim(array, place * count, count, axis=axis)

    blocks = []
    for b in range(depth):
        project_own = lax.dynamic_index_in_dim(
            project_weight[b].reshape(shard, 3, team, head_cols), place, axis=2, keepdims=False
        )
        project_full = lax.all_gather(project_own, "batch", axis=0, tiled=True)
        gap = jnp.zeros((head_cols, width), bf16)
        padded = jnp.concatenate([gap, attend_weight[b], gap], axis=0)
        start = jnp.clip(place * head_cols - rank * shard + head_cols, 0, shard + head_cols)
        attend_full = lax.psum(lax.dynamic_slice_in_dim(padded, start, head_cols, axis=0), "batch")
        expand_full = lax.all_gather(slice_of(expand_weight[b], 1, hidden_cols), "batch", axis=0, tiled=True)
        shrink_full = lax.all_gather(slice_of(shrink_weight[b], 0, hidden_cols), "batch", axis=1, tiled=True)
        blocks.append(
            (
                pad_heads(project_full, 2).reshape(width, -1),
                pad_heads(attend_full, 0),
                expand_full,
                shrink_full,
            )
        )

    (
        patch_full,
        patch_bias_full,
        adaptive_offset,
        project_offset,
        attend_offset,
        expand_offset,
        shrink_offset,
        final_offset_full,
        final_full,
        cond_all,
    ) = gather_small(
        [
            patch_weight,
            patch_bias,
            adaptive_bias,
            project_bias,
            attend_bias,
            expand_bias,
            shrink_bias,
            final_offset,
            final_weight,
            conditioning,
        ],
        [1, 0, 1, 1, 1, 1, 1, 0, 0, 0],
    )

    patch_tiles = to_tokens(latents, PATCH)
    grad_tiles = to_tokens(cotangent, PATCH)
    patch_in, patch_out = patch_tiles.shape[2], grad_tiles.shape[2]
    tiles = lax.all_gather(jnp.concatenate([patch_tiles, grad_tiles], axis=2), PLANE, axis=1)
    whole = tiles.reshape(images, rows, cols, rows_tile, cols_tile, -1).transpose(0, 1, 3, 2, 4, 5)
    whole = whole.reshape(images, sequence, patch_in + patch_out)
    grid_cols = cols * cols_tile
    own_ids = lax.dynamic_index_in_dim(
        kept_index.reshape(images, tile_tokens, team), place, axis=2, keepdims=False
    )
    pick = (own_ids[:, :, None] == jnp.arange(sequence, dtype=jnp.int32)).astype(bf16)
    own = jnp.einsum("ikt,itc->ikc", pick, whole, preferred_element_type=f32).astype(bf16)
    patches, grad_outputs = own[..., :patch_in], own[..., patch_in:]
    order = jnp.arange(kept_local, dtype=jnp.int32)[:, None] * team + jnp.arange(team, dtype=jnp.int32)
    kept_grid = order[None] < kept_count[:, None, None]
    chunk_order = kept_grid.reshape(images, kept_local, team // 2, 2).transpose(0, 3, 2, 1)
    key_bias = jnp.where(chunk_order.reshape(images, team * kept_local), 0.0, masked_score).astype(f32)
    kept_rows = lax.dynamic_index_in_dim(kept_grid, place, axis=2, keepdims=False).astype(f32)[:, :, None]

    count = width // 4
    omega = 1.0 / 10000.0 ** (jnp.arange(count, dtype=f32) / count)
    angles = jnp.arange(max(rows * rows_tile, grid_cols), dtype=f32)[:, None] * omega[None, :]
    along = jnp.concatenate([jnp.sin(angles), jnp.cos(angles)], axis=1)
    places = jnp.arange(along.shape[0], dtype=jnp.int32)

    def position_of(coords):
        chosen = (coords[..., None] == places).astype(f32)
        return jnp.einsum("ikt,tc->ikc", chosen, along, precision=highest)

    position = jnp.concatenate(
        [position_of(own_ids // grid_cols), position_of(own_ids % grid_cols)], axis=-1
    )
    resid = (
        jnp.einsum("ikc,cd->ikd", patches, patch_full, preferred_element_type=f32)
        + patch_bias_full.astype(f32)
        + position
    )

    silu_all = jax.nn.silu(cond_all.astype(f32)).astype(bf16)
    silu_rows = lax.dynamic_slice_in_dim(silu_all, rank * shard, shard, axis=1)
    mod_cols, final_cols = adaptive_weight.shape[2] // team, final_adaptive.shape[1] // team
    parts = [
        dot(silu_rows, slice_of(adaptive_weight[b], 1, mod_cols), ((1,), (0,))) for b in range(depth)
    ] + [dot(silu_rows, slice_of(final_adaptive, 1, final_cols), ((1,), (0,)))]
    mods = lax.psum_scatter(jnp.concatenate(parts, axis=1), "batch", scatter_dimension=0, tiled=True)
    mods = lax.all_gather(mods, PLANE, axis=1)
    pieces = []
    for b in range(depth):
        block_mod = mods[:, :, b * mod_cols : (b + 1) * mod_cols].reshape(images, -1)
        block_mod = (block_mod + adaptive_offset[b].astype(f32)).reshape(images, 6, 1, width)
        pieces.append([block_mod[:, s] for s in range(6)])
    final_mod = mods[:, :, depth * mod_cols :].reshape(images, -1) + final_offset_full.astype(f32)
    final_mod = final_mod.reshape(images, 2, 1, width)
    final_shift, final_scale = final_mod[:, 0], final_mod[:, 1]

    records = []
    for b in range(depth):
        project, attend, expand, shrink = blocks[b]
        shift1, scale1, gate1, shift2, scale2, gate2 = pieces[b]
        bias = project_offset[b].astype(f32).reshape(2, team, head_cols)
        bias = lax.dynamic_index_in_dim(bias, place, axis=1, keepdims=False)
        bias = pad_heads(jnp.stack([bias[0], jnp.zeros_like(bias[0]), bias[1]]), 1).reshape(-1)
        attention_weights = (project, bias, attend)
        mlp_weights = (expand, slice_of(expand_offset[b].astype(f32), 0, hidden_cols), shrink)
        routed = b > 0
        base = resid[:, :kept_local] if routed else resid
        gate_rows = kept_rows if routed else jnp.ones((images, tile_tokens, 1), f32)
        keys = key_bias if routed else jnp.zeros((images, sequence), f32)

        def rows_with(parts, bias_row):
            row = jnp.broadcast_to(bias_row.astype(f32), (images, 1, width))
            return jnp.concatenate(parts + [row], axis=1)

        *attention_saved, attended, mid = attention_forward(
            base,
            gate_rows,
            rows_with([shift1, scale1, gate1], attend_offset[b]),
            attention_weights,
            keys[:, None, :],
            4 * b,
        )
        *mlp_saved, expanded, after = mlp_forward(
            mid, gate_rows, rows_with([shift2, scale2, gate2], shrink_offset[b]), mlp_weights, 4 * b + 1
        )
        records.append(
            (base, mid, attended, expanded, attention_weights, mlp_weights, keys, gate_rows, attention_saved, mlp_saved)
        )
        resid = jnp.concatenate([after, resid[:, kept_local:]], axis=1) if routed else after

    final_normed = modulate(resid, final_shift, final_scale).astype(bf16)
    outputs = jnp.einsum("ikd,dc->ikc", final_normed, final_full, preferred_element_type=f32) + final_bias.astype(f32)
    final_bias_term = jnp.sum(grad_outputs.astype(f32), axis=(0, 1))
    final_weight_term = jnp.einsum("ikd,ikc->dc", final_normed, grad_outputs, preferred_element_type=f32)
    grad_final = jnp.einsum("ikc,dc->ikd", grad_outputs, final_full, preferred_element_type=f32)
    grad_resid, grad_final_shift, grad_final_scale = modulate_back(resid, final_scale, grad_final)
    final_mod_term = jnp.stack([grad_final_shift, grad_final_scale], axis=1)

    mod_terms = [None] * depth
    block_grads = [None] * depth
    for b in reversed(range(depth)):
        base, mid, attended, expanded, attention_weights, mlp_weights, keys, gate_rows, attention_saved, mlp_saved = records[b]
        shift1, scale1, gate1, shift2, scale2, gate2 = pieces[b]
        routed = b > 0
        grad_after = grad_resid[:, :kept_local] if routed else grad_resid
        grad_mid, mlp_sums, grad_expand, grad_shrink, grad_expand_bias = mlp_backward(
            grad_after,
            mid,
            expanded,
            gate_rows,
            jnp.concatenate([scale2, gate2], axis=1),
            mlp_weights,
            mlp_saved,
            4 * b + 2,
        )
        grad_base, attention_sums, grad_project, grad_attend, grad_project_bias = attention_backward(
            grad_mid,
            base,
            attended,
            gate_rows,
            jnp.concatenate([scale1, gate1], axis=1),
            attention_weights,
            keys[:, :, None],
            attention_saved,
            4 * b + 3,
        )
        grad_expand_bias, grad_project_bias = grad_expand_bias[0], grad_project_bias[0]
        grad_attend_bias = jnp.sum(attention_sums[:, 3], axis=0)
        grad_shrink_bias = jnp.sum(mlp_sums[:, 3], axis=0)
        grad_resid = jnp.concatenate([grad_base, grad_resid[:, kept_local:]], axis=1) if routed else grad_base
        mod_terms[b] = jnp.concatenate([attention_sums[:, :3], mlp_sums[:, :3]], axis=1)
        grad_project = unpad_heads(grad_project.reshape(width, 3, -1), 2).astype(bf16)
        grad_project = lax.psum_scatter(grad_project, "batch", scatter_dimension=0, tiled=True)
        grad_project = lax.all_gather(grad_project, PLANE, axis=2).reshape(shard, -1)
        grad_attend = lax.psum(unpad_heads(grad_attend, 0).astype(bf16), "batch")
        grad_attend = lax.all_gather(grad_attend, PLANE, axis=0, tiled=True)
        grad_attend = lax.dynamic_slice_in_dim(grad_attend, rank * shard, shard, axis=0)
        grad_expand = lax.psum_scatter(grad_expand.astype(bf16), "batch", scatter_dimension=0, tiled=True)
        grad_expand = lax.all_gather(grad_expand, PLANE, axis=1, tiled=True)
        grad_shrink = lax.psum_scatter(grad_shrink.astype(bf16), "batch", scatter_dimension=1, tiled=True)
        grad_shrink = lax.all_gather(grad_shrink, PLANE, axis=0, tiled=True)
        grad_bias = unpad_heads(grad_project_bias.reshape(3, -1), 1)
        grad_bias = jnp.stack([grad_bias[0], grad_bias[2]])
        block_grads[b] = (
            grad_project.astype(f32),
            grad_attend.astype(f32),
            grad_expand.astype(f32),
            grad_shrink.astype(f32),
            grad_bias,
            grad_attend_bias,
            grad_expand_bias,
            grad_shrink_bias,
        )

    mod_all = jnp.concatenate([jnp.stack(mod_terms, axis=1).reshape(images, -1), final_mod_term.reshape(images, -1)], axis=1)
    mod_low = lax.psum(mod_all, PLANE).astype(bf16)
    mod_every = lax.all_gather(mod_low, "batch", axis=0, tiled=True)
    mod_width = adaptive_weight.shape[2]
    block_mods = [mod_every[:, b * mod_width : (b + 1) * mod_width] for b in range(depth)]
    final_mods = mod_every[:, depth * mod_width :]
    adaptive_weight_grad = jnp.stack([dot(silu_rows, m, ((0,), (0,))) for m in block_mods])
    final_adaptive_grad = dot(silu_rows, final_mods, ((0,), (0,)))
    mod_sum = jnp.sum(mod_every.astype(f32), axis=0)
    offset_cols, final_offset_cols = adaptive_bias.shape[1], final_offset.shape[0]
    adaptive_bias_grad = lax.dynamic_slice_in_dim(
        mod_sum[: depth * mod_width].reshape(depth, mod_width), rank * offset_cols, offset_cols, axis=1
    )
    final_offset_grad = lax.dynamic_slice_in_dim(
        mod_sum[depth * mod_width :], rank * final_offset_cols, final_offset_cols
    )
    grad_silu = dot(final_mods, final_adaptive, ((1,), (1,)))
    for b in range(depth):
        grad_silu = grad_silu + dot(block_mods[b], adaptive_weight[b], ((1,), (1,)))
    grad_silu = lax.all_to_all(grad_silu.reshape(ranks, images, shard), "batch", 0, 0)
    grad_silu = grad_silu.transpose(1, 0, 2).reshape(images, width)
    conditioning_grad = jax.vjp(jax.nn.silu, conditioning.astype(f32))[1](grad_silu)[0]

    patch_bias_term = jnp.sum(grad_resid, axis=(0, 1))
    grad_embed = grad_resid.astype(bf16)
    patch_term = jnp.einsum("ikc,ikd->cd", patches, grad_embed, preferred_element_type=f32)
    grad_patches = jnp.einsum("ikd,cd->ikc", grad_embed, patch_full, preferred_element_type=f32)
    ordered = lax.all_gather(jnp.concatenate([outputs, grad_patches], axis=2), PLANE, axis=2)
    ordered = ordered.reshape(images, sequence, patch_out + patch_in)
    tile_rows = lax.axis_index("row") * rows_tile + jnp.arange(rows_tile, dtype=jnp.int32)
    tile_cols = lax.axis_index("col") * cols_tile + jnp.arange(cols_tile, dtype=jnp.int32)
    tile_ids = (tile_rows[:, None] * grid_cols + tile_cols).reshape(-1)
    back = (kept_index[:, None, :] == tile_ids[None, :, None]).astype(f32)
    tile_out = jnp.einsum("itj,ijc->itc", back, ordered, precision=highest)
    prediction = to_planes(tile_out[..., :patch_out], PATCH, channels_out, rows_tile, cols_tile)
    latent_grad = to_planes(tile_out[..., patch_out:], PATCH, channels_in, rows_tile, cols_tile)

    def scattered(full, axis, parted):
        return lax.psum_scatter(full, "batch", scatter_dimension=axis, tiled=True) if parted else full

    token_sums = lax.psum(
        (patch_term, patch_bias_term, final_weight_term, final_bias_term), ("batch", "row", "col")
    )
    patch_weight_grad = lax.dynamic_slice_in_dim(token_sums[0], rank * shard, shard, axis=1)
    patch_bias_grad = lax.dynamic_slice_in_dim(token_sums[1], rank * shard, shard)
    final_weight_grad = lax.dynamic_slice_in_dim(token_sums[2], rank * shard, shard, axis=0)
    final_bias_grad = token_sums[3]
    stacked = [jnp.stack([block_grads[b][n] for b in range(depth)]) for n in range(8)]
    project_sum, expand_sum = lax.psum((stacked[4], stacked[6]), "batch")
    attend_sum, shrink_sum = lax.psum((stacked[5], stacked[7]), ("batch", "row", "col"))
    project_sum = lax.all_gather(project_sum, PLANE, axis=2).reshape(depth, -1)
    expand_sum = lax.all_gather(expand_sum, PLANE, axis=1, tiled=True)

    def rank_part(full):
        part = full.shape[1] // ranks
        return lax.dynamic_slice_in_dim(full, rank * part, part, axis=1)

    return (
        prediction,
        latent_grad,
        conditioning_grad,
        patch_weight_grad,
        patch_bias_grad,
        adaptive_weight_grad,
        adaptive_bias_grad,
        stacked[0],
        rank_part(project_sum),
        stacked[1],
        rank_part(attend_sum),
        stacked[2],
        rank_part(expand_sum),
        stacked[3],
        rank_part(shrink_sum),
        final_adaptive_grad,
        final_offset_grad,
        final_weight_grad,
        final_bias_grad,
    )


def solution(mesh):
    tokens = P("batch", None, "row", "col")
    placed = (
        tokens,
        P("batch", None),
        P("batch", None),
        P("batch"),
        P(None, "batch"),
        P("batch"),
        P(None, "batch", None),
        P(None, "batch"),
        P(None, "batch", None),
        P(None, "batch"),
        P(None, "batch", None),
        P(None, "batch"),
        P(None, "batch", None),
        P(None, "batch"),
        P(None, None, "batch"),
        P(None, "batch"),
        P("batch", None),
        P("batch"),
        P("batch", None),
        P(),
        tokens,
    )
    return jax.shard_map(
        body,
        mesh=mesh,
        in_specs=placed,
        out_specs=(tokens, tokens, P("batch", None)) + placed[4:16] + (placed[16], P("batch"), P("batch", None), P()),
        check_vma=False,
    )
```

```python
import jax
import jax.numpy as jnp
from jax import lax
from jax.experimental import pallas as pl
from jax.experimental.pallas import tpu as pltpu
from jax.sharding import PartitionSpec as P

HEADS = 16
PATCH = 2
LANES = 128
PLANE = ("row", "col")

norm_epsilon = 1e-06
masked_score = -1e30
f32 = jnp.float32
bf16 = jnp.bfloat16


def to_tokens(planes, patch_side):
    images, channels, height, breadth = planes.shape
    shaped = planes.reshape(
        images, channels, height // patch_side, patch_side, breadth // patch_side, patch_side
    )
    return shaped.transpose(0, 2, 4, 3, 5, 1).reshape(
        images, height // patch_side * (breadth // patch_side), patch_side * patch_side * channels
    )


def to_planes(token_rows, patch_side, channels, rows_tile, cols_tile):
    images = token_rows.shape[0]
    shaped = token_rows.reshape(images, rows_tile, cols_tile, patch_side, patch_side, channels)
    return shaped.transpose(0, 5, 1, 3, 2, 4).reshape(
        images, channels, rows_tile * patch_side, cols_tile * patch_side
    )


def dot(left, right, dims, precision=None):
    return lax.dot_general(left, right, (dims, ((), ())), precision=precision, preferred_element_type=f32)


def norm_parts(resid):
    centered = resid - jnp.mean(resid, axis=-1, keepdims=True)
    rstd = lax.rsqrt(jnp.mean(centered * centered, axis=-1, keepdims=True) + norm_epsilon)
    return centered * rstd, rstd


def modulate(resid, shift_part, scale_part):
    return norm_parts(resid)[0] * (1.0 + scale_part) + shift_part


def modulate_back(resid, scale_part, grad):
    unit, rstd = norm_parts(resid)
    inner = grad * (1.0 + scale_part)
    grad_in = rstd * (
        inner
        - jnp.mean(inner, axis=-1, keepdims=True)
        - unit * jnp.mean(inner * unit, axis=-1, keepdims=True)
    )
    return grad_in, jnp.sum(grad, axis=1), jnp.sum(grad * unit, axis=1)


def sides():
    row, col = lax.axis_index("row"), lax.axis_index("col")
    core = lax.rem(col, 2)
    across = col // 2
    chip = row * 2 + across
    chips = {
        "own": chip,
        "x": (1 - row) * 2 + across,
        "y": row * 2 + 1 - across,
        "far": (1 - row) * 2 + 1 - across,
    }
    address = {
        "x": {"row": 1 - row},
        "y": {"col": lax.rem(col + 2, 4)},
        "core": {"col": col + 1 - 2 * core},
    }
    return core, chips, address


def greet(addresses):
    barrier = pltpu.get_barrier_semaphore()
    for who in addresses:
        pl.semaphore_signal(barrier, inc=1, device_id=who, device_id_type=pl.DeviceIdType.MESH)
    pl.semaphore_wait(barrier, len(addresses))


def remote(source, target, send, recv, who):
    return pltpu.make_async_remote_copy(
        src_ref=source,
        dst_ref=target,
        send_sem=send,
        recv_sem=recv,
        device_id=who,
        device_id_type=pl.DeviceIdType.MESH,
    )


def rank_at(offset):
    ranks = lax.axis_size("batch")
    return {"batch": lax.rem(lax.axis_index("batch") + offset + ranks, ranks)}


def other_ranks():
    return [rank_at(offset) for offset in range(1, lax.axis_size("batch"))]


def plane_peers():
    row, col = lax.axis_index("row"), lax.axis_index("col")
    rows, cols = lax.axis_size("row"), lax.axis_size("col")
    return [
        {"row": lax.rem(row + n // cols, rows), "col": lax.rem(col + n % cols, cols)}
        for n in range(1, rows * cols)
    ]


class Line:
    reach = 1

    def __init__(self, source):
        ranks = lax.axis_size("batch")
        self.ins = [source]
        self.outs = [jax.ShapeDtypeStruct((ranks,) + source.shape, source.dtype)]
        self.sems = [(2, ranks - 1), (2, ranks - 1), (1,)]

    def bind(self, ins, outs, sems):
        (self.source,), (self.target,) = ins, outs
        self.send, self.recv, self.own = sems
        self.rank, self.ranks = lax.axis_index("batch"), lax.axis_size("batch")
        self.steps = self.ranks
        self.late = 0

    def copy(self, way, r):
        block = self.rank - r if way == 0 else self.rank + r
        source = self.source if r == 0 else self.target.at[block]
        return remote(
            source, self.target.at[block], self.send.at[way, r], self.recv.at[way, r], rank_at(1 - 2 * way)
        )

    def holds(self, way, r):
        return self.rank >= r if way == 0 else self.rank + r < self.ranks

    def sends(self, way, r):
        edge = self.rank + 1 < self.ranks if way == 0 else self.rank > 0
        return jnp.logical_and(self.holds(way, r), edge)

    def step(self, r):
        for way in (0, 1):
            if r > 0:
                block = self.rank - r if way == 0 else self.rank + r

                @pl.when(self.holds(way, r))
                def _(way=way, block=block):
                    place = self.target.at[block]
                    remote(place, place, self.send.at[way, r - 1], self.recv.at[way, r - 1], rank_at(1)).wait_recv()

            if r < self.ranks - 1:

                @pl.when(self.sends(way, r))
                def _(way=way):
                    self.copy(way, r).start()

        if r == 0:
            self.stay().start()

    def stay(self):
        return pltpu.make_async_copy(self.source, self.target.at[self.rank], self.own.at[0])

    def finish(self):
        for way in (0, 1):
            for r in range(self.ranks - 1):

                @pl.when(self.sends(way, r))
                def _(way=way, r=r):
                    self.copy(way, r).wait_send()

        self.stay().wait()


class Chain:
    reach = 1

    def __init__(self, source, shard):
        pieces, self.rows, _ = source.shape
        self.shard = shard
        self.ins = [source]
        self.outs = [jax.ShapeDtypeStruct(source.shape, source.dtype)]
        self.sems = [(pieces, 2), (pieces, 2), (pieces,)]

    def bind(self, ins, outs, sems):
        (self.source,), (self.target,) = ins, outs
        self.send, self.recv, self.own = sems
        self.rank, self.ranks = lax.axis_index("batch"), lax.axis_size("batch")
        self.steps = self.ranks
        self.late = 0
        self.owners = owners_of(self.source.shape[0], self.rows, self.shard)

    def copy(self, j, way, first):
        source = self.source.at[j] if first else self.target.at[j]
        return remote(
            source, self.target.at[j], self.send.at[j, way], self.recv.at[j, way], rank_at(1 - 2 * way)
        )

    def edge(self, way):
        return self.rank + 1 < self.ranks if way == 0 else self.rank > 0

    def step(self, r):
        for j, owner in enumerate(self.owners):
            for way in (0, 1):
                away = self.rank - owner if way == 0 else owner - self.rank
                if r > 0:

                    @pl.when(away == r)
                    def _(j=j, way=way):
                        self.copy(j, way, False).wait_recv()

                @pl.when(jnp.logical_and(away == r, self.edge(way)))
                def _(j=j, way=way):
                    self.copy(j, way, r == 0).start()

            if r == 0:

                @pl.when(self.rank == owner)
                def _(j=j):
                    self.stay(j).start()

    def stay(self, j):
        return pltpu.make_async_copy(self.source.at[j], self.target.at[j], self.own.at[j])

    def finish(self):
        for j, owner in enumerate(self.owners):
            for way in (0, 1):
                away = self.rank - owner if way == 0 else owner - self.rank

                @pl.when(jnp.logical_and(away >= 0, self.edge(way)))
                def _(j=j, way=way):
                    self.copy(j, way, False).wait_send()

            @pl.when(self.rank == owner)
            def _(j=j):
                self.stay(j).wait()


def team_place():
    return lax.axis_index("row") * lax.axis_size("col") + lax.axis_index("col")


def owners_of(pieces, rows, shard):
    place = team_place()
    return [(place * pieces + j) * rows // shard for j in range(pieces)]


class Fold:
    reach = 2

    def __init__(self, source):
        ranks = lax.axis_size("batch")
        self.ins = [source]
        self.outs = [jax.ShapeDtypeStruct((ranks - 1,) + source.shape[1:], source.dtype)]
        self.sems = [(ranks - 1,), (ranks - 1,)]

    def bind(self, ins, outs, sems):
        (self.source,), (self.inbox,) = ins, outs
        self.send, self.recv = sems
        self.steps = 1
        self.late = 0

    def copies(self):
        for n in range(lax.axis_size("batch") - 1):
            who = rank_at(n + 1)
            yield remote(
                self.source.at[who["batch"]], self.inbox.at[n], self.send.at[n], self.recv.at[n], who
            )

    def step(self, r):
        for copy in self.copies():
            copy.start()

    def finish(self):
        for copy in self.copies():
            copy.wait()


class FoldTo:
    reach = 2

    def __init__(self, source, shard):
        pieces, self.rows, width = source.shape
        others = lax.axis_size("batch") - 1
        self.shard = shard
        self.ins = [source]
        self.outs = [jax.ShapeDtypeStruct((pieces, others, self.rows, width), source.dtype)]
        self.sems = [(pieces, others), (pieces, others)]

    def bind(self, ins, outs, sems):
        (self.source,), (self.inbox,) = ins, outs
        self.send, self.recv = sems
        self.steps = 1
        self.late = 0
        self.rank, self.others = lax.axis_index("batch"), lax.axis_size("batch") - 1
        self.owners = owners_of(self.source.shape[0], self.rows, self.shard)

    def copy(self, j, n):
        return remote(
            self.source.at[j], self.inbox.at[j, n], self.send.at[j, n], self.recv.at[j, n], rank_at(n + 1)
        )

    def leads(self, j, n):
        return rank_at(n + 1)["batch"] == self.owners[j]

    def step(self, r):
        for j in range(len(self.owners)):
            for n in range(self.others):

                @pl.when(self.leads(j, n))
                def _(j=j, n=n):
                    self.copy(j, n).start()

    def finish(self):
        for j, owner in enumerate(self.owners):
            for n in range(self.others):

                @pl.when(self.rank == owner)
                def _(j=j, n=n):
                    self.copy(j, n).wait_recv()

                @pl.when(self.leads(j, n))
                def _(j=j, n=n):
                    self.copy(j, n).wait_send()


class Copies:
    def __init__(self, send, recv, address):
        self.send, self.recv, self.address = send, recv, address
        self.started = {}

    def go(self, slot, source, target, who):
        copy = remote(source, target, self.send.at[slot], self.recv.at[slot], self.address[who])
        copy.start()
        self.started[slot] = copy

    def arrived(self, *slots):
        for slot in slots:
            self.started[slot].wait_recv()

    def drain(self):
        for copy in self.started.values():
            copy.wait_send()


class Gather(Copies):
    def __init__(self, full, send, recv, place):
        core, chips, address = place
        super().__init__(send, recv, address)
        self.full, self.half = full, full.shape[1] // 2
        self.source = None
        self.at = {name: core * 4 + chip for name, chip in chips.items()}

    def whole(self, name):
        return self.full.at[self.at[name]]

    def part(self, name, second):
        return self.full.at[self.at[name], pl.ds(self.half * second, self.half)]

    def first(self):
        own = self.whole("own")
        source = own if self.source is None else self.source
        self.go(0, source, own, "x")
        self.go(1, source, own, "y")
        self.go(2, source, own, "core")

    def second(self):
        self.arrived(0)
        self.go(3, self.part("x", 0), self.part("x", 0), "y")
        self.arrived(1)
        self.go(4, self.part("y", 1), self.part("y", 1), "x")
        self.go(5, self.whole("x"), self.whole("x"), "core")
        self.go(6, self.whole("y"), self.whole("y"), "core")

    def finish(self):
        self.arrived(3, 4)
        self.go(7, self.whole("far"), self.whole("far"), "core")
        self.arrived(2, 5, 6, 7)


class PlaneGather:
    reach = 0

    def __init__(self, source, late=0):
        self.ins = [source]
        self.outs = [jax.ShapeDtypeStruct((8,) + source.shape, source.dtype)]
        self.sems = [(8,), (8,), (1,)]
        self.late = late

    def bind(self, ins, outs, sems):
        (self.source,), (self.target,) = ins, outs
        send, recv, self.own = sems
        self.gather = Gather(self.target, send, recv, sides())
        self.gather.source = self.source
        self.steps = 3

    def stay(self):
        return pltpu.make_async_copy(self.source, self.gather.whole("own"), self.own.at[0])

    def step(self, r):
        if r == 0:
            self.gather.first()
            self.stay().start()
        elif r == 1:
            self.gather.second()
        else:
            self.gather.finish()

    def finish(self):
        self.gather.drain()
        self.stay().wait()


class Background:
    def __init__(self, tasks):
        self.tasks = tasks
        self.now = 0

    def partners(self):
        reach = max([task.reach for task in self.tasks], default=0)
        return [[], [rank_at(1), rank_at(-1)], other_ranks()][reach]

    def tick(self):
        for task in self.tasks:
            if 0 <= self.now - task.late < task.steps:
                task.step(self.now - task.late)
        self.now += 1

    def finish(self):
        for task in self.tasks:
            for r in range(max(self.now - task.late, 0), task.steps):
                task.step(r)
            task.finish()


class Scatter(Copies):
    def __init__(self, core_out, core_in, total, hop_out, hop_in, send, recv, place):
        _, self.chips, address = place
        super().__init__(send, recv, address)
        self.core_out, self.core_in, self.total = core_out, core_in, total
        self.hop_out, self.hop_in = hop_out, hop_in
        self.half = total.shape[1] // 2

    def cross(self):
        self.go(0, self.core_out, self.core_in, "core")

    def hop(self, slot, value, who):
        self.hop_out[slot] = value.astype(bf16)
        self.go(1 + slot, self.hop_out.at[slot], self.hop_in.at[slot], who)

    def first(self):
        self.arrived(0)
        half = self.half

        def summed(name):
            chip = self.chips[name]
            return self.total[chip] + self.core_in[chip].astype(f32)

        far = summed("far")
        self.hop(0, far[:half], "x")
        self.hop(2, far[half:], "y")
        x_sum = summed("x")
        self.hop(1, x_sum[:half], "x")
        self.total[self.chips["x"], half:] = x_sum[half:]
        y_sum = summed("y")
        self.hop(3, y_sum[half:], "y")
        self.total[self.chips["y"], :half] = y_sum[:half]

    def second(self):
        half = self.half
        self.arrived(1)
        self.hop(4, self.total[self.chips["y"], :half] + self.hop_in[0].astype(f32), "y")
        self.arrived(3)
        self.hop(5, self.total[self.chips["x"], half:] + self.hop_in[2].astype(f32), "x")

    def finish(self):
        self.arrived(2, 4, 5, 6)
        half, own = self.half, self.chips["own"]
        base = self.total[own] + self.core_in[own].astype(f32)
        low = base[:half] + self.hop_in[1].astype(f32) + self.hop_in[4].astype(f32)
        high = base[half:] + self.hop_in[3].astype(f32) + self.hop_in[5].astype(f32)
        return jnp.concatenate([low, high], axis=0)


def comm_scratch(images, length, width):
    half = length // 2
    return [
        pltpu.VMEM((images, 4, length, width), bf16),
        pltpu.VMEM((images, 4, length, width), bf16),
        pltpu.VMEM((images, 4, length, width), f32),
        pltpu.VMEM((images, 6, half, width), bf16),
        pltpu.VMEM((images, 6, half, width), bf16),
        pltpu.SemaphoreType.DMA((images, 8)),
        pltpu.SemaphoreType.DMA((images, 8)),
        pltpu.SemaphoreType.DMA((images, 7)),
        pltpu.SemaphoreType.DMA((images, 7)),
    ]


def exchanges(full, comm, place):
    core_out, core_in, total, hop_out, hop_in, gs, gr, ss, sr = comm
    images = full.shape[0]
    gathers = [Gather(full.at[i], gs.at[i], gr.at[i], place) for i in range(images)]
    scatters = [
        Scatter(
            core_out.at[i], core_in.at[i], total.at[i], hop_out.at[i], hop_in.at[i], ss.at[i], sr.at[i], place
        )
        for i in range(images)
    ]
    return gathers, scatters


def flat(value):
    return value.reshape(value.shape[0] * value.shape[1], value.shape[2])


def halves(core):
    return ((1 - core) * 4, True), (core * 4, False)


def keep_partial(partial, scatter, sibling):
    shape = scatter.total.shape
    if sibling:
        scatter.core_out[...] = partial.astype(bf16).reshape(shape)
        scatter.cross()
    else:
        scatter.total[...] = partial.reshape(shape)


def column_sum(value):
    return jnp.sum(value, axis=0, keepdims=True)


def row_sums(value):
    ones = jnp.ones((8, value.shape[0]), bf16)
    return dot(ones, value, ((1,), (0,)))


GELU_ROOT = 0.7978845608028654
GELU_CUBE = 0.044715
NN, NT, TN = ((1,), (0,)), ((1,), (1,)), ((0,), (0,))


def gelu(hidden):
    inner = GELU_ROOT * (hidden + GELU_CUBE * (hidden * hidden * hidden))
    return 0.5 * hidden * (1.0 + jnp.tanh(inner))


def gelu_with_slope(hidden):
    square = hidden * hidden
    bend = jnp.tanh(GELU_ROOT * hidden * (1.0 + GELU_CUBE * square))
    rise = 0.5 * (1.0 + bend)
    slope = rise + 0.5 * hidden * (1.0 - bend * bend) * (GELU_ROOT + 3.0 * GELU_ROOT * GELU_CUBE * square)
    return hidden * rise, slope


def modulate_back_rows(resid, scale_part, grad):
    unit, rstd = norm_parts(resid)
    inner = grad * (1.0 + scale_part)
    grad_in = rstd * (
        inner
        - jnp.mean(inner, axis=-1, keepdims=True)
        - unit * jnp.mean(inner * unit, axis=-1, keepdims=True)
    )
    return grad_in, column_sum(grad), column_sum(grad * unit)


def call(kernel, name, ident, outs, scratch, flops, args, tasks=()):
    vmem, anywhere = pl.BlockSpec(memory_space=pltpu.VMEM), pl.BlockSpec(memory_space=pl.ANY)
    moved = sum(a.size * a.dtype.itemsize for a in args) + sum(o.size * o.dtype.itemsize for o in outs)
    task_ins = [array for task in tasks for array in task.ins]
    task_outs = [shape for task in tasks for shape in task.outs]
    task_sems = [pltpu.SemaphoreType.DMA(shape) for task in tasks for shape in task.sems]

    def run(*refs):
        refs = list(refs)

        def take(count):
            taken = refs[:count]
            del refs[:count]
            return taken

        main_ins, bound_ins = take(len(args)), take(len(task_ins))
        main_outs, bound_outs = take(len(outs)), take(len(task_outs))
        main_scratch = take(len(scratch))
        for task in tasks:
            ins = [bound_ins.pop(0) for _ in task.ins]
            results = [bound_outs.pop(0) for _ in task.outs]
            task.bind(ins, results, take(len(task.sems)))
        kernel(Background(tasks), *main_ins, *main_outs, *main_scratch)

    results = pl.pallas_call(
        run,
        name=name,
        out_shape=list(outs) + task_outs,
        in_specs=[vmem] * len(args) + [anywhere] * len(task_ins),
        out_specs=[vmem] * len(outs) + [anywhere] * len(task_outs),
        scratch_shapes=list(scratch) + task_sems,
        compiler_params=pltpu.CompilerParams(
            collective_id=ident, has_side_effects=True, vmem_limit_bytes=60 * 2**20
        ),
        cost_estimate=pl.CostEstimate(flops=flops, bytes_accessed=moved, transcendentals=0),
    )(*args, *task_ins)
    return results[: len(outs)], results[len(outs) :]


def shaped(shape, kind):
    return jax.ShapeDtypeStruct(shape, kind)


def prologue_kernel(background, pack, tiles, packs, every_tile, zs, zr, ps, pr):
    ranks, peers = other_ranks(), plane_peers()
    greet(ranks + peers)
    rank, place = lax.axis_index("batch"), team_place()
    copies = [
        remote(pack, packs.at[rank], zs.at[n], zr.at[n], who) for n, who in enumerate(ranks)
    ] + [remote(tiles, every_tile.at[place], ps.at[n], pr.at[n], who) for n, who in enumerate(peers)]
    for copy in copies:
        copy.start()
    packs[rank] = pack[...]
    every_tile[place] = tiles[...]
    for copy in copies:
        copy.wait()


def prologue(pack, tiles, ident):
    ranks = lax.axis_size("batch")
    dma = pltpu.SemaphoreType.DMA
    (packs, every_tile), _ = call(
        prologue_kernel,
        "prologue",
        ident,
        [shaped((ranks,) + pack.shape, pack.dtype), shaped((8,) + tiles.shape, tiles.dtype)],
        [dma((ranks - 1,)), dma((ranks - 1,)), dma((7,)), dma((7,))],
        0,
        (pack, tiles),
    )
    return packs, every_tile


def conditioning_kernel(background, parts, mods, inbox, zs, zr, ps, pr):
    ranks, peers = other_ranks(), plane_peers()
    greet(ranks + peers)
    rank, place = lax.axis_index("batch"), team_place()
    first = [
        remote(parts.at[who["batch"]], inbox.at[n], zs.at[n], zr.at[n], who) for n, who in enumerate(ranks)
    ]
    for copy in first:
        copy.start()
    background.tick()
    total = parts[rank]
    for n, copy in enumerate(first):
        copy.wait()
        total = total + inbox[n]
    mods[place] = total
    second = [
        remote(mods.at[place], mods.at[place], ps.at[n], pr.at[n], who) for n, who in enumerate(peers)
    ]
    for copy in second:
        copy.start()
    background.tick()
    for copy in second:
        copy.wait()
    background.finish()


def conditioning_exchange(parts, ident, tasks):
    ranks = parts.shape[0]
    dma = pltpu.SemaphoreType.DMA
    (mods,), gathered = call(
        conditioning_kernel,
        "conditioning",
        ident,
        [shaped((8,) + parts.shape[1:], f32)],
        [
            pltpu.VMEM((ranks - 1,) + parts.shape[1:], f32),
            dma((ranks - 1,)),
            dma((ranks - 1,)),
            dma((7,)),
            dma((7,)),
        ],
        0,
        (parts,),
        tasks,
    )
    return mods, gathered


def epilogue_kernel(
    background, mods, sums, biases, tokens, all_mods, all_sums, all_biases, all_tokens,
    mods_in, sums_in, rank_mods, rank_sums, rank_sums_in, rank_biases_in, ps, pr, zs, zr, qs, qr,
):
    ranks, peers = other_ranks(), plane_peers()
    greet(ranks + peers)
    rank, place = lax.axis_index("batch"), team_place()
    cols = lax.axis_size("col")
    first, extra = [], []
    for n, who in enumerate(peers):
        there = who["row"] * cols + who["col"]
        first.append(remote(mods.at[there], mods_in.at[n], ps.at[0, n], pr.at[0, n], who))
        first.append(remote(sums.at[there], sums_in.at[n], ps.at[1, n], pr.at[1, n], who))
        extra.append(remote(tokens, all_tokens.at[place], ps.at[2, n], pr.at[2, n], who))
    second = [
        remote(biases, rank_biases_in.at[n], zs.at[0, n], zr.at[0, n], who) for n, who in enumerate(ranks)
    ]
    for copy in first + second:
        copy.start()
    background.tick()
    for copy in extra:
        copy.start()
    all_tokens[place] = tokens[...]
    for copy in first:
        copy.wait()
    mod_total, sum_total = mods[place], sums[place]
    for n in range(len(peers)):
        mod_total = mod_total + mods_in[n]
        sum_total = sum_total + sums_in[n]
    rank_mods[rank] = mod_total.astype(bf16)
    rank_sums[...] = sum_total
    third = []
    for n, who in enumerate(ranks):
        third.append(remote(rank_mods.at[rank], rank_mods.at[rank], zs.at[1, n], zr.at[1, n], who))
        third.append(remote(rank_sums.at[who["batch"]], rank_sums_in.at[n], zs.at[2, n], zr.at[2, n], who))
    for copy in third:
        copy.start()
    background.tick()
    bias_total = biases[...]
    for n, copy in enumerate(second):
        copy.wait()
        bias_total = bias_total + rank_biases_in[n]
    for copy in third:
        copy.wait()
    sum_own = rank_sums[rank]
    for n in range(len(ranks)):
        sum_own = sum_own + rank_sums_in[n]
    all_mods[place] = rank_mods[...]
    all_sums[place] = sum_own
    all_biases[place] = bias_total
    last = []
    for n, who in enumerate(peers):
        for m, target in enumerate((all_mods, all_sums, all_biases)):
            last.append(remote(target.at[place], target.at[place], qs.at[m, n], qr.at[m, n], who))
    for copy in last:
        copy.start()
    background.tick()
    for copy in last + extra:
        copy.wait()
    background.finish()


def epilogue(mods, sums, biases, tokens, ident, tasks):
    ranks = lax.axis_size("batch")
    dma = pltpu.SemaphoreType.DMA
    return call(
        epilogue_kernel,
        "epilogue",
        ident,
        [
            shaped((8, ranks) + mods.shape[1:], bf16),
            shaped((8,) + sums.shape[2:], f32),
            shaped((8,) + biases.shape, f32),
            shaped((8,) + tokens.shape, f32),
        ],
        [
            pltpu.VMEM((7,) + mods.shape[1:], f32),
            pltpu.VMEM((7,) + sums.shape[1:], f32),
            pltpu.VMEM((ranks,) + mods.shape[1:], bf16),
            pltpu.VMEM(sums.shape[1:], f32),
            pltpu.VMEM((ranks - 1,) + sums.shape[2:], f32),
            pltpu.VMEM((ranks - 1,) + biases.shape, f32),
            dma((3, 7)),
            dma((3, 7)),
            dma((3, ranks - 1)),
            dma((3, ranks - 1)),
            dma((3, 7)),
            dma((3, 7)),
        ],
        0,
        (mods, sums, biases, tokens),
        tasks,
    )


def closing_kernel(background, parts, every, zs, zr):
    ranks = other_ranks()
    address = sides()[2]
    greet(ranks + list(address.values()))
    rank = lax.axis_index("batch")
    copies = [
        remote(parts.at[who["batch"]], every.at[rank], zs.at[n], zr.at[n], who) for n, who in enumerate(ranks)
    ]
    background.tick()
    for copy in copies:
        copy.start()
    every[rank] = parts[rank]
    for copy in copies:
        copy.wait()
    background.finish()


def closing(parts, ident, tasks):
    ranks = parts.shape[0]
    dma = pltpu.SemaphoreType.DMA
    (every,), gathered = call(
        closing_kernel,
        "closing",
        ident,
        [shaped(parts.shape, f32)],
        [dma((ranks - 1,)), dma((ranks - 1,))],
        0,
        (parts,),
        tasks,
    )
    return every, gathered


def mlp_forward_kernel(
    background, mid, gate_rows, vecs, expand, expand_bias, shrink, full, hidden, expanded, after, *comm
):
    place = sides()
    core, chips, address = place
    images = full.shape[0]
    gathers, scatters = exchanges(full, comm, place)
    greet(list(address.values()) + background.partners())
    own = core * 4 + chips["own"]

    def begin(i):
        full[i, own] = modulate(mid[i], vecs[i, 0:1], vecs[i, 1:2]).astype(bf16)
        gathers[i].first()

    def compute(i, between):
        for step, (start, sibling) in enumerate(halves(core)):
            value = dot(flat(full[i, pl.ds(start, 4)]), expand[...], NN) + expand_bias[...]
            hidden[i, pl.ds(start, 4)] = value.reshape(4, -1, value.shape[1])
            partial = dot(gelu(value).astype(bf16), shrink[...], NT)
            keep_partial(partial, scatters[i], sibling)
            between[step]()

    def end(i):
        value = scatters[i].finish() + vecs[i, 3:4]
        expanded[i] = value
        after[i] = mid[i] + gate_rows[i] * vecs[i, 2:3] * value

    begin(0)
    background.tick()
    gathers[0].second()
    begin(1)
    gathers[0].finish()
    compute(0, (gathers[1].second, scatters[0].first))
    background.tick()
    gathers[1].finish()
    compute(1, (scatters[0].second, scatters[1].first))
    background.tick()
    end(0)
    scatters[1].second()
    end(1)
    for part in gathers + scatters:
        part.drain()
    background.finish()


def mlp_forward(mid, gate_rows, vecs, weights, ident, tasks=()):
    expand, expand_bias, shrink = weights
    images, length, width = mid.shape
    inner = expand.shape[1]
    return call(
        mlp_forward_kernel,
        "mlp_forward",
        ident,
        [
            shaped((images, 8, length, width), bf16),
            shaped((images, 8, length, inner), f32),
            shaped((images, length, width), f32),
            shaped((images, length, width), f32),
        ],
        comm_scratch(images, length, width),
        4 * images * 8 * length * width * inner * 6,
        (
            mid,
            gate_rows,
            vecs,
            expand,
            expand_bias.reshape(1, -1),
            shrink,
        ),
        tasks,
    )


def mlp_backward_kernel(
    background, grad_after, mid, expanded, gate_rows, vecs, expand, shrink, normed, hidden,
    grad_mid, sums, grad_expand, grad_shrink, grad_bias,
    full, grad_hidden, active, sum_expand, sum_shrink, *comm
):
    place = sides()
    core, chips, address = place
    gathers, scatters = exchanges(full, comm, place)
    greet(list(address.values()) + background.partners())
    own = core * 4 + chips["own"]

    def begin(i):
        gated = gate_rows[i] * grad_after[i]
        low = (gated * vecs[i, 1:2]).astype(bf16)
        full[i, own] = low
        gathers[i].first()
        sums[i, 2:3] = column_sum(gated * expanded[i])
        sums[i, 3:4] = column_sum(low.astype(f32))

    def compute(i, between):
        for step, (start, sibling) in enumerate(halves(core)):
            pull = dot(flat(full[i, pl.ds(start, 4)]), shrink[...], NN)
            value, slope = gelu_with_slope(flat(hidden[i, pl.ds(start, 4)]))
            active[i, pl.ds(start, 4)] = value.astype(bf16).reshape(4, -1, value.shape[1])
            low = (pull * slope).astype(bf16)
            grad_hidden[i, pl.ds(start, 4)] = low.reshape(4, -1, value.shape[1])
            keep_partial(dot(low, expand[...], NT), scatters[i], sibling)
            between[step]()

    def weigh_shrink(i):
        term = dot(flat(full[i]), flat(active[i]), TN)
        if i == 0:
            sum_shrink[...] = term
        else:
            grad_shrink[...] = (sum_shrink[...] + term).astype(bf16)

    def weigh_expand(i):
        low = flat(grad_hidden[i])
        term = dot(flat(normed[i]), low, TN)
        if i == 0:
            sum_expand[...] = term
            grad_bias[...] = row_sums(low)
        else:
            grad_expand[...] = (sum_expand[...] + term).astype(bf16)
            grad_bias[...] += row_sums(low)

    def end(i):
        grad, shift_sum, scale_sum = modulate_back_rows(mid[i], vecs[i, 0:1], scatters[i].finish())
        grad_mid[i] = grad + grad_after[i]
        sums[i, 0:1] = shift_sum
        sums[i, 1:2] = scale_sum

    begin(0)
    background.tick()
    gathers[0].second()
    begin(1)
    gathers[0].finish()
    compute(0, (gathers[1].second, scatters[0].first))
    gathers[1].finish()
    compute(1, (scatters[0].second, scatters[1].first))
    weigh_shrink(0)
    end(0)
    scatters[1].second()
    weigh_expand(0)
    weigh_shrink(1)
    weigh_expand(1)
    end(1)
    for part in gathers + scatters:
        part.drain()
    background.finish()


def mlp_backward(grad_after, mid, expanded, gate_rows, vecs, weights, saved, ident, tasks=()):
    expand, _, shrink = weights
    normed, hidden = saved
    images, length, width = mid.shape
    inner = expand.shape[1]
    return call(
        mlp_backward_kernel,
        "mlp_backward",
        ident,
        [
            shaped((images, length, width), f32),
            shaped((images, 8, width), f32),
            shaped((width, inner), bf16),
            shaped((width, inner), bf16),
            shaped((8, inner), f32),
        ],
        [
            pltpu.VMEM((images, 8, length, width), bf16),
            pltpu.VMEM((images, 8, length, inner), bf16),
            pltpu.VMEM((images, 8, length, inner), bf16),
            pltpu.VMEM((width, inner), f32),
            pltpu.VMEM((width, inner), f32),
        ]
        + comm_scratch(images, length, width),
        8 * images * 8 * length * width * inner * 6,
        (
            grad_after,
            mid,
            expanded,
            gate_rows,
            vecs,
            expand,
            shrink,
            normed,
            hidden,
        ),
        tasks,
    )


LOG2E = 1.4426950408889634


def attention_forward_kernel(
    background, base, gate_rows, vecs, project, project_bias, attend, key_bias,
    full, packed, mixed, log_total, attended, mid, *comm
):
    place = sides()
    core, chips, address = place
    images, _, length, _ = full.shape
    gathers, scatters = exchanges(full, comm, place)
    greet(list(address.values()) + background.partners())
    own = core * 4 + chips["own"]
    span = attend.shape[0]
    heads = span // LANES
    tile = 2 * length
    factor = HEAD_SIZE ** (-0.5) * LOG2E

    def begin(i):
        full[i, own] = modulate(base[i], vecs[i, 0:1], vecs[i, 1:2]).astype(bf16)
        gathers[i].first()

    def rows_of(start, count):
        return pl.ds(pl.multiple_of(start * length, length), count * length)

    def compute(i, between):
        for start, _ in halves(core):
            value = dot(flat(full[i, pl.ds(start, 4)]), project[...], NN) + project_bias[...]
            packed[i, rows_of(start, 4)] = value.astype(bf16)
        between[0]()
        for step, (start, sibling) in enumerate(halves(core)):

            def one(t, carry, start=start):
                rows = pl.ds(pl.multiple_of((start + 2 * t) * length, tile), tile)
                for h in range(heads):
                    q, k, v = (
                        pl.ds(part * span + h * LANES, LANES) for part in range(3)
                    )
                    scores = dot(packed[i, rows, q], packed[i, :, k], NT) * factor + key_bias[i]
                    peak = jnp.max(scores, axis=1, keepdims=True)
                    probs = jnp.exp2(scores - peak)
                    total = jnp.sum(probs, axis=1, keepdims=True)
                    out = dot(probs.astype(bf16), packed[i, :, v], NN) / total
                    mixed[i, rows, pl.ds(h * LANES, LANES)] = out.astype(bf16)
                    level = jnp.broadcast_to(peak + jnp.log2(total), (tile, LANES))
                    log_total[i, h, pl.ds(start // 2 + t, 1)] = level.T[0:1]
                return carry

            lax.fori_loop(0, 2, one, 0)
            partial = dot(mixed[i, rows_of(start, 4)], attend[...], NN)
            keep_partial(partial, scatters[i], sibling)
            between[1 + step]()

    def end(i):
        value = scatters[i].finish() + vecs[i, 3:4]
        attended[i] = value
        mid[i] = base[i] + gate_rows[i] * vecs[i, 2:3] * value

    begin(0)
    background.tick()
    gathers[0].second()
    begin(1)
    gathers[0].finish()
    compute(0, (gathers[1].second, background.tick, scatters[0].first))
    gathers[1].finish()
    compute(1, (scatters[0].second, background.tick, scatters[1].first))
    end(0)
    scatters[1].second()
    end(1)
    for part in gathers + scatters:
        part.drain()
    background.finish()


def attention_forward(base, gate_rows, vecs, weights, key_bias, ident, tasks=()):
    project, project_bias, attend = weights
    images, length, width = base.shape
    span = attend.shape[0]
    return call(
        attention_forward_kernel,
        "attention_forward",
        ident,
        [
            shaped((images, 8, length, width), bf16),
            shaped((images, 8 * length, 3 * span), bf16),
            shaped((images, 8 * length, span), bf16),
            shaped((images, span // LANES, 4, 2 * length), f32),
            shaped((images, length, width), f32),
            shaped((images, length, width), f32),
        ],
        comm_scratch(images, length, width),
        8 * images * 8 * length * width * span * 6,
        (
            base,
            gate_rows,
            vecs,
            project,
            project_bias.reshape(1, -1),
            attend,
            key_bias,
        ),
        tasks,
    )


def attention_backward_kernel(
    background, grad_mid, base, attended, gate_rows, vecs, project, attend, key_bias, normed, packed, mixed, log_total,
    grad_base, sums, grad_project, grad_attend, grad_bias,
    full, grad_mixed, grad_packed, grad_keys, grad_values, sum_project, sum_attend, *comm
):
    place = sides()
    core, chips, address = place
    images, _, length, _ = full.shape
    gathers, scatters = exchanges(full, comm, place)
    greet(list(address.values()) + background.partners())
    own = core * 4 + chips["own"]
    span = attend.shape[0]
    heads = span // LANES
    tile = 2 * length
    factor = HEAD_SIZE ** (-0.5)

    def begin(i):
        gated = gate_rows[i] * grad_mid[i]
        low = (gated * vecs[i, 1:2]).astype(bf16)
        full[i, own] = low
        gathers[i].first()
        sums[i, 2:3] = column_sum(gated * attended[i])
        sums[i, 3:4] = column_sum(low.astype(f32))

    def rows_of(start, count):
        return pl.ds(pl.multiple_of(start * length, length), count * length)

    def compute(i, between):
        grad_mixed[...] = dot(flat(full[i]), attend[...], NT).astype(bf16)
        between[0]()
        for h in range(heads):
            lane = pl.ds(h * LANES, LANES)
            q, k, v = (pl.ds(part * span + h * LANES, LANES) for part in range(3))
            keys_turned = packed[i, :, k].T

            def one(t, carry):
                rows = pl.ds(pl.multiple_of(t * tile, tile), tile)
                queries, pulls = packed[i, rows, q], grad_mixed[rows, lane]
                scores = dot(packed[i, :, k], queries, NT) * (factor * LOG2E) + key_bias[i]
                probs = jnp.exp2(scores - log_total[i, h, pl.ds(t, 1)])
                dprobs = dot(packed[i, :, v], pulls, NT)
                row_dot = column_sum(probs * dprobs)
                grad_scores = (probs * (dprobs - row_dot)).astype(bf16)
                value_term = dot(probs.astype(bf16), pulls, NN)
                key_term = dot(grad_scores, queries, NN)

                @pl.when(t == 0)
                def _():
                    grad_values[...] = value_term
                    grad_keys[...] = key_term

                @pl.when(t > 0)
                def _():
                    grad_values[...] += value_term
                    grad_keys[...] += key_term

                query_term = dot(keys_turned, grad_scores, NN) * factor
                grad_packed[i, rows, q] = query_term.T.astype(bf16)
                return carry

            lax.fori_loop(0, 4, one, 0)
            grad_packed[i, :, k] = (grad_keys[...] * factor).astype(bf16)
            grad_packed[i, :, v] = grad_values[...].astype(bf16)
            between[1 + h]()
        for step, (start, sibling) in enumerate(halves(core)):
            keep_partial(dot(grad_packed[i, rows_of(start, 4)], project[...], NT), scatters[i], sibling)

    def weigh_attend(i):
        term = dot(mixed[i], flat(full[i]), TN)
        if i == 0:
            sum_attend[...] = term
        else:
            grad_attend[...] = (sum_attend[...] + term).astype(bf16)

    def weigh_project(i):
        low = grad_packed[i]
        term = dot(flat(normed[i]), low, TN)
        if i == 0:
            sum_project[...] = term
            grad_bias[...] = row_sums(low)
        else:
            grad_project[...] = (sum_project[...] + term).astype(bf16)
            grad_bias[...] += row_sums(low)

    def end(i):
        grad, shift_sum, scale_sum = modulate_back_rows(base[i], vecs[i, 0:1], scatters[i].finish())
        grad_base[i] = grad + grad_mid[i]
        sums[i, 0:1] = shift_sum
        sums[i, 1:2] = scale_sum

    def nothing():
        pass

    begin(0)
    background.tick()
    gathers[0].second()
    begin(1)
    gathers[0].finish()
    compute(0, (gathers[1].second, nothing, gathers[1].finish))
    background.tick()
    scatters[0].first()
    compute(1, (scatters[0].second, background.tick, background.tick))
    weigh_attend(0)
    scatters[1].first()
    weigh_project(0)
    end(0)
    scatters[1].second()
    weigh_attend(1)
    weigh_project(1)
    end(1)
    for part in gathers + scatters:
        part.drain()
    background.finish()


def attention_backward(grad_mid, base, attended, gate_rows, vecs, weights, key_bias, saved, ident, tasks=()):
    project, _, attend = weights
    normed, packed, mixed, log_total = saved
    images, length, width = base.shape
    span = attend.shape[0]
    tokens = 8 * length
    return call(
        attention_backward_kernel,
        "attention_backward",
        ident,
        [
            shaped((images, length, width), f32),
            shaped((images, 8, width), f32),
            shaped((width, 3 * span), bf16),
            shaped((span, width), bf16),
            shaped((8, 3 * span), f32),
        ],
        [
            pltpu.VMEM((images, 8, length, width), bf16),
            pltpu.VMEM((tokens, span), bf16),
            pltpu.VMEM((images, tokens, 3 * span), bf16),
            pltpu.VMEM((tokens, LANES), f32),
            pltpu.VMEM((tokens, LANES), f32),
            pltpu.VMEM((width, 3 * span), f32),
            pltpu.VMEM((span, width), f32),
        ]
        + comm_scratch(images, length, width),
        16 * images * 8 * length * width * span * 6,
        (
            grad_mid,
            base,
            attended,
            gate_rows,
            vecs,
            project,
            attend,
            key_bias,
            normed,
            packed,
            mixed,
            log_total,
        ),
        tasks,
    )


HEAD_SIZE = 72


def pad_heads(array, axis):
    shape = array.shape
    heads = shape[axis] // HEAD_SIZE
    split = array.reshape(shape[:axis] + (heads, HEAD_SIZE) + shape[axis + 1 :])
    widths = [(0, 0)] * split.ndim
    widths[axis + 1] = (0, LANES - HEAD_SIZE)
    return jnp.pad(split, widths).reshape(shape[:axis] + (heads * LANES,) + shape[axis + 1 :])


def unpad_heads(array, axis):
    shape = array.shape
    heads = shape[axis] // LANES
    split = array.reshape(shape[:axis] + (heads, LANES) + shape[axis + 1 :])
    kept = lax.slice_in_dim(split, 0, HEAD_SIZE, axis=axis + 1)
    return kept.reshape(shape[:axis] + (heads * HEAD_SIZE,) + shape[axis + 1 :])


def pack_flat(arrays, multiple):
    flat = jnp.concatenate([array.reshape(-1) for array in arrays])
    return jnp.pad(flat, (0, -flat.size % multiple)).reshape(-1, LANES)


def unpack_ranks(packs, arrays, dims):
    every = packs.reshape(packs.shape[0], -1)
    out = []
    start = 0
    for array, dim in zip(arrays, dims):
        piece = every[:, start : start + array.size].reshape((-1,) + array.shape)
        start += array.size
        piece = jnp.moveaxis(piece, 0, dim)
        shape = list(array.shape)
        shape[dim] = -1
        out.append(piece.reshape(shape))
    return out


def body(
    latents,
    conditioning,
    kept_index,
    kept_count,
    patch_weight,
    patch_bias,
    adaptive_weight,
    adaptive_bias,
    project_weight,
    project_bias,
    attend_weight,
    attend_bias,
    expand_weight,
    expand_bias,
    shrink_weight,
    shrink_bias,
    final_adaptive,
    final_offset,
    final_weight,
    final_bias,
    cotangent,
):
    rows, cols, ranks = lax.axis_size("row"), lax.axis_size("col"), lax.axis_size("batch")
    team = rows * cols
    place = lax.axis_index("row") * cols + lax.axis_index("col")
    rank = lax.axis_index("batch")
    images, channels_in = latents.shape[:2]
    channels_out = cotangent.shape[1]
    rows_tile, cols_tile = latents.shape[2] // PATCH, latents.shape[3] // PATCH
    tile_tokens = rows_tile * cols_tile
    sequence = tile_tokens * team
    width = conditioning.shape[1]
    depth = adaptive_weight.shape[0]
    shard = adaptive_weight.shape[1]
    kept_local = tile_tokens * 3 // 4
    highest = lax.Precision.HIGHEST

    head_cols = width // team
    hidden_cols = expand_weight.shape[2] // team

    def slice_of(array, axis, count):
        return lax.dynamic_slice_in_dim(array, place * count, count, axis=axis)

    piece_rows = min(shard, head_cols)
    pieces_each = head_cols // piece_rows
    project_own = lax.dynamic_index_in_dim(
        project_weight.reshape(depth, shard, 3, team, head_cols), place, axis=3, keepdims=False
    ).reshape(depth, shard, 3 * head_cols)
    attend_own = jnp.stack(
        [
            lax.dynamic_slice_in_dim(
                attend_weight, (place * head_cols + j * piece_rows) % shard, piece_rows, axis=1
            )
            for j in range(pieces_each)
        ],
        axis=1,
    )
    expand_own = slice_of(expand_weight, 2, hidden_cols)
    shrink_own = slice_of(shrink_weight, 1, hidden_cols).transpose(0, 2, 1)

    smalls = [
        patch_weight,
        patch_bias,
        adaptive_bias,
        project_bias,
        attend_bias,
        expand_bias,
        shrink_bias,
        final_offset,
        final_weight,
        conditioning,
    ]
    patch_tiles = to_tokens(latents, PATCH)
    grad_tiles = to_tokens(cotangent, PATCH)
    patch_in, patch_out = patch_tiles.shape[2], grad_tiles.shape[2]
    tiles = jnp.concatenate([patch_tiles, grad_tiles], axis=2)
    packs, every_tile = prologue(pack_flat(smalls, 2048), tiles.reshape(-1, LANES), 8)
    (
        patch_full,
        patch_bias_full,
        adaptive_offset,
        project_offset,
        attend_offset,
        expand_offset,
        shrink_offset,
        final_offset_full,
        final_full,
        cond_all,
    ) = unpack_ranks(packs, smalls, [1, 0, 1, 1, 1, 1, 1, 0, 0, 0])

    whole = every_tile.reshape((rows, cols, images, rows_tile, cols_tile, -1)).transpose(2, 0, 3, 1, 4, 5)
    whole = whole.reshape(images, sequence, patch_in + patch_out)
    grid_cols = cols * cols_tile
    own_ids = lax.dynamic_index_in_dim(
        kept_index.reshape(images, tile_tokens, team), place, axis=2, keepdims=False
    )
    pick = (own_ids[:, :, None] == jnp.arange(sequence, dtype=jnp.int32)).astype(bf16)
    own = jnp.einsum("ikt,itc->ikc", pick, whole, preferred_element_type=f32).astype(bf16)
    patches, grad_outputs = own[..., :patch_in], own[..., patch_in:]
    order = jnp.arange(kept_local, dtype=jnp.int32)[:, None] * team + jnp.arange(team, dtype=jnp.int32)
    kept_grid = order[None] < kept_count[:, None, None]
    chunk_order = kept_grid.reshape(images, kept_local, team // 2, 2).transpose(0, 3, 2, 1)
    key_bias = jnp.where(chunk_order.reshape(images, team * kept_local), 0.0, masked_score).astype(f32)
    kept_rows = lax.dynamic_index_in_dim(kept_grid, place, axis=2, keepdims=False).astype(f32)[:, :, None]

    count = width // 4
    omega = 1.0 / 10000.0 ** (jnp.arange(count, dtype=f32) / count)
    angles = jnp.arange(max(rows * rows_tile, grid_cols), dtype=f32)[:, None] * omega[None, :]
    along = jnp.concatenate([jnp.sin(angles), jnp.cos(angles)], axis=1)
    places = jnp.arange(along.shape[0], dtype=jnp.int32)

    def position_of(coords):
        chosen = (coords[..., None] == places).astype(f32)
        return jnp.einsum("ikt,tc->ikc", chosen, along, precision=highest)

    position = jnp.concatenate(
        [position_of(own_ids // grid_cols), position_of(own_ids % grid_cols)], axis=-1
    )
    resid = (
        jnp.einsum("ikc,cd->ikd", patches, patch_full, preferred_element_type=f32)
        + patch_bias_full.astype(f32)
        + position
    )

    silu_all = jax.nn.silu(cond_all.astype(f32)).astype(bf16)
    silu_rows = lax.dynamic_slice_in_dim(silu_all, rank * shard, shard, axis=1)
    mod_cols, final_cols = adaptive_weight.shape[2] // team, final_adaptive.shape[1] // team
    parts = [
        dot(silu_rows, slice_of(adaptive_weight[b], 1, mod_cols), ((1,), (0,))) for b in range(depth)
    ] + [dot(silu_rows, slice_of(final_adaptive, 1, final_cols), ((1,), (0,)))]
    parts = jnp.concatenate(parts, axis=1).reshape(ranks, images, -1)
    mods, (project_next, attend_next) = conditioning_exchange(
        parts, 9, [Line(project_own[0]), Chain(attend_own[0], shard)]
    )
    mods = mods.transpose(1, 0, 2)

    def attention_matrices(project_parts, attend_parts):
        project = pad_heads(project_parts.reshape(width, 3, head_cols), 2).reshape(width, -1)
        return project, pad_heads(attend_parts.reshape(head_cols, width), 0)

    pieces = []
    for b in range(depth):
        block_mod = mods[:, :, b * mod_cols : (b + 1) * mod_cols].reshape(images, -1)
        block_mod = (block_mod + adaptive_offset[b].astype(f32)).reshape(images, 6, 1, width)
        pieces.append([block_mod[:, s] for s in range(6)])
    final_mod = mods[:, :, depth * mod_cols :].reshape(images, -1) + final_offset_full.astype(f32)
    final_mod = final_mod.reshape(images, 2, 1, width)
    final_shift, final_scale = final_mod[:, 0], final_mod[:, 1]

    records = []
    for b in range(depth):
        project, attend = attention_matrices(project_next, attend_next)
        shift1, scale1, gate1, shift2, scale2, gate2 = pieces[b]
        bias = project_offset[b].astype(f32).reshape(2, team, head_cols)
        bias = lax.dynamic_index_in_dim(bias, place, axis=1, keepdims=False)
        bias = pad_heads(jnp.stack([bias[0], jnp.zeros_like(bias[0]), bias[1]]), 1).reshape(-1)
        attention_weights = (project, bias, attend)
        routed = b > 0
        base = resid[:, :kept_local] if routed else resid
        gate_rows = kept_rows if routed else jnp.ones((images, tile_tokens, 1), f32)
        keys = key_bias if routed else jnp.zeros((images, sequence), f32)

        def rows_with(parts, bias_row):
            row = jnp.broadcast_to(bias_row.astype(f32), (images, 1, width))
            return jnp.concatenate(parts + [row], axis=1)

        tasks = [Line(expand_own[b])]
        if not routed:
            tasks.append(Line(shrink_own[b]))
        (*attention_saved, attended, mid), gathered = attention_forward(
            base,
            gate_rows,
            rows_with([shift1, scale1, gate1], attend_offset[b]),
            attention_weights,
            keys[:, None, :],
            4 * b,
            tasks,
        )
        expand = gathered[0].reshape(width, hidden_cols)
        shrink = (shrink_next if routed else gathered[1]).reshape(width, hidden_cols)
        mlp_weights = (expand, slice_of(expand_offset[b].astype(f32), 0, hidden_cols), shrink)
        tasks = []
        if b + 1 < depth:
            tasks = [Line(project_own[b + 1]), Chain(attend_own[b + 1], shard), Line(shrink_own[b + 1])]
        (*mlp_saved, expanded, after), gathered = mlp_forward(
            mid,
            gate_rows,
            rows_with([shift2, scale2, gate2], shrink_offset[b]),
            mlp_weights,
            4 * b + 1,
            tasks,
        )
        if tasks:
            project_next, attend_next, shrink_next = gathered
        records.append(
            (base, mid, attended, expanded, attention_weights, mlp_weights, keys, gate_rows, attention_saved, mlp_saved)
        )
        resid = jnp.concatenate([after, resid[:, kept_local:]], axis=1) if routed else after

    final_normed = modulate(resid, final_shift, final_scale).astype(bf16)
    outputs = jnp.einsum("ikd,dc->ikc", final_normed, final_full, preferred_element_type=f32) + final_bias.astype(f32)
    final_bias_term = jnp.sum(grad_outputs.astype(f32), axis=(0, 1))
    final_weight_term = jnp.einsum("ikd,ikc->dc", final_normed, grad_outputs, preferred_element_type=f32)
    grad_final = jnp.einsum("ikc,dc->ikd", grad_outputs, final_full, preferred_element_type=f32)
    grad_resid, grad_final_shift, grad_final_scale = modulate_back(resid, final_scale, grad_final)
    final_mod_term = jnp.stack([grad_final_shift, grad_final_scale], axis=1)

    mod_terms = [None] * depth
    bias_terms = [None] * depth
    token_terms = [None] * depth
    spread = [[None, None, None] for _ in range(depth)]

    def folded(source, inbox):
        own = lax.dynamic_index_in_dim(source, rank, axis=0, keepdims=False)
        return (own.astype(f32) + jnp.sum(inbox.astype(f32), axis=0)).astype(bf16)

    def fold_mlp(terms, inboxes):
        return jnp.stack([folded(term, inbox) for term, inbox in zip(terms, inboxes)])

    def fold_attention(terms, inboxes):
        project_part = folded(terms[0], inboxes[0]).reshape(2, shard // 2, -1)
        attend_part = terms[1].astype(f32) + jnp.sum(inboxes[1].astype(f32), axis=1)
        return project_part, attend_part.astype(bf16).reshape(2, head_cols // 2, width)

    attention_terms, waiting = None, []
    for b in reversed(range(depth)):
        base, mid, attended, expanded, attention_weights, mlp_weights, keys, gate_rows, attention_saved, mlp_saved = records[b]
        shift1, scale1, gate1, shift2, scale2, gate2 = pieces[b]
        routed = b > 0
        grad_after = grad_resid[:, :kept_local] if routed else grad_resid
        tasks = []
        if attention_terms is not None:
            tasks = [Fold(attention_terms[0]), FoldTo(attention_terms[1], shard)]
        (grad_mid, mlp_sums, grad_expand, grad_shrink, grad_expand_bias), inboxes = mlp_backward(
            grad_after,
            mid,
            expanded,
            gate_rows,
            jnp.concatenate([scale2, gate2], axis=1),
            mlp_weights,
            mlp_saved,
            4 * b + 2,
            tasks,
        )
        if tasks:
            waiting += [(b + 1, n, part) for n, part in zip((1, 2), fold_attention(attention_terms, inboxes))]
        mlp_terms = [term.reshape(ranks, shard, hidden_cols) for term in (grad_expand, grad_shrink)]
        tasks = [Fold(term) for term in mlp_terms] + [PlaneGather(part, late=1) for _, _, part in waiting]
        (grad_base, attention_sums, grad_project, grad_attend, grad_project_bias), inboxes = attention_backward(
            grad_mid,
            base,
            attended,
            gate_rows,
            jnp.concatenate([scale1, gate1], axis=1),
            attention_weights,
            keys[:, :, None],
            attention_saved,
            4 * b + 3,
            tasks,
        )
        for (block, n, _), every in zip(waiting, inboxes[2:]):
            spread[block][n] = every
        waiting = [(b, 0, fold_mlp(mlp_terms, inboxes[:2]))]
        attention_terms = (
            unpad_heads(grad_project.reshape(width, 3, -1), 2).reshape(ranks, shard, 3 * head_cols),
            unpad_heads(grad_attend, 0).reshape(pieces_each, piece_rows, width),
        )
        grad_bias = unpad_heads(grad_project_bias[0].reshape(3, -1), 1)
        bias_terms[b] = jnp.concatenate([grad_bias[0], grad_bias[2], grad_expand_bias[0]])
        token_terms[b] = jnp.sum(jnp.stack([attention_sums[:, 3], mlp_sums[:, 3]]), axis=1)
        grad_resid = jnp.concatenate([grad_base, grad_resid[:, kept_local:]], axis=1) if routed else grad_base
        mod_terms[b] = jnp.concatenate([attention_sums[:, :3], mlp_sums[:, :3]], axis=1)

    patch_bias_term = jnp.sum(grad_resid, axis=(0, 1))
    grad_embed = grad_resid.astype(bf16)
    patch_term = jnp.einsum("ikc,ikd->cd", patches, grad_embed, preferred_element_type=f32)
    grad_patches = jnp.einsum("ikd,cd->ikc", grad_embed, patch_full, preferred_element_type=f32)

    mod_slices = [
        term.reshape(images, team, -1) for term in mod_terms + [final_mod_term]
    ]
    mod_slices = jnp.concatenate(mod_slices, axis=2).transpose(1, 0, 2)
    bias_row = jnp.tile(jnp.pad(final_bias_term, (0, shard - patch_out)), ranks)
    token_rows = jnp.concatenate(
        [patch_term, patch_bias_term[None], final_weight_term.T] + token_terms + [bias_row[None]], axis=0
    )
    row_count = token_rows.shape[0]
    token_rows = jnp.pad(token_rows, ((0, -row_count % team), (0, 0)))
    token_rows = token_rows.reshape(team, -1, ranks, shard).transpose(0, 2, 1, 3)
    biases = pack_flat(bias_terms, 1024)
    tokens_out = jnp.concatenate([outputs, grad_patches], axis=2).reshape(-1, LANES)
    tasks = [Fold(attention_terms[0]), FoldTo(attention_terms[1], shard)]
    tasks += [PlaneGather(part) for _, _, part in waiting]
    (all_mods, all_sums, all_biases, all_tokens), inboxes = epilogue(
        mod_slices, token_rows, biases, tokens_out, 10, tasks
    )
    for (block, n, _), every in zip(waiting, inboxes[2:]):
        spread[block][n] = every
    last_parts = fold_attention(attention_terms, inboxes[:2])

    mod_every = all_mods.reshape(team, ranks * images, -1).transpose(1, 0, 2)
    mod_width = adaptive_weight.shape[2]
    block_mods = [
        mod_every[:, :, b * mod_cols : (b + 1) * mod_cols].reshape(ranks * images, mod_width) for b in range(depth)
    ]
    final_mods = mod_every[:, :, depth * mod_cols :].reshape(ranks * images, -1)
    grad_silu = dot(final_mods, final_adaptive, NT)
    for b in range(depth):
        grad_silu = grad_silu + dot(block_mods[b], adaptive_weight[b], NT)
    grad_silu, last = closing(
        grad_silu.reshape(ranks, images, shard), 11, [PlaneGather(part) for part in last_parts]
    )
    spread[0][1], spread[0][2] = last
    grad_silu = grad_silu.transpose(1, 0, 2).reshape(images, width)
    conditioning_grad = jax.vjp(jax.nn.silu, conditioning.astype(f32))[1](grad_silu)[0]
    adaptive_weight_grad = jnp.stack([dot(silu_rows, m, TN) for m in block_mods])
    final_adaptive_grad = dot(silu_rows, final_mods, TN)

    def rank_part(full):
        part = full.shape[-1] // ranks
        return lax.dynamic_slice_in_dim(full, rank * part, part, axis=full.ndim - 1)

    adaptive_bias_grad = rank_part(jnp.stack([jnp.sum(m.astype(f32), axis=0) for m in block_mods]))
    final_offset_grad = rank_part(jnp.sum(final_mods.astype(f32), axis=0))

    ordered = all_tokens.reshape(team, images, tile_tokens, -1).transpose(1, 2, 0, 3)
    ordered = ordered.reshape(images, sequence, patch_out + patch_in)
    tile_rows = lax.axis_index("row") * rows_tile + jnp.arange(rows_tile, dtype=jnp.int32)
    tile_cols = lax.axis_index("col") * cols_tile + jnp.arange(cols_tile, dtype=jnp.int32)
    tile_ids = (tile_rows[:, None] * grid_cols + tile_cols).reshape(-1)
    back = (kept_index[:, None, :] == tile_ids[None, :, None]).astype(f32)
    tile_out = jnp.einsum("itj,ijc->itc", back, ordered, precision=highest)
    prediction = to_planes(tile_out[..., :patch_out], PATCH, channels_out, rows_tile, cols_tile)
    latent_grad = to_planes(tile_out[..., patch_out:], PATCH, channels_in, rows_tile, cols_tile)

    def in_order(every):
        split = every.reshape((2, team // 2) + every.shape[1:])
        return jnp.swapaxes(split, 0, 1).reshape(every.shape)

    project_grads, attend_grads, expand_grads, shrink_grads = [], [], [], []
    for mlp_every, project_every, attend_every in spread:
        mlp_every = in_order(mlp_every)
        expand_grads.append(mlp_every[:, 0].transpose(1, 0, 2).reshape(shard, -1).astype(f32))
        shrink_grads.append(mlp_every[:, 1].transpose(0, 2, 1).reshape(-1, shard).astype(f32))
        project_every = in_order(project_every).reshape(team, shard, 3, head_cols)
        project_grads.append(project_every.transpose(1, 2, 0, 3).reshape(shard, -1).astype(f32))
        attend_every = in_order(attend_every).reshape(width, width)
        attend_grads.append(lax.dynamic_slice_in_dim(attend_every, rank * shard, shard, axis=0).astype(f32))

    sums = all_sums.reshape(-1, shard)
    biases = all_biases.reshape(team, -1)[:, : depth * (2 * head_cols + hidden_cols)]
    biases = biases.reshape(team, depth, -1).transpose(1, 0, 2)
    project_bias_grad = jnp.concatenate(
        [biases[:, :, part * head_cols : (part + 1) * head_cols].reshape(depth, width) for part in range(2)], axis=1
    )
    expand_bias_grad = biases[:, :, 2 * head_cols :].reshape(depth, -1)
    first = patch_in + 1 + patch_out
    block_sums = sums[first : first + 2 * depth].reshape(depth, 2, shard)

    return (
        prediction,
        latent_grad,
        conditioning_grad,
        sums[:patch_in],
        sums[patch_in],
        adaptive_weight_grad,
        adaptive_bias_grad,
        jnp.stack(project_grads),
        rank_part(project_bias_grad),
        jnp.stack(attend_grads),
        block_sums[:, 0],
        jnp.stack(expand_grads),
        rank_part(expand_bias_grad),
        jnp.stack(shrink_grads),
        block_sums[:, 1],
        final_adaptive_grad,
        final_offset_grad,
        sums[patch_in + 1 : first].T,
        sums[first + 2 * depth, :patch_out],
    )


def solution(mesh):
    tokens = P("batch", None, "row", "col")
    placed = (
        tokens,
        P("batch", None),
        P("batch", None),
        P("batch"),
        P(None, "batch"),
        P("batch"),
        P(None, "batch", None),
        P(None, "batch"),
        P(None, "batch", None),
        P(None, "batch"),
        P(None, "batch", None),
        P(None, "batch"),
        P(None, "batch", None),
        P(None, "batch"),
        P(None, None, "batch"),
        P(None, "batch"),
        P("batch", None),
        P("batch"),
        P("batch", None),
        P(),
        tokens,
    )
    return jax.shard_map(
        body,
        mesh=mesh,
        in_specs=placed,
        out_specs=(tokens, tokens, P("batch", None)) + placed[4:16] + (placed[16], P("batch"), P("batch", None), P()),
        check_vma=False,
    )
```

```python
from functools import partial

import jax
import jax.numpy as jnp
from jax import lax
from jax.experimental import pallas as pl
from jax.experimental.pallas import tpu as pltpu
from jax.sharding import PartitionSpec as P

HEADS = 16
PATCH = 2
LANES = 128
PLANE = ("row", "col")

norm_epsilon = 1e-06
masked_score = -1e30
f32 = jnp.float32
bf16 = jnp.bfloat16


def to_tokens(planes, patch_side):
    images, channels, height, breadth = planes.shape
    shaped = planes.reshape(
        images, channels, height // patch_side, patch_side, breadth // patch_side, patch_side
    )
    return shaped.transpose(0, 2, 4, 3, 5, 1).reshape(
        images, height // patch_side * (breadth // patch_side), patch_side * patch_side * channels
    )


def to_planes(token_rows, patch_side, channels, rows_tile, cols_tile):
    images = token_rows.shape[0]
    shaped = token_rows.reshape(images, rows_tile, cols_tile, patch_side, patch_side, channels)
    return shaped.transpose(0, 5, 1, 3, 2, 4).reshape(
        images, channels, rows_tile * patch_side, cols_tile * patch_side
    )


def dot(left, right, dims, precision=None):
    return lax.dot_general(left, right, (dims, ((), ())), precision=precision, preferred_element_type=f32)


def norm_parts(resid):
    centered = resid - jnp.mean(resid, axis=-1, keepdims=True)
    rstd = lax.rsqrt(jnp.mean(centered * centered, axis=-1, keepdims=True) + norm_epsilon)
    return centered * rstd, rstd


def modulate(resid, shift_part, scale_part):
    return norm_parts(resid)[0] * (1.0 + scale_part) + shift_part


def modulate_back(resid, scale_part, grad):
    unit, rstd = norm_parts(resid)
    inner = grad * (1.0 + scale_part)
    grad_in = rstd * (
        inner
        - jnp.mean(inner, axis=-1, keepdims=True)
        - unit * jnp.mean(inner * unit, axis=-1, keepdims=True)
    )
    return grad_in, jnp.sum(grad, axis=1), jnp.sum(grad * unit, axis=1)


def sides():
    row, col = lax.axis_index("row"), lax.axis_index("col")
    core = lax.rem(col, 2)
    across = col // 2
    chip = row * 2 + across
    chips = {
        "own": chip,
        "x": (1 - row) * 2 + across,
        "y": row * 2 + 1 - across,
        "far": (1 - row) * 2 + 1 - across,
    }
    address = {
        "x": {"row": 1 - row},
        "y": {"col": lax.rem(col + 2, 4)},
        "core": {"col": col + 1 - 2 * core},
    }
    return core, chips, address


def greet(addresses):
    barrier = pltpu.get_barrier_semaphore()
    for who in addresses:
        pl.semaphore_signal(barrier, inc=1, device_id=who, device_id_type=pl.DeviceIdType.MESH)
    pl.semaphore_wait(barrier, len(addresses))


def remote(source, target, send, recv, who):
    return pltpu.make_async_remote_copy(
        src_ref=source,
        dst_ref=target,
        send_sem=send,
        recv_sem=recv,
        device_id=who,
        device_id_type=pl.DeviceIdType.MESH,
    )


def rank_at(offset):
    ranks = lax.axis_size("batch")
    return {"batch": lax.rem(lax.axis_index("batch") + offset + ranks, ranks)}


def other_ranks():
    return [rank_at(offset) for offset in range(1, lax.axis_size("batch"))]


def plane_peers():
    row, col = lax.axis_index("row"), lax.axis_index("col")
    rows, cols = lax.axis_size("row"), lax.axis_size("col")
    return [
        {"row": lax.rem(row + n // cols, rows), "col": lax.rem(col + n % cols, cols)}
        for n in range(1, rows * cols)
    ]


class Line:
    reach = 1

    def __init__(self, source):
        ranks = lax.axis_size("batch")
        self.ins = [source]
        self.outs = [jax.ShapeDtypeStruct((ranks,) + source.shape, source.dtype)]
        self.sems = [(2, ranks - 1), (2, ranks - 1), (1,)]

    def bind(self, ins, outs, sems):
        (self.source,), (self.target,) = ins, outs
        self.send, self.recv, self.own = sems
        self.rank, self.ranks = lax.axis_index("batch"), lax.axis_size("batch")
        self.steps = self.ranks
        self.late = 0

    def copy(self, way, r):
        block = self.rank - r if way == 0 else self.rank + r
        source = self.source if r == 0 else self.target.at[block]
        return remote(
            source, self.target.at[block], self.send.at[way, r], self.recv.at[way, r], rank_at(1 - 2 * way)
        )

    def holds(self, way, r):
        return self.rank >= r if way == 0 else self.rank + r < self.ranks

    def sends(self, way, r):
        edge = self.rank + 1 < self.ranks if way == 0 else self.rank > 0
        return jnp.logical_and(self.holds(way, r), edge)

    def step(self, r):
        for way in (0, 1):
            if r > 0:
                block = self.rank - r if way == 0 else self.rank + r

                @pl.when(self.holds(way, r))
                def _(way=way, block=block):
                    place = self.target.at[block]
                    remote(place, place, self.send.at[way, r - 1], self.recv.at[way, r - 1], rank_at(1)).wait_recv()

            if r < self.ranks - 1:

                @pl.when(self.sends(way, r))
                def _(way=way):
                    self.copy(way, r).start()

        if r == 0:
            self.stay().start()

    def stay(self):
        return pltpu.make_async_copy(self.source, self.target.at[self.rank], self.own.at[0])

    def finish(self):
        for way in (0, 1):
            for r in range(self.ranks - 1):

                @pl.when(self.sends(way, r))
                def _(way=way, r=r):
                    self.copy(way, r).wait_send()

        self.stay().wait()


class Chain:
    reach = 1

    def __init__(self, source, shard):
        pieces, self.rows, _ = source.shape
        self.shard = shard
        self.ins = [source]
        self.outs = [jax.ShapeDtypeStruct(source.shape, source.dtype)]
        self.sems = [(pieces, 2), (pieces, 2), (pieces,)]

    def bind(self, ins, outs, sems):
        (self.source,), (self.target,) = ins, outs
        self.send, self.recv, self.own = sems
        self.rank, self.ranks = lax.axis_index("batch"), lax.axis_size("batch")
        self.steps = self.ranks
        self.late = 0
        self.owners = owners_of(self.source.shape[0], self.rows, self.shard)

    def copy(self, j, way, first):
        source = self.source.at[j] if first else self.target.at[j]
        return remote(
            source, self.target.at[j], self.send.at[j, way], self.recv.at[j, way], rank_at(1 - 2 * way)
        )

    def edge(self, way):
        return self.rank + 1 < self.ranks if way == 0 else self.rank > 0

    def step(self, r):
        for j, owner in enumerate(self.owners):
            for way in (0, 1):
                away = self.rank - owner if way == 0 else owner - self.rank
                if r > 0:

                    @pl.when(away == r)
                    def _(j=j, way=way):
                        self.copy(j, way, False).wait_recv()

                @pl.when(jnp.logical_and(away == r, self.edge(way)))
                def _(j=j, way=way):
                    self.copy(j, way, r == 0).start()

            if r == 0:

                @pl.when(self.rank == owner)
                def _(j=j):
                    self.stay(j).start()

    def stay(self, j):
        return pltpu.make_async_copy(self.source.at[j], self.target.at[j], self.own.at[j])

    def finish(self):
        for j, owner in enumerate(self.owners):
            for way in (0, 1):
                away = self.rank - owner if way == 0 else owner - self.rank

                @pl.when(jnp.logical_and(away >= 0, self.edge(way)))
                def _(j=j, way=way):
                    self.copy(j, way, False).wait_send()

            @pl.when(self.rank == owner)
            def _(j=j):
                self.stay(j).wait()


def team_place():
    return lax.axis_index("row") * lax.axis_size("col") + lax.axis_index("col")


def owners_of(pieces, rows, shard):
    place = team_place()
    return [(place * pieces + j) * rows // shard for j in range(pieces)]


class Fold:
    reach = 2

    def __init__(self, source):
        ranks = lax.axis_size("batch")
        self.ins = [source]
        self.outs = [jax.ShapeDtypeStruct((ranks - 1,) + source.shape[1:], source.dtype)]
        self.sems = [(ranks - 1,), (ranks - 1,)]

    def bind(self, ins, outs, sems):
        (self.source,), (self.inbox,) = ins, outs
        self.send, self.recv = sems
        self.steps = 1
        self.late = 0

    def copies(self):
        for n in range(lax.axis_size("batch") - 1):
            who = rank_at(n + 1)
            yield remote(
                self.source.at[who["batch"]], self.inbox.at[n], self.send.at[n], self.recv.at[n], who
            )

    def step(self, r):
        for copy in self.copies():
            copy.start()

    def finish(self):
        for copy in self.copies():
            copy.wait()


class FoldTo:
    reach = 2

    def __init__(self, shape, shard, late):
        pieces, self.rows, width = shape
        others = lax.axis_size("batch") - 1
        self.shard = shard
        self.ins = []
        self.outs = [jax.ShapeDtypeStruct((pieces, others, self.rows, width), bf16)]
        self.sems = [(pieces, others), (pieces, others)]
        self.late, self.pieces = late, pieces

    def bind(self, ins, outs, sems):
        (self.inbox,) = outs
        self.source = None
        self.send, self.recv = sems
        self.steps = 1
        self.rank, self.others = lax.axis_index("batch"), lax.axis_size("batch") - 1
        self.owners = owners_of(self.pieces, self.rows, self.shard)

    def copy(self, j, n):
        return remote(
            self.source.at[j], self.inbox.at[j, n], self.send.at[j, n], self.recv.at[j, n], rank_at(n + 1)
        )

    def leads(self, j, n):
        return rank_at(n + 1)["batch"] == self.owners[j]

    def step(self, r):
        for j in range(len(self.owners)):
            for n in range(self.others):

                @pl.when(self.leads(j, n))
                def _(j=j, n=n):
                    self.copy(j, n).start()

    def finish(self):
        for j, owner in enumerate(self.owners):
            for n in range(self.others):

                @pl.when(self.rank == owner)
                def _(j=j, n=n):
                    self.copy(j, n).wait_recv()

                @pl.when(self.leads(j, n))
                def _(j=j, n=n):
                    self.copy(j, n).wait_send()


class Copies:
    def __init__(self, send, recv, address):
        self.send, self.recv, self.address = send, recv, address
        self.started = {}

    def go(self, slot, source, target, who):
        copy = remote(source, target, self.send.at[slot], self.recv.at[slot], self.address[who])
        copy.start()
        self.started[slot] = copy

    def arrived(self, *slots):
        for slot in slots:
            self.started[slot].wait_recv()

    def drain(self):
        for copy in self.started.values():
            copy.wait_send()


class Gather(Copies):
    def __init__(self, full, send, recv, place):
        core, chips, address = place
        super().__init__(send, recv, address)
        self.full, self.half = full, full.shape[1] // 2
        self.source = None
        self.at = {name: core * 4 + chip for name, chip in chips.items()}

    def whole(self, name):
        return self.full.at[self.at[name]]

    def part(self, name, second):
        return self.full.at[self.at[name], pl.ds(self.half * second, self.half)]

    def first(self):
        own = self.whole("own")
        source = own if self.source is None else self.source
        self.go(0, source, own, "x")
        self.go(1, source, own, "y")
        self.go(2, source, own, "core")

    def second(self):
        self.arrived(0)
        self.go(3, self.part("x", 0), self.part("x", 0), "y")
        self.arrived(1)
        self.go(4, self.part("y", 1), self.part("y", 1), "x")
        self.go(5, self.whole("x"), self.whole("x"), "core")
        self.go(6, self.whole("y"), self.whole("y"), "core")

    def finish(self):
        self.arrived(3, 4)
        self.go(7, self.whole("far"), self.whole("far"), "core")
        self.arrived(2, 5, 6, 7)


class PlaneGather:
    reach = 0

    def __init__(self, source, late=0):
        self.ins = [source]
        self.outs = [jax.ShapeDtypeStruct((8,) + source.shape, source.dtype)]
        self.sems = [(8,), (8,), (1,)]
        self.late = late

    def bind(self, ins, outs, sems):
        (self.source,), (self.target,) = ins, outs
        send, recv, self.own = sems
        self.gather = Gather(self.target, send, recv, sides())
        self.gather.source = self.source
        self.steps = 3

    def stay(self):
        return pltpu.make_async_copy(self.source, self.gather.whole("own"), self.own.at[0])

    def step(self, r):
        if r == 0:
            self.gather.first()
            self.stay().start()
        elif r == 1:
            self.gather.second()
        else:
            self.gather.finish()

    def finish(self):
        self.gather.drain()
        self.stay().wait()


class Background:
    def __init__(self, tasks):
        self.tasks = tasks
        self.now = 0

    def partners(self):
        reach = max([task.reach for task in self.tasks], default=0)
        return [[], [rank_at(1), rank_at(-1)], other_ranks()][reach]

    def tick(self):
        for task in self.tasks:
            if 0 <= self.now - task.late < task.steps:
                task.step(self.now - task.late)
        self.now += 1

    def finish(self):
        for task in self.tasks:
            for r in range(max(self.now - task.late, 0), task.steps):
                task.step(r)
            task.finish()


class Scatter(Copies):
    def __init__(self, core_out, core_in, total, hop_out, hop_in, send, recv, place):
        _, self.chips, address = place
        super().__init__(send, recv, address)
        self.core_out, self.core_in, self.total = core_out, core_in, total
        self.hop_out, self.hop_in = hop_out, hop_in
        self.half = total.shape[1] // 2

    def cross(self):
        self.go(0, self.core_out, self.core_in, "core")

    def hop(self, slot, value, who):
        self.hop_out[slot] = value.astype(bf16)
        self.go(1 + slot, self.hop_out.at[slot], self.hop_in.at[slot], who)

    def first(self):
        self.arrived(0)
        half = self.half

        def summed(name):
            chip = self.chips[name]
            return self.total[chip] + self.core_in[chip].astype(f32)

        far = summed("far")
        self.hop(0, far[:half], "x")
        self.hop(2, far[half:], "y")
        x_sum = summed("x")
        self.hop(1, x_sum[:half], "x")
        self.total[self.chips["x"], half:] = x_sum[half:]
        y_sum = summed("y")
        self.hop(3, y_sum[half:], "y")
        self.total[self.chips["y"], :half] = y_sum[:half]

    def second(self):
        half = self.half
        self.arrived(1)
        self.hop(4, self.total[self.chips["y"], :half] + self.hop_in[0].astype(f32), "y")
        self.arrived(3)
        self.hop(5, self.total[self.chips["x"], half:] + self.hop_in[2].astype(f32), "x")

    def finish(self):
        self.arrived(2, 4, 5, 6)
        half, own = self.half, self.chips["own"]
        base = self.total[own] + self.core_in[own].astype(f32)
        low = base[:half] + self.hop_in[1].astype(f32) + self.hop_in[4].astype(f32)
        high = base[half:] + self.hop_in[3].astype(f32) + self.hop_in[5].astype(f32)
        return jnp.concatenate([low, high], axis=0)


def comm_scratch(images, length, width):
    half = length // 2
    return [
        pltpu.VMEM((images, 4, length, width), bf16),
        pltpu.VMEM((images, 4, length, width), bf16),
        pltpu.VMEM((images, 4, length, width), f32),
        pltpu.VMEM((images, 6, half, width), bf16),
        pltpu.VMEM((images, 6, half, width), bf16),
        pltpu.SemaphoreType.DMA((images, 8)),
        pltpu.SemaphoreType.DMA((images, 8)),
        pltpu.SemaphoreType.DMA((images, 7)),
        pltpu.SemaphoreType.DMA((images, 7)),
    ]


def exchanges(full, comm, place):
    core_out, core_in, total, hop_out, hop_in, gs, gr, ss, sr = comm
    images = full.shape[0]
    gathers = [Gather(full.at[i], gs.at[i], gr.at[i], place) for i in range(images)]
    scatters = [
        Scatter(
            core_out.at[i], core_in.at[i], total.at[i], hop_out.at[i], hop_in.at[i], ss.at[i], sr.at[i], place
        )
        for i in range(images)
    ]
    return gathers, scatters


def flat(value):
    return value.reshape(value.shape[0] * value.shape[1], value.shape[2])


def halves(core):
    return ((1 - core) * 4, True), (core * 4, False)


def keep_partial(partial, scatter, sibling):
    shape = scatter.total.shape
    if sibling:
        scatter.core_out[...] = partial.astype(bf16).reshape(shape)
        scatter.cross()
    else:
        scatter.total[...] = partial.reshape(shape)


def column_sum(value):
    return jnp.sum(value, axis=0, keepdims=True)


def row_sums(value):
    ones = jnp.ones((8, value.shape[0]), bf16)
    return dot(ones, value, ((1,), (0,)))


GELU_ROOT = 0.7978845608028654
GELU_CUBE = 0.044715
NN, NT, TN = ((1,), (0,)), ((1,), (1,)), ((0,), (0,))


def gelu(hidden):
    inner = GELU_ROOT * (hidden + GELU_CUBE * (hidden * hidden * hidden))
    return 0.5 * hidden * (1.0 + jnp.tanh(inner))


def gelu_with_slope(hidden):
    square = hidden * hidden
    bend = jnp.tanh(GELU_ROOT * hidden * (1.0 + GELU_CUBE * square))
    rise = 0.5 * (1.0 + bend)
    slope = rise + 0.5 * hidden * (1.0 - bend * bend) * (GELU_ROOT + 3.0 * GELU_ROOT * GELU_CUBE * square)
    return hidden * rise, slope


def modulate_back_rows(resid, scale_part, grad):
    unit, rstd = norm_parts(resid)
    inner = grad * (1.0 + scale_part)
    grad_in = rstd * (
        inner
        - jnp.mean(inner, axis=-1, keepdims=True)
        - unit * jnp.mean(inner * unit, axis=-1, keepdims=True)
    )
    return grad_in, column_sum(grad), column_sum(grad * unit)


def call(kernel, name, ident, outs, scratch, flops, args, tasks=()):
    vmem, anywhere = pl.BlockSpec(memory_space=pltpu.VMEM), pl.BlockSpec(memory_space=pl.ANY)
    moved = sum(a.size * a.dtype.itemsize for a in args) + sum(o.size * o.dtype.itemsize for o in outs)
    task_ins = [array for task in tasks for array in task.ins]
    task_outs = [shape for task in tasks for shape in task.outs]
    task_sems = [pltpu.SemaphoreType.DMA(shape) for task in tasks for shape in task.sems]

    def run(*refs):
        refs = list(refs)

        def take(count):
            taken = refs[:count]
            del refs[:count]
            return taken

        main_ins, bound_ins = take(len(args)), take(len(task_ins))
        main_outs, bound_outs = take(len(outs)), take(len(task_outs))
        main_scratch = take(len(scratch))
        for task in tasks:
            ins = [bound_ins.pop(0) for _ in task.ins]
            results = [bound_outs.pop(0) for _ in task.outs]
            task.bind(ins, results, take(len(task.sems)))
        kernel(Background(tasks), *main_ins, *main_outs, *main_scratch)

    results = pl.pallas_call(
        run,
        name=name,
        out_shape=list(outs) + task_outs,
        in_specs=[vmem] * len(args) + [anywhere] * len(task_ins),
        out_specs=[vmem] * len(outs) + [anywhere] * len(task_outs),
        scratch_shapes=list(scratch) + task_sems,
        compiler_params=pltpu.CompilerParams(
            collective_id=ident, has_side_effects=True, vmem_limit_bytes=60 * 2**20
        ),
        cost_estimate=pl.CostEstimate(flops=flops, bytes_accessed=moved, transcendentals=0),
    )(*args, *task_ins)
    return results[: len(outs)], results[len(outs) :]


def shaped(shape, kind):
    return jax.ShapeDtypeStruct(shape, kind)


def prologue_kernel(background, *refs):
    count = (len(refs) - 6) // 2
    smalls, tiles = refs[:count], refs[count]
    packs, every_tile = refs[count + 1 : 2 * count + 1], refs[2 * count + 1]
    zs, zr, ps, pr = refs[2 * count + 2 :]
    ranks, peers = other_ranks(), plane_peers()
    greet(ranks + peers)
    rank, place = lax.axis_index("batch"), team_place()
    copies = [
        remote(small, pack.at[rank], zs.at[m, n], zr.at[m, n], who)
        for m, (small, pack) in enumerate(zip(smalls, packs))
        for n, who in enumerate(ranks)
    ] + [remote(tiles, every_tile.at[place], ps.at[n], pr.at[n], who) for n, who in enumerate(peers)]
    for copy in copies:
        copy.start()
    for small, pack in zip(smalls, packs):
        pack[rank] = small[...]
    every_tile[place] = tiles[...]
    for copy in copies:
        copy.wait()


def prologue(smalls, tiles, ident):
    ranks = lax.axis_size("batch")
    dma = pltpu.SemaphoreType.DMA
    (*packs, every_tile), _ = call(
        prologue_kernel,
        "prologue",
        ident,
        [shaped((ranks,) + small.shape, small.dtype) for small in smalls]
        + [shaped((8,) + tiles.shape, tiles.dtype)],
        [dma((len(smalls), ranks - 1)), dma((len(smalls), ranks - 1)), dma((7,)), dma((7,))],
        0,
        (*smalls, tiles),
    )
    return packs, every_tile


def conditioning_kernel(background, parts, mods, inbox, zs, zr, ps, pr):
    ranks, peers = other_ranks(), plane_peers()
    greet(ranks + peers)
    rank, place = lax.axis_index("batch"), team_place()
    first = [
        remote(parts.at[who["batch"]], inbox.at[n], zs.at[n], zr.at[n], who) for n, who in enumerate(ranks)
    ]
    for copy in first:
        copy.start()
    background.tick()
    total = parts[rank]
    for n, copy in enumerate(first):
        copy.wait()
        total = total + inbox[n]
    mods[place] = total
    second = [
        remote(mods.at[place], mods.at[place], ps.at[n], pr.at[n], who) for n, who in enumerate(peers)
    ]
    for copy in second:
        copy.start()
    background.tick()
    for copy in second:
        copy.wait()
    background.finish()


def conditioning_exchange(parts, ident, tasks):
    ranks = parts.shape[0]
    dma = pltpu.SemaphoreType.DMA
    (mods,), gathered = call(
        conditioning_kernel,
        "conditioning",
        ident,
        [shaped((8,) + parts.shape[1:], f32)],
        [
            pltpu.VMEM((ranks - 1,) + parts.shape[1:], f32),
            dma((ranks - 1,)),
            dma((ranks - 1,)),
            dma((7,)),
            dma((7,)),
        ],
        0,
        (parts,),
        tasks,
    )
    return mods, gathered


def epilogue_kernel(
    depth, background, *refs,
):
    refs = list(refs)

    def take(count):
        taken = refs[:count]
        del refs[:count]
        return taken

    block_sums, (final_sums,) = take(2 * depth), take(1)
    block_biases = take(2 * depth)
    patch_term, final_term, edge_rows, tokens = take(4)
    all_mods, all_sums, all_biases, all_tokens = take(4)
    mods, sums, biases, mods_in, sums_in, rank_mods, rank_sums, rank_biases_in, ps, pr, zs, zr, qs, qr = refs
    ranks, peers = other_ranks(), plane_peers()
    rank, place = lax.axis_index("batch"), team_place()
    cols = lax.axis_size("col")
    images = final_sums.shape[0]
    each = sums.shape[1]

    mods[...] = jnp.zeros_like(mods)
    sums[...] = jnp.zeros_like(sums)
    biases[...] = jnp.zeros_like(biases)
    for i in range(images):
        for b in range(depth):
            for p in range(6):
                n = 6 * b + p
                source = block_sums[2 * b + p // 3]
                mods[n // 2, i * 2 + n % 2] = source[i, p % 3]
        for p in range(2):
            n = 6 * depth + p
            mods[n // 2, i * 2 + n % 2] = final_sums[i, p]
    rows = [patch_term[n] for n in range(patch_term.shape[0])]
    rows += [final_term[n] for n in range(final_term.shape[0])]
    rows += [edge_rows[n] for n in range(edge_rows.shape[0])]
    for source in block_sums:
        total = source[0, 3]
        for i in range(1, images):
            total = total + source[i, 3]
        rows.append(total)
    for n, row in enumerate(rows):
        sums[n // each, n % each] = row
    for n, source in enumerate(block_biases):
        biases[n, : source.shape[1]] = source[0]

    greet(ranks + peers)
    first, extra = [], []
    for n, who in enumerate(peers):
        there = who["row"] * cols + who["col"]
        first.append(remote(mods.at[there], mods_in.at[n], ps.at[0, n], pr.at[0, n], who))
        first.append(remote(sums.at[there], sums_in.at[n], ps.at[1, n], pr.at[1, n], who))
        extra.append(remote(tokens, all_tokens.at[place], ps.at[2, n], pr.at[2, n], who))
    second = [
        remote(biases, rank_biases_in.at[n], zs.at[0, n], zr.at[0, n], who) for n, who in enumerate(ranks)
    ]
    for copy in first + second:
        copy.start()
    background.tick()
    for copy in extra:
        copy.start()
    all_tokens[place] = tokens[...]
    for copy in first:
        copy.wait()
    mod_total, sum_total = mods[place], sums[place]
    for n in range(len(peers)):
        mod_total = mod_total + mods_in[n]
        sum_total = sum_total + sums_in[n]
    rank_mods[rank] = mod_total.astype(bf16)
    rank_sums[rank] = sum_total
    third = []
    for n, who in enumerate(ranks):
        third.append(remote(rank_mods.at[rank], rank_mods.at[rank], zs.at[1, n], zr.at[1, n], who))
        third.append(remote(rank_sums.at[rank], rank_sums.at[rank], zs.at[2, n], zr.at[2, n], who))
    for copy in third:
        copy.start()
    background.tick()
    bias_total = biases[...]
    for n, copy in enumerate(second):
        copy.wait()
        bias_total = bias_total + rank_biases_in[n]
    for copy in third:
        copy.wait()
    sum_own = rank_sums[0]
    for n in range(1, rank_sums.shape[0]):
        sum_own = sum_own + rank_sums[n]
    all_mods[place] = rank_mods[...]
    all_sums[place] = sum_own
    all_biases[place] = bias_total
    last = []
    for n, who in enumerate(peers):
        for m, target in enumerate((all_mods, all_sums, all_biases)):
            last.append(remote(target.at[place], target.at[place], qs.at[m, n], qr.at[m, n], who))
    for copy in last:
        copy.start()
    background.tick()
    for copy in last + extra:
        copy.wait()
    background.finish()


def epilogue(block_sums, final_sums, block_biases, patch_term, final_term, edge_rows, tokens, ident, tasks):
    ranks = lax.axis_size("batch")
    dma = pltpu.SemaphoreType.DMA
    depth = len(block_sums) // 2
    images, _, width = final_sums.shape
    count = patch_term.shape[0] + final_term.shape[0] + edge_rows.shape[0] + len(block_sums)
    each = -(-count // 8)
    widest = max(source.shape[1] for source in block_biases)
    mods, sums = (8, 2 * images, width), (8, each, width)
    biases = (8, widest)
    return call(
        partial(epilogue_kernel, depth),
        "epilogue",
        ident,
        [
            shaped((8, ranks) + mods[1:], bf16),
            shaped(sums, f32),
            shaped((8,) + biases, f32),
            shaped((8,) + tokens.shape, f32),
        ],
        [
            pltpu.VMEM(mods, f32),
            pltpu.VMEM(sums, f32),
            pltpu.VMEM(biases, f32),
            pltpu.VMEM((7,) + mods[1:], f32),
            pltpu.VMEM((7,) + sums[1:], f32),
            pltpu.VMEM((ranks,) + mods[1:], bf16),
            pltpu.VMEM((ranks,) + sums[1:], f32),
            pltpu.VMEM((ranks - 1,) + biases, f32),
            dma((3, 7)),
            dma((3, 7)),
            dma((3, ranks - 1)),
            dma((3, ranks - 1)),
            dma((3, 7)),
            dma((3, 7)),
        ],
        0,
        (*block_sums, final_sums, *block_biases, patch_term, final_term, edge_rows, tokens),
        tasks,
    )


def closing_kernel(background, parts, every, zs, zr):
    ranks = other_ranks()
    address = sides()[2]
    greet(ranks + list(address.values()))
    rank = lax.axis_index("batch")
    copies = [
        remote(parts.at[who["batch"]], every.at[rank], zs.at[n], zr.at[n], who) for n, who in enumerate(ranks)
    ]
    background.tick()
    for copy in copies:
        copy.start()
    every[rank] = parts[rank]
    for copy in copies:
        copy.wait()
    background.finish()


def closing(parts, ident, tasks):
    ranks = parts.shape[0]
    dma = pltpu.SemaphoreType.DMA
    (every,), gathered = call(
        closing_kernel,
        "closing",
        ident,
        [shaped(parts.shape, f32)],
        [dma((ranks - 1,)), dma((ranks - 1,))],
        0,
        (parts,),
        tasks,
    )
    return every, gathered


def mlp_forward_kernel(
    block, background, mid, gate_rows, vecs, expand, expand_bias, shrink, full, hidden, expanded, after, *comm
):
    place = sides()
    core, chips, address = place
    images = full.shape[0]
    gathers, scatters = exchanges(full, comm, place)
    greet(list(address.values()) + background.partners())

    def row(i, n):
        return vecs[i, n : n + 1]

    def gate(i):
        return gate_rows[i] if block > 0 else 1.0

    own = core * 4 + chips["own"]

    def begin(i):
        full[i, own] = modulate(mid[i], row(i, 6 * block + 3), row(i, 6 * block + 4)).astype(bf16)
        gathers[i].first()

    def compute(i, between):
        for step, (start, sibling) in enumerate(halves(core)):
            value = dot(flat(full[i, pl.ds(start, 4)]), expand[...], NN) + expand_bias[...]
            hidden[i, pl.ds(start, 4)] = value.reshape(4, -1, value.shape[1])
            partial = dot(gelu(value).astype(bf16), shrink[...], NT)
            keep_partial(partial, scatters[i], sibling)
            between[step]()

    def end(i):
        value = scatters[i].finish() + row(i, offset_row(vecs, block, 1))
        expanded[i] = value
        after[i] = mid[i] + gate(i) * row(i, 6 * block + 5) * value

    begin(0)
    background.tick()
    gathers[0].second()
    begin(1)
    gathers[0].finish()
    compute(0, (gathers[1].second, scatters[0].first))
    background.tick()
    gathers[1].finish()
    compute(1, (scatters[0].second, scatters[1].first))
    background.tick()
    end(0)
    scatters[1].second()
    end(1)
    for part in gathers + scatters:
        part.drain()
    background.finish()


def mlp_forward(block, mid, gate_rows, vecs, weights, ident, tasks=()):
    expand, expand_bias, shrink = weights
    images, length, width = mid.shape
    inner = expand.shape[1]
    return call(
        partial(mlp_forward_kernel, block),
        "mlp_forward",
        ident,
        [
            shaped((images, 8, length, width), bf16),
            shaped((images, 8, length, inner), f32),
            shaped((images, length, width), f32),
            shaped((images, length, width), f32),
        ],
        comm_scratch(images, length, width),
        4 * images * 8 * length * width * inner * 6,
        (
            mid,
            gate_rows,
            vecs,
            expand,
            expand_bias.reshape(1, -1),
            shrink,
        ),
        tasks,
    )


def mlp_backward_kernel(
    block, background, grad_after, mid, expanded, gate_rows, vecs, expand, shrink, normed, hidden,
    grad_mid, sums, grad_expand, grad_shrink, grad_bias,
    full, grad_hidden, active, sum_expand, sum_shrink, *comm
):
    place = sides()
    core, chips, address = place
    gathers, scatters = exchanges(full, comm, place)
    greet(list(address.values()) + background.partners())

    def row(i, n):
        return vecs[i, n : n + 1]

    def gate(i):
        return gate_rows[i] if block > 0 else 1.0

    own = core * 4 + chips["own"]
    length = full.shape[2]

    def begin(i):
        gated = gate(i) * grad_after[i, :length]
        low = (gated * row(i, 6 * block + 5)).astype(bf16)
        full[i, own] = low
        gathers[i].first()
        sums[i, 2:3] = column_sum(gated * expanded[i])
        sums[i, 3:4] = column_sum(low.astype(f32))

    def compute(i, between):
        for step, (start, sibling) in enumerate(halves(core)):
            pull = dot(flat(full[i, pl.ds(start, 4)]), shrink[...], NN)
            value, slope = gelu_with_slope(flat(hidden[i, pl.ds(start, 4)]))
            active[i, pl.ds(start, 4)] = value.astype(bf16).reshape(4, -1, value.shape[1])
            low = (pull * slope).astype(bf16)
            grad_hidden[i, pl.ds(start, 4)] = low.reshape(4, -1, value.shape[1])
            keep_partial(dot(low, expand[...], NT), scatters[i], sibling)
            between[step]()

    def weigh_shrink(i):
        term = dot(flat(full[i]), flat(active[i]), TN)
        if i == 0:
            sum_shrink[...] = term
        else:
            grad_shrink[...] = (sum_shrink[...] + term).astype(bf16)

    def weigh_expand(i):
        low = flat(grad_hidden[i])
        term = dot(flat(normed[i]), low, TN)
        if i == 0:
            sum_expand[...] = term
            grad_bias[...] = row_sums(low)
        else:
            grad_expand[...] = (sum_expand[...] + term).astype(bf16)
            grad_bias[...] += row_sums(low)

    def end(i):
        grad, shift_sum, scale_sum = modulate_back_rows(mid[i], row(i, 6 * block + 4), scatters[i].finish())
        grad_mid[i] = grad + grad_after[i, :length]
        sums[i, 0:1] = shift_sum
        sums[i, 1:2] = scale_sum

    begin(0)
    background.tick()
    gathers[0].second()
    begin(1)
    gathers[0].finish()
    compute(0, (gathers[1].second, scatters[0].first))
    gathers[1].finish()
    compute(1, (scatters[0].second, scatters[1].first))
    weigh_shrink(0)
    end(0)
    scatters[1].second()
    weigh_expand(0)
    weigh_shrink(1)
    weigh_expand(1)
    end(1)
    for part in gathers + scatters:
        part.drain()
    background.finish()


def mlp_backward(block, grad_after, mid, expanded, gate_rows, vecs, weights, saved, ident, tasks=()):
    expand, _, shrink = weights
    normed, hidden = saved
    images, length, width = mid.shape
    inner = expand.shape[1]
    return call(
        partial(mlp_backward_kernel, block),
        "mlp_backward",
        ident,
        [
            shaped((images, length, width), f32),
            shaped((images, 8, width), f32),
            shaped((width, inner), bf16),
            shaped((width, inner), bf16),
            shaped((8, inner), f32),
        ],
        [
            pltpu.VMEM((images, 8, length, width), bf16),
            pltpu.VMEM((images, 8, length, inner), bf16),
            pltpu.VMEM((images, 8, length, inner), bf16),
            pltpu.VMEM((width, inner), f32),
            pltpu.VMEM((width, inner), f32),
        ]
        + comm_scratch(images, length, width),
        8 * images * 8 * length * width * inner * 6,
        (
            grad_after,
            mid,
            expanded,
            gate_rows,
            vecs,
            expand,
            shrink,
            normed,
            hidden,
        ),
        tasks,
    )


LOG2E = 1.4426950408889634


def offset_row(vecs, block, kind):
    depth = (vecs.shape[1] - 2) // 8
    return 6 * depth + 2 + 2 * block + kind


def pad_lanes(value):
    gap = jnp.zeros((value.shape[0], LANES - HEAD_SIZE), value.dtype)
    parts = []
    for start in range(0, value.shape[1], HEAD_SIZE):
        parts += [value[:, start : start + HEAD_SIZE], gap]
    return jnp.concatenate(parts, axis=1)


def pad_rows(value):
    gap = jnp.zeros((LANES - HEAD_SIZE, value.shape[1]), value.dtype)
    parts = []
    for start in range(0, value.shape[0], HEAD_SIZE):
        parts += [value[start : start + HEAD_SIZE], gap]
    return jnp.concatenate(parts, axis=0)


def cut_lanes(value):
    return jnp.concatenate(
        [value[:, start : start + HEAD_SIZE] for start in range(0, value.shape[1], LANES)], axis=1
    )


def cut_rows(value):
    return jnp.concatenate(
        [value[start : start + HEAD_SIZE] for start in range(0, value.shape[0], LANES)], axis=0
    )


def attention_forward_kernel(
    block, background, base, gate_rows, vecs, project_own, project_bias, attend_own, key_bias,
    full, packed, mixed, log_total, attended, mid, project, attend, *comm
):
    place = sides()
    core, chips, address = place
    images, _, length, _ = full.shape
    gathers, scatters = exchanges(full, comm, place)
    greet(list(address.values()) + background.partners())

    def row(i, n):
        return vecs[i, n : n + 1]

    def gate(i):
        return gate_rows[i] if block > 0 else 1.0

    own = core * 4 + chips["own"]
    span = attend.shape[0]
    heads = span // LANES
    tile = 2 * length
    factor = HEAD_SIZE ** (-0.5) * LOG2E

    def begin(i):
        full[i, own] = modulate(base[i, :length], row(i, 6 * block), row(i, 6 * block + 1)).astype(bf16)
        gathers[i].first()

    def rows_of(start, count):
        return pl.ds(pl.multiple_of(start * length, length), count * length)

    def compute(i, between):
        for start, _ in halves(core):
            value = dot(flat(full[i, pl.ds(start, 4)]), project[...], NN) + project_bias[...]
            packed[i, rows_of(start, 4)] = value.astype(bf16)
        between[0]()
        for step, (start, sibling) in enumerate(halves(core)):

            def one(t, carry, start=start):
                rows = pl.ds(pl.multiple_of((start + 2 * t) * length, tile), tile)
                for h in range(heads):
                    q, k, v = (
                        pl.ds(part * span + h * LANES, LANES) for part in range(3)
                    )
                    scores = dot(packed[i, rows, q], packed[i, :, k], NT) * factor
                    if block > 0:
                        scores = scores + key_bias[i]
                    peak = jnp.max(scores, axis=1, keepdims=True)
                    probs = jnp.exp2(scores - peak)
                    total = jnp.sum(probs, axis=1, keepdims=True)
                    out = dot(probs.astype(bf16), packed[i, :, v], NN) / total
                    mixed[i, rows, pl.ds(h * LANES, LANES)] = out.astype(bf16)
                    level = jnp.broadcast_to(peak + jnp.log2(total), (tile, LANES))
                    log_total[i, h, pl.ds(start // 2 + t, 1)] = level.T[0:1]
                return carry

            lax.fori_loop(0, 2, one, 0)
            partial = dot(mixed[i, rows_of(start, 4)], attend[...], NN)
            keep_partial(partial, scatters[i], sibling)
            between[1 + step]()

    def end(i):
        value = scatters[i].finish() + row(i, offset_row(vecs, block, 0))
        attended[i] = value
        mid[i] = base[i, :length] + gate(i) * row(i, 6 * block + 2) * value

    begin(0)
    background.tick()
    project[...] = pad_lanes(project_own[...])
    attend[...] = pad_rows(attend_own[...])
    gathers[0].second()
    begin(1)
    gathers[0].finish()
    compute(0, (gathers[1].second, background.tick, scatters[0].first))
    gathers[1].finish()
    compute(1, (scatters[0].second, background.tick, scatters[1].first))
    end(0)
    scatters[1].second()
    end(1)
    for part in gathers + scatters:
        part.drain()
    background.finish()


def attention_forward(block, length, base, gate_rows, vecs, weights, key_bias, ident, tasks=()):
    project, project_bias, attend = weights
    images, _, width = base.shape
    span = attend.shape[0] // HEAD_SIZE * LANES
    return call(
        partial(attention_forward_kernel, block),
        "attention_forward",
        ident,
        [
            shaped((images, 8, length, width), bf16),
            shaped((images, 8 * length, 3 * span), bf16),
            shaped((images, 8 * length, span), bf16),
            shaped((images, span // LANES, 4, 2 * length), f32),
            shaped((images, length, width), f32),
            shaped((images, length, width), f32),
            shaped((width, 3 * span), bf16),
            shaped((span, width), bf16),
        ],
        comm_scratch(images, length, width),
        8 * images * 8 * length * width * span * 6,
        (
            base,
            gate_rows,
            vecs,
            project,
            project_bias.reshape(1, -1),
            attend,
            key_bias,
        ),
        tasks,
    )


def attention_backward_kernel(
    block, background, grad_mid, base, attended, gate_rows, vecs, project, attend, key_bias, normed, packed, mixed, log_total,
    grad_base, sums, grad_project, grad_attend, grad_bias,
    full, grad_mixed, grad_packed, grad_keys, grad_values, sum_project, sum_attend, *comm
):
    place = sides()
    core, chips, address = place
    images, _, length, _ = full.shape
    gathers, scatters = exchanges(full, comm, place)
    greet(list(address.values()) + background.partners())

    def row(i, n):
        return vecs[i, n : n + 1]

    def gate(i):
        return gate_rows[i] if block > 0 else 1.0

    own = core * 4 + chips["own"]
    span = attend.shape[0]
    heads = span // LANES
    tile = 2 * length
    factor = HEAD_SIZE ** (-0.5)

    def begin(i):
        gated = gate(i) * grad_mid[i]
        low = (gated * row(i, 6 * block + 2)).astype(bf16)
        full[i, own] = low
        gathers[i].first()
        sums[i, 2:3] = column_sum(gated * attended[i])
        sums[i, 3:4] = column_sum(low.astype(f32))

    def rows_of(start, count):
        return pl.ds(pl.multiple_of(start * length, length), count * length)

    def compute(i, between):
        grad_mixed[...] = dot(flat(full[i]), attend[...], NT).astype(bf16)
        between[0]()
        for h in range(heads):
            lane = pl.ds(h * LANES, LANES)
            q, k, v = (pl.ds(part * span + h * LANES, LANES) for part in range(3))
            keys_turned = packed[i, :, k].T

            def one(t, carry):
                rows = pl.ds(pl.multiple_of(t * tile, tile), tile)
                queries, pulls = packed[i, rows, q], grad_mixed[rows, lane]
                scores = dot(packed[i, :, k], queries, NT) * (factor * LOG2E)
                if block > 0:
                    scores = scores + key_bias[i]
                probs = jnp.exp2(scores - log_total[i, h, pl.ds(t, 1)])
                dprobs = dot(packed[i, :, v], pulls, NT)
                row_dot = column_sum(probs * dprobs)
                grad_scores = (probs * (dprobs - row_dot)).astype(bf16)
                value_term = dot(probs.astype(bf16), pulls, NN)
                key_term = dot(grad_scores, queries, NN)

                @pl.when(t == 0)
                def _():
                    grad_values[...] = value_term
                    grad_keys[...] = key_term

                @pl.when(t > 0)
                def _():
                    grad_values[...] += value_term
                    grad_keys[...] += key_term

                query_term = dot(keys_turned, grad_scores, NN) * factor
                grad_packed[i, rows, q] = query_term.T.astype(bf16)
                return carry

            lax.fori_loop(0, 4, one, 0)
            grad_packed[i, :, k] = (grad_keys[...] * factor).astype(bf16)
            grad_packed[i, :, v] = grad_values[...].astype(bf16)
            between[1 + h]()
        for step, (start, sibling) in enumerate(halves(core)):
            keep_partial(dot(grad_packed[i, rows_of(start, 4)], project[...], NT), scatters[i], sibling)

    def weigh_attend(i):
        term = dot(mixed[i], flat(full[i]), TN)
        if i == 0:
            sum_attend[...] = term
        else:
            grad_attend[...] = cut_rows(sum_attend[...] + term).astype(bf16).reshape(grad_attend.shape)

    def weigh_project(i):
        low = grad_packed[i]
        term = dot(flat(normed[i]), low, TN)
        if i == 0:
            sum_project[...] = term
            grad_bias[...] = row_sums(low)
        else:
            grad_project[...] = cut_lanes(sum_project[...] + term).astype(bf16)
            grad_bias[...] += row_sums(low)

    def end(i):
        grad, shift_sum, scale_sum = modulate_back_rows(base[i, :length], row(i, 6 * block + 1), scatters[i].finish())
        grad_base[i] = grad + grad_mid[i]
        sums[i, 0:1] = shift_sum
        sums[i, 1:2] = scale_sum

    def nothing():
        pass

    def begin_extra():
        gathers[1].second()
        background.tick()

    def early_attend():
        weigh_attend(0)
        weigh_attend(1)
        for task in background.tasks:
            if task.source is None:
                task.source = grad_attend
        background.tick()

    def middle():
        scatters[0].second()
        background.tick()

    begin(0)
    background.tick()
    gathers[0].second()
    begin(1)
    gathers[0].finish()
    compute(0, (begin_extra, gathers[1].finish, nothing))
    scatters[0].first()
    compute(1, (early_attend, middle, background.tick))
    scatters[1].first()
    weigh_project(0)
    end(0)
    scatters[1].second()
    weigh_project(1)
    end(1)
    for part in gathers + scatters:
        part.drain()
    background.finish()


def attention_backward(
    block, attend_shape, grad_mid, base, attended, gate_rows, vecs, weights, key_bias, saved, ident, tasks=()
):
    project, attend = weights
    normed, packed, mixed, log_total = saved
    images, length, width = grad_mid.shape
    span = attend.shape[0]
    tokens = 8 * length
    return call(
        partial(attention_backward_kernel, block),
        "attention_backward",
        ident,
        [
            shaped((images, length, width), f32),
            shaped((images, 8, width), f32),
            shaped((width, 3 * span // LANES * HEAD_SIZE), bf16),
            shaped(attend_shape, bf16),
            shaped((8, 3 * span), f32),
        ],
        [
            pltpu.VMEM((images, 8, length, width), bf16),
            pltpu.VMEM((tokens, span), bf16),
            pltpu.VMEM((images, tokens, 3 * span), bf16),
            pltpu.VMEM((tokens, LANES), f32),
            pltpu.VMEM((tokens, LANES), f32),
            pltpu.VMEM((width, 3 * span), f32),
            pltpu.VMEM((span, width), f32),
        ]
        + comm_scratch(images, length, width),
        16 * images * 8 * length * width * span * 6,
        (
            grad_mid,
            base,
            attended,
            gate_rows,
            vecs,
            project,
            attend,
            key_bias,
            normed,
            packed,
            mixed,
            log_total,
        ),
        tasks,
    )


HEAD_SIZE = 72


def pad_heads(array, axis):
    shape = array.shape
    heads = shape[axis] // HEAD_SIZE
    split = array.reshape(shape[:axis] + (heads, HEAD_SIZE) + shape[axis + 1 :])
    widths = [(0, 0)] * split.ndim
    widths[axis + 1] = (0, LANES - HEAD_SIZE)
    return jnp.pad(split, widths).reshape(shape[:axis] + (heads * LANES,) + shape[axis + 1 :])


def unpad_heads(array, axis):
    shape = array.shape
    heads = shape[axis] // LANES
    split = array.reshape(shape[:axis] + (heads, LANES) + shape[axis + 1 :])
    kept = lax.slice_in_dim(split, 0, HEAD_SIZE, axis=axis + 1)
    return kept.reshape(shape[:axis] + (heads * HEAD_SIZE,) + shape[axis + 1 :])


def join_ranks(pack, dim):
    moved = jnp.moveaxis(pack, 0, dim)
    shape = list(pack.shape[1:])
    shape[dim] = -1
    return moved.reshape(shape)


def turn(block, own, step, last):
    return jnp.where(block == own, step, jnp.where(block < own, 0, last))


def local_call(kernel, name, grid, in_specs, out_specs, outs, moved, args, prefetch=0):
    return pl.pallas_call(
        kernel,
        name=name,
        grid_spec=pltpu.PrefetchScalarGridSpec(
            num_scalar_prefetch=prefetch, grid=grid, in_specs=in_specs, out_specs=out_specs
        ),
        out_shape=outs,
        compiler_params=pltpu.CompilerParams(vmem_limit_bytes=56 * 2**20),
        cost_estimate=pl.CostEstimate(flops=0, bytes_accessed=moved, transcendentals=0),
    )(*args)


def mlp_unpack_kernel(*refs):
    *everys, expand, shrink = refs
    for k, every in enumerate(everys):

        @pl.when(pl.program_id(0) == k)
        def _(every=every):
            parts = [[every[core, 0, n].astype(f32) for core in range(2)] for n in range(2)]
            expand[0] = jnp.concatenate(parts[0], axis=1)
            shrink[0] = jnp.concatenate([part.T for part in parts[1]], axis=0)


def mlp_unpack(everys):
    depth = len(everys)
    _, _, shard, inner = everys[0].shape
    everys = [every.reshape(2, 4, 2, shard, inner) for every in everys]
    block = (2, 1, 2, shard, inner)
    return local_call(
        mlp_unpack_kernel,
        "mlp_unpack",
        (depth, 4),
        [pl.BlockSpec(block, lambda b, j, k=k: (0, turn(b, k, j, 3), 0, 0, 0)) for k in range(depth)],
        [
            pl.BlockSpec((1, shard, 2 * inner), lambda b, j: (b, 0, j)),
            pl.BlockSpec((1, 2 * inner, shard), lambda b, j: (b, j, 0)),
        ],
        [shaped((depth, shard, 8 * inner), f32), shaped((depth, 8 * inner, shard), f32)],
        depth * shard * inner * 96,
        everys,
    )


def project_unpack_kernel(*refs):
    *everys, project = refs
    for k, every in enumerate(everys):

        @pl.when(pl.program_id(0) == k)
        def _(every=every):
            each = every.shape[-1] // 3
            parts = [
                every[d % 2, d // 2, 0].astype(f32)[:, n * each : (n + 1) * each] for n in range(3) for d in range(8)
            ]
            project[0, 0] = jnp.concatenate(parts, axis=1)


def project_unpack(everys):
    depth = len(everys)
    _, _, half, columns = everys[0].shape
    everys = [every.reshape(2, 4, 2, half, columns) for every in everys]
    (project,) = local_call(
        project_unpack_kernel,
        "project_unpack",
        (depth, 2),
        [
            pl.BlockSpec((2, 4, 1, half, columns), lambda b, j, k=k: (0, 0, turn(b, k, j, 1), 0, 0))
            for k in range(depth)
        ],
        [pl.BlockSpec((1, 1, half, 8 * columns), lambda b, j: (b, j, 0, 0))],
        [shaped((depth, 2, half, 8 * columns), f32)],
        depth * half * columns * 96,
        everys,
    )
    return project.reshape(depth, 2 * half, 8 * columns)


def attend_unpack_kernel(rank, *refs):
    *everys, attend = refs
    for k, every in enumerate(everys):

        @pl.when(pl.program_id(0) == k)
        def _(every=every):
            attend[0, 0] = every[0, 0].astype(f32)


def attend_unpack(everys, rank, shard, pieces, rows):
    depth = len(everys)
    width = everys[0].shape[-1]
    everys = [every.reshape(8, pieces, rows, width) for every in everys]
    steps = shard // rows

    def chosen(b, i, ranks, k):
        g = ranks[0] * steps + i
        d = g // pieces
        own = b == k
        return jnp.where(own, d % 2 * 4 + d // 2, 0), jnp.where(own, g % pieces, 0), 0, 0

    (attend,) = local_call(
        attend_unpack_kernel,
        "attend_unpack",
        (depth, steps),
        [pl.BlockSpec((1, 1, rows, width), partial(chosen, k=k)) for k in range(depth)],
        [pl.BlockSpec((1, 1, rows, width), lambda b, i, ranks: (b, i, 0, 0))],
        [shaped((depth, steps, rows, width), f32)],
        depth * shard * width * 6,
        [rank.reshape(1), *everys],
        1,
    )
    return attend.reshape(depth, shard, width)


def adaptive_grad_kernel(silu, mods, out):
    out[0] = dot(silu[...], mods[0], TN)


def adaptive_grad(silu, mods):
    depth, count, columns = mods.shape
    shard = silu.shape[1]
    (grad,) = local_call(
        adaptive_grad_kernel,
        "adaptive_grad",
        (depth, 3),
        [
            pl.BlockSpec((count, shard), lambda b, j: (0, 0)),
            pl.BlockSpec((1, count, columns // 3), lambda b, j: (b, 0, j)),
        ],
        [pl.BlockSpec((1, shard, columns // 3), lambda b, j: (b, 0, j))],
        [shaped((depth, shard, columns), f32)],
        depth * shard * columns * 4,
        [silu, mods],
    )
    return grad


def body(
    latents,
    conditioning,
    kept_index,
    kept_count,
    patch_weight,
    patch_bias,
    adaptive_weight,
    adaptive_bias,
    project_weight,
    project_bias,
    attend_weight,
    attend_bias,
    expand_weight,
    expand_bias,
    shrink_weight,
    shrink_bias,
    final_adaptive,
    final_offset,
    final_weight,
    final_bias,
    cotangent,
):
    rows, cols, ranks = lax.axis_size("row"), lax.axis_size("col"), lax.axis_size("batch")
    team = rows * cols
    place = lax.axis_index("row") * cols + lax.axis_index("col")
    rank = lax.axis_index("batch")
    images, channels_in = latents.shape[:2]
    channels_out = cotangent.shape[1]
    rows_tile, cols_tile = latents.shape[2] // PATCH, latents.shape[3] // PATCH
    tile_tokens = rows_tile * cols_tile
    sequence = tile_tokens * team
    width = conditioning.shape[1]
    depth = adaptive_weight.shape[0]
    shard = adaptive_weight.shape[1]
    kept_local = tile_tokens * 3 // 4
    highest = lax.Precision.HIGHEST

    head_cols = width // team
    hidden_cols = expand_weight.shape[2] // team

    def slice_of(array, axis, count):
        return lax.dynamic_slice_in_dim(array, place * count, count, axis=axis)

    piece_rows = min(shard, head_cols)
    pieces_each = head_cols // piece_rows
    project_own = jnp.concatenate(
        [
            lax.dynamic_slice_in_dim(project_weight, part * width + place * head_cols, head_cols, axis=2)
            for part in range(3)
        ],
        axis=2,
    )
    attend_own = jnp.stack(
        [
            lax.dynamic_slice_in_dim(
                attend_weight, (place * head_cols + j * piece_rows) % shard, piece_rows, axis=1
            )
            for j in range(pieces_each)
        ],
        axis=1,
    )
    expand_own = slice_of(expand_weight, 2, hidden_cols)
    shrink_own = slice_of(shrink_weight, 1, hidden_cols).transpose(0, 2, 1)

    smalls = [
        patch_weight,
        patch_bias[None],
        adaptive_bias,
        project_bias,
        attend_bias,
        expand_bias,
        shrink_bias,
        final_offset[None],
        final_weight,
        conditioning,
    ]
    patch_tiles = to_tokens(latents, PATCH)
    grad_tiles = to_tokens(cotangent, PATCH)
    patch_in, patch_out = patch_tiles.shape[2], grad_tiles.shape[2]
    tiles = jnp.concatenate([patch_tiles, grad_tiles], axis=2)
    packs, every_tile = prologue(smalls, tiles.reshape(-1, LANES), 8)
    (
        patch_full,
        patch_bias_full,
        adaptive_offset,
        project_offset,
        attend_offset,
        expand_offset,
        shrink_offset,
        final_offset_full,
        final_full,
        cond_all,
    ) = [join_ranks(pack, dim) for pack, dim in zip(packs, [1, 1, 1, 1, 1, 1, 1, 1, 0, 0])]

    whole = every_tile.reshape((rows, cols, images, rows_tile, cols_tile, -1)).transpose(2, 0, 3, 1, 4, 5)
    whole = whole.reshape(images, sequence, patch_in + patch_out)
    grid_cols = cols * cols_tile
    own_ids = lax.dynamic_index_in_dim(
        kept_index.reshape(images, tile_tokens, team), place, axis=2, keepdims=False
    )
    pick = (own_ids[:, :, None] == jnp.arange(sequence, dtype=jnp.int32)).astype(bf16)
    own = jnp.einsum("ikt,itc->ikc", pick, whole, preferred_element_type=f32).astype(bf16)
    patches, grad_outputs = own[..., :patch_in], own[..., patch_in:]
    order = jnp.arange(kept_local, dtype=jnp.int32)[:, None] * team + jnp.arange(team, dtype=jnp.int32)
    kept_grid = order[None] < kept_count[:, None, None]
    chunk_order = kept_grid.reshape(images, kept_local, team // 2, 2).transpose(0, 3, 2, 1)
    key_bias = jnp.where(chunk_order.reshape(images, team * kept_local), 0.0, masked_score).astype(f32)
    kept_rows = lax.dynamic_index_in_dim(kept_grid, place, axis=2, keepdims=False).astype(f32)[:, :, None]

    count = width // 4
    omega = 1.0 / 10000.0 ** (jnp.arange(count, dtype=f32) / count)
    angles = jnp.arange(max(rows * rows_tile, grid_cols), dtype=f32)[:, None] * omega[None, :]
    along = jnp.concatenate([jnp.sin(angles), jnp.cos(angles)], axis=1)
    places = jnp.arange(along.shape[0], dtype=jnp.int32)

    def position_of(coords):
        chosen = (coords[..., None] == places).astype(f32)
        return jnp.einsum("ikt,tc->ikc", chosen, along, precision=highest)

    position = jnp.concatenate(
        [position_of(own_ids // grid_cols), position_of(own_ids % grid_cols)], axis=-1
    )
    resid = (
        jnp.einsum("ikc,cd->ikd", patches, patch_full, preferred_element_type=f32)
        + patch_bias_full.astype(f32)
        + position
    )

    silu_all = jax.nn.silu(cond_all.astype(f32)).astype(bf16)
    silu_rows = lax.dynamic_slice_in_dim(silu_all, rank * shard, shard, axis=1)
    pair = 2 * width
    block_of = jnp.minimum(place // 3, depth - 1)
    pair_weight = lax.dynamic_slice(adaptive_weight, (block_of, 0, place % 3 * pair), (1, shard, pair))[0]
    pair_weight = jnp.where(place < 3 * depth, pair_weight, final_adaptive)
    parts = dot(silu_rows, pair_weight, NN).reshape(ranks, images * 2, width)
    mods, (project_next, attend_next) = conditioning_exchange(
        parts, 9, [Line(project_own[0]), Chain(attend_own[0], shard)]
    )
    mods = mods.reshape(team, images, 2, width).transpose(1, 0, 2, 3).reshape(images, 2 * team, width)
    offsets = [adaptive_offset.reshape(6 * depth, width), final_offset_full.reshape(2, width)]
    mods = mods[:, : 6 * depth + 2] + jnp.concatenate(offsets, axis=0).astype(f32)
    added = jnp.stack([attend_offset, shrink_offset], axis=1).reshape(2 * depth, width).astype(f32)
    vecs = jnp.concatenate([mods, jnp.broadcast_to(added, (images, 2 * depth, width))], axis=1)
    final_shift, final_scale = mods[:, 6 * depth, None], mods[:, 6 * depth + 1, None]
    head_biases = jnp.moveaxis(project_offset.astype(f32).reshape(depth, 2, team, head_cols), 2, 0)
    head_biases = lax.dynamic_index_in_dim(head_biases, place, axis=0, keepdims=False)
    head_biases = jnp.stack([head_biases[:, 0], jnp.zeros((depth, head_cols), f32), head_biases[:, 1]], axis=1)
    head_biases = pad_heads(head_biases, 2).reshape(depth, -1)
    hidden_biases = slice_of(expand_offset.astype(f32), 1, hidden_cols)

    records = []
    for b in range(depth):
        routed = b > 0
        length = kept_local if routed else tile_tokens
        base = resid
        tasks = [Line(expand_own[b])]
        if not routed:
            tasks.append(Line(shrink_own[b]))
        (*attention_saved, attended, mid, project, attend), gathered = attention_forward(
            b,
            length,
            base,
            kept_rows,
            vecs,
            (project_next.reshape(width, -1), head_biases[b], attend_next.reshape(-1, width)),
            key_bias[:, None, :],
            4 * b,
            tasks,
        )
        expand = gathered[0].reshape(width, hidden_cols)
        shrink = (shrink_next if routed else gathered[1]).reshape(width, hidden_cols)
        mlp_weights = (expand, hidden_biases[b], shrink)
        tasks = []
        if b + 1 < depth:
            tasks = [Line(project_own[b + 1]), Chain(attend_own[b + 1], shard), Line(shrink_own[b + 1])]
        (*mlp_saved, expanded, after), gathered = mlp_forward(
            b, mid, kept_rows, vecs, mlp_weights, 4 * b + 1, tasks
        )
        if tasks:
            project_next, attend_next, shrink_next = gathered
        records.append((base, mid, attended, expanded, (project, attend), mlp_weights, attention_saved, mlp_saved))
        resid = jnp.concatenate([after, resid[:, kept_local:]], axis=1) if routed else after

    final_normed = modulate(resid, final_shift, final_scale).astype(bf16)
    outputs = jnp.einsum("ikd,dc->cik", final_normed, final_full, preferred_element_type=f32)
    outputs = outputs + final_bias.astype(f32)[:, None, None]
    final_bias_term = jnp.sum(grad_outputs.astype(f32), axis=(0, 1))
    final_weight_term = jnp.einsum("ikd,ikc->cd", final_normed, grad_outputs, preferred_element_type=f32)
    grad_final = jnp.einsum("ikc,dc->ikd", grad_outputs, final_full, preferred_element_type=f32)
    grad_resid, grad_final_shift, grad_final_scale = modulate_back(resid, final_scale, grad_final)
    final_mod_term = jnp.stack([grad_final_shift, grad_final_scale], axis=1)

    block_sums, block_biases = [], []
    spread = [[None, None, None] for _ in range(depth)]

    def folded(source, inbox):
        own = lax.dynamic_index_in_dim(source, rank, axis=0, keepdims=False)
        return (own.astype(f32) + jnp.sum(inbox.astype(f32), axis=0)).astype(bf16)

    def fold_mlp(terms, inboxes):
        return jnp.stack([folded(term, inbox) for term, inbox in zip(terms, inboxes)])

    def fold_project(term, inbox):
        return folded(term, inbox).reshape(2, shard // 2, -1)

    def fold_attend(term, inbox):
        total = term.astype(f32) + jnp.sum(inbox.astype(f32), axis=1)
        return total.astype(bf16).reshape(2, head_cols // 2, width)

    attend_shape = (pieces_each, piece_rows, width)
    project_term, waiting = None, []
    for b in reversed(range(depth)):
        base, mid, attended, expanded, attention_weights, mlp_weights, attention_saved, mlp_saved = records[b]
        routed = b > 0
        tasks = [] if project_term is None else [Fold(project_term)]
        (grad_mid, mlp_sums, grad_expand, grad_shrink, grad_expand_bias), inboxes = mlp_backward(
            b, grad_resid, mid, expanded, kept_rows, vecs, mlp_weights, mlp_saved, 4 * b + 2, tasks
        )
        if tasks:
            waiting.append((b + 1, 1, fold_project(project_term, inboxes[0])))
        mlp_terms = [term.reshape(ranks, shard, hidden_cols) for term in (grad_expand, grad_shrink)]
        tasks = [Fold(term) for term in mlp_terms] + [FoldTo(attend_shape, shard, 2)]
        tasks += [PlaneGather(part, late=1) for _, _, part in waiting]
        (grad_base, attention_sums, grad_project, grad_attend, grad_project_bias), inboxes = attention_backward(
            b,
            attend_shape,
            grad_mid,
            base,
            attended,
            kept_rows,
            vecs,
            attention_weights,
            key_bias[:, :, None],
            attention_saved,
            4 * b + 3,
            tasks,
        )
        for (block, n, _), every in zip(waiting, inboxes[3:]):
            spread[block][n] = every
        waiting = [(b, 0, fold_mlp(mlp_terms, inboxes[:2])), (b, 2, fold_attend(grad_attend, inboxes[2]))]
        project_term = grad_project.reshape(ranks, shard, 3 * head_cols)
        block_sums = [attention_sums, mlp_sums] + block_sums
        block_biases = [grad_project_bias, grad_expand_bias] + block_biases
        grad_resid = jnp.concatenate([grad_base, grad_resid[:, kept_local:]], axis=1) if routed else grad_base

    patch_bias_term = jnp.sum(grad_resid, axis=(0, 1))
    grad_embed = grad_resid.astype(bf16)
    patch_term = jnp.einsum("ikc,ikd->cd", patches, grad_embed, preferred_element_type=f32)
    grad_patches = jnp.einsum("ikd,cd->cik", grad_embed, patch_full, preferred_element_type=f32)

    edge_rows = jnp.stack([patch_bias_term, jnp.pad(final_bias_term, (0, width - patch_out))])
    tokens_out = jnp.concatenate([outputs, grad_patches], axis=0).reshape(patch_out + patch_in, -1)
    tasks = [Fold(project_term)] + [PlaneGather(part) for _, _, part in waiting]
    (all_mods, all_sums, all_biases, all_tokens), inboxes = epilogue(
        block_sums,
        final_mod_term,
        block_biases,
        patch_term,
        final_weight_term,
        edge_rows,
        tokens_out,
        10,
        tasks,
    )
    for (block, n, _), every in zip(waiting, inboxes[1:]):
        spread[block][n] = every
    last_part = fold_project(project_term, inboxes[0])

    mod_every = all_mods.reshape(team, ranks * images, pair)
    mod_width = 3 * pair
    block_mods = jnp.stack(
        [mod_every[3 * b : 3 * b + 3].transpose(1, 0, 2).reshape(ranks * images, mod_width) for b in range(depth)]
    )
    final_mods = mod_every[3 * depth]
    grad_silu = dot(final_mods, final_adaptive, NT)
    for b in range(depth):
        grad_silu = grad_silu + dot(block_mods[b], adaptive_weight[b], NT)
    grad_silu, last = closing(
        grad_silu.reshape(ranks, images, shard), 11, [PlaneGather(last_part)]
    )
    spread[0][1] = last[0]
    grad_silu = grad_silu.transpose(1, 0, 2).reshape(images, width)
    conditioning_grad = jax.vjp(jax.nn.silu, conditioning.astype(f32))[1](grad_silu)[0]
    adaptive_weight_grad = adaptive_grad(silu_rows, block_mods)
    final_adaptive_grad = dot(silu_rows, final_mods, TN)

    def rank_part(full):
        part = full.shape[-1] // ranks
        return lax.dynamic_slice_in_dim(full, rank * part, part, axis=full.ndim - 1)

    adaptive_bias_grad = rank_part(jnp.sum(block_mods.astype(f32), axis=1))
    final_offset_grad = rank_part(jnp.sum(final_mods.astype(f32), axis=0))

    ordered = all_tokens.reshape(team, patch_out + patch_in, images, tile_tokens)
    ordered = ordered.transpose(2, 3, 0, 1).reshape(images, sequence, patch_out + patch_in)
    tile_rows = lax.axis_index("row") * rows_tile + jnp.arange(rows_tile, dtype=jnp.int32)
    tile_cols = lax.axis_index("col") * cols_tile + jnp.arange(cols_tile, dtype=jnp.int32)
    tile_ids = (tile_rows[:, None] * grid_cols + tile_cols).reshape(-1)
    back = (kept_index[:, None, :] == tile_ids[None, :, None]).astype(f32)
    tile_out = jnp.einsum("itj,ijc->itc", back, ordered, precision=highest)
    prediction = to_planes(tile_out[..., :patch_out], PATCH, channels_out, rows_tile, cols_tile)
    latent_grad = to_planes(tile_out[..., patch_out:], PATCH, channels_in, rows_tile, cols_tile)

    expand_weight_grad, shrink_weight_grad = mlp_unpack([parts[0] for parts in spread])
    project_weight_grad = project_unpack([parts[1] for parts in spread])
    attend_weight_grad = attend_unpack([parts[2] for parts in spread], rank, shard, pieces_each, piece_rows)

    sums = lax.dynamic_slice_in_dim(all_sums.reshape(-1, width), rank * shard, shard, axis=1)
    first = patch_in + patch_out
    token_sums = sums[first + 2 : first + 2 + 2 * depth].reshape(depth, 2, shard)
    final_bias_grad = all_sums.reshape(-1, width)[first + 1, :patch_out]
    rows_of = all_biases.transpose(1, 0, 2)[: 2 * depth].reshape(depth, 2, team, -1)
    expand_bias_grad = rows_of[:, 1, :, :hidden_cols].reshape(depth, -1)
    head_rows = unpad_heads(rows_of[:, 0].reshape(depth, team, 3, -1), 3)
    project_bias_grad = jnp.stack([head_rows[:, :, 0], head_rows[:, :, 2]], axis=1).reshape(depth, -1)

    return (
        prediction,
        latent_grad,
        conditioning_grad,
        sums[:patch_in],
        sums[first],
        adaptive_weight_grad,
        adaptive_bias_grad,
        project_weight_grad,
        rank_part(project_bias_grad),
        attend_weight_grad,
        token_sums[:, 0],
        expand_weight_grad,
        rank_part(expand_bias_grad),
        shrink_weight_grad,
        token_sums[:, 1],
        final_adaptive_grad,
        final_offset_grad,
        sums[patch_in:first].T,
        final_bias_grad,
    )


def solution(mesh):
    tokens = P("batch", None, "row", "col")
    placed = (
        tokens,
        P("batch", None),
        P("batch", None),
        P("batch"),
        P(None, "batch"),
        P("batch"),
        P(None, "batch", None),
        P(None, "batch"),
        P(None, "batch", None),
        P(None, "batch"),
        P(None, "batch", None),
        P(None, "batch"),
        P(None, "batch", None),
        P(None, "batch"),
        P(None, None, "batch"),
        P(None, "batch"),
        P("batch", None),
        P("batch"),
        P("batch", None),
        P(),
        tokens,
    )
    return jax.shard_map(
        body,
        mesh=mesh,
        in_specs=placed,
        out_specs=(tokens, tokens, P("batch", None)) + placed[4:16] + (placed[16], P("batch"), P("batch", None), P()),
        check_vma=False,
    )
```

```python
from functools import partial

import jax
import jax.numpy as jnp
from jax import lax
from jax.experimental import pallas as pl
from jax.experimental.pallas import tpu as pltpu
from jax.sharding import PartitionSpec as P

HEADS = 16
PATCH = 2
LANES = 128
PLANE = ("row", "col")

norm_epsilon = 1e-06
masked_score = -1e30
f32 = jnp.float32
bf16 = jnp.bfloat16


def to_tokens(planes, patch_side):
    images, channels, height, breadth = planes.shape
    shaped = planes.reshape(
        images, channels, height // patch_side, patch_side, breadth // patch_side, patch_side
    )
    return shaped.transpose(0, 2, 4, 3, 5, 1).reshape(
        images, height // patch_side * (breadth // patch_side), patch_side * patch_side * channels
    )


def to_planes(token_rows, patch_side, channels, rows_tile, cols_tile):
    images = token_rows.shape[0]
    shaped = token_rows.reshape(images, rows_tile, cols_tile, patch_side, patch_side, channels)
    return shaped.transpose(0, 5, 1, 3, 2, 4).reshape(
        images, channels, rows_tile * patch_side, cols_tile * patch_side
    )


def dot(left, right, dims, precision=None):
    return lax.dot_general(left, right, (dims, ((), ())), precision=precision, preferred_element_type=f32)


def norm_parts(resid):
    centered = resid - jnp.mean(resid, axis=-1, keepdims=True)
    rstd = lax.rsqrt(jnp.mean(centered * centered, axis=-1, keepdims=True) + norm_epsilon)
    return centered * rstd, rstd


def modulate(resid, shift_part, scale_part):
    return norm_parts(resid)[0] * (1.0 + scale_part) + shift_part


def modulate_back(resid, scale_part, grad):
    unit, rstd = norm_parts(resid)
    inner = grad * (1.0 + scale_part)
    grad_in = rstd * (
        inner
        - jnp.mean(inner, axis=-1, keepdims=True)
        - unit * jnp.mean(inner * unit, axis=-1, keepdims=True)
    )
    return grad_in, jnp.sum(grad, axis=1), jnp.sum(grad * unit, axis=1)


def sides():
    row, col = lax.axis_index("row"), lax.axis_index("col")
    core = lax.rem(col, 2)
    across = col // 2
    chip = row * 2 + across
    chips = {
        "own": chip,
        "x": (1 - row) * 2 + across,
        "y": row * 2 + 1 - across,
        "far": (1 - row) * 2 + 1 - across,
    }
    address = {
        "x": {"row": 1 - row},
        "y": {"col": lax.rem(col + 2, 4)},
        "core": {"col": col + 1 - 2 * core},
    }
    return core, chips, address


def greet(addresses):
    barrier = pltpu.get_barrier_semaphore()
    for who in addresses:
        pl.semaphore_signal(barrier, inc=1, device_id=who, device_id_type=pl.DeviceIdType.MESH)
    pl.semaphore_wait(barrier, len(addresses))


def remote(source, target, send, recv, who):
    return pltpu.make_async_remote_copy(
        src_ref=source,
        dst_ref=target,
        send_sem=send,
        recv_sem=recv,
        device_id=who,
        device_id_type=pl.DeviceIdType.MESH,
    )


def rank_at(offset):
    ranks = lax.axis_size("batch")
    return {"batch": lax.rem(lax.axis_index("batch") + offset + ranks, ranks)}


def other_ranks():
    return [rank_at(offset) for offset in range(1, lax.axis_size("batch"))]


def plane_peers():
    row, col = lax.axis_index("row"), lax.axis_index("col")
    rows, cols = lax.axis_size("row"), lax.axis_size("col")
    return [
        {"row": lax.rem(row + n // cols, rows), "col": lax.rem(col + n % cols, cols)}
        for n in range(1, rows * cols)
    ]


class Line:
    reach = 1

    def __init__(self, source):
        ranks = lax.axis_size("batch")
        self.ins = [source]
        self.outs = [jax.ShapeDtypeStruct((ranks,) + source.shape, source.dtype)]
        self.sems = [(2, ranks - 1), (2, ranks - 1), (1,)]

    def bind(self, ins, outs, sems):
        (self.source,), (self.target,) = ins, outs
        self.send, self.recv, self.own = sems
        self.rank, self.ranks = lax.axis_index("batch"), lax.axis_size("batch")
        self.steps = self.ranks
        self.late = 0

    def copy(self, way, r):
        block = self.rank - r if way == 0 else self.rank + r
        source = self.source if r == 0 else self.target.at[block]
        return remote(
            source, self.target.at[block], self.send.at[way, r], self.recv.at[way, r], rank_at(1 - 2 * way)
        )

    def holds(self, way, r):
        return self.rank >= r if way == 0 else self.rank + r < self.ranks

    def sends(self, way, r):
        edge = self.rank + 1 < self.ranks if way == 0 else self.rank > 0
        return jnp.logical_and(self.holds(way, r), edge)

    def step(self, r):
        for way in (0, 1):
            if r > 0:
                block = self.rank - r if way == 0 else self.rank + r

                @pl.when(self.holds(way, r))
                def _(way=way, block=block):
                    place = self.target.at[block]
                    remote(place, place, self.send.at[way, r - 1], self.recv.at[way, r - 1], rank_at(1)).wait_recv()

            if r < self.ranks - 1:

                @pl.when(self.sends(way, r))
                def _(way=way):
                    self.copy(way, r).start()

        if r == 0:
            self.stay().start()

    def stay(self):
        return pltpu.make_async_copy(self.source, self.target.at[self.rank], self.own.at[0])

    def finish(self):
        for way in (0, 1):
            for r in range(self.ranks - 1):

                @pl.when(self.sends(way, r))
                def _(way=way, r=r):
                    self.copy(way, r).wait_send()

        self.stay().wait()


class Chain:
    reach = 1

    def __init__(self, source, shard):
        pieces, self.rows, _ = source.shape
        self.shard = shard
        self.ins = [source]
        self.outs = [jax.ShapeDtypeStruct(source.shape, source.dtype)]
        self.sems = [(pieces, 2), (pieces, 2), (pieces,)]

    def bind(self, ins, outs, sems):
        (self.source,), (self.target,) = ins, outs
        self.send, self.recv, self.own = sems
        self.rank, self.ranks = lax.axis_index("batch"), lax.axis_size("batch")
        self.steps = self.ranks
        self.late = 0
        self.owners = owners_of(self.source.shape[0], self.rows, self.shard)

    def copy(self, j, way, first):
        source = self.source.at[j] if first else self.target.at[j]
        return remote(
            source, self.target.at[j], self.send.at[j, way], self.recv.at[j, way], rank_at(1 - 2 * way)
        )

    def edge(self, way):
        return self.rank + 1 < self.ranks if way == 0 else self.rank > 0

    def step(self, r):
        for j, owner in enumerate(self.owners):
            for way in (0, 1):
                away = self.rank - owner if way == 0 else owner - self.rank
                if r > 0:

                    @pl.when(away == r)
                    def _(j=j, way=way):
                        self.copy(j, way, False).wait_recv()

                @pl.when(jnp.logical_and(away == r, self.edge(way)))
                def _(j=j, way=way):
                    self.copy(j, way, r == 0).start()

            if r == 0:

                @pl.when(self.rank == owner)
                def _(j=j):
                    self.stay(j).start()

    def stay(self, j):
        return pltpu.make_async_copy(self.source.at[j], self.target.at[j], self.own.at[j])

    def finish(self):
        for j, owner in enumerate(self.owners):
            for way in (0, 1):
                away = self.rank - owner if way == 0 else owner - self.rank

                @pl.when(jnp.logical_and(away >= 0, self.edge(way)))
                def _(j=j, way=way):
                    self.copy(j, way, False).wait_send()

            @pl.when(self.rank == owner)
            def _(j=j):
                self.stay(j).wait()


def team_place():
    return lax.axis_index("row") * lax.axis_size("col") + lax.axis_index("col")


def owners_of(pieces, rows, shard):
    place = team_place()
    return [(place * pieces + j) * rows // shard for j in range(pieces)]


class Fold:
    reach = 2

    def __init__(self, source, late=0):
        ranks = lax.axis_size("batch")
        self.ins = [source]
        self.late = late
        self.outs = [jax.ShapeDtypeStruct((ranks - 1,) + source.shape[1:], source.dtype)]
        self.sems = [(ranks - 1,), (ranks - 1,)]

    def bind(self, ins, outs, sems):
        (self.source,), (self.inbox,) = ins, outs
        self.send, self.recv = sems
        self.steps = 1

    def copies(self):
        for n in range(lax.axis_size("batch") - 1):
            who = rank_at(n + 1)
            yield remote(
                self.source.at[who["batch"]], self.inbox.at[n], self.send.at[n], self.recv.at[n], who
            )

    def step(self, r):
        for copy in self.copies():
            copy.start()

    def finish(self):
        for copy in self.copies():
            copy.wait()


class FoldTo:
    reach = 2

    def __init__(self, shape, shard, late, source=None):
        pieces, self.rows, width = shape
        others = lax.axis_size("batch") - 1
        self.shard = shard
        self.ins = [] if source is None else [source]
        self.outs = [jax.ShapeDtypeStruct((pieces, others, self.rows, width), bf16)]
        self.sems = [(pieces, others), (pieces, others)]
        self.late, self.pieces = late, pieces

    def bind(self, ins, outs, sems):
        (self.inbox,) = outs
        self.source = ins[0] if ins else None
        self.send, self.recv = sems
        self.steps = 1
        self.rank, self.others = lax.axis_index("batch"), lax.axis_size("batch") - 1
        self.owners = owners_of(self.pieces, self.rows, self.shard)

    def copy(self, j, n):
        return remote(
            self.source.at[j], self.inbox.at[j, n], self.send.at[j, n], self.recv.at[j, n], rank_at(n + 1)
        )

    def leads(self, j, n):
        return rank_at(n + 1)["batch"] == self.owners[j]

    def step(self, r):
        for j in range(len(self.owners)):
            for n in range(self.others):

                @pl.when(self.leads(j, n))
                def _(j=j, n=n):
                    self.copy(j, n).start()

    def finish(self):
        for j, owner in enumerate(self.owners):
            for n in range(self.others):

                @pl.when(self.rank == owner)
                def _(j=j, n=n):
                    self.copy(j, n).wait_recv()

                @pl.when(self.leads(j, n))
                def _(j=j, n=n):
                    self.copy(j, n).wait_send()


class Copies:
    def __init__(self, send, recv, address):
        self.send, self.recv, self.address = send, recv, address
        self.started = {}

    def go(self, slot, source, target, who):
        copy = remote(source, target, self.send.at[slot], self.recv.at[slot], self.address[who])
        copy.start()
        self.started[slot] = copy

    def arrived(self, *slots):
        for slot in slots:
            self.started[slot].wait_recv()

    def drain(self):
        for copy in self.started.values():
            copy.wait_send()


class Gather(Copies):
    def __init__(self, full, send, recv, place):
        core, chips, address = place
        super().__init__(send, recv, address)
        self.full, self.half = full, full.shape[1] // 2
        self.source = None
        self.at = {name: core * 4 + chip for name, chip in chips.items()}

    def whole(self, name):
        return self.full.at[self.at[name]]

    def part(self, name, second):
        return self.full.at[self.at[name], pl.ds(self.half * second, self.half)]

    def first(self):
        own = self.whole("own")
        source = own if self.source is None else self.source
        parts = [pl.ds(0, self.half), pl.ds(self.half, self.half)]
        for slot, part, who in ((0, 0, "x"), (1, 1, "y"), (8, 1, "x"), (9, 0, "y")):
            self.go(slot, source.at[parts[part]], self.part("own", part), who)
        self.go(2, source, own, "core")

    def second(self):
        self.arrived(0)
        self.go(3, self.part("x", 0), self.part("x", 0), "y")
        self.arrived(1)
        self.go(4, self.part("y", 1), self.part("y", 1), "x")
        self.arrived(8)
        self.go(5, self.whole("x"), self.whole("x"), "core")
        self.arrived(9)
        self.go(6, self.whole("y"), self.whole("y"), "core")

    def finish(self):
        self.arrived(3, 4)
        self.go(7, self.whole("far"), self.whole("far"), "core")
        self.arrived(2, 5, 6, 7)


class PlaneGather:
    reach = 0

    def __init__(self, source, plan=(0, 1, 2)):
        self.ins = [source]
        self.plan = plan
        self.outs = [jax.ShapeDtypeStruct((8,) + source.shape, source.dtype)]
        self.sems = [(10,), (10,), (1,)]
        self.late = 0

    def bind(self, ins, outs, sems):
        (self.source,), (self.target,) = ins, outs
        send, recv, self.own = sems
        self.gather = Gather(self.target, send, recv, sides())
        self.gather.source = self.source
        self.steps = 3

    def stay(self):
        return pltpu.make_async_copy(self.source, self.gather.whole("own"), self.own.at[0])

    def step(self, r):
        if r == 0:
            self.gather.first()
            self.stay().start()
        elif r == 1:
            self.gather.second()
        else:
            self.gather.finish()

    def finish(self):
        self.gather.drain()
        self.stay().wait()


class Background:
    def __init__(self, tasks):
        self.tasks = tasks
        self.now = 0
        self.done = [[] for _ in tasks]

    def partners(self):
        reach = max([task.reach for task in self.tasks], default=0)
        return [[], [rank_at(1), rank_at(-1)], other_ranks()][reach]

    def tick(self):
        for task, done in zip(self.tasks, self.done):
            plan = getattr(task, "plan", None) or range(task.late, task.late + task.steps)
            if len(done) < task.steps and len(done) < len(plan) and plan[len(done)] <= self.now:
                task.step(len(done))
                done.append(self.now)
        self.now += 1

    def finish(self):
        for most in range(max([task.steps for task in self.tasks], default=0)):
            for task, done in zip(self.tasks, self.done):
                if len(done) == most and most < task.steps:
                    task.step(most)
                    done.append(self.now)
        for task in self.tasks:
            task.finish()


class Scatter(Copies):
    def __init__(self, core_out, core_in, total, hop_out, hop_in, send, recv, place):
        _, self.chips, address = place
        super().__init__(send, recv, address)
        self.core_out, self.core_in, self.total = core_out, core_in, total
        self.hop_out, self.hop_in = hop_out, hop_in
        self.half = total.shape[1] // 2

    def cross(self):
        self.go(0, self.core_out, self.core_in, "core")

    def hop(self, slot, value, who):
        self.hop_out[slot] = value.astype(bf16)
        self.go(1 + slot, self.hop_out.at[slot], self.hop_in.at[slot], who)

    def first(self):
        self.arrived(0)
        half = self.half

        def summed(name):
            chip = self.chips[name]
            return self.total[chip] + self.core_in[chip].astype(f32)

        far = summed("far")
        self.hop(0, far[:half], "x")
        self.hop(2, far[half:], "y")
        x_sum = summed("x")
        self.hop(1, x_sum[:half], "x")
        self.total[self.chips["x"], half:] = x_sum[half:]
        y_sum = summed("y")
        self.hop(3, y_sum[half:], "y")
        self.total[self.chips["y"], :half] = y_sum[:half]

    def second(self):
        half = self.half
        self.arrived(1)
        self.hop(4, self.total[self.chips["y"], :half] + self.hop_in[0].astype(f32), "y")
        self.arrived(3)
        self.hop(5, self.total[self.chips["x"], half:] + self.hop_in[2].astype(f32), "x")

    def finish(self):
        self.arrived(2, 4, 5, 6)
        half, own = self.half, self.chips["own"]
        base = self.total[own] + self.core_in[own].astype(f32)
        low = base[:half] + self.hop_in[1].astype(f32) + self.hop_in[4].astype(f32)
        high = base[half:] + self.hop_in[3].astype(f32) + self.hop_in[5].astype(f32)
        return jnp.concatenate([low, high], axis=0)


def comm_scratch(images, length, width):
    half = length // 2
    return [
        pltpu.VMEM((images, 4, length, width), bf16),
        pltpu.VMEM((images, 4, length, width), bf16),
        pltpu.VMEM((images, 4, length, width), f32),
        pltpu.VMEM((images, 6, half, width), bf16),
        pltpu.VMEM((images, 6, half, width), bf16),
        pltpu.SemaphoreType.DMA((images, 10)),
        pltpu.SemaphoreType.DMA((images, 10)),
        pltpu.SemaphoreType.DMA((images, 7)),
        pltpu.SemaphoreType.DMA((images, 7)),
    ]


def exchanges(full, comm, place):
    core_out, core_in, total, hop_out, hop_in, gs, gr, ss, sr = comm
    images = full.shape[0]
    gathers = [Gather(full.at[i], gs.at[i], gr.at[i], place) for i in range(images)]
    scatters = [
        Scatter(
            core_out.at[i], core_in.at[i], total.at[i], hop_out.at[i], hop_in.at[i], ss.at[i], sr.at[i], place
        )
        for i in range(images)
    ]
    return gathers, scatters


def flat(value):
    return value.reshape(value.shape[0] * value.shape[1], value.shape[2])


def halves(core):
    return ((1 - core) * 4, True), (core * 4, False)


def keep_partial(partial, scatter, sibling):
    shape = scatter.total.shape
    if sibling:
        scatter.core_out[...] = partial.astype(bf16).reshape(shape)
        scatter.cross()
    else:
        scatter.total[...] = partial.reshape(shape)


def column_sum(value):
    return jnp.sum(value, axis=0, keepdims=True)


def row_sums(value):
    ones = jnp.ones((8, value.shape[0]), bf16)
    return dot(ones, value, ((1,), (0,)))


GELU_ROOT = 0.7978845608028654
GELU_CUBE = 0.044715
NN, NT, TN = ((1,), (0,)), ((1,), (1,)), ((0,), (0,))


def gelu(hidden):
    inner = GELU_ROOT * (hidden + GELU_CUBE * (hidden * hidden * hidden))
    return 0.5 * hidden * (1.0 + jnp.tanh(inner))


def gelu_with_slope(hidden):
    square = hidden * hidden
    bend = jnp.tanh(GELU_ROOT * hidden * (1.0 + GELU_CUBE * square))
    rise = 0.5 * (1.0 + bend)
    slope = rise + 0.5 * hidden * (1.0 - bend * bend) * (GELU_ROOT + 3.0 * GELU_ROOT * GELU_CUBE * square)
    return hidden * rise, slope


def modulate_back_rows(resid, scale_part, grad):
    unit, rstd = norm_parts(resid)
    inner = grad * (1.0 + scale_part)
    grad_in = rstd * (
        inner
        - jnp.mean(inner, axis=-1, keepdims=True)
        - unit * jnp.mean(inner * unit, axis=-1, keepdims=True)
    )
    return grad_in, column_sum(grad), column_sum(grad * unit)


class Far:
    def __init__(self, what):
        self.what = what


class Copying:
    def __init__(self, sems):
        self.sems = sems
        self.open = {}

    def start(self, name, source, target):
        copy = pltpu.make_async_copy(source, target, self.sems.at[len(self.open)])
        copy.start()
        self.open[name] = copy

    def wait(self, *names):
        for name in names:
            self.open[name].wait()


def scratch_like(array):
    return pltpu.VMEM(array.shape, array.dtype)


def call(kernel, name, ident, outs, scratch, flops, args, tasks=()):
    vmem, anywhere = pl.BlockSpec(memory_space=pltpu.VMEM), pl.BlockSpec(memory_space=pl.ANY)
    in_specs = [anywhere if isinstance(a, Far) else vmem for a in args]
    out_specs = [anywhere if isinstance(o, Far) else vmem for o in outs]
    args = [a.what if isinstance(a, Far) else a for a in args]
    outs = [o.what if isinstance(o, Far) else o for o in outs]
    moved = sum(a.size * a.dtype.itemsize for a in args) + sum(o.size * o.dtype.itemsize for o in outs)
    task_ins = [array for task in tasks for array in task.ins]
    task_outs = [shape for task in tasks for shape in task.outs]
    task_sems = [pltpu.SemaphoreType.DMA(shape) for task in tasks for shape in task.sems]

    def run(*refs):
        refs = list(refs)

        def take(count):
            taken = refs[:count]
            del refs[:count]
            return taken

        main_ins, bound_ins = take(len(args)), take(len(task_ins))
        main_outs, bound_outs = take(len(outs)), take(len(task_outs))
        main_scratch = take(len(scratch))
        for task in tasks:
            ins = [bound_ins.pop(0) for _ in task.ins]
            results = [bound_outs.pop(0) for _ in task.outs]
            task.bind(ins, results, take(len(task.sems)))
        kernel(Background(tasks), *main_ins, *main_outs, *main_scratch)

    results = pl.pallas_call(
        run,
        name=name,
        out_shape=list(outs) + task_outs,
        in_specs=in_specs + [anywhere] * len(task_ins),
        out_specs=out_specs + [anywhere] * len(task_outs),
        scratch_shapes=list(scratch) + task_sems,
        compiler_params=pltpu.CompilerParams(
            collective_id=ident, has_side_effects=True, vmem_limit_bytes=60 * 2**20
        ),
        cost_estimate=pl.CostEstimate(flops=flops, bytes_accessed=moved, transcendentals=0),
    )(*args, *task_ins)
    return results[: len(outs)], results[len(outs) :]


def shaped(shape, kind):
    return jax.ShapeDtypeStruct(shape, kind)


def prologue_kernel(background, *refs):
    smalls = refs[:-8]
    tiles, packs, every_tile, pack, zs, zr, ps, pr = refs[-8:]
    lanes = pack.shape[1]
    rows = []
    for small in smalls:
        value = small[...].astype(f32)
        rows += [value[:, start : start + lanes] for start in range(0, value.shape[1], lanes)]
    used = sum(value.shape[0] for value in rows)
    if used < pack.shape[0]:
        rows.append(jnp.zeros((pack.shape[0] - used, lanes), f32))
    pack[...] = jnp.concatenate(rows, axis=0).astype(bf16)
    ranks, peers = other_ranks(), plane_peers()
    greet(ranks + peers)
    rank, place = lax.axis_index("batch"), team_place()
    copies = [remote(pack, packs.at[rank], zs.at[n], zr.at[n], who) for n, who in enumerate(ranks)]
    for n, who in enumerate(peers):
        copies.append(remote(tiles, every_tile.at[place], ps.at[n], pr.at[n], who))
    for copy in copies:
        copy.start()
    packs[rank] = pack[...]
    every_tile[place] = tiles[...]
    for copy in copies:
        copy.wait()


def prologue(smalls, dims, tiles, ident):
    ranks = lax.axis_size("batch")
    dma = pltpu.SemaphoreType.DMA
    lanes = min(small.shape[1] for small in smalls)
    rows = sum(small.size // lanes for small in smalls)
    pack = (rows + -rows % 16, lanes)
    (packs, every_tile), _ = call(
        prologue_kernel,
        "prologue",
        ident,
        [shaped((ranks,) + pack, bf16), shaped((8,) + tiles.shape, tiles.dtype)],
        [pltpu.VMEM(pack, bf16), dma((ranks - 1,)), dma((ranks - 1,)), dma((7,)), dma((7,))],
        0,
        (*smalls, tiles),
    )
    parts, start = [], 0
    for small, dim in zip(smalls, dims):
        count, each = small.shape[0], small.shape[1] // lanes
        part = packs[:, start : start + count * each].reshape(ranks, each, count, lanes)
        start += count * each
        if dim == 0:
            parts.append(part.transpose(0, 2, 1, 3).reshape(ranks * count, -1))
        else:
            parts.append(part.transpose(2, 0, 1, 3).reshape(count, -1))
    return parts, every_tile


def conditioning_kernel(background, parts, mods, inbox, zs, zr, ps, pr):
    ranks, peers = other_ranks(), plane_peers()
    greet(ranks + peers)
    rank, place = lax.axis_index("batch"), team_place()
    first = [
        remote(parts.at[who["batch"]], inbox.at[n], zs.at[n], zr.at[n], who) for n, who in enumerate(ranks)
    ]
    for copy in first:
        copy.start()
    background.tick()
    total = parts[rank]
    for n, copy in enumerate(first):
        copy.wait()
        total = total + inbox[n]
    mods[place] = total
    second = [
        remote(mods.at[place], mods.at[place], ps.at[n], pr.at[n], who) for n, who in enumerate(peers)
    ]
    for copy in second:
        copy.start()
    background.tick()
    for copy in second:
        copy.wait()
    background.finish()


def conditioning_exchange(parts, ident, tasks):
    ranks = parts.shape[0]
    dma = pltpu.SemaphoreType.DMA
    (mods,), gathered = call(
        conditioning_kernel,
        "conditioning",
        ident,
        [shaped((8,) + parts.shape[1:], f32)],
        [
            pltpu.VMEM((ranks - 1,) + parts.shape[1:], f32),
            dma((ranks - 1,)),
            dma((ranks - 1,)),
            dma((7,)),
            dma((7,)),
        ],
        0,
        (parts,),
        tasks,
    )
    return mods, gathered


def epilogue_kernel(
    depth, background, *refs,
):
    refs = list(refs)

    def take(count):
        taken = refs[:count]
        del refs[:count]
        return taken

    block_sums, (final_sums,) = take(2 * depth), take(1)
    block_biases = take(2 * depth)
    patch_term, final_term, edge_rows, tokens = take(4)
    all_mods, all_rows, all_tokens = take(3)
    mods, sums, biases, mods_in, sums_in, rank_mods, rank_sums, rank_biases_in, ps, pr, zs, zr, qs, qr = refs
    ranks, peers = other_ranks(), plane_peers()
    rank = lax.axis_index("batch")
    around = sides()
    place = around[0] * 4 + around[1]["own"]
    gather_tokens, gather_mods, gather_rows = [
        Gather(full, qs.at[n], qr.at[n], around) for n, full in enumerate((all_tokens, all_mods, all_rows))
    ]
    images = final_sums.shape[0]
    each = sums.shape[1]

    mods[...] = jnp.zeros_like(mods)
    sums[...] = jnp.zeros_like(sums)
    biases[...] = jnp.zeros_like(biases)
    for i in range(images):
        for b in range(depth):
            for p in range(6):
                n = 6 * b + p
                source = block_sums[2 * b + p // 3]
                mods[n // 2, i * 2 + n % 2] = source[i, p % 3]
        for p in range(2):
            n = 6 * depth + p
            mods[n // 2, i * 2 + n % 2] = final_sums[i, p]
    rows = [patch_term[n] for n in range(patch_term.shape[0])]
    rows += [final_term[n] for n in range(final_term.shape[0])]
    rows += [edge_rows[n] for n in range(edge_rows.shape[0])]
    for source in block_sums:
        total = source[0, 3]
        for i in range(1, images):
            total = total + source[i, 3]
        rows.append(total)
    for n, row in enumerate(rows):
        sums[n // each, n % each] = row
    for n, source in enumerate(block_biases):
        biases[n, : source.shape[1]] = source[0]

    greet(ranks + peers)
    first = []
    for n, who in enumerate(peers):
        there = lax.rem(who["col"], 2) * 4 + who["row"] * 2 + who["col"] // 2
        first.append(remote(mods.at[there], mods_in.at[n], ps.at[0, n], pr.at[0, n], who))
        first.append(remote(sums.at[there], sums_in.at[n], ps.at[1, n], pr.at[1, n], who))
    second = [
        remote(biases, rank_biases_in.at[n], zs.at[0, n], zr.at[0, n], who) for n, who in enumerate(ranks)
    ]
    for copy in first + second:
        copy.start()
    all_tokens[place] = tokens[...]
    gather_tokens.first()
    background.tick()
    for copy in first:
        copy.wait()
    mod_total, sum_total = mods[place], sums[place]
    for n in range(len(peers)):
        mod_total = mod_total + mods_in[n]
        sum_total = sum_total + sums_in[n]
    rank_mods[rank] = mod_total.astype(bf16)
    rank_sums[rank] = sum_total
    third = []
    for n, who in enumerate(ranks):
        third.append(remote(rank_mods.at[rank], rank_mods.at[rank], zs.at[1, n], zr.at[1, n], who))
        third.append(remote(rank_sums.at[rank], rank_sums.at[rank], zs.at[2, n], zr.at[2, n], who))
    for copy in third:
        copy.start()
    background.tick()
    bias_total = biases[...]
    for n, copy in enumerate(second):
        copy.wait()
        bias_total = bias_total + rank_biases_in[n]
    for copy in third:
        copy.wait()
    sum_own = rank_sums[0]
    for n in range(1, rank_sums.shape[0]):
        sum_own = sum_own + rank_sums[n]
    all_mods[place] = rank_mods[...]
    all_rows[place, 0, :each] = sum_own
    all_rows[place, 1, :, : biases.shape[1]] = bias_total
    gather_mods.first()
    gather_rows.first()
    gather_tokens.second()
    background.tick()
    for gather in (gather_mods, gather_rows):
        gather.second()
    for gather in (gather_tokens, gather_mods, gather_rows):
        gather.finish()
        gather.drain()
    background.finish()


def epilogue(block_sums, final_sums, block_biases, patch_term, final_term, edge_rows, tokens, ident, tasks):
    ranks = lax.axis_size("batch")
    dma = pltpu.SemaphoreType.DMA
    depth = len(block_sums) // 2
    images, _, width = final_sums.shape
    count = patch_term.shape[0] + final_term.shape[0] + edge_rows.shape[0] + len(block_sums)
    each = -(-count // 8)
    widest = max(source.shape[1] for source in block_biases)
    mods, sums = (8, 2 * images, width), (8, each, width)
    biases = (8, widest)
    return call(
        partial(epilogue_kernel, depth),
        "epilogue",
        ident,
        [
            shaped((8, ranks) + mods[1:], bf16),
            shaped((8, 2, 8, width), f32),
            shaped((8,) + tokens.shape, f32),
        ],
        [
            pltpu.VMEM(mods, f32),
            pltpu.VMEM(sums, f32),
            pltpu.VMEM(biases, f32),
            pltpu.VMEM((7,) + mods[1:], f32),
            pltpu.VMEM((7,) + sums[1:], f32),
            pltpu.VMEM((ranks,) + mods[1:], bf16),
            pltpu.VMEM((ranks,) + sums[1:], f32),
            pltpu.VMEM((ranks - 1,) + biases, f32),
            dma((2, 7)),
            dma((2, 7)),
            dma((3, ranks - 1)),
            dma((3, ranks - 1)),
            dma((3, 10)),
            dma((3, 10)),
        ],
        0,
        (*block_sums, final_sums, *block_biases, patch_term, final_term, edge_rows, tokens),
        tasks,
    )


def closing_kernel(background, parts, every, zs, zr):
    ranks = other_ranks()
    address = sides()[2]
    greet(ranks + list(address.values()))
    rank = lax.axis_index("batch")
    copies = [
        remote(parts.at[who["batch"]], every.at[rank], zs.at[n], zr.at[n], who) for n, who in enumerate(ranks)
    ]
    background.tick()
    for copy in copies:
        copy.start()
    every[rank] = parts[rank]
    for copy in copies:
        copy.wait()
    background.finish()


def closing(parts, ident, tasks):
    ranks = parts.shape[0]
    dma = pltpu.SemaphoreType.DMA
    (every,), gathered = call(
        closing_kernel,
        "closing",
        ident,
        [shaped(parts.shape, f32)],
        [dma((ranks - 1,)), dma((ranks - 1,))],
        0,
        (parts,),
        tasks,
    )
    return every, gathered


def mlp_forward_kernel(
    block, background, mid, gate_rows, vecs, pair_far, expand_bias, full_far, hidden_far, expanded, after,
    full, hidden, pair, expand, shrink, moves, *comm
):
    moving = Copying(moves)
    moving.start("pair", pair_far, pair)
    place = sides()
    core, chips, address = place
    images = full.shape[0]
    gathers, scatters = exchanges(full, comm, place)
    greet(list(address.values()) + background.partners())

    def row(i, n):
        return vecs[i, n : n + 1]

    def gate(i):
        return gate_rows[i] if block > 0 else 1.0

    own = core * 4 + chips["own"]

    def begin(i):
        full[i, own] = modulate(mid[i], row(i, 6 * block + 3), row(i, 6 * block + 4)).astype(bf16)
        gathers[i].first()

    def compute(i, between):
        for step, (start, sibling) in enumerate(halves(core)):
            value = dot(flat(full[i, pl.ds(start, 4)]), expand[...], NN) + expand_bias[...]
            hidden[i, pl.ds(start, 4)] = value.reshape(4, -1, value.shape[1])
            partial = dot(gelu(value).astype(bf16), shrink[...], NT)
            keep_partial(partial, scatters[i], sibling)
            between[step]()

    def end(i):
        value = scatters[i].finish() + row(i, offset_row(vecs, block, 1))
        expanded[i] = value
        after[i] = mid[i] + gate(i) * row(i, 6 * block + 5) * value

    def keep(i):
        moving.start(("full", i), full.at[i], full_far.at[i])
        moving.start(("hidden", i), hidden.at[i], hidden_far.at[i])

    begin(0)
    background.tick()
    moving.wait("pair")
    expand[...] = pair[:, : expand.shape[1]]
    shrink[...] = pair[:, expand.shape[1] :]
    gathers[0].second()
    begin(1)
    gathers[0].finish()
    compute(0, (gathers[1].second, scatters[0].first))
    keep(0)
    background.tick()
    gathers[1].finish()
    compute(1, (scatters[0].second, scatters[1].first))
    keep(1)
    background.tick()
    end(0)
    scatters[1].second()
    end(1)
    for part in gathers + scatters:
        part.drain()
    moving.wait(*[(name, i) for name in ("full", "hidden") for i in range(images)])
    background.finish()


def mlp_forward(block, mid, gate_rows, vecs, weights, ident, tasks=()):
    pair, expand_bias = weights
    images, length, width = mid.shape
    inner = pair.shape[1] // 2
    return call(
        partial(mlp_forward_kernel, block),
        "mlp_forward",
        ident,
        [
            Far(shaped((images, 8, length, width), bf16)),
            Far(shaped((images, 8, length, inner), f32)),
            shaped((images, length, width), f32),
            shaped((images, length, width), f32),
        ],
        [
            pltpu.VMEM((images, 8, length, width), bf16),
            pltpu.VMEM((images, 8, length, inner), f32),
            scratch_like(pair),
            pltpu.VMEM((width, inner), bf16),
            pltpu.VMEM((width, inner), bf16),
            pltpu.SemaphoreType.DMA((1 + 2 * images,)),
        ]
        + comm_scratch(images, length, width),
        4 * images * 8 * length * width * inner * 6,
        (
            mid,
            gate_rows,
            vecs,
            Far(pair),
            expand_bias.reshape(1, -1),
        ),
        tasks,
    )


def mlp_backward_kernel(
    block, background, grad_after, mid, expanded, gate_rows, vecs, pair_far, normed_far, hidden_far,
    grad_mid, sums, grad_pair, grad_bias,
    full, grad_hidden, active, sum_expand, sum_shrink, pair, expand, shrink, normed, hidden, moves, *comm
):
    moving = Copying(moves)
    moving.start("pair", pair_far, pair)
    moving.start("hidden", hidden_far, hidden)
    moving.start("normed", normed_far, normed)
    place = sides()
    core, chips, address = place
    gathers, scatters = exchanges(full, comm, place)
    greet(list(address.values()) + background.partners())

    def row(i, n):
        return vecs[i, n : n + 1]

    def gate(i):
        return gate_rows[i] if block > 0 else 1.0

    own = core * 4 + chips["own"]
    length = full.shape[2]

    def begin(i):
        gated = gate(i) * grad_after[i, :length]
        low = (gated * row(i, 6 * block + 5)).astype(bf16)
        full[i, own] = low
        gathers[i].first()
        sums[i, 2:3] = column_sum(gated * expanded[i])
        sums[i, 3:4] = column_sum(low.astype(f32))

    def compute(i, between):
        for step, (start, sibling) in enumerate(halves(core)):
            pull = dot(flat(full[i, pl.ds(start, 4)]), shrink[...], NN)
            value, slope = gelu_with_slope(flat(hidden[i, pl.ds(start, 4)]))
            active[i, pl.ds(start, 4)] = value.astype(bf16).reshape(4, -1, value.shape[1])
            low = (pull * slope).astype(bf16)
            grad_hidden[i, pl.ds(start, 4)] = low.reshape(4, -1, value.shape[1])
            keep_partial(dot(low, expand[...], NT), scatters[i], sibling)
            between[step]()

    def weigh_shrink(i):
        term = dot(flat(full[i]), flat(active[i]), TN)
        if i == 0:
            sum_shrink[...] = term
        else:
            sum_shrink[...] += term

    def weigh_expand(i):
        low = flat(grad_hidden[i])
        term = dot(flat(normed[i]), low, TN)
        if i == 0:
            sum_expand[...] = term
            grad_bias[...] = row_sums(low)
        else:
            grad_pair[...] = jnp.concatenate([sum_expand[...] + term, sum_shrink[...]], axis=1).astype(bf16)
            grad_bias[...] += row_sums(low)

    def end(i):
        grad, shift_sum, scale_sum = modulate_back_rows(mid[i], row(i, 6 * block + 4), scatters[i].finish())
        grad_mid[i] = grad + grad_after[i, :length]
        sums[i, 0:1] = shift_sum
        sums[i, 1:2] = scale_sum

    begin(0)
    background.tick()
    moving.wait("pair")
    expand[...] = pair[:, : expand.shape[1]]
    shrink[...] = pair[:, expand.shape[1] :]
    gathers[0].second()
    begin(1)
    gathers[0].finish()
    moving.wait("hidden")
    compute(0, (gathers[1].second, scatters[0].first))
    background.tick()
    gathers[1].finish()
    compute(1, (scatters[0].second, scatters[1].first))
    background.tick()
    weigh_shrink(0)
    end(0)
    scatters[1].second()
    background.tick()
    moving.wait("normed")
    weigh_expand(0)
    weigh_shrink(1)
    weigh_expand(1)
    end(1)
    for part in gathers + scatters:
        part.drain()
    background.finish()


def mlp_backward(block, grad_after, mid, expanded, gate_rows, vecs, weights, saved, ident, tasks=()):
    pair, _ = weights
    normed, hidden = saved
    images, length, width = mid.shape
    inner = pair.shape[1] // 2
    return call(
        partial(mlp_backward_kernel, block),
        "mlp_backward",
        ident,
        [
            shaped((images, length, width), f32),
            shaped((images, 8, width), f32),
            shaped((width, 2 * inner), bf16),
            shaped((8, inner), f32),
        ],
        [
            pltpu.VMEM((images, 8, length, width), bf16),
            pltpu.VMEM((images, 8, length, inner), bf16),
            pltpu.VMEM((images, 8, length, inner), bf16),
            pltpu.VMEM((width, inner), f32),
            pltpu.VMEM((width, inner), f32),
            scratch_like(pair),
            pltpu.VMEM((width, inner), bf16),
            pltpu.VMEM((width, inner), bf16),
            scratch_like(normed),
            scratch_like(hidden),
            pltpu.SemaphoreType.DMA((3,)),
        ]
        + comm_scratch(images, length, width),
        8 * images * 8 * length * width * inner * 6,
        (
            grad_after,
            mid,
            expanded,
            gate_rows,
            vecs,
            Far(pair),
            Far(normed),
            Far(hidden),
        ),
        tasks,
    )


LOG2E = 1.4426950408889634


def offset_row(vecs, block, kind):
    depth = (vecs.shape[1] - 2) // 8
    return 6 * depth + 2 + 2 * block + kind


def pad_lanes(value):
    gap = jnp.zeros((value.shape[0], LANES - HEAD_SIZE), value.dtype)
    parts = []
    for start in range(0, value.shape[1], HEAD_SIZE):
        parts += [value[:, start : start + HEAD_SIZE], gap]
    return jnp.concatenate(parts, axis=1)


def pad_rows(value):
    gap = jnp.zeros((LANES - HEAD_SIZE, value.shape[1]), value.dtype)
    parts = []
    for start in range(0, value.shape[0], HEAD_SIZE):
        parts += [value[start : start + HEAD_SIZE], gap]
    return jnp.concatenate(parts, axis=0)


def cut_lanes(value):
    return jnp.concatenate(
        [value[:, start : start + HEAD_SIZE] for start in range(0, value.shape[1], LANES)], axis=1
    )


def cut_rows(value):
    return jnp.concatenate(
        [value[start : start + HEAD_SIZE] for start in range(0, value.shape[0], LANES)], axis=0
    )


def attention_forward_kernel(
    block, background, base, gate_rows, vecs, project_own, project_bias, attend_own, key_bias,
    full_far, packed_far, mixed_far, log_total, attended, mid, project, attend,
    full, packed, mixed, moves, *comm
):
    moving = Copying(moves)
    place = sides()
    core, chips, address = place
    images, _, length, _ = full.shape
    gathers, scatters = exchanges(full, comm, place)
    greet(list(address.values()) + background.partners())

    def row(i, n):
        return vecs[i, n : n + 1]

    def gate(i):
        return gate_rows[i] if block > 0 else 1.0

    own = core * 4 + chips["own"]
    span = attend.shape[0]
    heads = span // LANES
    tile = 2 * length
    factor = HEAD_SIZE ** (-0.5) * LOG2E

    def begin(i):
        full[i, own] = modulate(base[i, :length], row(i, 6 * block), row(i, 6 * block + 1)).astype(bf16)
        gathers[i].first()

    def rows_of(start, count):
        return pl.ds(pl.multiple_of(start * length, length), count * length)

    def compute(i, between):
        for start, _ in halves(core):
            value = dot(flat(full[i, pl.ds(start, 4)]), project[...], NN) + project_bias[...]
            packed[i, rows_of(start, 4)] = value.astype(bf16)
        between[0]()
        for step, (start, sibling) in enumerate(halves(core)):

            def one(t, carry, start=start):
                rows = pl.ds(pl.multiple_of((start + 2 * t) * length, tile), tile)
                for h in range(heads):
                    q, k, v = (
                        pl.ds(part * span + h * LANES, LANES) for part in range(3)
                    )
                    scores = dot(packed[i, rows, q], packed[i, :, k], NT) * factor
                    if block > 0:
                        scores = scores + key_bias[i]
                    peak = jnp.max(scores, axis=1, keepdims=True)
                    probs = jnp.exp2(scores - peak)
                    total = jnp.sum(probs, axis=1, keepdims=True)
                    out = dot(probs.astype(bf16), packed[i, :, v], NN) / total
                    mixed[i, rows, pl.ds(h * LANES, LANES)] = out.astype(bf16)
                    level = jnp.broadcast_to(peak + jnp.log2(total), (tile, LANES))
                    log_total[i, h, pl.ds(start // 2 + t, 1)] = level.T[0:1]
                return carry

            lax.fori_loop(0, 2, one, 0)
            partial = dot(mixed[i, rows_of(start, 4)], attend[...], NN)
            keep_partial(partial, scatters[i], sibling)
            between[1 + step]()

    def end(i):
        value = scatters[i].finish() + row(i, offset_row(vecs, block, 0))
        attended[i] = value
        mid[i] = base[i, :length] + gate(i) * row(i, 6 * block + 2) * value

    def nothing():
        pass

    def keep(i):
        for name, near, far in (("full", full, full_far), ("packed", packed, packed_far), ("mixed", mixed, mixed_far)):
            moving.start((name, i), near.at[i], far.at[i])

    begin(0)
    background.tick()
    project[...] = pad_lanes(project_own[...])
    attend[...] = pad_rows(attend_own[...])
    gathers[0].second()
    begin(1)
    gathers[0].finish()
    compute(0, (gathers[1].second, background.tick, scatters[0].first))
    keep(0)
    gathers[1].finish()
    compute(1, (scatters[0].second, nothing, scatters[1].first))
    keep(1)
    background.tick()
    end(0)
    scatters[1].second()
    end(1)
    for part in gathers + scatters:
        part.drain()
    moving.wait(*moving.open)
    background.finish()


def attention_forward(block, length, base, gate_rows, vecs, weights, key_bias, ident, tasks=()):
    project, project_bias, attend = weights
    images, _, width = base.shape
    span = attend.shape[0] // HEAD_SIZE * LANES
    return call(
        partial(attention_forward_kernel, block),
        "attention_forward",
        ident,
        [
            Far(shaped((images, 8, length, width), bf16)),
            Far(shaped((images, 8 * length, 3 * span), bf16)),
            Far(shaped((images, 8 * length, span), bf16)),
            shaped((images, span // LANES, 4, 2 * length), f32),
            shaped((images, length, width), f32),
            shaped((images, length, width), f32),
            shaped((width, 3 * span), bf16),
            shaped((span, width), bf16),
        ],
        [
            pltpu.VMEM((images, 8, length, width), bf16),
            pltpu.VMEM((images, 8 * length, 3 * span), bf16),
            pltpu.VMEM((images, 8 * length, span), bf16),
            pltpu.SemaphoreType.DMA((3 * images,)),
        ]
        + comm_scratch(images, length, width),
        8 * images * 8 * length * width * span * 6,
        (
            base,
            gate_rows,
            vecs,
            project,
            project_bias.reshape(1, -1),
            attend,
            key_bias,
        ),
        tasks,
    )


def attention_backward_kernel(
    block, background, grad_mid, base, attended, gate_rows, vecs, project_far, attend_far, key_bias, normed_far, packed_far, mixed_far, log_total,
    grad_base, sums, grad_project, grad_attend, grad_bias,
    full, grad_mixed, grad_packed, grad_keys, grad_values, sum_project, sum_attend,
    project, attend, normed, packed, mixed, moves, *comm
):
    moving = Copying(moves)
    moving.start("attend", attend_far, attend)
    moving.start("packed", packed_far, packed)
    moving.start("mixed", mixed_far, mixed)
    moving.start("project", project_far, project)
    moving.start("normed", normed_far, normed)
    place = sides()
    core, chips, address = place
    images, _, length, _ = full.shape
    gathers, scatters = exchanges(full, comm, place)
    greet(list(address.values()) + background.partners())

    def row(i, n):
        return vecs[i, n : n + 1]

    def gate(i):
        return gate_rows[i] if block > 0 else 1.0

    own = core * 4 + chips["own"]
    span = attend.shape[0]
    heads = span // LANES
    tile = 2 * length
    factor = HEAD_SIZE ** (-0.5)

    def begin(i):
        gated = gate(i) * grad_mid[i]
        low = (gated * row(i, 6 * block + 2)).astype(bf16)
        full[i, own] = low
        gathers[i].first()
        sums[i, 2:3] = column_sum(gated * attended[i])
        sums[i, 3:4] = column_sum(low.astype(f32))

    def rows_of(start, count):
        return pl.ds(pl.multiple_of(start * length, length), count * length)

    def compute(i, between):
        grad_mixed[...] = dot(flat(full[i]), attend[...], NT).astype(bf16)
        between[0]()
        for h in range(heads):
            lane = pl.ds(h * LANES, LANES)
            q, k, v = (pl.ds(part * span + h * LANES, LANES) for part in range(3))
            keys_turned = packed[i, :, k].T

            def one(t, carry):
                rows = pl.ds(pl.multiple_of(t * tile, tile), tile)
                queries, pulls = packed[i, rows, q], grad_mixed[rows, lane]
                scores = dot(packed[i, :, k], queries, NT) * (factor * LOG2E)
                if block > 0:
                    scores = scores + key_bias[i]
                probs = jnp.exp2(scores - log_total[i, h, pl.ds(t, 1)])
                dprobs = dot(packed[i, :, v], pulls, NT)
                row_dot = column_sum(probs * dprobs)
                grad_scores = (probs * (dprobs - row_dot)).astype(bf16)
                value_term = dot(probs.astype(bf16), pulls, NN)
                key_term = dot(grad_scores, queries, NN)

                @pl.when(t == 0)
                def _():
                    grad_values[...] = value_term
                    grad_keys[...] = key_term

                @pl.when(t > 0)
                def _():
                    grad_values[...] += value_term
                    grad_keys[...] += key_term

                query_term = dot(keys_turned, grad_scores, NN) * factor
                grad_packed[i, rows, q] = query_term.T.astype(bf16)
                return carry

            lax.fori_loop(0, 4, one, 0)
            grad_packed[i, :, k] = (grad_keys[...] * factor).astype(bf16)
            grad_packed[i, :, v] = grad_values[...].astype(bf16)
            between[1 + h]()
        for step, (start, sibling) in enumerate(halves(core)):
            keep_partial(dot(grad_packed[i, rows_of(start, 4)], project[...], NT), scatters[i], sibling)

    def weigh_attend(i):
        term = dot(mixed[i], flat(full[i]), TN)
        if i == 0:
            sum_attend[...] = term
        else:
            grad_attend[...] = cut_rows(sum_attend[...] + term).reshape(grad_attend.shape).astype(bf16)

    def weigh_project(i):
        low = grad_packed[i]
        term = dot(flat(normed[i]), low, TN)
        if i == 0:
            sum_project[...] = term
            grad_bias[...] = row_sums(low)
        else:
            grad_project[...] = cut_lanes(sum_project[...] + term).astype(bf16)
            grad_bias[...] += row_sums(low)

    def end(i):
        grad, shift_sum, scale_sum = modulate_back_rows(base[i, :length], row(i, 6 * block + 1), scatters[i].finish())
        grad_base[i] = grad + grad_mid[i]
        sums[i, 0:1] = shift_sum
        sums[i, 1:2] = scale_sum

    def nothing():
        pass

    def finish_extra():
        gathers[1].finish()
        background.tick()

    def early_attend():
        for i in range(images):
            weigh_attend(i)
        for task in background.tasks:
            if task.source is None:
                task.source = grad_attend
        background.tick()

    def middle():
        scatters[0].second()
        background.tick()

    begin(0)
    background.tick()
    gathers[0].second()
    begin(1)
    gathers[0].finish()
    moving.wait("attend", "packed", "mixed", "project", "normed")
    compute(0, (gathers[1].second, finish_extra, nothing))
    scatters[0].first()
    compute(1, (early_attend, middle, background.tick))
    scatters[1].first()
    weigh_project(0)
    end(0)
    scatters[1].second()
    background.tick()
    weigh_project(1)
    end(1)
    for part in gathers + scatters:
        part.drain()
    background.finish()


def attention_backward(
    block, attend_shape, grad_mid, base, attended, gate_rows, vecs, weights, key_bias, saved, ident, tasks=()
):
    project, attend = weights
    normed, packed, mixed, log_total = saved
    images, length, width = grad_mid.shape
    span = attend.shape[0]
    tokens = 8 * length
    return call(
        partial(attention_backward_kernel, block),
        "attention_backward",
        ident,
        [
            shaped((images, length, width), f32),
            shaped((images, 8, width), f32),
            shaped((width, 3 * span // LANES * HEAD_SIZE), bf16),
            shaped(attend_shape, bf16),
            shaped((8, 3 * span), f32),
        ],
        [
            pltpu.VMEM((images, 8, length, width), bf16),
            pltpu.VMEM((tokens, span), bf16),
            pltpu.VMEM((images, tokens, 3 * span), bf16),
            pltpu.VMEM((tokens, LANES), f32),
            pltpu.VMEM((tokens, LANES), f32),
            pltpu.VMEM((width, 3 * span), f32),
            pltpu.VMEM((span, width), f32),
            scratch_like(project),
            scratch_like(attend),
            scratch_like(normed),
            scratch_like(packed),
            scratch_like(mixed),
            pltpu.SemaphoreType.DMA((5,)),
        ]
        + comm_scratch(images, length, width),
        16 * images * 8 * length * width * span * 6,
        (
            grad_mid,
            base,
            attended,
            gate_rows,
            vecs,
            Far(project),
            Far(attend),
            key_bias,
            Far(normed),
            Far(packed),
            Far(mixed),
            log_total,
        ),
        tasks,
    )


HEAD_SIZE = 72


def pad_heads(array, axis):
    shape = array.shape
    heads = shape[axis] // HEAD_SIZE
    split = array.reshape(shape[:axis] + (heads, HEAD_SIZE) + shape[axis + 1 :])
    widths = [(0, 0)] * split.ndim
    widths[axis + 1] = (0, LANES - HEAD_SIZE)
    return jnp.pad(split, widths).reshape(shape[:axis] + (heads * LANES,) + shape[axis + 1 :])


def unpad_heads(array, axis):
    shape = array.shape
    heads = shape[axis] // LANES
    split = array.reshape(shape[:axis] + (heads, LANES) + shape[axis + 1 :])
    kept = lax.slice_in_dim(split, 0, HEAD_SIZE, axis=axis + 1)
    return kept.reshape(shape[:axis] + (heads * HEAD_SIZE,) + shape[axis + 1 :])


def turn(block, own, step, last):
    return jnp.where(block == own, step, jnp.where(block < own, 0, last))


def local_call(kernel, name, grid, in_specs, out_specs, outs, moved, args, prefetch=0):
    return pl.pallas_call(
        kernel,
        name=name,
        grid_spec=pltpu.PrefetchScalarGridSpec(
            num_scalar_prefetch=prefetch, grid=grid, in_specs=in_specs, out_specs=out_specs
        ),
        out_shape=outs,
        compiler_params=pltpu.CompilerParams(vmem_limit_bytes=56 * 2**20),
        cost_estimate=pl.CostEstimate(flops=0, bytes_accessed=moved, transcendentals=0),
    )(*args)


def mlp_unpack_kernel(*refs):
    *everys, expand, shrink = refs
    for k, every in enumerate(everys):

        @pl.when(pl.program_id(0) == k)
        def _(every=every):
            first, second = every[0, 0].astype(f32), every[1, 0].astype(f32)
            inner = first.shape[1] // 2
            expand[0] = jnp.concatenate([first[:, :inner], second[:, :inner]], axis=1)
            shrink[0] = jnp.concatenate([first[:, inner:], second[:, inner:]], axis=1)


def mlp_unpack(everys):
    depth = len(everys)
    _, _, half, pair = everys[0].shape
    shard, inner = 2 * half, pair // 2
    everys = [every.reshape(2, 4, shard, pair) for every in everys]
    block = (2, 1, shard, pair)
    return local_call(
        mlp_unpack_kernel,
        "mlp_unpack",
        (depth, 4),
        [pl.BlockSpec(block, lambda b, j, k=k: (0, turn(b, k, j, 3), 0, 0)) for k in range(depth)],
        [
            pl.BlockSpec((1, shard, 2 * inner), lambda b, j: (b, 0, j)),
            pl.BlockSpec((1, shard, 2 * inner), lambda b, j: (b, 0, j)),
        ],
        [shaped((depth, shard, 8 * inner), f32), shaped((depth, shard, 8 * inner), f32)],
        depth * shard * inner * 96,
        everys,
    )


def project_unpack_kernel(*refs):
    *everys, project = refs
    for k, every in enumerate(everys):

        @pl.when(pl.program_id(0) == k)
        def _(every=every):
            each = every.shape[-1] // 3
            parts = [
                every[d % 2, d // 2, 0].astype(f32)[:, n * each : (n + 1) * each] for n in range(3) for d in range(8)
            ]
            project[0, 0] = jnp.concatenate(parts, axis=1)


def project_unpack(everys):
    depth = len(everys)
    _, _, half, columns = everys[0].shape
    everys = [every.reshape(2, 4, 2, half, columns) for every in everys]
    (project,) = local_call(
        project_unpack_kernel,
        "project_unpack",
        (depth, 2),
        [
            pl.BlockSpec((2, 4, 1, half, columns), lambda b, j, k=k: (0, 0, turn(b, k, j, 1), 0, 0))
            for k in range(depth)
        ],
        [pl.BlockSpec((1, 1, half, 8 * columns), lambda b, j: (b, j, 0, 0))],
        [shaped((depth, 2, half, 8 * columns), f32)],
        depth * half * columns * 96,
        everys,
    )
    return project.reshape(depth, 2 * half, 8 * columns)


def attend_unpack_kernel(rank, *refs):
    *everys, attend = refs
    for k, every in enumerate(everys):

        @pl.when(pl.program_id(0) == k)
        def _(every=every):
            attend[0, 0] = every[0, 0].astype(f32)


def attend_unpack(everys, rank, shard, pieces, rows):
    depth = len(everys)
    width = everys[0].shape[-1]
    everys = [every.reshape(8, pieces, rows, width) for every in everys]
    steps = shard // rows

    def chosen(b, i, ranks, k):
        g = ranks[0] * steps + i
        d = g // pieces
        own = b == k
        return jnp.where(own, d % 2 * 4 + d // 2, 0), jnp.where(own, g % pieces, 0), 0, 0

    (attend,) = local_call(
        attend_unpack_kernel,
        "attend_unpack",
        (depth, steps),
        [pl.BlockSpec((1, 1, rows, width), partial(chosen, k=k)) for k in range(depth)],
        [pl.BlockSpec((1, 1, rows, width), lambda b, i, ranks: (b, i, 0, 0))],
        [shaped((depth, steps, rows, width), f32)],
        depth * shard * width * 6,
        [rank.reshape(1), *everys],
        1,
    )
    return attend.reshape(depth, shard, width)


def adaptive_grad_kernel(silu, mods, out):
    out[0] = dot(silu[...], mods[0], TN)


def adaptive_grad(silu, mods):
    depth, count, columns = mods.shape
    shard = silu.shape[1]
    (grad,) = local_call(
        adaptive_grad_kernel,
        "adaptive_grad",
        (depth, 3),
        [
            pl.BlockSpec((count, shard), lambda b, j: (0, 0)),
            pl.BlockSpec((1, count, columns // 3), lambda b, j: (b, 0, j)),
        ],
        [pl.BlockSpec((1, shard, columns // 3), lambda b, j: (b, 0, j))],
        [shaped((depth, shard, columns), f32)],
        depth * shard * columns * 4,
        [silu, mods],
    )
    return grad


def body(
    latents,
    conditioning,
    kept_index,
    kept_count,
    patch_weight,
    patch_bias,
    adaptive_weight,
    adaptive_bias,
    project_weight,
    project_bias,
    attend_weight,
    attend_bias,
    expand_weight,
    expand_bias,
    shrink_weight,
    shrink_bias,
    final_adaptive,
    final_offset,
    final_weight,
    final_bias,
    cotangent,
):
    rows, cols, ranks = lax.axis_size("row"), lax.axis_size("col"), lax.axis_size("batch")
    team = rows * cols
    place = lax.axis_index("row") * cols + lax.axis_index("col")
    rank = lax.axis_index("batch")
    images, channels_in = latents.shape[:2]
    channels_out = cotangent.shape[1]
    rows_tile, cols_tile = latents.shape[2] // PATCH, latents.shape[3] // PATCH
    tile_tokens = rows_tile * cols_tile
    sequence = tile_tokens * team
    width = conditioning.shape[1]
    depth = adaptive_weight.shape[0]
    shard = adaptive_weight.shape[1]
    kept_local = tile_tokens * 3 // 4
    highest = lax.Precision.HIGHEST

    head_cols = width // team
    hidden_cols = expand_weight.shape[2] // team

    def slice_of(array, axis, count):
        return lax.dynamic_slice_in_dim(array, place * count, count, axis=axis)

    piece_rows = min(shard, HEAD_SIZE)
    pieces_each = head_cols // piece_rows
    project_own = jnp.concatenate(
        [
            lax.dynamic_slice_in_dim(project_weight, part * width + place * head_cols, head_cols, axis=2)
            for part in range(3)
        ],
        axis=2,
    )
    attend_own = jnp.stack(
        [
            lax.dynamic_slice_in_dim(
                attend_weight, (place * head_cols + j * piece_rows) % shard, piece_rows, axis=1
            )
            for j in range(pieces_each)
        ],
        axis=1,
    )
    pair_own = jnp.concatenate(
        [slice_of(expand_weight, 2, hidden_cols), slice_of(shrink_weight, 1, hidden_cols).transpose(0, 2, 1)], axis=2
    )

    smalls = [
        patch_weight,
        final_weight.T,
        patch_bias[None],
        adaptive_bias,
        project_bias,
        attend_bias,
        expand_bias,
        shrink_bias,
        final_offset[None],
        conditioning,
    ]
    patch_tiles = to_tokens(latents, PATCH)
    grad_tiles = to_tokens(cotangent, PATCH)
    patch_in, patch_out = patch_tiles.shape[2], grad_tiles.shape[2]
    tiles = jnp.concatenate([patch_tiles, grad_tiles], axis=2)
    packs, every_tile = prologue(smalls, [1] * 9 + [0], tiles.reshape(-1, LANES), 8)
    (
        patch_full,
        final_turned,
        patch_bias_full,
        adaptive_offset,
        project_offset,
        attend_offset,
        expand_offset,
        shrink_offset,
        final_offset_full,
        cond_all,
    ) = packs
    patch_bias_full, final_offset_full = patch_bias_full[0], final_offset_full[0]
    final_full = final_turned.T

    whole = every_tile.reshape((rows, cols, images, rows_tile, cols_tile, -1)).transpose(2, 0, 3, 1, 4, 5)
    whole = whole.reshape(images, sequence, patch_in + patch_out)
    grid_cols = cols * cols_tile
    own_ids = lax.dynamic_index_in_dim(
        kept_index.reshape(images, tile_tokens, team), place, axis=2, keepdims=False
    )
    pick = (own_ids[:, :, None] == jnp.arange(sequence, dtype=jnp.int32)).astype(bf16)
    own = jnp.einsum("ikt,itc->ikc", pick, whole, preferred_element_type=f32).astype(bf16)
    patches, grad_outputs = own[..., :patch_in], own[..., patch_in:]
    order = jnp.arange(kept_local, dtype=jnp.int32)[:, None] * team + jnp.arange(team, dtype=jnp.int32)
    kept_grid = order[None] < kept_count[:, None, None]
    chunk_order = kept_grid.reshape(images, kept_local, team // 2, 2).transpose(0, 3, 2, 1)
    key_bias = jnp.where(chunk_order.reshape(images, team * kept_local), 0.0, masked_score).astype(f32)
    kept_rows = lax.dynamic_index_in_dim(kept_grid, place, axis=2, keepdims=False).astype(f32)[:, :, None]

    count = width // 4
    omega = 1.0 / 10000.0 ** (jnp.arange(count, dtype=f32) / count)
    angles = jnp.arange(max(rows * rows_tile, grid_cols), dtype=f32)[:, None] * omega[None, :]
    along = jnp.concatenate([jnp.sin(angles), jnp.cos(angles)], axis=1)
    places = jnp.arange(along.shape[0], dtype=jnp.int32)

    def position_of(coords):
        chosen = (coords[..., None] == places).astype(f32)
        return jnp.einsum("ikt,tc->ikc", chosen, along, precision=highest)

    position = jnp.concatenate(
        [position_of(own_ids // grid_cols), position_of(own_ids % grid_cols)], axis=-1
    )
    resid = (
        jnp.einsum("ikc,cd->ikd", patches, patch_full, preferred_element_type=f32)
        + patch_bias_full.astype(f32)
        + position
    )

    silu_all = jax.nn.silu(cond_all.astype(f32)).astype(bf16)
    silu_rows = lax.dynamic_slice_in_dim(silu_all, rank * shard, shard, axis=1)
    pair = 2 * width
    block_of = jnp.minimum(place // 3, depth - 1)
    pair_weight = lax.dynamic_slice(adaptive_weight, (block_of, 0, place % 3 * pair), (1, shard, pair))[0]
    pair_weight = jnp.where(place < 3 * depth, pair_weight, final_adaptive)
    parts = dot(silu_rows, pair_weight, NN).reshape(ranks, images * 2, width)
    mods, (project_next, attend_next) = conditioning_exchange(
        parts, 9, [Line(project_own[0]), Chain(attend_own[0], shard)]
    )
    mods = mods.reshape(team, images, 2, width).transpose(1, 0, 2, 3).reshape(images, 2 * team, width)
    offsets = [adaptive_offset.reshape(6 * depth, width), final_offset_full.reshape(2, width)]
    mods = mods[:, : 6 * depth + 2] + jnp.concatenate(offsets, axis=0).astype(f32)
    added = jnp.stack([attend_offset, shrink_offset], axis=1).reshape(2 * depth, width).astype(f32)
    vecs = jnp.concatenate([mods, jnp.broadcast_to(added, (images, 2 * depth, width))], axis=1)
    final_shift, final_scale = mods[:, 6 * depth, None], mods[:, 6 * depth + 1, None]
    head_biases = jnp.moveaxis(project_offset.astype(f32).reshape(depth, 2, team, head_cols), 2, 0)
    head_biases = lax.dynamic_index_in_dim(head_biases, place, axis=0, keepdims=False)
    head_biases = jnp.stack([head_biases[:, 0], jnp.zeros((depth, head_cols), f32), head_biases[:, 1]], axis=1)
    head_biases = pad_heads(head_biases, 2).reshape(depth, -1)
    hidden_biases = slice_of(expand_offset.astype(f32), 1, hidden_cols)

    records = []
    for b in range(depth):
        routed = b > 0
        length = kept_local if routed else tile_tokens
        base = resid
        tasks = [Line(pair_own[b])]
        (*attention_saved, attended, mid, project, attend), gathered = attention_forward(
            b,
            length,
            base,
            kept_rows,
            vecs,
            (project_next.reshape(width, -1), head_biases[b], attend_next.reshape(-1, width)),
            key_bias[:, None, :],
            4 * b,
            tasks,
        )
        mlp_weights = (gathered[0].reshape(width, 2 * hidden_cols), hidden_biases[b])
        tasks = []
        if b + 1 < depth:
            tasks = [Line(project_own[b + 1]), Chain(attend_own[b + 1], shard)]
        (*mlp_saved, expanded, after), gathered = mlp_forward(
            b, mid, kept_rows, vecs, mlp_weights, 4 * b + 1, tasks
        )
        if tasks:
            project_next, attend_next = gathered
        records.append((base, mid, attended, expanded, (project, attend), mlp_weights, attention_saved, mlp_saved))
        resid = jnp.concatenate([after, resid[:, kept_local:]], axis=1) if routed else after

    final_normed = modulate(resid, final_shift, final_scale).astype(bf16)
    outputs = jnp.einsum("ikd,dc->cik", final_normed, final_full, preferred_element_type=f32)
    outputs = outputs + final_bias.astype(f32)[:, None, None]
    final_bias_term = jnp.sum(grad_outputs.astype(f32), axis=(0, 1))
    final_weight_term = jnp.einsum("ikd,ikc->cd", final_normed, grad_outputs, preferred_element_type=f32)
    grad_final = jnp.einsum("ikc,dc->ikd", grad_outputs, final_full, preferred_element_type=f32)
    grad_resid, grad_final_shift, grad_final_scale = modulate_back(resid, final_scale, grad_final)
    final_mod_term = jnp.stack([grad_final_shift, grad_final_scale], axis=1)

    block_sums, block_biases = [], []
    spread = [[None, None, None] for _ in range(depth)]

    def folded(source, inbox):
        own = lax.dynamic_index_in_dim(source, rank, axis=0, keepdims=False)
        return (own.astype(f32) + jnp.sum(inbox.astype(f32), axis=0)).astype(bf16)

    def fold_project(term, inbox):
        return folded(term, inbox).reshape(2, shard // 2, -1)

    def fold_attend(term, inbox):
        total = term.astype(f32) + jnp.sum(inbox.astype(f32), axis=1)
        return total.astype(bf16).reshape(2, head_cols // 2, width)

    attend_shape = (pieces_each, piece_rows, width)
    project_term = None
    for b in reversed(range(depth)):
        base, mid, attended, expanded, attention_weights, mlp_weights, attention_saved, mlp_saved = records[b]
        routed = b > 0
        tasks = []
        if project_term is not None:
            tasks = [Fold(project_term), FoldTo(attend_shape, shard, 0, grad_attend)]
        (grad_mid, mlp_sums, grad_pair, grad_expand_bias), inboxes = mlp_backward(
            b, grad_resid, mid, expanded, kept_rows, vecs, mlp_weights, mlp_saved, 4 * b + 2, tasks
        )
        mlp_term = grad_pair.reshape(ranks, shard, 2 * hidden_cols)
        waiting = []
        early = b == 0
        tasks = [Fold(mlp_term)] + ([FoldTo(attend_shape, shard, 2)] if early else [])
        if project_term is not None:
            waiting = [
                (b + 1, 0, mlp_part),
                (b + 1, 1, fold_project(project_term, inboxes[0])),
                (b + 1, 2, fold_attend(grad_attend, inboxes[1])),
            ]
        folds = len(tasks)
        tasks += [PlaneGather(part, plan) for (_, _, part), plan in zip(waiting, ((1, 3), (3, 5), (5,)))]
        (grad_base, attention_sums, grad_project, grad_attend, grad_project_bias), inboxes = attention_backward(
            b,
            attend_shape,
            grad_mid,
            base,
            attended,
            kept_rows,
            vecs,
            attention_weights,
            key_bias[:, :, None],
            attention_saved,
            4 * b + 3,
            tasks,
        )
        for (block, n, _), every in zip(waiting, inboxes[folds:]):
            spread[block][n] = every
        mlp_part = folded(mlp_term, inboxes[0]).reshape(2, shard // 2, -1)
        if early:
            waiting = [(b, 0, mlp_part), (b, 2, fold_attend(grad_attend, inboxes[1]))]
        project_term = grad_project.reshape(ranks, shard, 3 * head_cols)
        block_sums = [attention_sums, mlp_sums] + block_sums
        block_biases = [grad_project_bias, grad_expand_bias] + block_biases
        grad_resid = jnp.concatenate([grad_base, grad_resid[:, kept_local:]], axis=1) if routed else grad_base

    patch_bias_term = jnp.sum(grad_resid, axis=(0, 1))
    grad_embed = grad_resid.astype(bf16)
    patch_term = jnp.einsum("ikc,ikd->cd", patches, grad_embed, preferred_element_type=f32)
    grad_patches = jnp.einsum("ikd,cd->cik", grad_embed, patch_full, preferred_element_type=f32)

    edge_rows = jnp.stack([patch_bias_term, jnp.pad(final_bias_term, (0, width - patch_out))])
    tokens_out = jnp.concatenate([outputs, grad_patches], axis=0).reshape(2, (patch_out + patch_in) // 2, -1)
    tasks = [Fold(project_term, late=1)] + [PlaneGather(part, (0, 2)) for _, _, part in waiting]
    (all_mods, all_rows, all_tokens), inboxes = epilogue(
        block_sums,
        final_mod_term,
        block_biases,
        patch_term,
        final_weight_term,
        edge_rows,
        tokens_out,
        10,
        tasks,
    )
    for (block, n, _), every in zip(waiting, inboxes[1:]):
        spread[block][n] = every
    last_part = fold_project(project_term, inboxes[0])

    mod_every = all_mods.reshape(team, ranks * images, pair)
    mod_width = 3 * pair
    block_mods = jnp.stack(
        [mod_every[3 * b : 3 * b + 3].transpose(1, 0, 2).reshape(ranks * images, mod_width) for b in range(depth)]
    )
    final_mods = mod_every[3 * depth]
    grad_silu = dot(final_mods, final_adaptive, NT)
    for b in range(depth):
        grad_silu = grad_silu + dot(block_mods[b], adaptive_weight[b], NT)
    grad_silu, last = closing(
        grad_silu.reshape(ranks, images, shard), 11, [PlaneGather(last_part)]
    )
    spread[0][1] = last[0]
    grad_silu = grad_silu.transpose(1, 0, 2).reshape(images, width)
    conditioning_grad = jax.vjp(jax.nn.silu, conditioning.astype(f32))[1](grad_silu)[0]
    adaptive_weight_grad = adaptive_grad(silu_rows, block_mods)
    final_adaptive_grad = dot(silu_rows, final_mods, TN)

    def rank_part(full):
        part = full.shape[-1] // ranks
        return lax.dynamic_slice_in_dim(full, rank * part, part, axis=full.ndim - 1)

    adaptive_bias_grad = rank_part(jnp.sum(block_mods.astype(f32), axis=1))
    final_offset_grad = rank_part(jnp.sum(final_mods.astype(f32), axis=0))

    def in_order(every):
        split = every.reshape((2, team // 2) + every.shape[1:])
        return jnp.swapaxes(split, 0, 1).reshape(every.shape)

    ordered = in_order(all_tokens).reshape(team, patch_out + patch_in, images, tile_tokens)
    ordered = ordered.transpose(2, 3, 0, 1).reshape(images, sequence, patch_out + patch_in)
    tile_rows = lax.axis_index("row") * rows_tile + jnp.arange(rows_tile, dtype=jnp.int32)
    tile_cols = lax.axis_index("col") * cols_tile + jnp.arange(cols_tile, dtype=jnp.int32)
    tile_ids = (tile_rows[:, None] * grid_cols + tile_cols).reshape(-1)
    back = (kept_index[:, None, :] == tile_ids[None, :, None]).astype(f32)
    tile_out = jnp.einsum("itj,ijc->itc", back, ordered, precision=highest)
    prediction = to_planes(tile_out[..., :patch_out], PATCH, channels_out, rows_tile, cols_tile)
    latent_grad = to_planes(tile_out[..., patch_out:], PATCH, channels_in, rows_tile, cols_tile)

    expand_weight_grad, shrink_weight_grad = mlp_unpack([parts[0] for parts in spread])
    project_weight_grad = project_unpack([parts[1] for parts in spread])
    attend_weight_grad = attend_unpack([parts[2] for parts in spread], rank, shard, pieces_each, piece_rows)

    first = patch_in + patch_out
    each = -(-(first + 2 + 2 * depth) // team)
    all_sums = all_rows[:, 0, :each].reshape(-1, width)
    all_biases = in_order(all_rows[:, 1])
    sums = lax.dynamic_slice_in_dim(all_sums, rank * shard, shard, axis=1)
    token_sums = sums[first + 2 : first + 2 + 2 * depth].reshape(depth, 2, shard)
    final_bias_grad = all_sums[first + 1, :patch_out]
    rows_of = all_biases.transpose(1, 0, 2)[: 2 * depth].reshape(depth, 2, team, -1)
    expand_bias_grad = rows_of[:, 1, :, :hidden_cols].reshape(depth, -1)
    head_rows = rows_of[:, 0, :, : 3 * head_cols // HEAD_SIZE * LANES]
    head_rows = unpad_heads(head_rows.reshape(depth, team, 3, -1), 3)
    project_bias_grad = jnp.stack([head_rows[:, :, 0], head_rows[:, :, 2]], axis=1).reshape(depth, -1)

    return (
        prediction,
        latent_grad,
        conditioning_grad,
        sums[:patch_in],
        sums[first],
        adaptive_weight_grad,
        adaptive_bias_grad,
        project_weight_grad,
        rank_part(project_bias_grad),
        attend_weight_grad,
        token_sums[:, 0],
        expand_weight_grad,
        rank_part(expand_bias_grad),
        shrink_weight_grad.transpose(0, 2, 1),
        token_sums[:, 1],
        final_adaptive_grad,
        final_offset_grad,
        sums[patch_in:first].T,
        final_bias_grad,
    )


def solution(mesh):
    tokens = P("batch", None, "row", "col")
    placed = (
        tokens,
        P("batch", None),
        P("batch", None),
        P("batch"),
        P(None, "batch"),
        P("batch"),
        P(None, "batch", None),
        P(None, "batch"),
        P(None, "batch", None),
        P(None, "batch"),
        P(None, "batch", None),
        P(None, "batch"),
        P(None, "batch", None),
        P(None, "batch"),
        P(None, None, "batch"),
        P(None, "batch"),
        P("batch", None),
        P("batch"),
        P("batch", None),
        P(),
        tokens,
    )
    return jax.shard_map(
        body,
        mesh=mesh,
        in_specs=placed,
        out_specs=(tokens, tokens, P("batch", None)) + placed[4:16] + (placed[16], P("batch"), P("batch", None), P()),
        check_vma=False,
    )
```

```python
from functools import partial

import jax
import jax.numpy as jnp
from jax import lax
from jax.experimental import pallas as pl
from jax.experimental.pallas import tpu as pltpu
from jax.sharding import PartitionSpec as P

HEADS = 16
PATCH = 2
LANES = 128
PLANE = ("row", "col")

norm_epsilon = 1e-06
masked_score = -1e30
f32 = jnp.float32
bf16 = jnp.bfloat16


def to_tokens(planes, patch_side):
    images, channels, height, breadth = planes.shape
    shaped = planes.reshape(
        images, channels, height // patch_side, patch_side, breadth // patch_side, patch_side
    )
    return shaped.transpose(0, 2, 4, 3, 5, 1).reshape(
        images, height // patch_side * (breadth // patch_side), patch_side * patch_side * channels
    )


def to_planes(token_rows, patch_side, channels, rows_tile, cols_tile):
    images = token_rows.shape[0]
    shaped = token_rows.reshape(images, rows_tile, cols_tile, patch_side, patch_side, channels)
    return shaped.transpose(0, 5, 1, 3, 2, 4).reshape(
        images, channels, rows_tile * patch_side, cols_tile * patch_side
    )


def dot(left, right, dims, precision=None):
    return lax.dot_general(left, right, (dims, ((), ())), precision=precision, preferred_element_type=f32)


def norm_parts(resid):
    centered = resid - jnp.mean(resid, axis=-1, keepdims=True)
    rstd = lax.rsqrt(jnp.mean(centered * centered, axis=-1, keepdims=True) + norm_epsilon)
    return centered * rstd, rstd


def modulate(resid, shift_part, scale_part):
    return norm_parts(resid)[0] * (1.0 + scale_part) + shift_part


def modulate_back(resid, scale_part, grad):
    unit, rstd = norm_parts(resid)
    inner = grad * (1.0 + scale_part)
    grad_in = rstd * (
        inner
        - jnp.mean(inner, axis=-1, keepdims=True)
        - unit * jnp.mean(inner * unit, axis=-1, keepdims=True)
    )
    return grad_in, jnp.sum(grad, axis=1), jnp.sum(grad * unit, axis=1)


def sides():
    row, col = lax.axis_index("row"), lax.axis_index("col")
    core = lax.rem(col, 2)
    across = col // 2
    chip = row * 2 + across
    chips = {
        "own": chip,
        "x": (1 - row) * 2 + across,
        "y": row * 2 + 1 - across,
        "far": (1 - row) * 2 + 1 - across,
    }
    address = {
        "x": {"row": 1 - row},
        "y": {"col": lax.rem(col + 2, 4)},
        "core": {"col": col + 1 - 2 * core},
    }
    return core, chips, address


def greet(addresses):
    barrier = pltpu.get_barrier_semaphore()
    for who in addresses:
        pl.semaphore_signal(barrier, inc=1, device_id=who, device_id_type=pl.DeviceIdType.MESH)
    pl.semaphore_wait(barrier, len(addresses))


def remote(source, target, send, recv, who):
    return pltpu.make_async_remote_copy(
        src_ref=source,
        dst_ref=target,
        send_sem=send,
        recv_sem=recv,
        device_id=who,
        device_id_type=pl.DeviceIdType.MESH,
    )


def rank_at(offset):
    ranks = lax.axis_size("batch")
    return {"batch": lax.rem(lax.axis_index("batch") + offset + ranks, ranks)}


def other_ranks():
    return [rank_at(offset) for offset in range(1, lax.axis_size("batch"))]


def plane_peers():
    row, col = lax.axis_index("row"), lax.axis_index("col")
    rows, cols = lax.axis_size("row"), lax.axis_size("col")
    return [
        {"row": lax.rem(row + n // cols, rows), "col": lax.rem(col + n % cols, cols)}
        for n in range(1, rows * cols)
    ]


class Line:
    reach = 1

    def __init__(self, source):
        ranks = lax.axis_size("batch")
        self.ins = [source]
        self.outs = [jax.ShapeDtypeStruct((ranks,) + source.shape, source.dtype)]
        self.sems = [(2, ranks - 1), (2, ranks - 1), (1,)]

    def bind(self, ins, outs, sems):
        (self.source,), (self.target,) = ins, outs
        self.send, self.recv, self.own = sems
        self.rank, self.ranks = lax.axis_index("batch"), lax.axis_size("batch")
        self.steps = self.ranks
        self.late = 0

    def copy(self, way, r):
        block = self.rank - r if way == 0 else self.rank + r
        source = self.source if r == 0 else self.target.at[block]
        return remote(
            source, self.target.at[block], self.send.at[way, r], self.recv.at[way, r], rank_at(1 - 2 * way)
        )

    def holds(self, way, r):
        return self.rank >= r if way == 0 else self.rank + r < self.ranks

    def sends(self, way, r):
        edge = self.rank + 1 < self.ranks if way == 0 else self.rank > 0
        return jnp.logical_and(self.holds(way, r), edge)

    def step(self, r):
        for way in (0, 1):
            if r > 0:
                block = self.rank - r if way == 0 else self.rank + r

                @pl.when(self.holds(way, r))
                def _(way=way, block=block):
                    place = self.target.at[block]
                    remote(place, place, self.send.at[way, r - 1], self.recv.at[way, r - 1], rank_at(1)).wait_recv()

            if r < self.ranks - 1:

                @pl.when(self.sends(way, r))
                def _(way=way):
                    self.copy(way, r).start()

        if r == 0:
            self.stay().start()

    def stay(self):
        return pltpu.make_async_copy(self.source, self.target.at[self.rank], self.own.at[0])

    def finish(self):
        for way in (0, 1):
            for r in range(self.ranks - 1):

                @pl.when(self.sends(way, r))
                def _(way=way, r=r):
                    self.copy(way, r).wait_send()

        self.stay().wait()


class Chain:
    reach = 1

    def __init__(self, source, shard):
        pieces, self.rows, _ = source.shape
        self.shard = shard
        self.ins = [source]
        self.outs = [jax.ShapeDtypeStruct(source.shape, source.dtype)]
        self.sems = [(pieces, 2), (pieces, 2), (pieces,)]

    def bind(self, ins, outs, sems):
        (self.source,), (self.target,) = ins, outs
        self.send, self.recv, self.own = sems
        self.rank, self.ranks = lax.axis_index("batch"), lax.axis_size("batch")
        self.steps = self.ranks
        self.late = 0
        self.owners = owners_of(self.source.shape[0], self.rows, self.shard)

    def copy(self, j, way, first):
        source = self.source.at[j] if first else self.target.at[j]
        return remote(
            source, self.target.at[j], self.send.at[j, way], self.recv.at[j, way], rank_at(1 - 2 * way)
        )

    def edge(self, way):
        return self.rank + 1 < self.ranks if way == 0 else self.rank > 0

    def step(self, r):
        for j, owner in enumerate(self.owners):
            for way in (0, 1):
                away = self.rank - owner if way == 0 else owner - self.rank
                if r > 0:

                    @pl.when(away == r)
                    def _(j=j, way=way):
                        self.copy(j, way, False).wait_recv()

                @pl.when(jnp.logical_and(away == r, self.edge(way)))
                def _(j=j, way=way):
                    self.copy(j, way, r == 0).start()

            if r == 0:

                @pl.when(self.rank == owner)
                def _(j=j):
                    self.stay(j).start()

    def stay(self, j):
        return pltpu.make_async_copy(self.source.at[j], self.target.at[j], self.own.at[j])

    def finish(self):
        for j, owner in enumerate(self.owners):
            for way in (0, 1):
                away = self.rank - owner if way == 0 else owner - self.rank

                @pl.when(jnp.logical_and(away >= 0, self.edge(way)))
                def _(j=j, way=way):
                    self.copy(j, way, False).wait_send()

            @pl.when(self.rank == owner)
            def _(j=j):
                self.stay(j).wait()


def team_place():
    return lax.axis_index("row") * lax.axis_size("col") + lax.axis_index("col")


def owners_of(pieces, rows, shard):
    place = team_place()
    return [(place * pieces + j) * rows // shard for j in range(pieces)]


class Fold:
    reach = 2

    def __init__(self, source, late=0):
        ranks = lax.axis_size("batch")
        self.ins = [source]
        self.late = late
        self.outs = [jax.ShapeDtypeStruct((ranks - 1,) + source.shape[1:], source.dtype)]
        self.sems = [(ranks - 1,), (ranks - 1,)]

    def bind(self, ins, outs, sems):
        (self.source,), (self.inbox,) = ins, outs
        self.send, self.recv = sems
        self.steps = 1

    def copies(self):
        for n in range(lax.axis_size("batch") - 1):
            who = rank_at(n + 1)
            yield remote(
                self.source.at[who["batch"]], self.inbox.at[n], self.send.at[n], self.recv.at[n], who
            )

    def step(self, r):
        for copy in self.copies():
            copy.start()

    def finish(self):
        for copy in self.copies():
            copy.wait()


class FoldTo:
    reach = 2

    def __init__(self, shape, shard, late, source=None):
        pieces, self.rows, width = shape
        others = lax.axis_size("batch") - 1
        self.shard = shard
        self.ins = [] if source is None else [source]
        self.outs = [jax.ShapeDtypeStruct((pieces, others, self.rows, width), bf16)]
        self.sems = [(pieces, others), (pieces, others)]
        self.late, self.pieces = late, pieces

    def bind(self, ins, outs, sems):
        (self.inbox,) = outs
        self.source = ins[0] if ins else None
        self.send, self.recv = sems
        self.steps = 1
        self.rank, self.others = lax.axis_index("batch"), lax.axis_size("batch") - 1
        self.owners = owners_of(self.pieces, self.rows, self.shard)

    def copy(self, j, n):
        return remote(
            self.source.at[j], self.inbox.at[j, n], self.send.at[j, n], self.recv.at[j, n], rank_at(n + 1)
        )

    def leads(self, j, n):
        return rank_at(n + 1)["batch"] == self.owners[j]

    def step(self, r):
        for j in range(len(self.owners)):
            for n in range(self.others):

                @pl.when(self.leads(j, n))
                def _(j=j, n=n):
                    self.copy(j, n).start()

    def finish(self):
        for j, owner in enumerate(self.owners):
            for n in range(self.others):

                @pl.when(self.rank == owner)
                def _(j=j, n=n):
                    self.copy(j, n).wait_recv()

                @pl.when(self.leads(j, n))
                def _(j=j, n=n):
                    self.copy(j, n).wait_send()


class Copies:
    def __init__(self, send, recv, address):
        self.send, self.recv, self.address = send, recv, address
        self.started = {}

    def go(self, slot, source, target, who):
        copy = remote(source, target, self.send.at[slot], self.recv.at[slot], self.address[who])
        copy.start()
        self.started[slot] = copy

    def arrived(self, *slots):
        for slot in slots:
            self.started[slot].wait_recv()

    def drain(self):
        for copy in self.started.values():
            copy.wait_send()


class Gather(Copies):
    def __init__(self, full, send, recv, place):
        core, chips, address = place
        super().__init__(send, recv, address)
        self.full, self.half = full, full.shape[1] // 2
        self.source = None
        self.at = {name: core * 4 + chip for name, chip in chips.items()}

    def whole(self, name):
        return self.full.at[self.at[name]]

    def part(self, name, second):
        return self.full.at[self.at[name], pl.ds(self.half * second, self.half)]

    def first(self):
        own = self.whole("own")
        source = own if self.source is None else self.source
        parts = [pl.ds(0, self.half), pl.ds(self.half, self.half)]
        for slot, part, who in ((0, 0, "x"), (1, 1, "y"), (8, 1, "x"), (9, 0, "y")):
            self.go(slot, source.at[parts[part]], self.part("own", part), who)
        self.go(2, source, own, "core")

    def second(self):
        self.arrived(0)
        self.go(3, self.part("x", 0), self.part("x", 0), "y")
        self.arrived(1)
        self.go(4, self.part("y", 1), self.part("y", 1), "x")
        self.arrived(8)
        self.go(5, self.whole("x"), self.whole("x"), "core")
        self.arrived(9)
        self.go(6, self.whole("y"), self.whole("y"), "core")

    def finish(self):
        self.arrived(3, 4)
        self.go(7, self.whole("far"), self.whole("far"), "core")
        self.arrived(2, 5, 6, 7)


class PlaneGather:
    reach = 0

    def __init__(self, source, plan=(0, 1, 2)):
        self.ins = [source]
        self.plan = plan
        self.outs = [jax.ShapeDtypeStruct((8,) + source.shape, source.dtype)]
        self.sems = [(10,), (10,), (1,)]
        self.late = 0

    def bind(self, ins, outs, sems):
        (self.source,), (self.target,) = ins, outs
        send, recv, self.own = sems
        self.gather = Gather(self.target, send, recv, sides())
        self.gather.source = self.source
        self.steps = 3

    def stay(self):
        return pltpu.make_async_copy(self.source, self.gather.whole("own"), self.own.at[0])

    def step(self, r):
        if r == 0:
            self.gather.first()
            self.stay().start()
        elif r == 1:
            self.gather.second()
        else:
            self.gather.finish()

    def finish(self):
        self.gather.drain()
        self.stay().wait()


class Background:
    def __init__(self, tasks):
        self.tasks = tasks
        self.now = 0
        self.done = [[] for _ in tasks]

    def partners(self):
        reach = max([task.reach for task in self.tasks], default=0)
        return [[], [rank_at(1), rank_at(-1)], other_ranks()][reach]

    def tick(self):
        for task, done in zip(self.tasks, self.done):
            plan = getattr(task, "plan", None) or range(task.late, task.late + task.steps)
            if len(done) < task.steps and len(done) < len(plan) and plan[len(done)] <= self.now:
                task.step(len(done))
                done.append(self.now)
        self.now += 1

    def finish(self):
        for most in range(max([task.steps for task in self.tasks], default=0)):
            for task, done in zip(self.tasks, self.done):
                if len(done) == most and most < task.steps:
                    task.step(most)
                    done.append(self.now)
        for task in self.tasks:
            task.finish()


class Scatter(Copies):
    def __init__(self, core_out, core_in, total, hop_out, hop_in, send, recv, place):
        _, self.chips, address = place
        super().__init__(send, recv, address)
        self.core_out, self.core_in, self.total = core_out, core_in, total
        self.hop_out, self.hop_in = hop_out, hop_in
        self.half = total.shape[1] // 2

    def cross(self):
        self.go(0, self.core_out, self.core_in, "core")

    def hop(self, slot, value, who):
        self.hop_out[slot] = value.astype(bf16)
        self.go(1 + slot, self.hop_out.at[slot], self.hop_in.at[slot], who)

    def first(self):
        self.arrived(0)
        half = self.half

        def summed(name):
            chip = self.chips[name]
            return self.total[chip] + self.core_in[chip].astype(f32)

        far = summed("far")
        self.hop(0, far[:half], "x")
        self.hop(2, far[half:], "y")
        x_sum = summed("x")
        self.hop(1, x_sum[:half], "x")
        self.total[self.chips["x"], half:] = x_sum[half:]
        y_sum = summed("y")
        self.hop(3, y_sum[half:], "y")
        self.total[self.chips["y"], :half] = y_sum[:half]

    def second(self):
        half = self.half
        self.arrived(1)
        self.hop(4, self.total[self.chips["y"], :half] + self.hop_in[0].astype(f32), "y")
        self.arrived(3)
        self.hop(5, self.total[self.chips["x"], half:] + self.hop_in[2].astype(f32), "x")

    def finish(self):
        self.arrived(2, 4, 5, 6)
        half, own = self.half, self.chips["own"]
        base = self.total[own] + self.core_in[own].astype(f32)
        low = base[:half] + self.hop_in[1].astype(f32) + self.hop_in[4].astype(f32)
        high = base[half:] + self.hop_in[3].astype(f32) + self.hop_in[5].astype(f32)
        return jnp.concatenate([low, high], axis=0)


def comm_scratch(images, length, width):
    half = length // 2
    return [
        pltpu.VMEM((images, 4, length, width), bf16),
        pltpu.VMEM((images, 4, length, width), bf16),
        pltpu.VMEM((images, 4, length, width), f32),
        pltpu.VMEM((images, 6, half, width), bf16),
        pltpu.VMEM((images, 6, half, width), bf16),
        pltpu.SemaphoreType.DMA((images, 10)),
        pltpu.SemaphoreType.DMA((images, 10)),
        pltpu.SemaphoreType.DMA((images, 7)),
        pltpu.SemaphoreType.DMA((images, 7)),
    ]


def exchanges(full, comm, place):
    core_out, core_in, total, hop_out, hop_in, gs, gr, ss, sr = comm
    images = full.shape[0]
    gathers = [Gather(full.at[i], gs.at[i], gr.at[i], place) for i in range(images)]
    scatters = [
        Scatter(
            core_out.at[i], core_in.at[i], total.at[i], hop_out.at[i], hop_in.at[i], ss.at[i], sr.at[i], place
        )
        for i in range(images)
    ]
    return gathers, scatters


def flat(value):
    return value.reshape(value.shape[0] * value.shape[1], value.shape[2])


def halves(core):
    return ((1 - core) * 4, True), (core * 4, False)


def keep_partial(partial, scatter, sibling):
    shape = scatter.total.shape
    if sibling:
        scatter.core_out[...] = partial.astype(bf16).reshape(shape)
        scatter.cross()
    else:
        scatter.total[...] = partial.reshape(shape)


def column_sum(value):
    return jnp.sum(value, axis=0, keepdims=True)


def row_sums(value):
    ones = jnp.ones((8, value.shape[0]), bf16)
    return dot(ones, value, ((1,), (0,)))


GELU_ROOT = 0.7978845608028654
GELU_CUBE = 0.044715
NN, NT, TN = ((1,), (0,)), ((1,), (1,)), ((0,), (0,))


def gelu(hidden):
    inner = GELU_ROOT * (hidden + GELU_CUBE * (hidden * hidden * hidden))
    return 0.5 * hidden * (1.0 + jnp.tanh(inner))


def gelu_with_slope(hidden):
    square = hidden * hidden
    bend = jnp.tanh(GELU_ROOT * hidden * (1.0 + GELU_CUBE * square))
    rise = 0.5 * (1.0 + bend)
    slope = rise + 0.5 * hidden * (1.0 - bend * bend) * (GELU_ROOT + 3.0 * GELU_ROOT * GELU_CUBE * square)
    return hidden * rise, slope


def modulate_back_rows(resid, scale_part, grad):
    unit, rstd = norm_parts(resid)
    inner = grad * (1.0 + scale_part)
    grad_in = rstd * (
        inner
        - jnp.mean(inner, axis=-1, keepdims=True)
        - unit * jnp.mean(inner * unit, axis=-1, keepdims=True)
    )
    return grad_in, column_sum(grad), column_sum(grad * unit)


class Far:
    def __init__(self, what):
        self.what = what


class Copying:
    def __init__(self, sems):
        self.sems = sems
        self.open = {}

    def start(self, name, source, target):
        copy = pltpu.make_async_copy(source, target, self.sems.at[len(self.open)])
        copy.start()
        self.open[name] = copy

    def wait(self, *names):
        for name in names:
            self.open[name].wait()


def scratch_like(array):
    return pltpu.VMEM(array.shape, array.dtype)


def call(kernel, name, ident, outs, scratch, flops, args, tasks=()):
    vmem, anywhere = pl.BlockSpec(memory_space=pltpu.VMEM), pl.BlockSpec(memory_space=pl.ANY)
    in_specs = [anywhere if isinstance(a, Far) else vmem for a in args]
    out_specs = [anywhere if isinstance(o, Far) else vmem for o in outs]
    args = [a.what if isinstance(a, Far) else a for a in args]
    outs = [o.what if isinstance(o, Far) else o for o in outs]
    moved = sum(a.size * a.dtype.itemsize for a in args) + sum(o.size * o.dtype.itemsize for o in outs)
    task_ins = [array for task in tasks for array in task.ins]
    task_outs = [shape for task in tasks for shape in task.outs]
    task_sems = [pltpu.SemaphoreType.DMA(shape) for task in tasks for shape in task.sems]

    def run(*refs):
        refs = list(refs)

        def take(count):
            taken = refs[:count]
            del refs[:count]
            return taken

        main_ins, bound_ins = take(len(args)), take(len(task_ins))
        main_outs, bound_outs = take(len(outs)), take(len(task_outs))
        main_scratch = take(len(scratch))
        for task in tasks:
            ins = [bound_ins.pop(0) for _ in task.ins]
            results = [bound_outs.pop(0) for _ in task.outs]
            task.bind(ins, results, take(len(task.sems)))
        kernel(Background(tasks), *main_ins, *main_outs, *main_scratch)

    results = pl.pallas_call(
        run,
        name=name,
        out_shape=list(outs) + task_outs,
        in_specs=in_specs + [anywhere] * len(task_ins),
        out_specs=out_specs + [anywhere] * len(task_outs),
        scratch_shapes=list(scratch) + task_sems,
        compiler_params=pltpu.CompilerParams(
            collective_id=ident, has_side_effects=True, vmem_limit_bytes=60 * 2**20
        ),
        cost_estimate=pl.CostEstimate(flops=flops, bytes_accessed=moved, transcendentals=0),
    )(*args, *task_ins)
    return results[: len(outs)], results[len(outs) :]


def shaped(shape, kind):
    return jax.ShapeDtypeStruct(shape, kind)


def prologue_kernel(background, *refs):
    smalls = refs[:-21]
    (
        cond, pair_weight, tiles, packs, every_tile, silu_rows, mods,
        pack, cond_in, parts, parts_in, zs, zr, ps, pr, cs, cr, qs, qr, ms, mr,
    ) = refs[-21:]
    lanes = pack.shape[1]
    rows = []
    for small in smalls:
        value = small[...].astype(f32)
        rows += [value[:, start : start + lanes] for start in range(0, value.shape[1], lanes)]
    used = sum(value.shape[0] for value in rows)
    if used < pack.shape[0]:
        rows.append(jnp.zeros((pack.shape[0] - used, lanes), f32))
    pack[...] = jnp.concatenate(rows, axis=0).astype(bf16)
    ranks, peers = other_ranks(), plane_peers()
    greet(ranks + peers)
    rank, place = lax.axis_index("batch"), team_place()
    first = [remote(cond.at[who["batch"]], cond_in.at[rank], cs.at[n], cr.at[n], who) for n, who in enumerate(ranks)]
    copies = [remote(pack, packs.at[rank], zs.at[n], zr.at[n], who) for n, who in enumerate(ranks)]
    for n, who in enumerate(peers):
        copies.append(remote(tiles, every_tile.at[place], ps.at[n], pr.at[n], who))
    for copy in first + copies:
        copy.start()
    cond_in[rank] = cond[rank]
    packs[rank] = pack[...]
    every_tile[place] = tiles[...]
    for copy in first:
        copy.wait()

    count, images, width = cond_in.shape[0], cond_in.shape[1], parts.shape[2]
    value = jnp.concatenate([cond_in[z].astype(f32) for z in range(count)], axis=0)
    low = (value / (1.0 + jnp.exp(-value))).astype(bf16)
    silu_rows[...] = low
    value = dot(low, pair_weight[...], NN)
    for z in range(count):
        for i in range(images):
            n = z * images + i
            for p in range(2):
                parts[z, i * 2 + p] = value[n, p * width : (p + 1) * width]
    second = [
        remote(parts.at[who["batch"]], parts_in.at[n], qs.at[n], qr.at[n], who) for n, who in enumerate(ranks)
    ]
    for copy in second:
        copy.start()
    background.tick()
    total = parts[rank]
    for n, copy in enumerate(second):
        copy.wait()
        total = total + parts_in[n]
    mods[place] = total
    third = [
        remote(mods.at[place], mods.at[place], ms.at[n], mr.at[n], who) for n, who in enumerate(peers)
    ]
    for copy in third:
        copy.start()
    background.tick()
    for copy in copies + third:
        copy.wait()
    background.finish()


def prologue(smalls, dims, cond, pair_weight, tiles, ident, tasks):
    ranks, images, _ = cond.shape
    dma = pltpu.SemaphoreType.DMA
    lanes = min(small.shape[1] for small in smalls)
    rows = sum(small.size // lanes for small in smalls)
    pack = (rows + -rows % 16, lanes)
    width = pair_weight.shape[1] // 2
    part = (2 * images, width)
    others = [dma((ranks - 1,)), dma((ranks - 1,))]
    seven = [dma((7,)), dma((7,))]
    (packs, every_tile, silu_rows, mods), gathered = call(
        prologue_kernel,
        "prologue",
        ident,
        [
            shaped((ranks,) + pack, bf16),
            shaped((8,) + tiles.shape, tiles.dtype),
            shaped((ranks * images, cond.shape[2]), bf16),
            shaped((8,) + part, f32),
        ],
        [
            pltpu.VMEM(pack, bf16),
            pltpu.VMEM(cond.shape, bf16),
            pltpu.VMEM((ranks,) + part, f32),
            pltpu.VMEM((ranks - 1,) + part, f32),
        ]
        + others
        + seven
        + others
        + others
        + seven,
        0,
        (*smalls, cond, pair_weight, tiles),
        tasks,
    )
    parts, start = [], 0
    for small, dim in zip(smalls, dims):
        count, each = small.shape[0], small.shape[1] // lanes
        part = packs[:, start : start + count * each].reshape(ranks, each, count, lanes)
        start += count * each
        if dim == 0:
            parts.append(part.transpose(0, 2, 1, 3).reshape(ranks * count, -1))
        else:
            parts.append(part.transpose(2, 0, 1, 3).reshape(count, -1))
    return parts, every_tile, silu_rows, mods, gathered


def epilogue_kernel(
    depth, background, *refs,
):
    refs = list(refs)

    def take(count):
        taken = refs[:count]
        del refs[:count]
        return taken

    block_sums, (final_sums,) = take(2 * depth), take(1)
    block_biases = take(2 * depth)
    patch_term, final_term, edge_rows, tokens = take(4)
    all_mods, all_rows, all_tokens = take(3)
    mods, sums, biases, mods_in, sums_in, rank_mods, rank_sums, rank_biases_in, ps, pr, zs, zr, qs, qr = refs
    ranks, peers = other_ranks(), plane_peers()
    rank = lax.axis_index("batch")
    around = sides()
    place = around[0] * 4 + around[1]["own"]
    gather_tokens, gather_mods, gather_rows = [
        Gather(full, qs.at[n], qr.at[n], around) for n, full in enumerate((all_tokens, all_mods, all_rows))
    ]
    images = final_sums.shape[0]
    each = sums.shape[1]

    mods[...] = jnp.zeros_like(mods)
    sums[...] = jnp.zeros_like(sums)
    biases[...] = jnp.zeros_like(biases)
    for i in range(images):
        for b in range(depth):
            for p in range(6):
                n = 6 * b + p
                source = block_sums[2 * b + p // 3]
                mods[n // 2, i * 2 + n % 2] = source[i, p % 3]
        for p in range(2):
            n = 6 * depth + p
            mods[n // 2, i * 2 + n % 2] = final_sums[i, p]
    rows = [patch_term[n] for n in range(patch_term.shape[0])]
    rows += [final_term[n] for n in range(final_term.shape[0])]
    rows += [edge_rows[n] for n in range(edge_rows.shape[0])]
    for source in block_sums:
        total = source[0, 3]
        for i in range(1, images):
            total = total + source[i, 3]
        rows.append(total)
    for n, row in enumerate(rows):
        sums[n // each, n % each] = row
    for n, source in enumerate(block_biases):
        biases[n, : source.shape[1]] = source[0]

    greet(ranks + peers)
    first = []
    for n, who in enumerate(peers):
        there = lax.rem(who["col"], 2) * 4 + who["row"] * 2 + who["col"] // 2
        first.append(remote(mods.at[there], mods_in.at[n], ps.at[0, n], pr.at[0, n], who))
        first.append(remote(sums.at[there], sums_in.at[n], ps.at[1, n], pr.at[1, n], who))
    second = [
        remote(biases, rank_biases_in.at[n], zs.at[0, n], zr.at[0, n], who) for n, who in enumerate(ranks)
    ]
    for copy in first + second:
        copy.start()
    all_tokens[place] = tokens[...]
    gather_tokens.first()
    background.tick()
    for copy in first:
        copy.wait()
    mod_total, sum_total = mods[place], sums[place]
    for n in range(len(peers)):
        mod_total = mod_total + mods_in[n]
        sum_total = sum_total + sums_in[n]
    rank_mods[rank] = mod_total.astype(bf16)
    rank_sums[rank] = sum_total
    third = []
    for n, who in enumerate(ranks):
        third.append(remote(rank_mods.at[rank], rank_mods.at[rank], zs.at[1, n], zr.at[1, n], who))
        third.append(remote(rank_sums.at[rank], rank_sums.at[rank], zs.at[2, n], zr.at[2, n], who))
    for copy in third:
        copy.start()
    background.tick()
    bias_total = biases[...]
    for n, copy in enumerate(second):
        copy.wait()
        bias_total = bias_total + rank_biases_in[n]
    for copy in third:
        copy.wait()
    sum_own = rank_sums[0]
    for n in range(1, rank_sums.shape[0]):
        sum_own = sum_own + rank_sums[n]
    all_mods[place] = rank_mods[...]
    all_rows[place, 0, :each] = sum_own
    all_rows[place, 1, :, : biases.shape[1]] = bias_total
    gather_mods.first()
    gather_rows.first()
    for gather in (gather_tokens, gather_mods, gather_rows):
        gather.second()
    background.tick()
    for gather in (gather_tokens, gather_mods, gather_rows):
        gather.finish()
        gather.drain()
    background.finish()


def epilogue(block_sums, final_sums, block_biases, patch_term, final_term, edge_rows, tokens, ident, tasks):
    ranks = lax.axis_size("batch")
    dma = pltpu.SemaphoreType.DMA
    depth = len(block_sums) // 2
    images, _, width = final_sums.shape
    count = patch_term.shape[0] + final_term.shape[0] + edge_rows.shape[0] + len(block_sums)
    each = -(-count // 8)
    widest = max(source.shape[1] for source in block_biases)
    mods, sums = (8, 2 * images, width), (8, each, width)
    biases = (8, widest)
    return call(
        partial(epilogue_kernel, depth),
        "epilogue",
        ident,
        [
            shaped((8, ranks) + mods[1:], bf16),
            shaped((8, 2, 8, width), f32),
            shaped((8,) + tokens.shape, f32),
        ],
        [
            pltpu.VMEM(mods, f32),
            pltpu.VMEM(sums, f32),
            pltpu.VMEM(biases, f32),
            pltpu.VMEM((7,) + mods[1:], f32),
            pltpu.VMEM((7,) + sums[1:], f32),
            pltpu.VMEM((ranks,) + mods[1:], bf16),
            pltpu.VMEM((ranks,) + sums[1:], f32),
            pltpu.VMEM((ranks - 1,) + biases, f32),
            dma((2, 7)),
            dma((2, 7)),
            dma((3, ranks - 1)),
            dma((3, ranks - 1)),
            dma((3, 10)),
            dma((3, 10)),
        ],
        0,
        (*block_sums, final_sums, *block_biases, patch_term, final_term, edge_rows, tokens),
        tasks,
    )


def closing_kernel(background, parts, every, zs, zr):
    ranks = other_ranks()
    address = sides()[2]
    greet(ranks + list(address.values()))
    rank = lax.axis_index("batch")
    copies = [
        remote(parts.at[who["batch"]], every.at[rank], zs.at[n], zr.at[n], who) for n, who in enumerate(ranks)
    ]
    background.tick()
    for copy in copies:
        copy.start()
    every[rank] = parts[rank]
    for copy in copies:
        copy.wait()
    background.finish()


def closing(parts, ident, tasks):
    ranks = parts.shape[0]
    dma = pltpu.SemaphoreType.DMA
    (every,), gathered = call(
        closing_kernel,
        "closing",
        ident,
        [shaped(parts.shape, f32)],
        [dma((ranks - 1,)), dma((ranks - 1,))],
        0,
        (parts,),
        tasks,
    )
    return every, gathered


def mlp_forward_kernel(
    block, background, mid, gate_rows, vecs, pair_far, expand_bias, full_far, hidden_far, expanded, after,
    full, hidden, pair, expand, shrink, moves, *comm
):
    moving = Copying(moves)
    moving.start("pair", pair_far, pair)
    place = sides()
    core, chips, address = place
    images = full.shape[0]
    gathers, scatters = exchanges(full, comm, place)
    greet(list(address.values()) + background.partners())

    def row(i, n):
        return vecs[i, n : n + 1]

    def gate(i):
        return gate_rows[i] if block > 0 else 1.0

    own = core * 4 + chips["own"]

    def begin(i):
        full[i, own] = modulate(mid[i], row(i, 6 * block + 3), row(i, 6 * block + 4)).astype(bf16)
        gathers[i].first()

    def compute(i, between):
        for step, (start, sibling) in enumerate(halves(core)):
            value = dot(flat(full[i, pl.ds(start, 4)]), expand[...], NN) + expand_bias[...]
            hidden[i, pl.ds(start, 4)] = value.reshape(4, -1, value.shape[1])
            partial = dot(gelu(value).astype(bf16), shrink[...], NT)
            keep_partial(partial, scatters[i], sibling)
            between[step]()

    def end(i):
        value = scatters[i].finish() + row(i, offset_row(vecs, block, 1))
        expanded[i] = value
        after[i] = mid[i] + gate(i) * row(i, 6 * block + 5) * value

    def keep(i):
        moving.start(("full", i), full.at[i], full_far.at[i])
        moving.start(("hidden", i), hidden.at[i], hidden_far.at[i])

    background.tick()
    begin(0)
    moving.wait("pair")
    expand[...] = pair[:, : expand.shape[1]]
    shrink[...] = pair[:, expand.shape[1] :]
    gathers[0].second()
    begin(1)
    gathers[0].finish()
    compute(0, (gathers[1].second, scatters[0].first))
    keep(0)
    background.tick()
    gathers[1].finish()
    compute(1, (scatters[0].second, scatters[1].first))
    keep(1)
    background.tick()
    end(0)
    scatters[1].second()
    end(1)
    for part in gathers + scatters:
        part.drain()
    moving.wait(*[(name, i) for name in ("full", "hidden") for i in range(images)])
    background.finish()


def mlp_forward(block, mid, gate_rows, vecs, weights, ident, tasks=()):
    pair, expand_bias = weights
    images, length, width = mid.shape
    inner = pair.shape[1] // 2
    return call(
        partial(mlp_forward_kernel, block),
        "mlp_forward",
        ident,
        [
            Far(shaped((images, 8, length, width), bf16)),
            Far(shaped((images, 8, length, inner), f32)),
            shaped((images, length, width), f32),
            shaped((images, length, width), f32),
        ],
        [
            pltpu.VMEM((images, 8, length, width), bf16),
            pltpu.VMEM((images, 8, length, inner), f32),
            scratch_like(pair),
            pltpu.VMEM((width, inner), bf16),
            pltpu.VMEM((width, inner), bf16),
            pltpu.SemaphoreType.DMA((1 + 2 * images,)),
        ]
        + comm_scratch(images, length, width),
        4 * images * 8 * length * width * inner * 6,
        (
            mid,
            gate_rows,
            vecs,
            Far(pair),
            expand_bias.reshape(1, -1),
        ),
        tasks,
    )


def mlp_backward_kernel(
    block, background, grad_after, mid, expanded, gate_rows, vecs, pair_far, normed_far, hidden_far,
    grad_mid, sums, grad_pair, grad_bias,
    full, grad_hidden, active, sum_expand, sum_shrink, pair, expand, shrink, normed, hidden, moves, *comm
):
    moving = Copying(moves)
    moving.start("pair", pair_far, pair)
    moving.start("hidden", hidden_far, hidden)
    moving.start("normed", normed_far, normed)
    place = sides()
    core, chips, address = place
    gathers, scatters = exchanges(full, comm, place)
    greet(list(address.values()) + background.partners())

    def row(i, n):
        return vecs[i, n : n + 1]

    def gate(i):
        return gate_rows[i] if block > 0 else 1.0

    own = core * 4 + chips["own"]
    length = full.shape[2]

    def begin(i):
        gated = gate(i) * grad_after[i, :length]
        low = (gated * row(i, 6 * block + 5)).astype(bf16)
        full[i, own] = low
        gathers[i].first()
        sums[i, 2:3] = column_sum(gated * expanded[i])
        sums[i, 3:4] = column_sum(low.astype(f32))

    def compute(i, between):
        for step, (start, sibling) in enumerate(halves(core)):
            pull = dot(flat(full[i, pl.ds(start, 4)]), shrink[...], NN)
            value, slope = gelu_with_slope(flat(hidden[i, pl.ds(start, 4)]))
            active[i, pl.ds(start, 4)] = value.astype(bf16).reshape(4, -1, value.shape[1])
            low = (pull * slope).astype(bf16)
            grad_hidden[i, pl.ds(start, 4)] = low.reshape(4, -1, value.shape[1])
            keep_partial(dot(low, expand[...], NT), scatters[i], sibling)
            between[step]()

    def weigh_shrink(i):
        term = dot(flat(full[i]), flat(active[i]), TN)
        if i == 0:
            sum_shrink[...] = term
        else:
            sum_shrink[...] += term

    def weigh_expand(i):
        low = flat(grad_hidden[i])
        term = dot(flat(normed[i]), low, TN)
        if i == 0:
            sum_expand[...] = term
            grad_bias[...] = row_sums(low)
        else:
            grad_pair[...] = jnp.concatenate([sum_expand[...] + term, sum_shrink[...]], axis=1).astype(bf16)
            grad_bias[...] += row_sums(low)

    def end(i):
        grad, shift_sum, scale_sum = modulate_back_rows(mid[i], row(i, 6 * block + 4), scatters[i].finish())
        grad_mid[i] = grad + grad_after[i, :length]
        sums[i, 0:1] = shift_sum
        sums[i, 1:2] = scale_sum

    background.tick()
    begin(0)
    moving.wait("pair")
    expand[...] = pair[:, : expand.shape[1]]
    shrink[...] = pair[:, expand.shape[1] :]
    gathers[0].second()
    begin(1)
    gathers[0].finish()
    moving.wait("hidden")
    compute(0, (gathers[1].second, scatters[0].first))
    background.tick()
    gathers[1].finish()
    compute(1, (scatters[0].second, scatters[1].first))
    background.tick()
    weigh_shrink(0)
    end(0)
    scatters[1].second()
    background.tick()
    moving.wait("normed")
    weigh_expand(0)
    weigh_shrink(1)
    weigh_expand(1)
    end(1)
    for part in gathers + scatters:
        part.drain()
    background.finish()


def mlp_backward(block, grad_after, mid, expanded, gate_rows, vecs, weights, saved, ident, tasks=()):
    pair, _ = weights
    normed, hidden = saved
    images, length, width = mid.shape
    inner = pair.shape[1] // 2
    return call(
        partial(mlp_backward_kernel, block),
        "mlp_backward",
        ident,
        [
            shaped((images, length, width), f32),
            shaped((images, 8, width), f32),
            shaped((width, 2 * inner), bf16),
            shaped((8, inner), f32),
        ],
        [
            pltpu.VMEM((images, 8, length, width), bf16),
            pltpu.VMEM((images, 8, length, inner), bf16),
            pltpu.VMEM((images, 8, length, inner), bf16),
            pltpu.VMEM((width, inner), f32),
            pltpu.VMEM((width, inner), f32),
            scratch_like(pair),
            pltpu.VMEM((width, inner), bf16),
            pltpu.VMEM((width, inner), bf16),
            scratch_like(normed),
            scratch_like(hidden),
            pltpu.SemaphoreType.DMA((3,)),
        ]
        + comm_scratch(images, length, width),
        8 * images * 8 * length * width * inner * 6,
        (
            grad_after,
            mid,
            expanded,
            gate_rows,
            vecs,
            Far(pair),
            Far(normed),
            Far(hidden),
        ),
        tasks,
    )


LOG2E = 1.4426950408889634


def offset_row(vecs, block, kind):
    depth = (vecs.shape[1] - 2) // 8
    return 6 * depth + 2 + 2 * block + kind


def pad_lanes(value):
    gap = jnp.zeros((value.shape[0], LANES - HEAD_SIZE), value.dtype)
    parts = []
    for start in range(0, value.shape[1], HEAD_SIZE):
        parts += [value[:, start : start + HEAD_SIZE], gap]
    return jnp.concatenate(parts, axis=1)


def pad_rows(value):
    gap = jnp.zeros((LANES - HEAD_SIZE, value.shape[1]), value.dtype)
    parts = []
    for start in range(0, value.shape[0], HEAD_SIZE):
        parts += [value[start : start + HEAD_SIZE], gap]
    return jnp.concatenate(parts, axis=0)


def cut_lanes(value):
    return jnp.concatenate(
        [value[:, start : start + HEAD_SIZE] for start in range(0, value.shape[1], LANES)], axis=1
    )


def cut_rows(value):
    return jnp.concatenate(
        [value[start : start + HEAD_SIZE] for start in range(0, value.shape[0], LANES)], axis=0
    )


def attention_forward_kernel(
    block, background, base, gate_rows, vecs, project_own, project_bias, attend_own, key_bias,
    full_far, packed_far, mixed_far, log_total, attended, mid, project, attend,
    full, packed, mixed, moves, *comm
):
    moving = Copying(moves)
    place = sides()
    core, chips, address = place
    images, _, length, _ = full.shape
    gathers, scatters = exchanges(full, comm, place)
    greet(list(address.values()) + background.partners())

    def row(i, n):
        return vecs[i, n : n + 1]

    def gate(i):
        return gate_rows[i] if block > 0 else 1.0

    own = core * 4 + chips["own"]
    span = attend.shape[0]
    heads = span // LANES
    tile = 2 * length
    factor = HEAD_SIZE ** (-0.5) * LOG2E

    def begin(i):
        full[i, own] = modulate(base[i, :length], row(i, 6 * block), row(i, 6 * block + 1)).astype(bf16)
        gathers[i].first()

    def rows_of(start, count):
        return pl.ds(pl.multiple_of(start * length, length), count * length)

    def compute(i, between):
        for start, _ in halves(core):
            value = dot(flat(full[i, pl.ds(start, 4)]), project[...], NN) + project_bias[...]
            packed[i, rows_of(start, 4)] = value.astype(bf16)
        between[0]()
        for step, (start, sibling) in enumerate(halves(core)):

            def one(t, carry, start=start):
                rows = pl.ds(pl.multiple_of((start + 2 * t) * length, tile), tile)
                for h in range(heads):
                    q, k, v = (
                        pl.ds(part * span + h * LANES, LANES) for part in range(3)
                    )
                    scores = dot(packed[i, rows, q], packed[i, :, k], NT) * factor
                    if block > 0:
                        scores = scores + key_bias[i]
                    peak = jnp.max(scores, axis=1, keepdims=True)
                    probs = jnp.exp2(scores - peak)
                    total = jnp.sum(probs, axis=1, keepdims=True)
                    out = dot(probs.astype(bf16), packed[i, :, v], NN) / total
                    mixed[i, rows, pl.ds(h * LANES, LANES)] = out.astype(bf16)
                    level = jnp.broadcast_to(peak + jnp.log2(total), (tile, LANES))
                    log_total[i, h, pl.ds(start // 2 + t, 1)] = level.T[0:1]
                return carry

            lax.fori_loop(0, 2, one, 0)
            partial = dot(mixed[i, rows_of(start, 4)], attend[...], NN)
            keep_partial(partial, scatters[i], sibling)
            between[1 + step]()

    def end(i):
        value = scatters[i].finish() + row(i, offset_row(vecs, block, 0))
        attended[i] = value
        mid[i] = base[i, :length] + gate(i) * row(i, 6 * block + 2) * value

    def nothing():
        pass

    def keep(i):
        for name, near, far in (("full", full, full_far), ("packed", packed, packed_far), ("mixed", mixed, mixed_far)):
            moving.start((name, i), near.at[i], far.at[i])

    background.tick()
    begin(0)
    project[...] = pad_lanes(project_own[...])
    attend[...] = pad_rows(attend_own[...])
    gathers[0].second()
    begin(1)
    gathers[0].finish()
    compute(0, (gathers[1].second, background.tick, scatters[0].first))
    keep(0)
    gathers[1].finish()
    compute(1, (scatters[0].second, nothing, scatters[1].first))
    keep(1)
    background.tick()
    end(0)
    scatters[1].second()
    end(1)
    for part in gathers + scatters:
        part.drain()
    moving.wait(*moving.open)
    background.finish()


def attention_forward(block, length, base, gate_rows, vecs, weights, key_bias, ident, tasks=()):
    project, project_bias, attend = weights
    images, _, width = base.shape
    span = attend.shape[0] // HEAD_SIZE * LANES
    return call(
        partial(attention_forward_kernel, block),
        "attention_forward",
        ident,
        [
            Far(shaped((images, 8, length, width), bf16)),
            Far(shaped((images, 8 * length, 3 * span), bf16)),
            Far(shaped((images, 8 * length, span), bf16)),
            shaped((images, span // LANES, 4, 2 * length), f32),
            shaped((images, length, width), f32),
            shaped((images, length, width), f32),
            shaped((width, 3 * span), bf16),
            shaped((span, width), bf16),
        ],
        [
            pltpu.VMEM((images, 8, length, width), bf16),
            pltpu.VMEM((images, 8 * length, 3 * span), bf16),
            pltpu.VMEM((images, 8 * length, span), bf16),
            pltpu.SemaphoreType.DMA((3 * images,)),
        ]
        + comm_scratch(images, length, width),
        8 * images * 8 * length * width * span * 6,
        (
            base,
            gate_rows,
            vecs,
            project,
            project_bias.reshape(1, -1),
            attend,
            key_bias,
        ),
        tasks,
    )


def attention_backward_kernel(
    block, background, grad_mid, base, attended, gate_rows, vecs, project_far, attend_far, key_bias, normed_far, packed_far, mixed_far, log_total,
    grad_base, sums, grad_project, grad_attend, grad_bias,
    full, grad_mixed, grad_packed, grad_keys, grad_values, sum_project, sum_attend,
    project, attend, normed, packed, mixed, moves, *comm
):
    moving = Copying(moves)
    moving.start("attend", attend_far, attend)
    moving.start("packed", packed_far, packed)
    moving.start("mixed", mixed_far, mixed)
    moving.start("project", project_far, project)
    moving.start("normed", normed_far, normed)
    place = sides()
    core, chips, address = place
    images, _, length, _ = full.shape
    gathers, scatters = exchanges(full, comm, place)
    greet(list(address.values()) + background.partners())

    def row(i, n):
        return vecs[i, n : n + 1]

    def gate(i):
        return gate_rows[i] if block > 0 else 1.0

    own = core * 4 + chips["own"]
    span = attend.shape[0]
    heads = span // LANES
    tile = 2 * length
    factor = HEAD_SIZE ** (-0.5)

    def begin(i):
        gated = gate(i) * grad_mid[i]
        low = (gated * row(i, 6 * block + 2)).astype(bf16)
        full[i, own] = low
        gathers[i].first()
        sums[i, 2:3] = column_sum(gated * attended[i])
        sums[i, 3:4] = column_sum(low.astype(f32))

    def rows_of(start, count):
        return pl.ds(pl.multiple_of(start * length, length), count * length)

    def compute(i, between):
        grad_mixed[...] = dot(flat(full[i]), attend[...], NT).astype(bf16)
        between[0]()
        for h in range(heads):
            lane = pl.ds(h * LANES, LANES)
            q, k, v = (pl.ds(part * span + h * LANES, LANES) for part in range(3))
            keys_turned = packed[i, :, k].T

            def one(t, carry):
                rows = pl.ds(pl.multiple_of(t * tile, tile), tile)
                queries, pulls = packed[i, rows, q], grad_mixed[rows, lane]
                scores = dot(packed[i, :, k], queries, NT) * (factor * LOG2E)
                if block > 0:
                    scores = scores + key_bias[i]
                probs = jnp.exp2(scores - log_total[i, h, pl.ds(t, 1)])
                dprobs = dot(packed[i, :, v], pulls, NT)
                row_dot = column_sum(probs * dprobs)
                grad_scores = (probs * (dprobs - row_dot)).astype(bf16)
                value_term = dot(probs.astype(bf16), pulls, NN)
                key_term = dot(grad_scores, queries, NN)

                @pl.when(t == 0)
                def _():
                    grad_values[...] = value_term
                    grad_keys[...] = key_term

                @pl.when(t > 0)
                def _():
                    grad_values[...] += value_term
                    grad_keys[...] += key_term

                query_term = dot(keys_turned, grad_scores, NN) * factor
                grad_packed[i, rows, q] = query_term.T.astype(bf16)
                return carry

            lax.fori_loop(0, 4, one, 0)
            grad_packed[i, :, k] = (grad_keys[...] * factor).astype(bf16)
            grad_packed[i, :, v] = grad_values[...].astype(bf16)
            between[1 + h]()
        for step, (start, sibling) in enumerate(halves(core)):
            keep_partial(dot(grad_packed[i, rows_of(start, 4)], project[...], NT), scatters[i], sibling)

    def weigh_attend(i):
        term = dot(mixed[i], flat(full[i]), TN)
        if i == 0:
            sum_attend[...] = term
        else:
            grad_attend[...] = cut_rows(sum_attend[...] + term).reshape(grad_attend.shape).astype(bf16)

    def weigh_project(i):
        low = grad_packed[i]
        term = dot(flat(normed[i]), low, TN)
        if i == 0:
            sum_project[...] = term
            grad_bias[...] = row_sums(low)
        else:
            grad_project[...] = cut_lanes(sum_project[...] + term).astype(bf16)
            grad_bias[...] += row_sums(low)

    def end(i):
        grad, shift_sum, scale_sum = modulate_back_rows(base[i, :length], row(i, 6 * block + 1), scatters[i].finish())
        grad_base[i] = grad + grad_mid[i]
        sums[i, 0:1] = shift_sum
        sums[i, 1:2] = scale_sum

    def nothing():
        pass

    def begin_extra():
        gathers[1].second()
        background.tick()

    def early_attend():
        for i in range(images):
            weigh_attend(i)
        for task in background.tasks:
            if task.source is None:
                task.source = grad_attend
        background.tick()

    def middle():
        scatters[0].second()
        background.tick()

    background.tick()
    begin(0)
    gathers[0].second()
    begin(1)
    gathers[0].finish()
    moving.wait("attend", "packed", "mixed", "project", "normed")
    compute(0, (begin_extra, gathers[1].finish, nothing))
    scatters[0].first()
    compute(1, (early_attend, middle, background.tick))
    scatters[1].first()
    weigh_project(0)
    end(0)
    scatters[1].second()
    weigh_project(1)
    end(1)
    for part in gathers + scatters:
        part.drain()
    background.finish()


def attention_backward(
    block, attend_shape, grad_mid, base, attended, gate_rows, vecs, weights, key_bias, saved, ident, tasks=()
):
    project, attend = weights
    normed, packed, mixed, log_total = saved
    images, length, width = grad_mid.shape
    span = attend.shape[0]
    tokens = 8 * length
    return call(
        partial(attention_backward_kernel, block),
        "attention_backward",
        ident,
        [
            shaped((images, length, width), f32),
            shaped((images, 8, width), f32),
            shaped((width, 3 * span // LANES * HEAD_SIZE), bf16),
            shaped(attend_shape, bf16),
            shaped((8, 3 * span), f32),
        ],
        [
            pltpu.VMEM((images, 8, length, width), bf16),
            pltpu.VMEM((tokens, span), bf16),
            pltpu.VMEM((images, tokens, 3 * span), bf16),
            pltpu.VMEM((tokens, LANES), f32),
            pltpu.VMEM((tokens, LANES), f32),
            pltpu.VMEM((width, 3 * span), f32),
            pltpu.VMEM((span, width), f32),
            scratch_like(project),
            scratch_like(attend),
            scratch_like(normed),
            scratch_like(packed),
            scratch_like(mixed),
            pltpu.SemaphoreType.DMA((5,)),
        ]
        + comm_scratch(images, length, width),
        16 * images * 8 * length * width * span * 6,
        (
            grad_mid,
            base,
            attended,
            gate_rows,
            vecs,
            Far(project),
            Far(attend),
            key_bias,
            Far(normed),
            Far(packed),
            Far(mixed),
            log_total,
        ),
        tasks,
    )


HEAD_SIZE = 72


def pad_heads(array, axis):
    shape = array.shape
    heads = shape[axis] // HEAD_SIZE
    split = array.reshape(shape[:axis] + (heads, HEAD_SIZE) + shape[axis + 1 :])
    widths = [(0, 0)] * split.ndim
    widths[axis + 1] = (0, LANES - HEAD_SIZE)
    return jnp.pad(split, widths).reshape(shape[:axis] + (heads * LANES,) + shape[axis + 1 :])


def unpad_heads(array, axis):
    shape = array.shape
    heads = shape[axis] // LANES
    split = array.reshape(shape[:axis] + (heads, LANES) + shape[axis + 1 :])
    kept = lax.slice_in_dim(split, 0, HEAD_SIZE, axis=axis + 1)
    return kept.reshape(shape[:axis] + (heads * HEAD_SIZE,) + shape[axis + 1 :])


def turn(block, own, step, last):
    return jnp.where(block == own, step, jnp.where(block < own, 0, last))


def local_call(kernel, name, grid, in_specs, out_specs, outs, moved, args, prefetch=0):
    return pl.pallas_call(
        kernel,
        name=name,
        grid_spec=pltpu.PrefetchScalarGridSpec(
            num_scalar_prefetch=prefetch, grid=grid, in_specs=in_specs, out_specs=out_specs
        ),
        out_shape=outs,
        compiler_params=pltpu.CompilerParams(vmem_limit_bytes=56 * 2**20),
        cost_estimate=pl.CostEstimate(flops=0, bytes_accessed=moved, transcendentals=0),
    )(*args)


def mlp_unpack_kernel(*refs):
    *everys, expand, shrink = refs
    for k, every in enumerate(everys):

        @pl.when(pl.program_id(0) == k)
        def _(every=every):
            first, second = every[0, 0].astype(f32), every[1, 0].astype(f32)
            inner = first.shape[1] // 2
            expand[0] = jnp.concatenate([first[:, :inner], second[:, :inner]], axis=1)
            shrink[0] = jnp.concatenate([first[:, inner:], second[:, inner:]], axis=1)


def mlp_unpack(everys):
    depth = len(everys)
    _, _, half, pair = everys[0].shape
    shard, inner = 2 * half, pair // 2
    everys = [every.reshape(2, 4, shard, pair) for every in everys]
    block = (2, 1, shard, pair)
    return local_call(
        mlp_unpack_kernel,
        "mlp_unpack",
        (depth, 4),
        [pl.BlockSpec(block, lambda b, j, k=k: (0, turn(b, k, j, 3), 0, 0)) for k in range(depth)],
        [
            pl.BlockSpec((1, shard, 2 * inner), lambda b, j: (b, 0, j)),
            pl.BlockSpec((1, shard, 2 * inner), lambda b, j: (b, 0, j)),
        ],
        [shaped((depth, shard, 8 * inner), f32), shaped((depth, shard, 8 * inner), f32)],
        depth * shard * inner * 96,
        everys,
    )


def project_unpack_kernel(*refs):
    *everys, project = refs
    for k, every in enumerate(everys):

        @pl.when(pl.program_id(0) == k)
        def _(every=every):
            each = every.shape[-1] // 3
            parts = [
                every[d % 2, d // 2, 0].astype(f32)[:, n * each : (n + 1) * each] for n in range(3) for d in range(8)
            ]
            project[0, 0] = jnp.concatenate(parts, axis=1)


def project_unpack(everys):
    depth = len(everys)
    _, _, half, columns = everys[0].shape
    everys = [every.reshape(2, 4, 2, half, columns) for every in everys]
    (project,) = local_call(
        project_unpack_kernel,
        "project_unpack",
        (depth, 2),
        [
            pl.BlockSpec((2, 4, 1, half, columns), lambda b, j, k=k: (0, 0, turn(b, k, j, 1), 0, 0))
            for k in range(depth)
        ],
        [pl.BlockSpec((1, 1, half, 8 * columns), lambda b, j: (b, j, 0, 0))],
        [shaped((depth, 2, half, 8 * columns), f32)],
        depth * half * columns * 96,
        everys,
    )
    return project.reshape(depth, 2 * half, 8 * columns)


def attend_unpack_kernel(rank, *refs):
    *everys, attend = refs
    for k, every in enumerate(everys):

        @pl.when(pl.program_id(0) == k)
        def _(every=every):
            cores, _, pieces = every.shape[:3]
            for n in range(attend.shape[1]):
                attend[0, n] = every[n // pieces, 0, n % pieces].astype(f32)


def attend_unpack(everys, rank, shard, pieces, rows):
    depth = len(everys)
    width = everys[0].shape[-1]
    everys = [every.reshape(2, 4, pieces, rows, width) for every in everys]
    steps = shard // rows
    if steps == 2 * pieces:
        block, count = (2, 1, pieces, rows, width), steps

        def chosen(b, i, ranks):
            return 0, ranks[0], 0, 0, 0

    else:
        block, count = (1, 1, 1, rows, width), 1

        def chosen(b, i, ranks):
            g = ranks[0] * steps + i
            d = g // pieces
            return d % 2, d // 2, g % pieces, 0, 0

    (attend,) = local_call(
        attend_unpack_kernel,
        "attend_unpack",
        (depth, steps // count),
        [pl.BlockSpec(block, chosen) for _ in range(depth)],
        [pl.BlockSpec((1, count, rows, width), lambda b, i, ranks: (b, i, 0, 0))],
        [shaped((depth, steps, rows, width), f32)],
        depth * shard * width * 6,
        [rank.reshape(1), *everys],
        1,
    )
    return attend.reshape(depth, shard, width)


def adaptive_grad_kernel(silu, mods, out):
    out[0] = dot(silu[...], mods[0], TN)


def adaptive_grad(silu, mods):
    depth, count, columns = mods.shape
    shard = silu.shape[1]
    (grad,) = local_call(
        adaptive_grad_kernel,
        "adaptive_grad",
        (depth, 3),
        [
            pl.BlockSpec((count, shard), lambda b, j: (0, 0)),
            pl.BlockSpec((1, count, columns // 3), lambda b, j: (b, 0, j)),
        ],
        [pl.BlockSpec((1, shard, columns // 3), lambda b, j: (b, 0, j))],
        [shaped((depth, shard, columns), f32)],
        depth * shard * columns * 4,
        [silu, mods],
    )
    return grad


def body(
    latents,
    conditioning,
    kept_index,
    kept_count,
    patch_weight,
    patch_bias,
    adaptive_weight,
    adaptive_bias,
    project_weight,
    project_bias,
    attend_weight,
    attend_bias,
    expand_weight,
    expand_bias,
    shrink_weight,
    shrink_bias,
    final_adaptive,
    final_offset,
    final_weight,
    final_bias,
    cotangent,
):
    rows, cols, ranks = lax.axis_size("row"), lax.axis_size("col"), lax.axis_size("batch")
    team = rows * cols
    place = lax.axis_index("row") * cols + lax.axis_index("col")
    rank = lax.axis_index("batch")
    images, channels_in = latents.shape[:2]
    channels_out = cotangent.shape[1]
    rows_tile, cols_tile = latents.shape[2] // PATCH, latents.shape[3] // PATCH
    tile_tokens = rows_tile * cols_tile
    sequence = tile_tokens * team
    width = conditioning.shape[1]
    depth = adaptive_weight.shape[0]
    shard = adaptive_weight.shape[1]
    kept_local = tile_tokens * 3 // 4
    highest = lax.Precision.HIGHEST

    head_cols = width // team
    hidden_cols = expand_weight.shape[2] // team

    def slice_of(array, axis, count):
        return lax.dynamic_slice_in_dim(array, place * count, count, axis=axis)

    piece_rows = min(shard, HEAD_SIZE)
    pieces_each = head_cols // piece_rows
    project_own = jnp.concatenate(
        [
            lax.dynamic_slice_in_dim(project_weight, part * width + place * head_cols, head_cols, axis=2)
            for part in range(3)
        ],
        axis=2,
    )
    attend_own = jnp.stack(
        [
            lax.dynamic_slice_in_dim(
                attend_weight, (place * head_cols + j * piece_rows) % shard, piece_rows, axis=1
            )
            for j in range(pieces_each)
        ],
        axis=1,
    )
    pair_own = jnp.concatenate(
        [slice_of(expand_weight, 2, hidden_cols), slice_of(shrink_weight, 1, hidden_cols).transpose(0, 2, 1)], axis=2
    )

    smalls = [
        patch_weight,
        final_weight.T,
        patch_bias[None],
        adaptive_bias,
        project_bias,
        attend_bias,
        expand_bias,
        shrink_bias,
        final_offset[None],
    ]
    patch_tiles = to_tokens(latents, PATCH)
    grad_tiles = to_tokens(cotangent, PATCH)
    patch_in, patch_out = patch_tiles.shape[2], grad_tiles.shape[2]
    tiles = jnp.concatenate([patch_tiles, grad_tiles], axis=2)
    pair = 2 * width
    block_of = jnp.minimum(place // 3, depth - 1)
    pair_weight = lax.dynamic_slice(adaptive_weight, (block_of, 0, place % 3 * pair), (1, shard, pair))[0]
    pair_weight = jnp.where(place < 3 * depth, pair_weight, final_adaptive)
    packs, every_tile, silu_rows, mods, (project_next, attend_next) = prologue(
        smalls,
        [1] * 9,
        conditioning.reshape(images, ranks, shard).transpose(1, 0, 2),
        pair_weight,
        tiles.reshape(-1, LANES),
        8,
        [Line(project_own[0]), Chain(attend_own[0], shard)],
    )
    (
        patch_full,
        final_turned,
        patch_bias_full,
        adaptive_offset,
        project_offset,
        attend_offset,
        expand_offset,
        shrink_offset,
        final_offset_full,
    ) = packs
    patch_bias_full, final_offset_full = patch_bias_full[0], final_offset_full[0]
    final_full = final_turned.T

    whole = every_tile.reshape((rows, cols, images, rows_tile, cols_tile, -1)).transpose(2, 0, 3, 1, 4, 5)
    whole = whole.reshape(images, sequence, patch_in + patch_out)
    grid_cols = cols * cols_tile
    own_ids = lax.dynamic_index_in_dim(
        kept_index.reshape(images, tile_tokens, team), place, axis=2, keepdims=False
    )
    pick = (own_ids[:, :, None] == jnp.arange(sequence, dtype=jnp.int32)).astype(bf16)
    own = jnp.einsum("ikt,itc->ikc", pick, whole, preferred_element_type=f32).astype(bf16)
    patches, grad_outputs = own[..., :patch_in], own[..., patch_in:]
    order = jnp.arange(kept_local, dtype=jnp.int32)[:, None] * team + jnp.arange(team, dtype=jnp.int32)
    kept_grid = order[None] < kept_count[:, None, None]
    chunk_order = kept_grid.reshape(images, kept_local, team // 2, 2).transpose(0, 3, 2, 1)
    key_bias = jnp.where(chunk_order.reshape(images, team * kept_local), 0.0, masked_score).astype(f32)
    kept_rows = lax.dynamic_index_in_dim(kept_grid, place, axis=2, keepdims=False).astype(f32)[:, :, None]

    count = width // 4
    omega = 1.0 / 10000.0 ** (jnp.arange(count, dtype=f32) / count)
    angles = jnp.arange(max(rows * rows_tile, grid_cols), dtype=f32)[:, None] * omega[None, :]
    along = jnp.concatenate([jnp.sin(angles), jnp.cos(angles)], axis=1)
    places = jnp.arange(along.shape[0], dtype=jnp.int32)

    def position_of(coords):
        chosen = (coords[..., None] == places).astype(f32)
        return jnp.einsum("ikt,tc->ikc", chosen, along, precision=highest)

    position = jnp.concatenate(
        [position_of(own_ids // grid_cols), position_of(own_ids % grid_cols)], axis=-1
    )
    resid = (
        jnp.einsum("ikc,cd->ikd", patches, patch_full, preferred_element_type=f32)
        + patch_bias_full.astype(f32)
        + position
    )

    mods = mods.reshape(team, images, 2, width).transpose(1, 0, 2, 3).reshape(images, 2 * team, width)
    offsets = [adaptive_offset.reshape(6 * depth, width), final_offset_full.reshape(2, width)]
    mods = mods[:, : 6 * depth + 2] + jnp.concatenate(offsets, axis=0).astype(f32)
    added = jnp.stack([attend_offset, shrink_offset], axis=1).reshape(2 * depth, width).astype(f32)
    vecs = jnp.concatenate([mods, jnp.broadcast_to(added, (images, 2 * depth, width))], axis=1)
    final_shift, final_scale = mods[:, 6 * depth, None], mods[:, 6 * depth + 1, None]
    head_biases = jnp.moveaxis(project_offset.astype(f32).reshape(depth, 2, team, head_cols), 2, 0)
    head_biases = lax.dynamic_index_in_dim(head_biases, place, axis=0, keepdims=False)
    head_biases = jnp.stack([head_biases[:, 0], jnp.zeros((depth, head_cols), f32), head_biases[:, 1]], axis=1)
    head_biases = pad_heads(head_biases, 2).reshape(depth, -1)
    hidden_biases = slice_of(expand_offset.astype(f32), 1, hidden_cols)

    records = []
    for b in range(depth):
        routed = b > 0
        length = kept_local if routed else tile_tokens
        base = resid
        tasks = [Line(pair_own[b])]
        (*attention_saved, attended, mid, project, attend), gathered = attention_forward(
            b,
            length,
            base,
            kept_rows,
            vecs,
            (project_next.reshape(width, -1), head_biases[b], attend_next.reshape(-1, width)),
            key_bias[:, None, :],
            4 * b,
            tasks,
        )
        mlp_weights = (gathered[0].reshape(width, 2 * hidden_cols), hidden_biases[b])
        tasks = []
        if b + 1 < depth:
            tasks = [Line(project_own[b + 1]), Chain(attend_own[b + 1], shard)]
        (*mlp_saved, expanded, after), gathered = mlp_forward(
            b, mid, kept_rows, vecs, mlp_weights, 4 * b + 1, tasks
        )
        if tasks:
            project_next, attend_next = gathered
        records.append((base, mid, attended, expanded, (project, attend), mlp_weights, attention_saved, mlp_saved))
        resid = jnp.concatenate([after, resid[:, kept_local:]], axis=1) if routed else after

    final_normed = modulate(resid, final_shift, final_scale).astype(bf16)
    outputs = jnp.einsum("ikd,dc->cik", final_normed, final_full, preferred_element_type=f32)
    outputs = outputs + final_bias.astype(f32)[:, None, None]
    final_bias_term = jnp.sum(grad_outputs.astype(f32), axis=(0, 1))
    final_weight_term = jnp.einsum("ikd,ikc->cd", final_normed, grad_outputs, preferred_element_type=f32)
    grad_final = jnp.einsum("ikc,dc->ikd", grad_outputs, final_full, preferred_element_type=f32)
    grad_resid, grad_final_shift, grad_final_scale = modulate_back(resid, final_scale, grad_final)
    final_mod_term = jnp.stack([grad_final_shift, grad_final_scale], axis=1)

    block_sums, block_biases = [], []
    spread = [[None, None, None] for _ in range(depth)]

    def folded(source, inbox):
        own = lax.dynamic_index_in_dim(source, rank, axis=0, keepdims=False)
        return (own.astype(f32) + jnp.sum(inbox.astype(f32), axis=0)).astype(bf16)

    def fold_project(term, inbox):
        return folded(term, inbox).reshape(2, shard // 2, -1)

    def fold_attend(term, inbox):
        total = term.astype(f32) + jnp.sum(inbox.astype(f32), axis=1)
        return total.astype(bf16).reshape(2, head_cols // 2, width)

    attend_shape = (pieces_each, piece_rows, width)
    project_term = None
    for b in reversed(range(depth)):
        base, mid, attended, expanded, attention_weights, mlp_weights, attention_saved, mlp_saved = records[b]
        routed = b > 0
        tasks = []
        if project_term is not None:
            tasks = [Fold(project_term), FoldTo(attend_shape, shard, 0, grad_attend)]
        (grad_mid, mlp_sums, grad_pair, grad_expand_bias), inboxes = mlp_backward(
            b, grad_resid, mid, expanded, kept_rows, vecs, mlp_weights, mlp_saved, 4 * b + 2, tasks
        )
        mlp_term = grad_pair.reshape(ranks, shard, 2 * hidden_cols)
        waiting = []
        early = b == 0
        tasks = [Fold(mlp_term)] + ([FoldTo(attend_shape, shard, 2)] if early else [])
        if project_term is not None:
            waiting = [
                (b + 1, 0, mlp_part),
                (b + 1, 1, fold_project(project_term, inboxes[0])),
                (b + 1, 2, fold_attend(grad_attend, inboxes[1])),
            ]
        folds = len(tasks)
        tasks += [PlaneGather(part, (1, 3)) for _, _, part in waiting]
        (grad_base, attention_sums, grad_project, grad_attend, grad_project_bias), inboxes = attention_backward(
            b,
            attend_shape,
            grad_mid,
            base,
            attended,
            kept_rows,
            vecs,
            attention_weights,
            key_bias[:, :, None],
            attention_saved,
            4 * b + 3,
            tasks,
        )
        for (block, n, _), every in zip(waiting, inboxes[folds:]):
            spread[block][n] = every
        mlp_part = folded(mlp_term, inboxes[0]).reshape(2, shard // 2, -1)
        if early:
            waiting = [(b, 0, mlp_part), (b, 2, fold_attend(grad_attend, inboxes[1]))]
        project_term = grad_project.reshape(ranks, shard, 3 * head_cols)
        block_sums = [attention_sums, mlp_sums] + block_sums
        block_biases = [grad_project_bias, grad_expand_bias] + block_biases
        grad_resid = jnp.concatenate([grad_base, grad_resid[:, kept_local:]], axis=1) if routed else grad_base

    patch_bias_term = jnp.sum(grad_resid, axis=(0, 1))
    grad_embed = grad_resid.astype(bf16)
    patch_term = jnp.einsum("ikc,ikd->cd", patches, grad_embed, preferred_element_type=f32)
    grad_patches = jnp.einsum("ikd,cd->cik", grad_embed, patch_full, preferred_element_type=f32)

    edge_rows = jnp.stack([patch_bias_term, jnp.pad(final_bias_term, (0, width - patch_out))])
    tokens_out = jnp.concatenate([outputs, grad_patches], axis=0).reshape(2, (patch_out + patch_in) // 2, -1)
    tasks = [Fold(project_term, late=1)] + [PlaneGather(part, plan) for (_, _, part), plan in zip(waiting, ((0, 2), (2,)))]
    (all_mods, all_rows, all_tokens), inboxes = epilogue(
        block_sums,
        final_mod_term,
        block_biases,
        patch_term,
        final_weight_term,
        edge_rows,
        tokens_out,
        10,
        tasks,
    )
    for (block, n, _), every in zip(waiting, inboxes[1:]):
        spread[block][n] = every
    last_part = fold_project(project_term, inboxes[0])

    mod_every = all_mods.reshape(team, ranks * images, pair)
    mod_width = 3 * pair
    block_mods = jnp.stack(
        [mod_every[3 * b : 3 * b + 3].transpose(1, 0, 2).reshape(ranks * images, mod_width) for b in range(depth)]
    )
    final_mods = mod_every[3 * depth]
    grad_silu = dot(final_mods, final_adaptive, NT)
    for b in range(depth):
        grad_silu = grad_silu + dot(block_mods[b], adaptive_weight[b], NT)
    grad_silu, last = closing(
        grad_silu.reshape(ranks, images, shard), 11, [PlaneGather(last_part)]
    )
    spread[0][1] = last[0]
    grad_silu = grad_silu.transpose(1, 0, 2).reshape(images, width)
    conditioning_grad = jax.vjp(jax.nn.silu, conditioning.astype(f32))[1](grad_silu)[0]
    adaptive_weight_grad = adaptive_grad(silu_rows, block_mods)
    final_adaptive_grad = dot(silu_rows, final_mods, TN)

    def rank_part(full):
        part = full.shape[-1] // ranks
        return lax.dynamic_slice_in_dim(full, rank * part, part, axis=full.ndim - 1)

    adaptive_bias_grad = rank_part(jnp.sum(block_mods.astype(f32), axis=1))
    final_offset_grad = rank_part(jnp.sum(final_mods.astype(f32), axis=0))

    def in_order(every):
        split = every.reshape((2, team // 2) + every.shape[1:])
        return jnp.swapaxes(split, 0, 1).reshape(every.shape)

    ordered = in_order(all_tokens).reshape(team, patch_out + patch_in, images, tile_tokens)
    ordered = ordered.transpose(2, 3, 0, 1).reshape(images, sequence, patch_out + patch_in)
    tile_rows = lax.axis_index("row") * rows_tile + jnp.arange(rows_tile, dtype=jnp.int32)
    tile_cols = lax.axis_index("col") * cols_tile + jnp.arange(cols_tile, dtype=jnp.int32)
    tile_ids = (tile_rows[:, None] * grid_cols + tile_cols).reshape(-1)
    back = (kept_index[:, None, :] == tile_ids[None, :, None]).astype(f32)
    tile_out = jnp.einsum("itj,ijc->itc", back, ordered, precision=highest)
    prediction = to_planes(tile_out[..., :patch_out], PATCH, channels_out, rows_tile, cols_tile)
    latent_grad = to_planes(tile_out[..., patch_out:], PATCH, channels_in, rows_tile, cols_tile)

    expand_weight_grad, shrink_weight_grad = mlp_unpack([parts[0] for parts in spread])
    project_weight_grad = project_unpack([parts[1] for parts in spread])
    attend_weight_grad = attend_unpack([parts[2] for parts in spread], rank, shard, pieces_each, piece_rows)

    first = patch_in + patch_out
    each = -(-(first + 2 + 2 * depth) // team)
    all_sums = all_rows[:, 0, :each].reshape(-1, width)
    all_biases = in_order(all_rows[:, 1])
    sums = lax.dynamic_slice_in_dim(all_sums, rank * shard, shard, axis=1)
    token_sums = sums[first + 2 : first + 2 + 2 * depth].reshape(depth, 2, shard)
    final_bias_grad = all_sums[first + 1, :patch_out]
    rows_of = all_biases.transpose(1, 0, 2)[: 2 * depth].reshape(depth, 2, team, -1)
    expand_bias_grad = rows_of[:, 1, :, :hidden_cols].reshape(depth, -1)
    head_rows = rows_of[:, 0, :, : 3 * head_cols // HEAD_SIZE * LANES]
    head_rows = unpad_heads(head_rows.reshape(depth, team, 3, -1), 3)
    project_bias_grad = jnp.stack([head_rows[:, :, 0], head_rows[:, :, 2]], axis=1).reshape(depth, -1)

    return (
        prediction,
        latent_grad,
        conditioning_grad,
        sums[:patch_in],
        sums[first],
        adaptive_weight_grad,
        adaptive_bias_grad,
        project_weight_grad,
        rank_part(project_bias_grad),
        attend_weight_grad,
        token_sums[:, 0],
        expand_weight_grad,
        rank_part(expand_bias_grad),
        shrink_weight_grad.transpose(0, 2, 1),
        token_sums[:, 1],
        final_adaptive_grad,
        final_offset_grad,
        sums[patch_in:first].T,
        final_bias_grad,
    )


def solution(mesh):
    tokens = P("batch", None, "row", "col")
    placed = (
        tokens,
        P("batch", None),
        P("batch", None),
        P("batch"),
        P(None, "batch"),
        P("batch"),
        P(None, "batch", None),
        P(None, "batch"),
        P(None, "batch", None),
        P(None, "batch"),
        P(None, "batch", None),
        P(None, "batch"),
        P(None, "batch", None),
        P(None, "batch"),
        P(None, None, "batch"),
        P(None, "batch"),
        P("batch", None),
        P("batch"),
        P("batch", None),
        P(),
        tokens,
    )
    return jax.shard_map(
        body,
        mesh=mesh,
        in_specs=placed,
        out_specs=(tokens, tokens, P("batch", None)) + placed[4:16] + (placed[16], P("batch"), P("batch", None), P()),
        check_vma=False,
    )
```

```python
from functools import partial

import jax
import jax.numpy as jnp
from jax import lax
from jax.experimental import pallas as pl
from jax.experimental.pallas import tpu as pltpu
from jax.sharding import PartitionSpec as P

HEADS = 16
PATCH = 2
LANES = 128
PLANE = ("row", "col")

norm_epsilon = 1e-06
masked_score = -1e30
f32 = jnp.float32
bf16 = jnp.bfloat16


def to_tokens(planes, patch_side):
    images, channels, height, breadth = planes.shape
    shaped = planes.reshape(
        images, channels, height // patch_side, patch_side, breadth // patch_side, patch_side
    )
    return shaped.transpose(0, 2, 4, 3, 5, 1).reshape(
        images, height // patch_side * (breadth // patch_side), patch_side * patch_side * channels
    )


def to_planes(token_rows, patch_side, channels, rows_tile, cols_tile):
    images = token_rows.shape[0]
    shaped = token_rows.reshape(images, rows_tile, cols_tile, patch_side, patch_side, channels)
    return shaped.transpose(0, 5, 1, 3, 2, 4).reshape(
        images, channels, rows_tile * patch_side, cols_tile * patch_side
    )


def dot(left, right, dims, precision=None):
    return lax.dot_general(left, right, (dims, ((), ())), precision=precision, preferred_element_type=f32)


def norm_parts(resid):
    centered = resid - jnp.mean(resid, axis=-1, keepdims=True)
    rstd = lax.rsqrt(jnp.mean(centered * centered, axis=-1, keepdims=True) + norm_epsilon)
    return centered * rstd, rstd


def modulate(resid, shift_part, scale_part):
    return norm_parts(resid)[0] * (1.0 + scale_part) + shift_part


def modulate_back(resid, scale_part, grad):
    unit, rstd = norm_parts(resid)
    inner = grad * (1.0 + scale_part)
    grad_in = rstd * (
        inner
        - jnp.mean(inner, axis=-1, keepdims=True)
        - unit * jnp.mean(inner * unit, axis=-1, keepdims=True)
    )
    return grad_in, jnp.sum(grad, axis=1), jnp.sum(grad * unit, axis=1)


def sides():
    row, col = lax.axis_index("row"), lax.axis_index("col")
    core = lax.rem(col, 2)
    across = col // 2
    chip = row * 2 + across
    chips = {
        "own": chip,
        "x": (1 - row) * 2 + across,
        "y": row * 2 + 1 - across,
        "far": (1 - row) * 2 + 1 - across,
    }
    address = {
        "x": {"row": 1 - row},
        "y": {"col": lax.rem(col + 2, 4)},
        "core": {"col": col + 1 - 2 * core},
    }
    return core, chips, address


def greet(addresses):
    barrier = pltpu.get_barrier_semaphore()
    for who in addresses:
        pl.semaphore_signal(barrier, inc=1, device_id=who, device_id_type=pl.DeviceIdType.MESH)
    pl.semaphore_wait(barrier, len(addresses))


def remote(source, target, send, recv, who):
    return pltpu.make_async_remote_copy(
        src_ref=source,
        dst_ref=target,
        send_sem=send,
        recv_sem=recv,
        device_id=who,
        device_id_type=pl.DeviceIdType.MESH,
    )


def rank_at(offset):
    ranks = lax.axis_size("batch")
    return {"batch": lax.rem(lax.axis_index("batch") + offset + ranks, ranks)}


def other_ranks():
    return [rank_at(offset) for offset in range(1, lax.axis_size("batch"))]


def plane_peers():
    row, col = lax.axis_index("row"), lax.axis_index("col")
    rows, cols = lax.axis_size("row"), lax.axis_size("col")
    return [
        {"row": lax.rem(row + n // cols, rows), "col": lax.rem(col + n % cols, cols)}
        for n in range(1, rows * cols)
    ]


class Line:
    reach = 1

    def __init__(self, source):
        ranks = lax.axis_size("batch")
        self.ins = [source]
        self.outs = [jax.ShapeDtypeStruct((ranks,) + source.shape, source.dtype)]
        self.sems = [(2, ranks - 1), (2, ranks - 1), (1,)]

    def bind(self, ins, outs, sems):
        (self.source,), (self.target,) = ins, outs
        self.send, self.recv, self.own = sems
        self.rank, self.ranks = lax.axis_index("batch"), lax.axis_size("batch")
        self.steps = self.ranks
        self.late = 0

    def copy(self, way, r):
        block = self.rank - r if way == 0 else self.rank + r
        source = self.source if r == 0 else self.target.at[block]
        return remote(
            source, self.target.at[block], self.send.at[way, r], self.recv.at[way, r], rank_at(1 - 2 * way)
        )

    def holds(self, way, r):
        return self.rank >= r if way == 0 else self.rank + r < self.ranks

    def sends(self, way, r):
        edge = self.rank + 1 < self.ranks if way == 0 else self.rank > 0
        return jnp.logical_and(self.holds(way, r), edge)

    def step(self, r):
        for way in (0, 1):
            if r > 0:
                block = self.rank - r if way == 0 else self.rank + r

                @pl.when(self.holds(way, r))
                def _(way=way, block=block):
                    place = self.target.at[block]
                    remote(place, place, self.send.at[way, r - 1], self.recv.at[way, r - 1], rank_at(1)).wait_recv()

            if r < self.ranks - 1:

                @pl.when(self.sends(way, r))
                def _(way=way):
                    self.copy(way, r).start()

        if r == 0:
            self.stay().start()

    def stay(self):
        return pltpu.make_async_copy(self.source, self.target.at[self.rank], self.own.at[0])

    def finish(self):
        for way in (0, 1):
            for r in range(self.ranks - 1):

                @pl.when(self.sends(way, r))
                def _(way=way, r=r):
                    self.copy(way, r).wait_send()

        self.stay().wait()


class Chain:
    reach = 1

    def __init__(self, source, shard):
        pieces, self.rows, _ = source.shape
        self.shard = shard
        self.ins = [source]
        self.outs = [jax.ShapeDtypeStruct(source.shape, source.dtype)]
        self.sems = [(pieces, 2), (pieces, 2), (pieces,)]

    def bind(self, ins, outs, sems):
        (self.source,), (self.target,) = ins, outs
        self.send, self.recv, self.own = sems
        self.rank, self.ranks = lax.axis_index("batch"), lax.axis_size("batch")
        self.steps = self.ranks
        self.late = 0
        self.owners = owners_of(self.source.shape[0], self.rows, self.shard)

    def copy(self, j, way, first):
        source = self.source.at[j] if first else self.target.at[j]
        return remote(
            source, self.target.at[j], self.send.at[j, way], self.recv.at[j, way], rank_at(1 - 2 * way)
        )

    def edge(self, way):
        return self.rank + 1 < self.ranks if way == 0 else self.rank > 0

    def step(self, r):
        for j, owner in enumerate(self.owners):
            for way in (0, 1):
                away = self.rank - owner if way == 0 else owner - self.rank
                if r > 0:

                    @pl.when(away == r)
                    def _(j=j, way=way):
                        self.copy(j, way, False).wait_recv()

                @pl.when(jnp.logical_and(away == r, self.edge(way)))
                def _(j=j, way=way):
                    self.copy(j, way, r == 0).start()

            if r == 0:

                @pl.when(self.rank == owner)
                def _(j=j):
                    self.stay(j).start()

    def stay(self, j):
        return pltpu.make_async_copy(self.source.at[j], self.target.at[j], self.own.at[j])

    def finish(self):
        for j, owner in enumerate(self.owners):
            for way in (0, 1):
                away = self.rank - owner if way == 0 else owner - self.rank

                @pl.when(jnp.logical_and(away >= 0, self.edge(way)))
                def _(j=j, way=way):
                    self.copy(j, way, False).wait_send()

            @pl.when(self.rank == owner)
            def _(j=j):
                self.stay(j).wait()


def team_place():
    return lax.axis_index("row") * lax.axis_size("col") + lax.axis_index("col")


def owners_of(pieces, rows, shard):
    place = team_place()
    return [(place * pieces + j) * rows // shard for j in range(pieces)]


class Fold:
    reach = 2

    def __init__(self, source, late=0):
        ranks = lax.axis_size("batch")
        self.ins = [source]
        self.late = late
        self.outs = [jax.ShapeDtypeStruct((ranks - 1,) + source.shape[1:], source.dtype)]
        self.sems = [(ranks - 1,), (ranks - 1,)]

    def bind(self, ins, outs, sems):
        (self.source,), (self.inbox,) = ins, outs
        self.send, self.recv = sems
        self.steps = 1

    def copies(self):
        for n in range(lax.axis_size("batch") - 1):
            who = rank_at(n + 1)
            yield remote(
                self.source.at[who["batch"]], self.inbox.at[n], self.send.at[n], self.recv.at[n], who
            )

    def step(self, r):
        for copy in self.copies():
            copy.start()

    def finish(self):
        for copy in self.copies():
            copy.wait()


class FoldTo:
    reach = 2

    def __init__(self, shape, shard, late, source=None):
        pieces, self.rows, width = shape
        others = lax.axis_size("batch") - 1
        self.shard = shard
        self.ins = [] if source is None else [source]
        self.outs = [jax.ShapeDtypeStruct((pieces, others, self.rows, width), bf16)]
        self.sems = [(pieces, others), (pieces, others)]
        self.late, self.pieces = late, pieces

    def bind(self, ins, outs, sems):
        (self.inbox,) = outs
        self.source = ins[0] if ins else None
        self.send, self.recv = sems
        self.steps = 1
        self.rank, self.others = lax.axis_index("batch"), lax.axis_size("batch") - 1
        self.owners = owners_of(self.pieces, self.rows, self.shard)

    def copy(self, j, n):
        return remote(
            self.source.at[j], self.inbox.at[j, n], self.send.at[j, n], self.recv.at[j, n], rank_at(n + 1)
        )

    def leads(self, j, n):
        return rank_at(n + 1)["batch"] == self.owners[j]

    def step(self, r):
        for j in range(len(self.owners)):
            for n in range(self.others):

                @pl.when(self.leads(j, n))
                def _(j=j, n=n):
                    self.copy(j, n).start()

    def finish(self):
        for j, owner in enumerate(self.owners):
            for n in range(self.others):

                @pl.when(self.rank == owner)
                def _(j=j, n=n):
                    self.copy(j, n).wait_recv()

                @pl.when(self.leads(j, n))
                def _(j=j, n=n):
                    self.copy(j, n).wait_send()


class Copies:
    def __init__(self, send, recv, address):
        self.send, self.recv, self.address = send, recv, address
        self.started = {}

    def go(self, slot, source, target, who):
        copy = remote(source, target, self.send.at[slot], self.recv.at[slot], self.address[who])
        copy.start()
        self.started[slot] = copy

    def arrived(self, *slots):
        for slot in slots:
            self.started[slot].wait_recv()

    def drain(self):
        for copy in self.started.values():
            copy.wait_send()


class Gather(Copies):
    def __init__(self, full, send, recv, place):
        core, chips, address = place
        super().__init__(send, recv, address)
        self.full, self.half = full, full.shape[1] // 2
        self.source = None
        self.at = {name: core * 4 + chip for name, chip in chips.items()}

    def whole(self, name):
        return self.full.at[self.at[name]]

    def part(self, name, second):
        return self.full.at[self.at[name], pl.ds(self.half * second, self.half)]

    def first(self):
        own = self.whole("own")
        source = own if self.source is None else self.source
        parts = [pl.ds(0, self.half), pl.ds(self.half, self.half)]
        for slot, part, who in ((0, 0, "x"), (1, 1, "y"), (8, 1, "x"), (9, 0, "y")):
            self.go(slot, source.at[parts[part]], self.part("own", part), who)
        self.go(2, source, own, "core")

    def second(self):
        self.arrived(0)
        self.go(3, self.part("x", 0), self.part("x", 0), "y")
        self.arrived(1)
        self.go(4, self.part("y", 1), self.part("y", 1), "x")
        self.arrived(8)
        self.go(5, self.whole("x"), self.whole("x"), "core")
        self.arrived(9)
        self.go(6, self.whole("y"), self.whole("y"), "core")

    def finish(self):
        self.arrived(3, 4)
        self.go(7, self.whole("far"), self.whole("far"), "core")
        self.arrived(2, 5, 6, 7)


class PlaneGather:
    reach = 0

    def __init__(self, source, plan=(0, 1, 2)):
        self.ins = [source]
        self.plan = plan
        self.outs = [jax.ShapeDtypeStruct((8,) + source.shape, source.dtype)]
        self.sems = [(10,), (10,), (1,)]
        self.late = 0

    def bind(self, ins, outs, sems):
        (self.source,), (self.target,) = ins, outs
        send, recv, self.own = sems
        self.gather = Gather(self.target, send, recv, sides())
        self.gather.source = self.source
        self.steps = 3

    def stay(self):
        return pltpu.make_async_copy(self.source, self.gather.whole("own"), self.own.at[0])

    def step(self, r):
        if r == 0:
            self.gather.first()
            self.stay().start()
        elif r == 1:
            self.gather.second()
        else:
            self.gather.finish()

    def finish(self):
        self.gather.drain()
        self.stay().wait()


class Background:
    def __init__(self, tasks):
        self.tasks = tasks
        self.now = 0
        self.done = [[] for _ in tasks]

    def partners(self):
        reach = max([task.reach for task in self.tasks], default=0)
        return [[], [rank_at(1), rank_at(-1)], other_ranks()][reach]

    def tick(self):
        for task, done in zip(self.tasks, self.done):
            plan = getattr(task, "plan", None) or range(task.late, task.late + task.steps)
            if len(done) < task.steps and len(done) < len(plan) and plan[len(done)] <= self.now:
                task.step(len(done))
                done.append(self.now)
        self.now += 1

    def finish(self):
        for most in range(max([task.steps for task in self.tasks], default=0)):
            for task, done in zip(self.tasks, self.done):
                if len(done) == most and most < task.steps:
                    task.step(most)
                    done.append(self.now)
        for task in self.tasks:
            task.finish()


class Scatter(Copies):
    def __init__(self, core_out, core_in, total, hop_out, hop_in, send, recv, place):
        _, self.chips, address = place
        super().__init__(send, recv, address)
        self.core_out, self.core_in, self.total = core_out, core_in, total
        self.hop_out, self.hop_in = hop_out, hop_in
        self.half = total.shape[1] // 2

    def cross(self):
        self.go(0, self.core_out, self.core_in, "core")

    def hop(self, slot, value, who):
        self.hop_out[slot] = value.astype(bf16)
        self.go(1 + slot, self.hop_out.at[slot], self.hop_in.at[slot], who)

    def first(self):
        self.arrived(0)
        half = self.half

        def summed(name):
            chip = self.chips[name]
            return self.total[chip] + self.core_in[chip].astype(f32)

        far = summed("far")
        self.hop(0, far[:half], "x")
        self.hop(2, far[half:], "y")
        x_sum = summed("x")
        self.hop(1, x_sum[:half], "x")
        self.total[self.chips["x"], half:] = x_sum[half:]
        y_sum = summed("y")
        self.hop(3, y_sum[half:], "y")
        self.total[self.chips["y"], :half] = y_sum[:half]

    def second(self):
        half = self.half
        self.arrived(1)
        self.hop(4, self.total[self.chips["y"], :half] + self.hop_in[0].astype(f32), "y")
        self.arrived(3)
        self.hop(5, self.total[self.chips["x"], half:] + self.hop_in[2].astype(f32), "x")

    def finish(self):
        self.arrived(2, 4, 5, 6)
        half, own = self.half, self.chips["own"]
        base = self.total[own] + self.core_in[own].astype(f32)
        low = base[:half] + self.hop_in[1].astype(f32) + self.hop_in[4].astype(f32)
        high = base[half:] + self.hop_in[3].astype(f32) + self.hop_in[5].astype(f32)
        return jnp.concatenate([low, high], axis=0)


def comm_scratch(images, length, width):
    half = length // 2
    return [
        pltpu.VMEM((images, 4, length, width), bf16),
        pltpu.VMEM((images, 4, length, width), bf16),
        pltpu.VMEM((images, 4, length, width), f32),
        pltpu.VMEM((images, 6, half, width), bf16),
        pltpu.VMEM((images, 6, half, width), bf16),
        pltpu.SemaphoreType.DMA((images, 10)),
        pltpu.SemaphoreType.DMA((images, 10)),
        pltpu.SemaphoreType.DMA((images, 7)),
        pltpu.SemaphoreType.DMA((images, 7)),
    ]


def exchanges(full, comm, place):
    core_out, core_in, total, hop_out, hop_in, gs, gr, ss, sr = comm
    images = full.shape[0]
    gathers = [Gather(full.at[i], gs.at[i], gr.at[i], place) for i in range(images)]
    scatters = [
        Scatter(
            core_out.at[i], core_in.at[i], total.at[i], hop_out.at[i], hop_in.at[i], ss.at[i], sr.at[i], place
        )
        for i in range(images)
    ]
    return gathers, scatters


def flat(value):
    return value.reshape(value.shape[0] * value.shape[1], value.shape[2])


def halves(core):
    return ((1 - core) * 4, True), (core * 4, False)


def keep_partial(partial, scatter, sibling):
    shape = scatter.total.shape
    if sibling:
        scatter.core_out[...] = partial.astype(bf16).reshape(shape)
        scatter.cross()
    else:
        scatter.total[...] = partial.reshape(shape)


def column_sum(value):
    return jnp.sum(value, axis=0, keepdims=True)


def row_sums(value):
    ones = jnp.ones((8, value.shape[0]), bf16)
    return dot(ones, value, ((1,), (0,)))


GELU_ROOT = 0.7978845608028654
GELU_CUBE = 0.044715
NN, NT, TN = ((1,), (0,)), ((1,), (1,)), ((0,), (0,))


def gelu(hidden):
    inner = GELU_ROOT * (hidden + GELU_CUBE * (hidden * hidden * hidden))
    return 0.5 * hidden * (1.0 + jnp.tanh(inner))


def gelu_with_slope(hidden):
    square = hidden * hidden
    bend = jnp.tanh(GELU_ROOT * hidden * (1.0 + GELU_CUBE * square))
    rise = 0.5 * (1.0 + bend)
    slope = rise + 0.5 * hidden * (1.0 - bend * bend) * (GELU_ROOT + 3.0 * GELU_ROOT * GELU_CUBE * square)
    return hidden * rise, slope


def modulate_back_rows(resid, scale_part, grad):
    unit, rstd = norm_parts(resid)
    inner = grad * (1.0 + scale_part)
    grad_in = rstd * (
        inner
        - jnp.mean(inner, axis=-1, keepdims=True)
        - unit * jnp.mean(inner * unit, axis=-1, keepdims=True)
    )
    return grad_in, column_sum(grad), column_sum(grad * unit)


class Far:
    def __init__(self, what):
        self.what = what


class Copying:
    def __init__(self, sems):
        self.sems = sems
        self.open = {}

    def start(self, name, source, target):
        copy = pltpu.make_async_copy(source, target, self.sems.at[len(self.open)])
        copy.start()
        self.open[name] = copy

    def wait(self, *names):
        for name in names:
            self.open[name].wait()


def scratch_like(array):
    return pltpu.VMEM(array.shape, array.dtype)


def call(kernel, name, ident, outs, scratch, flops, args, tasks=()):
    vmem, anywhere = pl.BlockSpec(memory_space=pltpu.VMEM), pl.BlockSpec(memory_space=pl.ANY)
    in_specs = [anywhere if isinstance(a, Far) else vmem for a in args]
    out_specs = [anywhere if isinstance(o, Far) else vmem for o in outs]
    args = [a.what if isinstance(a, Far) else a for a in args]
    outs = [o.what if isinstance(o, Far) else o for o in outs]
    moved = sum(a.size * a.dtype.itemsize for a in args) + sum(o.size * o.dtype.itemsize for o in outs)
    task_ins = [array for task in tasks for array in task.ins]
    task_outs = [shape for task in tasks for shape in task.outs]
    task_sems = [pltpu.SemaphoreType.DMA(shape) for task in tasks for shape in task.sems]

    def run(*refs):
        refs = list(refs)

        def take(count):
            taken = refs[:count]
            del refs[:count]
            return taken

        main_ins, bound_ins = take(len(args)), take(len(task_ins))
        main_outs, bound_outs = take(len(outs)), take(len(task_outs))
        main_scratch = take(len(scratch))
        for task in tasks:
            ins = [bound_ins.pop(0) for _ in task.ins]
            results = [bound_outs.pop(0) for _ in task.outs]
            task.bind(ins, results, take(len(task.sems)))
        kernel(Background(tasks), *main_ins, *main_outs, *main_scratch)

    results = pl.pallas_call(
        run,
        name=name,
        out_shape=list(outs) + task_outs,
        in_specs=in_specs + [anywhere] * len(task_ins),
        out_specs=out_specs + [anywhere] * len(task_outs),
        scratch_shapes=list(scratch) + task_sems,
        compiler_params=pltpu.CompilerParams(
            collective_id=ident, has_side_effects=True, vmem_limit_bytes=60 * 2**20
        ),
        cost_estimate=pl.CostEstimate(flops=flops, bytes_accessed=moved, transcendentals=0),
    )(*args, *task_ins)
    return results[: len(outs)], results[len(outs) :]


def shaped(shape, kind):
    return jax.ShapeDtypeStruct(shape, kind)


def prologue_kernel(background, *refs):
    smalls = refs[:-21]
    (
        cond, pair_weight, tiles, packs, every_tile, silu_rows, mods,
        pack, cond_in, parts, parts_in, zs, zr, ps, pr, cs, cr, qs, qr, ms, mr,
    ) = refs[-21:]
    lanes = pack.shape[1]
    rows = []
    for small in smalls:
        value = small[...].astype(f32)
        rows += [value[:, start : start + lanes] for start in range(0, value.shape[1], lanes)]
    used = sum(value.shape[0] for value in rows)
    if used < pack.shape[0]:
        rows.append(jnp.zeros((pack.shape[0] - used, lanes), f32))
    pack[...] = jnp.concatenate(rows, axis=0).astype(bf16)
    ranks, peers = other_ranks(), plane_peers()
    greet(ranks + peers)
    rank, place = lax.axis_index("batch"), team_place()
    first = [remote(cond.at[who["batch"]], cond_in.at[rank], cs.at[n], cr.at[n], who) for n, who in enumerate(ranks)]
    copies = [remote(pack, packs.at[rank], zs.at[n], zr.at[n], who) for n, who in enumerate(ranks)]
    for n, who in enumerate(peers):
        copies.append(remote(tiles, every_tile.at[place], ps.at[n], pr.at[n], who))
    for copy in first + copies:
        copy.start()
    cond_in[rank] = cond[rank]
    packs[rank] = pack[...]
    every_tile[place] = tiles[...]
    for copy in first:
        copy.wait()

    count, images, width = cond_in.shape[0], cond_in.shape[1], parts.shape[2]
    value = jnp.concatenate([cond_in[z].astype(f32) for z in range(count)], axis=0)
    low = (value / (1.0 + jnp.exp(-value))).astype(bf16)
    silu_rows[...] = low
    value = dot(low, pair_weight[...], NN)
    for z in range(count):
        for i in range(images):
            n = z * images + i
            for p in range(2):
                parts[z, i * 2 + p] = value[n, p * width : (p + 1) * width]
    second = [
        remote(parts.at[who["batch"]], parts_in.at[n], qs.at[n], qr.at[n], who) for n, who in enumerate(ranks)
    ]
    for copy in second:
        copy.start()
    background.tick()
    total = parts[rank]
    for n, copy in enumerate(second):
        copy.wait()
        total = total + parts_in[n]
    mods[place] = total
    third = [
        remote(mods.at[place], mods.at[place], ms.at[n], mr.at[n], who) for n, who in enumerate(peers)
    ]
    for copy in third:
        copy.start()
    background.tick()
    for copy in copies + third:
        copy.wait()
    background.finish()


def prologue(smalls, dims, cond, pair_weight, tiles, ident, tasks):
    ranks, images, _ = cond.shape
    dma = pltpu.SemaphoreType.DMA
    lanes = min(small.shape[1] for small in smalls)
    rows = sum(small.size // lanes for small in smalls)
    pack = (rows + -rows % 16, lanes)
    width = pair_weight.shape[1] // 2
    part = (2 * images, width)
    others = [dma((ranks - 1,)), dma((ranks - 1,))]
    seven = [dma((7,)), dma((7,))]
    (packs, every_tile, silu_rows, mods), gathered = call(
        prologue_kernel,
        "prologue",
        ident,
        [
            shaped((ranks,) + pack, bf16),
            shaped((8,) + tiles.shape, tiles.dtype),
            shaped((ranks * images, cond.shape[2]), bf16),
            shaped((8,) + part, f32),
        ],
        [
            pltpu.VMEM(pack, bf16),
            pltpu.VMEM(cond.shape, bf16),
            pltpu.VMEM((ranks,) + part, f32),
            pltpu.VMEM((ranks - 1,) + part, f32),
        ]
        + others
        + seven
        + others
        + others
        + seven,
        0,
        (*smalls, cond, pair_weight, tiles),
        tasks,
    )
    parts, start = [], 0
    for small, dim in zip(smalls, dims):
        count, each = small.shape[0], small.shape[1] // lanes
        part = packs[:, start : start + count * each].reshape(ranks, each, count, lanes)
        start += count * each
        if dim == 0:
            parts.append(part.transpose(0, 2, 1, 3).reshape(ranks * count, -1))
        else:
            parts.append(part.transpose(2, 0, 1, 3).reshape(count, -1))
    return parts, every_tile, silu_rows, mods, gathered


def epilogue_kernel(
    depth, background, *refs,
):
    refs = list(refs)

    def take(count):
        taken = refs[:count]
        del refs[:count]
        return taken

    block_sums, (final_sums,) = take(2 * depth), take(1)
    block_biases = take(2 * depth)
    patch_term, final_term, edge_rows, tokens = take(4)
    all_mods, all_rows, all_tokens = take(3)
    mods, sums, biases, mods_low, sums_low, mods_in, sums_in, rank_mods, rank_sums, rank_biases_in, ps, pr, zs, zr, qs, qr = refs
    ranks, peers = other_ranks(), plane_peers()
    rank = lax.axis_index("batch")
    around = sides()
    place = around[0] * 4 + around[1]["own"]
    gather_tokens, gather_mods, gather_rows = [
        Gather(full, qs.at[n], qr.at[n], around) for n, full in enumerate((all_tokens, all_mods, all_rows))
    ]
    images = final_sums.shape[0]
    each = sums.shape[1]

    mods[...] = jnp.zeros_like(mods)
    sums[...] = jnp.zeros_like(sums)
    biases[...] = jnp.zeros_like(biases)
    for i in range(images):
        for b in range(depth):
            for p in range(6):
                n = 6 * b + p
                source = block_sums[2 * b + p // 3]
                mods[n // 2, i * 2 + n % 2] = source[i, p % 3]
        for p in range(2):
            n = 6 * depth + p
            mods[n // 2, i * 2 + n % 2] = final_sums[i, p]
    rows = [patch_term[n] for n in range(patch_term.shape[0])]
    rows += [final_term[n] for n in range(final_term.shape[0])]
    rows += [edge_rows[n] for n in range(edge_rows.shape[0])]
    for source in block_sums:
        total = source[0, 3]
        for i in range(1, images):
            total = total + source[i, 3]
        rows.append(total)
    for n, row in enumerate(rows):
        sums[n // each, n % each] = row
    for n, source in enumerate(block_biases):
        biases[n, : source.shape[1]] = source[0]

    mods_low[...] = mods[...].astype(bf16)
    sums_low[...] = sums[...].astype(bf16)
    greet(ranks + peers)
    first = []
    for n, who in enumerate(peers):
        there = lax.rem(who["col"], 2) * 4 + who["row"] * 2 + who["col"] // 2
        first.append(remote(mods_low.at[there], mods_in.at[n], ps.at[0, n], pr.at[0, n], who))
        first.append(remote(sums_low.at[there], sums_in.at[n], ps.at[1, n], pr.at[1, n], who))
    second = [
        remote(biases, rank_biases_in.at[n], zs.at[0, n], zr.at[0, n], who) for n, who in enumerate(ranks)
    ]
    for copy in first + second:
        copy.start()
    all_tokens[place] = tokens[...]
    gather_tokens.first()
    background.tick()
    for copy in first:
        copy.wait()
    mod_total, sum_total = mods[place], sums[place]
    for n in range(len(peers)):
        mod_total = mod_total + mods_in[n].astype(f32)
        sum_total = sum_total + sums_in[n].astype(f32)
    rank_mods[rank] = mod_total.astype(bf16)
    rank_sums[rank] = sum_total
    third = []
    for n, who in enumerate(ranks):
        third.append(remote(rank_mods.at[rank], rank_mods.at[rank], zs.at[1, n], zr.at[1, n], who))
        third.append(remote(rank_sums.at[rank], rank_sums.at[rank], zs.at[2, n], zr.at[2, n], who))
    for copy in third:
        copy.start()
    background.tick()
    bias_total = biases[...]
    for n, copy in enumerate(second):
        copy.wait()
        bias_total = bias_total + rank_biases_in[n]
    for copy in third:
        copy.wait()
    sum_own = rank_sums[0]
    for n in range(1, rank_sums.shape[0]):
        sum_own = sum_own + rank_sums[n]
    all_mods[place] = rank_mods[...]
    all_rows[place, 0, :each] = sum_own
    all_rows[place, 1, :, : biases.shape[1]] = bias_total
    gather_mods.first()
    gather_rows.first()
    for gather in (gather_tokens, gather_mods, gather_rows):
        gather.second()
    background.tick()
    for gather in (gather_tokens, gather_mods, gather_rows):
        gather.finish()
        gather.drain()
    background.finish()


def epilogue(block_sums, final_sums, block_biases, patch_term, final_term, edge_rows, tokens, ident, tasks):
    ranks = lax.axis_size("batch")
    dma = pltpu.SemaphoreType.DMA
    depth = len(block_sums) // 2
    images, _, width = final_sums.shape
    count = patch_term.shape[0] + final_term.shape[0] + edge_rows.shape[0] + len(block_sums)
    each = -(-count // 8)
    widest = max(source.shape[1] for source in block_biases)
    mods, sums = (8, 2 * images, width), (8, each, width)
    biases = (8, widest)
    return call(
        partial(epilogue_kernel, depth),
        "epilogue",
        ident,
        [
            shaped((8, ranks) + mods[1:], bf16),
            shaped((8, 2, 8, width), f32),
            shaped((8,) + tokens.shape, f32),
        ],
        [
            pltpu.VMEM(mods, f32),
            pltpu.VMEM(sums, f32),
            pltpu.VMEM(biases, f32),
            pltpu.VMEM(mods, bf16),
            pltpu.VMEM(sums, bf16),
            pltpu.VMEM((7,) + mods[1:], bf16),
            pltpu.VMEM((7,) + sums[1:], bf16),
            pltpu.VMEM((ranks,) + mods[1:], bf16),
            pltpu.VMEM((ranks,) + sums[1:], f32),
            pltpu.VMEM((ranks - 1,) + biases, f32),
            dma((2, 7)),
            dma((2, 7)),
            dma((3, ranks - 1)),
            dma((3, ranks - 1)),
            dma((3, 10)),
            dma((3, 10)),
        ],
        0,
        (*block_sums, final_sums, *block_biases, patch_term, final_term, edge_rows, tokens),
        tasks,
    )


def closing_kernel(background, parts, every, zs, zr):
    ranks = other_ranks()
    address = sides()[2]
    greet(ranks + list(address.values()))
    rank = lax.axis_index("batch")
    copies = [
        remote(parts.at[who["batch"]], every.at[rank], zs.at[n], zr.at[n], who) for n, who in enumerate(ranks)
    ]
    background.tick()
    for copy in copies:
        copy.start()
    every[rank] = parts[rank]
    for copy in copies:
        copy.wait()
    background.finish()


def closing(parts, ident, tasks):
    ranks = parts.shape[0]
    dma = pltpu.SemaphoreType.DMA
    (every,), gathered = call(
        closing_kernel,
        "closing",
        ident,
        [shaped(parts.shape, f32)],
        [dma((ranks - 1,)), dma((ranks - 1,))],
        0,
        (parts,),
        tasks,
    )
    return every, gathered


def mlp_forward_kernel(
    block, background, mid, gate_rows, vecs, pair_far, expand_bias, full_far, hidden_far, expanded, after,
    full, hidden, pair, expand, shrink, moves, *comm
):
    moving = Copying(moves)
    moving.start("pair", pair_far, pair)
    place = sides()
    core, chips, address = place
    images = full.shape[0]
    gathers, scatters = exchanges(full, comm, place)
    greet(list(address.values()) + background.partners())

    def row(i, n):
        return vecs[i, n : n + 1]

    def gate(i):
        return gate_rows[i] if block > 0 else 1.0

    own = core * 4 + chips["own"]

    def begin(i):
        full[i, own] = modulate(mid[i], row(i, 6 * block + 3), row(i, 6 * block + 4)).astype(bf16)
        gathers[i].first()

    def compute(i, between):
        for step, (start, sibling) in enumerate(halves(core)):
            value = dot(flat(full[i, pl.ds(start, 4)]), expand[...], NN) + expand_bias[...]
            hidden[i, pl.ds(start, 4)] = value.reshape(4, -1, value.shape[1])
            partial = dot(gelu(value).astype(bf16), shrink[...], NT)
            keep_partial(partial, scatters[i], sibling)
            between[step]()

    def end(i):
        value = scatters[i].finish() + row(i, offset_row(vecs, block, 1))
        expanded[i] = value
        after[i] = mid[i] + gate(i) * row(i, 6 * block + 5) * value

    def keep(i):
        moving.start(("full", i), full.at[i], full_far.at[i])
        moving.start(("hidden", i), hidden.at[i], hidden_far.at[i])

    background.tick()
    begin(0)
    gathers[0].second()
    begin(1)
    moving.wait("pair")
    expand[...] = pair[:, : expand.shape[1]]
    shrink[...] = pair[:, expand.shape[1] :]
    gathers[0].finish()
    compute(0, (gathers[1].second, scatters[0].first))
    keep(0)
    background.tick()
    gathers[1].finish()
    compute(1, (scatters[0].second, scatters[1].first))
    keep(1)
    background.tick()
    end(0)
    scatters[1].second()
    end(1)
    for part in gathers + scatters:
        part.drain()
    moving.wait(*[(name, i) for name in ("full", "hidden") for i in range(images)])
    background.finish()


def mlp_forward(block, mid, gate_rows, vecs, weights, ident, tasks=()):
    pair, expand_bias = weights
    images, length, width = mid.shape
    inner = pair.shape[1] // 2
    return call(
        partial(mlp_forward_kernel, block),
        "mlp_forward",
        ident,
        [
            Far(shaped((images, 8, length, width), bf16)),
            Far(shaped((images, 8, length, inner), f32)),
            shaped((images, length, width), f32),
            shaped((images, length, width), f32),
        ],
        [
            pltpu.VMEM((images, 8, length, width), bf16),
            pltpu.VMEM((images, 8, length, inner), f32),
            scratch_like(pair),
            pltpu.VMEM((width, inner), bf16),
            pltpu.VMEM((width, inner), bf16),
            pltpu.SemaphoreType.DMA((1 + 2 * images,)),
        ]
        + comm_scratch(images, length, width),
        4 * images * 8 * length * width * inner * 6,
        (
            mid,
            gate_rows,
            vecs,
            Far(pair),
            expand_bias.reshape(1, -1),
        ),
        tasks,
    )


def mlp_backward_kernel(
    block, background, grad_after, mid, expanded, gate_rows, vecs, pair_far, normed_far, hidden_far,
    grad_mid, sums, grad_pair, grad_bias,
    full, grad_hidden, active, sum_expand, sum_shrink, pair, expand, shrink, normed, hidden, moves, *comm
):
    moving = Copying(moves)
    moving.start("pair", pair_far, pair)
    moving.start("hidden", hidden_far, hidden)
    moving.start("normed", normed_far, normed)
    place = sides()
    core, chips, address = place
    gathers, scatters = exchanges(full, comm, place)
    greet(list(address.values()) + background.partners())

    def row(i, n):
        return vecs[i, n : n + 1]

    def gate(i):
        return gate_rows[i] if block > 0 else 1.0

    own = core * 4 + chips["own"]
    length = full.shape[2]

    def begin(i):
        gated = gate(i) * grad_after[i, :length]
        low = (gated * row(i, 6 * block + 5)).astype(bf16)
        full[i, own] = low
        gathers[i].first()
        sums[i, 2:3] = column_sum(gated * expanded[i])
        sums[i, 3:4] = column_sum(low.astype(f32))

    def compute(i, between):
        for step, (start, sibling) in enumerate(halves(core)):
            pull = dot(flat(full[i, pl.ds(start, 4)]), shrink[...], NN)
            value, slope = gelu_with_slope(flat(hidden[i, pl.ds(start, 4)]))
            active[i, pl.ds(start, 4)] = value.astype(bf16).reshape(4, -1, value.shape[1])
            low = (pull * slope).astype(bf16)
            grad_hidden[i, pl.ds(start, 4)] = low.reshape(4, -1, value.shape[1])
            keep_partial(dot(low, expand[...], NT), scatters[i], sibling)
            between[step]()

    def weigh_shrink(i):
        term = dot(flat(full[i]), flat(active[i]), TN)
        if i == 0:
            sum_shrink[...] = term
        else:
            sum_shrink[...] += term

    def weigh_expand(i):
        low = flat(grad_hidden[i])
        term = dot(flat(normed[i]), low, TN)
        if i == 0:
            sum_expand[...] = term
            grad_bias[...] = row_sums(low)
        else:
            grad_pair[...] = jnp.concatenate([sum_expand[...] + term, sum_shrink[...]], axis=1).astype(bf16)
            grad_bias[...] += row_sums(low)

    def end(i):
        grad, shift_sum, scale_sum = modulate_back_rows(mid[i], row(i, 6 * block + 4), scatters[i].finish())
        grad_mid[i] = grad + grad_after[i, :length]
        sums[i, 0:1] = shift_sum
        sums[i, 1:2] = scale_sum

    background.tick()
    begin(0)
    gathers[0].second()
    begin(1)
    moving.wait("pair")
    expand[...] = pair[:, : expand.shape[1]]
    shrink[...] = pair[:, expand.shape[1] :]
    gathers[0].finish()
    moving.wait("hidden")
    compute(0, (gathers[1].second, scatters[0].first))
    background.tick()
    gathers[1].finish()
    compute(1, (scatters[0].second, scatters[1].first))
    background.tick()
    weigh_shrink(0)
    end(0)
    scatters[1].second()
    background.tick()
    moving.wait("normed")
    weigh_expand(0)
    weigh_shrink(1)
    weigh_expand(1)
    end(1)
    for part in gathers + scatters:
        part.drain()
    background.finish()


def mlp_backward(block, grad_after, mid, expanded, gate_rows, vecs, weights, saved, ident, tasks=()):
    pair, _ = weights
    normed, hidden = saved
    images, length, width = mid.shape
    inner = pair.shape[1] // 2
    return call(
        partial(mlp_backward_kernel, block),
        "mlp_backward",
        ident,
        [
            shaped((images, length, width), f32),
            shaped((images, 8, width), f32),
            shaped((width, 2 * inner), bf16),
            shaped((8, inner), f32),
        ],
        [
            pltpu.VMEM((images, 8, length, width), bf16),
            pltpu.VMEM((images, 8, length, inner), bf16),
            pltpu.VMEM((images, 8, length, inner), bf16),
            pltpu.VMEM((width, inner), f32),
            pltpu.VMEM((width, inner), f32),
            scratch_like(pair),
            pltpu.VMEM((width, inner), bf16),
            pltpu.VMEM((width, inner), bf16),
            scratch_like(normed),
            scratch_like(hidden),
            pltpu.SemaphoreType.DMA((3,)),
        ]
        + comm_scratch(images, length, width),
        8 * images * 8 * length * width * inner * 6,
        (
            grad_after,
            mid,
            expanded,
            gate_rows,
            vecs,
            Far(pair),
            Far(normed),
            Far(hidden),
        ),
        tasks,
    )


LOG2E = 1.4426950408889634


def offset_row(vecs, block, kind):
    depth = (vecs.shape[1] - 2) // 8
    return 6 * depth + 2 + 2 * block + kind


def pad_lanes(value):
    gap = jnp.zeros((value.shape[0], LANES - HEAD_SIZE), value.dtype)
    parts = []
    for start in range(0, value.shape[1], HEAD_SIZE):
        parts += [value[:, start : start + HEAD_SIZE], gap]
    return jnp.concatenate(parts, axis=1)


def pad_rows(value):
    gap = jnp.zeros((LANES - HEAD_SIZE, value.shape[1]), value.dtype)
    parts = []
    for start in range(0, value.shape[0], HEAD_SIZE):
        parts += [value[start : start + HEAD_SIZE], gap]
    return jnp.concatenate(parts, axis=0)


def cut_lanes(value):
    return jnp.concatenate(
        [value[:, start : start + HEAD_SIZE] for start in range(0, value.shape[1], LANES)], axis=1
    )


def cut_rows(value):
    return jnp.concatenate(
        [value[start : start + HEAD_SIZE] for start in range(0, value.shape[0], LANES)], axis=0
    )


def attention_forward_kernel(
    block, background, base, gate_rows, vecs, project_own, project_bias, attend_own, key_bias,
    full_far, packed_far, mixed_far, log_total, attended, mid, project, attend,
    full, packed, mixed, moves, *comm
):
    moving = Copying(moves)
    place = sides()
    core, chips, address = place
    images, _, length, _ = full.shape
    gathers, scatters = exchanges(full, comm, place)
    greet(list(address.values()) + background.partners())

    def row(i, n):
        return vecs[i, n : n + 1]

    def gate(i):
        return gate_rows[i] if block > 0 else 1.0

    own = core * 4 + chips["own"]
    span = attend.shape[0]
    heads = span // LANES
    tile = 2 * length
    factor = HEAD_SIZE ** (-0.5) * LOG2E

    def begin(i):
        full[i, own] = modulate(base[i, :length], row(i, 6 * block), row(i, 6 * block + 1)).astype(bf16)
        gathers[i].first()

    def rows_of(start, count):
        return pl.ds(pl.multiple_of(start * length, length), count * length)

    def compute(i, between):
        for start, _ in halves(core):
            value = dot(flat(full[i, pl.ds(start, 4)]), project[...], NN) + project_bias[...]
            packed[i, rows_of(start, 4)] = value.astype(bf16)
        between[0]()
        for step, (start, sibling) in enumerate(halves(core)):

            def one(t, carry, start=start):
                rows = pl.ds(pl.multiple_of((start + 2 * t) * length, tile), tile)
                for h in range(heads):
                    q, k, v = (
                        pl.ds(part * span + h * LANES, LANES) for part in range(3)
                    )
                    scores = dot(packed[i, rows, q], packed[i, :, k], NT) * factor
                    if block > 0:
                        scores = scores + key_bias[i]
                    peak = jnp.max(scores, axis=1, keepdims=True)
                    probs = jnp.exp2(scores - peak)
                    total = jnp.sum(probs, axis=1, keepdims=True)
                    out = dot(probs.astype(bf16), packed[i, :, v], NN) / total
                    mixed[i, rows, pl.ds(h * LANES, LANES)] = out.astype(bf16)
                    level = jnp.broadcast_to(peak + jnp.log2(total), (tile, LANES))
                    log_total[i, h, pl.ds(start // 2 + t, 1)] = level.T[0:1]
                return carry

            lax.fori_loop(0, 2, one, 0)
            partial = dot(mixed[i, rows_of(start, 4)], attend[...], NN)
            keep_partial(partial, scatters[i], sibling)
            between[1 + step]()

    def end(i):
        value = scatters[i].finish() + row(i, offset_row(vecs, block, 0))
        attended[i] = value
        mid[i] = base[i, :length] + gate(i) * row(i, 6 * block + 2) * value

    def nothing():
        pass

    def keep(i):
        for name, near, far in (("full", full, full_far), ("packed", packed, packed_far), ("mixed", mixed, mixed_far)):
            moving.start((name, i), near.at[i], far.at[i])

    background.tick()
    begin(0)
    gathers[0].second()
    begin(1)
    project[...] = pad_lanes(project_own[...])
    attend[...] = pad_rows(attend_own[...])
    gathers[0].finish()
    compute(0, (gathers[1].second, background.tick, scatters[0].first))
    keep(0)
    gathers[1].finish()
    compute(1, (scatters[0].second, background.tick, scatters[1].first))
    keep(1)
    end(0)
    scatters[1].second()
    end(1)
    for part in gathers + scatters:
        part.drain()
    moving.wait(*moving.open)
    background.finish()


def attention_forward(block, length, base, gate_rows, vecs, weights, key_bias, ident, tasks=()):
    project, project_bias, attend = weights
    images, _, width = base.shape
    span = attend.shape[0] // HEAD_SIZE * LANES
    return call(
        partial(attention_forward_kernel, block),
        "attention_forward",
        ident,
        [
            Far(shaped((images, 8, length, width), bf16)),
            Far(shaped((images, 8 * length, 3 * span), bf16)),
            Far(shaped((images, 8 * length, span), bf16)),
            shaped((images, span // LANES, 4, 2 * length), f32),
            shaped((images, length, width), f32),
            shaped((images, length, width), f32),
            shaped((width, 3 * span), bf16),
            shaped((span, width), bf16),
        ],
        [
            pltpu.VMEM((images, 8, length, width), bf16),
            pltpu.VMEM((images, 8 * length, 3 * span), bf16),
            pltpu.VMEM((images, 8 * length, span), bf16),
            pltpu.SemaphoreType.DMA((3 * images,)),
        ]
        + comm_scratch(images, length, width),
        8 * images * 8 * length * width * span * 6,
        (
            base,
            gate_rows,
            vecs,
            project,
            project_bias.reshape(1, -1),
            attend,
            key_bias,
        ),
        tasks,
    )


def attention_backward_kernel(
    block, background, grad_mid, base, attended, gate_rows, vecs, project_far, attend_far, key_bias, normed_far, packed_far, mixed_far, log_total,
    grad_base, sums, grad_project, grad_attend, grad_bias,
    full, grad_mixed, grad_packed, grad_keys, grad_values, sum_project, sum_attend,
    project, attend, normed, packed, mixed, moves, *comm
):
    moving = Copying(moves)
    moving.start("attend", attend_far, attend)
    moving.start("packed", packed_far, packed)
    moving.start("mixed", mixed_far, mixed)
    moving.start("project", project_far, project)
    moving.start("normed", normed_far, normed)
    place = sides()
    core, chips, address = place
    images, _, length, _ = full.shape
    gathers, scatters = exchanges(full, comm, place)
    greet(list(address.values()) + background.partners())

    def row(i, n):
        return vecs[i, n : n + 1]

    def gate(i):
        return gate_rows[i] if block > 0 else 1.0

    own = core * 4 + chips["own"]
    span = attend.shape[0]
    heads = span // LANES
    tile = 2 * length
    factor = HEAD_SIZE ** (-0.5)

    def begin(i):
        gated = gate(i) * grad_mid[i]
        low = (gated * row(i, 6 * block + 2)).astype(bf16)
        full[i, own] = low
        gathers[i].first()
        sums[i, 2:3] = column_sum(gated * attended[i])
        sums[i, 3:4] = column_sum(low.astype(f32))

    def rows_of(start, count):
        return pl.ds(pl.multiple_of(start * length, length), count * length)

    def compute(i, between):
        grad_mixed[...] = dot(flat(full[i]), attend[...], NT).astype(bf16)
        between[0]()
        for h in range(heads):
            lane = pl.ds(h * LANES, LANES)
            q, k, v = (pl.ds(part * span + h * LANES, LANES) for part in range(3))
            keys_turned = packed[i, :, k].T

            def one(t, carry):
                rows = pl.ds(pl.multiple_of(t * tile, tile), tile)
                queries, pulls = packed[i, rows, q], grad_mixed[rows, lane]
                scores = dot(packed[i, :, k], queries, NT) * (factor * LOG2E)
                if block > 0:
                    scores = scores + key_bias[i]
                probs = jnp.exp2(scores - log_total[i, h, pl.ds(t, 1)])
                dprobs = dot(packed[i, :, v], pulls, NT)
                row_dot = column_sum(probs * dprobs)
                grad_scores = (probs * (dprobs - row_dot)).astype(bf16)
                value_term = dot(probs.astype(bf16), pulls, NN)
                key_term = dot(grad_scores, queries, NN)

                @pl.when(t == 0)
                def _():
                    grad_values[...] = value_term
                    grad_keys[...] = key_term

                @pl.when(t > 0)
                def _():
                    grad_values[...] += value_term
                    grad_keys[...] += key_term

                query_term = dot(keys_turned, grad_scores, NN) * factor
                grad_packed[i, rows, q] = query_term.T.astype(bf16)
                return carry

            lax.fori_loop(0, 4, one, 0)
            grad_packed[i, :, k] = (grad_keys[...] * factor).astype(bf16)
            grad_packed[i, :, v] = grad_values[...].astype(bf16)
            between[1 + h]()
        for step, (start, sibling) in enumerate(halves(core)):
            keep_partial(dot(grad_packed[i, rows_of(start, 4)], project[...], NT), scatters[i], sibling)

    def weigh_attend(i):
        term = dot(mixed[i], flat(full[i]), TN)
        if i == 0:
            sum_attend[...] = term
        else:
            grad_attend[...] = cut_rows(sum_attend[...] + term).reshape(grad_attend.shape).astype(bf16)

    def weigh_project(i):
        low = grad_packed[i]
        term = dot(flat(normed[i]), low, TN)
        if i == 0:
            sum_project[...] = term
            grad_bias[...] = row_sums(low)
        else:
            grad_project[...] = cut_lanes(sum_project[...] + term).astype(bf16)
            grad_bias[...] += row_sums(low)

    def end(i):
        grad, shift_sum, scale_sum = modulate_back_rows(base[i, :length], row(i, 6 * block + 1), scatters[i].finish())
        grad_base[i] = grad + grad_mid[i]
        sums[i, 0:1] = shift_sum
        sums[i, 1:2] = scale_sum

    def nothing():
        pass

    def begin_extra():
        gathers[1].second()
        background.tick()

    def early_attend():
        for i in range(images):
            weigh_attend(i)
        for task in background.tasks:
            if task.source is None:
                task.source = grad_attend
        background.tick()

    def middle():
        scatters[0].second()
        background.tick()

    background.tick()
    begin(0)
    gathers[0].second()
    begin(1)
    gathers[0].finish()
    moving.wait("attend", "packed", "mixed", "project", "normed")
    compute(0, (begin_extra, gathers[1].finish, nothing))
    scatters[0].first()
    compute(1, (early_attend, middle, background.tick))
    scatters[1].first()
    weigh_project(0)
    end(0)
    scatters[1].second()
    weigh_project(1)
    end(1)
    for part in gathers + scatters:
        part.drain()
    background.finish()


def attention_backward(
    block, attend_shape, grad_mid, base, attended, gate_rows, vecs, weights, key_bias, saved, ident, tasks=()
):
    project, attend = weights
    normed, packed, mixed, log_total = saved
    images, length, width = grad_mid.shape
    span = attend.shape[0]
    tokens = 8 * length
    return call(
        partial(attention_backward_kernel, block),
        "attention_backward",
        ident,
        [
            shaped((images, length, width), f32),
            shaped((images, 8, width), f32),
            shaped((width, 3 * span // LANES * HEAD_SIZE), bf16),
            shaped(attend_shape, bf16),
            shaped((8, 3 * span), f32),
        ],
        [
            pltpu.VMEM((images, 8, length, width), bf16),
            pltpu.VMEM((tokens, span), bf16),
            pltpu.VMEM((images, tokens, 3 * span), bf16),
            pltpu.VMEM((tokens, LANES), f32),
            pltpu.VMEM((tokens, LANES), f32),
            pltpu.VMEM((width, 3 * span), f32),
            pltpu.VMEM((span, width), f32),
            scratch_like(project),
            scratch_like(attend),
            scratch_like(normed),
            scratch_like(packed),
            scratch_like(mixed),
            pltpu.SemaphoreType.DMA((5,)),
        ]
        + comm_scratch(images, length, width),
        16 * images * 8 * length * width * span * 6,
        (
            grad_mid,
            base,
            attended,
            gate_rows,
            vecs,
            Far(project),
            Far(attend),
            key_bias,
            Far(normed),
            Far(packed),
            Far(mixed),
            log_total,
        ),
        tasks,
    )


HEAD_SIZE = 72


def pad_heads(array, axis):
    shape = array.shape
    heads = shape[axis] // HEAD_SIZE
    split = array.reshape(shape[:axis] + (heads, HEAD_SIZE) + shape[axis + 1 :])
    widths = [(0, 0)] * split.ndim
    widths[axis + 1] = (0, LANES - HEAD_SIZE)
    return jnp.pad(split, widths).reshape(shape[:axis] + (heads * LANES,) + shape[axis + 1 :])


def unpad_heads(array, axis):
    shape = array.shape
    heads = shape[axis] // LANES
    split = array.reshape(shape[:axis] + (heads, LANES) + shape[axis + 1 :])
    kept = lax.slice_in_dim(split, 0, HEAD_SIZE, axis=axis + 1)
    return kept.reshape(shape[:axis] + (heads * HEAD_SIZE,) + shape[axis + 1 :])


def turn(block, own, step, last):
    return jnp.where(block == own, step, jnp.where(block < own, 0, last))


def local_call(kernel, name, grid, in_specs, out_specs, outs, moved, args, prefetch=0):
    return pl.pallas_call(
        kernel,
        name=name,
        grid_spec=pltpu.PrefetchScalarGridSpec(
            num_scalar_prefetch=prefetch, grid=grid, in_specs=in_specs, out_specs=out_specs
        ),
        out_shape=outs,
        compiler_params=pltpu.CompilerParams(vmem_limit_bytes=56 * 2**20),
        cost_estimate=pl.CostEstimate(flops=0, bytes_accessed=moved, transcendentals=0),
    )(*args)


def mlp_unpack_kernel(*refs):
    *everys, expand, shrink = refs
    for k, every in enumerate(everys):

        @pl.when(pl.program_id(0) == k)
        def _(every=every):
            pair = every.shape[3]
            inner = pair // 2
            for chip in range(4):
                first, second = every[0, chip].astype(f32), every[1, chip].astype(f32)
                lanes = pl.ds(chip * pair, pair)
                expand[0, :, lanes] = jnp.concatenate([first[:, :inner], second[:, :inner]], axis=1)
                shrink[0, :, lanes] = jnp.concatenate([first[:, inner:], second[:, inner:]], axis=1)


def mlp_unpack(everys):
    depth = len(everys)
    _, _, half, pair = everys[0].shape
    shard, inner = 2 * half, pair // 2
    everys = [every.reshape(2, 4, shard, pair) for every in everys]
    steps = 3 if shard % 48 == 0 else 1
    rows = shard // steps
    block = (2, 4, rows, pair)
    return local_call(
        mlp_unpack_kernel,
        "mlp_unpack",
        (depth, steps),
        [pl.BlockSpec(block, lambda b, j, k=k: (0, 0, turn(b, k, j, steps - 1), 0)) for k in range(depth)],
        [
            pl.BlockSpec((1, rows, 8 * inner), lambda b, j: (b, j, 0)),
            pl.BlockSpec((1, rows, 8 * inner), lambda b, j: (b, j, 0)),
        ],
        [shaped((depth, shard, 8 * inner), f32), shaped((depth, shard, 8 * inner), f32)],
        depth * shard * inner * 96,
        everys,
    )


def project_unpack_kernel(*refs):
    *everys, project = refs
    for k, every in enumerate(everys):

        @pl.when(pl.program_id(0) == k)
        def _(every=every):
            each = every.shape[-1] // 3
            parts = [
                every[d % 2, d // 2, 0].astype(f32)[:, n * each : (n + 1) * each] for n in range(3) for d in range(8)
            ]
            project[0, 0] = jnp.concatenate(parts, axis=1)


def project_unpack(everys):
    depth = len(everys)
    _, _, half, columns = everys[0].shape
    everys = [every.reshape(2, 4, 2, half, columns) for every in everys]
    (project,) = local_call(
        project_unpack_kernel,
        "project_unpack",
        (depth, 2),
        [
            pl.BlockSpec((2, 4, 1, half, columns), lambda b, j, k=k: (0, 0, turn(b, k, j, 1), 0, 0))
            for k in range(depth)
        ],
        [pl.BlockSpec((1, 1, half, 8 * columns), lambda b, j: (b, j, 0, 0))],
        [shaped((depth, 2, half, 8 * columns), f32)],
        depth * half * columns * 96,
        everys,
    )
    return project.reshape(depth, 2 * half, 8 * columns)


def attend_unpack_kernel(rank, *refs):
    *everys, attend = refs
    for k, every in enumerate(everys):

        @pl.when(pl.program_id(0) == k)
        def _(every=every):
            cores, _, pieces = every.shape[:3]
            for n in range(attend.shape[1]):
                attend[0, n] = every[n // pieces, 0, n % pieces].astype(f32)


def attend_unpack(everys, rank, shard, pieces, rows):
    depth = len(everys)
    width = everys[0].shape[-1]
    everys = [every.reshape(2, 4, pieces, rows, width) for every in everys]
    steps = shard // rows
    if steps == 2 * pieces:
        block, count = (2, 1, pieces, rows, width), steps

        def chosen(b, i, ranks):
            return 0, ranks[0], 0, 0, 0

    else:
        block, count = (1, 1, 1, rows, width), 1

        def chosen(b, i, ranks):
            g = ranks[0] * steps + i
            d = g // pieces
            return d % 2, d // 2, g % pieces, 0, 0

    (attend,) = local_call(
        attend_unpack_kernel,
        "attend_unpack",
        (depth, steps // count),
        [pl.BlockSpec(block, chosen) for _ in range(depth)],
        [pl.BlockSpec((1, count, rows, width), lambda b, i, ranks: (b, i, 0, 0))],
        [shaped((depth, steps, rows, width), f32)],
        depth * shard * width * 6,
        [rank.reshape(1), *everys],
        1,
    )
    return attend.reshape(depth, shard, width)


def adaptive_grad_kernel(silu, mods, out):
    out[0] = dot(silu[...], mods[0], TN)


def adaptive_grad(silu, mods):
    depth, count, columns = mods.shape
    shard = silu.shape[1]
    (grad,) = local_call(
        adaptive_grad_kernel,
        "adaptive_grad",
        (depth, 1),
        [
            pl.BlockSpec((count, shard), lambda b, j: (0, 0)),
            pl.BlockSpec((1, count, columns), lambda b, j: (b, 0, j)),
        ],
        [pl.BlockSpec((1, shard, columns), lambda b, j: (b, 0, j))],
        [shaped((depth, shard, columns), f32)],
        depth * shard * columns * 4,
        [silu, mods],
    )
    return grad


def body(
    latents,
    conditioning,
    kept_index,
    kept_count,
    patch_weight,
    patch_bias,
    adaptive_weight,
    adaptive_bias,
    project_weight,
    project_bias,
    attend_weight,
    attend_bias,
    expand_weight,
    expand_bias,
    shrink_weight,
    shrink_bias,
    final_adaptive,
    final_offset,
    final_weight,
    final_bias,
    cotangent,
):
    rows, cols, ranks = lax.axis_size("row"), lax.axis_size("col"), lax.axis_size("batch")
    team = rows * cols
    place = lax.axis_index("row") * cols + lax.axis_index("col")
    rank = lax.axis_index("batch")
    images, channels_in = latents.shape[:2]
    channels_out = cotangent.shape[1]
    rows_tile, cols_tile = latents.shape[2] // PATCH, latents.shape[3] // PATCH
    tile_tokens = rows_tile * cols_tile
    sequence = tile_tokens * team
    width = conditioning.shape[1]
    depth = adaptive_weight.shape[0]
    shard = adaptive_weight.shape[1]
    kept_local = tile_tokens * 3 // 4
    highest = lax.Precision.HIGHEST

    head_cols = width // team
    hidden_cols = expand_weight.shape[2] // team

    def slice_of(array, axis, count):
        return lax.dynamic_slice_in_dim(array, place * count, count, axis=axis)

    piece_rows = min(shard, HEAD_SIZE)
    pieces_each = head_cols // piece_rows
    project_own = jnp.concatenate(
        [
            lax.dynamic_slice_in_dim(project_weight, part * width + place * head_cols, head_cols, axis=2)
            for part in range(3)
        ],
        axis=2,
    )
    attend_own = jnp.stack(
        [
            lax.dynamic_slice_in_dim(
                attend_weight, (place * head_cols + j * piece_rows) % shard, piece_rows, axis=1
            )
            for j in range(pieces_each)
        ],
        axis=1,
    )
    pair_own = jnp.concatenate(
        [slice_of(expand_weight, 2, hidden_cols), slice_of(shrink_weight, 1, hidden_cols).transpose(0, 2, 1)], axis=2
    )

    smalls = [
        patch_weight,
        final_weight.T,
        patch_bias[None],
        adaptive_bias,
        project_bias,
        attend_bias,
        expand_bias,
        shrink_bias,
        final_offset[None],
    ]
    patch_tiles = to_tokens(latents, PATCH)
    grad_tiles = to_tokens(cotangent, PATCH)
    patch_in, patch_out = patch_tiles.shape[2], grad_tiles.shape[2]
    tiles = jnp.concatenate([patch_tiles, grad_tiles], axis=2)
    pair = 2 * width
    block_of = jnp.minimum(place // 3, depth - 1)
    pair_weight = lax.dynamic_slice(adaptive_weight, (block_of, 0, place % 3 * pair), (1, shard, pair))[0]
    pair_weight = jnp.where(place < 3 * depth, pair_weight, final_adaptive)
    packs, every_tile, silu_rows, mods, (project_next, attend_next) = prologue(
        smalls,
        [1] * 9,
        conditioning.reshape(images, ranks, shard).transpose(1, 0, 2),
        pair_weight,
        tiles.reshape(-1, LANES),
        8,
        [Line(project_own[0]), Chain(attend_own[0], shard)],
    )
    (
        patch_full,
        final_turned,
        patch_bias_full,
        adaptive_offset,
        project_offset,
        attend_offset,
        expand_offset,
        shrink_offset,
        final_offset_full,
    ) = packs
    patch_bias_full, final_offset_full = patch_bias_full[0], final_offset_full[0]
    final_full = final_turned.T

    whole = every_tile.reshape((rows, cols, images, rows_tile, cols_tile, -1)).transpose(2, 0, 3, 1, 4, 5)
    whole = whole.reshape(images, sequence, patch_in + patch_out)
    grid_cols = cols * cols_tile
    own_ids = lax.dynamic_index_in_dim(
        kept_index.reshape(images, tile_tokens, team), place, axis=2, keepdims=False
    )
    pick = (own_ids[:, :, None] == jnp.arange(sequence, dtype=jnp.int32)).astype(bf16)
    own = jnp.einsum("ikt,itc->ikc", pick, whole, preferred_element_type=f32).astype(bf16)
    patches, grad_outputs = own[..., :patch_in], own[..., patch_in:]
    order = jnp.arange(kept_local, dtype=jnp.int32)[:, None] * team + jnp.arange(team, dtype=jnp.int32)
    kept_grid = order[None] < kept_count[:, None, None]
    chunk_order = kept_grid.reshape(images, kept_local, team // 2, 2).transpose(0, 3, 2, 1)
    key_bias = jnp.where(chunk_order.reshape(images, team * kept_local), 0.0, masked_score).astype(f32)
    kept_rows = lax.dynamic_index_in_dim(kept_grid, place, axis=2, keepdims=False).astype(f32)[:, :, None]

    count = width // 4
    omega = 1.0 / 10000.0 ** (jnp.arange(count, dtype=f32) / count)
    angles = jnp.arange(max(rows * rows_tile, grid_cols), dtype=f32)[:, None] * omega[None, :]
    along = jnp.concatenate([jnp.sin(angles), jnp.cos(angles)], axis=1)
    places = jnp.arange(along.shape[0], dtype=jnp.int32)

    def position_of(coords):
        chosen = (coords[..., None] == places).astype(f32)
        return jnp.einsum("ikt,tc->ikc", chosen, along, precision=highest)

    position = jnp.concatenate(
        [position_of(own_ids // grid_cols), position_of(own_ids % grid_cols)], axis=-1
    )
    resid = (
        jnp.einsum("ikc,cd->ikd", patches, patch_full, preferred_element_type=f32)
        + patch_bias_full.astype(f32)
        + position
    )

    mods = mods.reshape(team, images, 2, width).transpose(1, 0, 2, 3).reshape(images, 2 * team, width)
    offsets = [adaptive_offset.reshape(6 * depth, width), final_offset_full.reshape(2, width)]
    mods = mods[:, : 6 * depth + 2] + jnp.concatenate(offsets, axis=0).astype(f32)
    added = jnp.stack([attend_offset, shrink_offset], axis=1).reshape(2 * depth, width).astype(f32)
    vecs = jnp.concatenate([mods, jnp.broadcast_to(added, (images, 2 * depth, width))], axis=1)
    final_shift, final_scale = mods[:, 6 * depth, None], mods[:, 6 * depth + 1, None]
    head_biases = jnp.moveaxis(project_offset.astype(f32).reshape(depth, 2, team, head_cols), 2, 0)
    head_biases = lax.dynamic_index_in_dim(head_biases, place, axis=0, keepdims=False)
    head_biases = jnp.stack([head_biases[:, 0], jnp.zeros((depth, head_cols), f32), head_biases[:, 1]], axis=1)
    head_biases = pad_heads(head_biases, 2).reshape(depth, -1)
    hidden_biases = slice_of(expand_offset.astype(f32), 1, hidden_cols)

    records = []
    for b in range(depth):
        routed = b > 0
        length = kept_local if routed else tile_tokens
        base = resid
        tasks = [Line(pair_own[b])]
        (*attention_saved, attended, mid, project, attend), gathered = attention_forward(
            b,
            length,
            base,
            kept_rows,
            vecs,
            (project_next.reshape(width, -1), head_biases[b], attend_next.reshape(-1, width)),
            key_bias[:, None, :],
            4 * b,
            tasks,
        )
        mlp_weights = (gathered[0].reshape(width, 2 * hidden_cols), hidden_biases[b])
        tasks = []
        if b + 1 < depth:
            tasks = [Line(project_own[b + 1]), Chain(attend_own[b + 1], shard)]
        (*mlp_saved, expanded, after), gathered = mlp_forward(
            b, mid, kept_rows, vecs, mlp_weights, 4 * b + 1, tasks
        )
        if tasks:
            project_next, attend_next = gathered
        records.append((base, mid, attended, expanded, (project, attend), mlp_weights, attention_saved, mlp_saved))
        resid = jnp.concatenate([after, resid[:, kept_local:]], axis=1) if routed else after

    final_normed = modulate(resid, final_shift, final_scale).astype(bf16)
    outputs = jnp.einsum("ikd,dc->cik", final_normed, final_full, preferred_element_type=f32)
    outputs = outputs + final_bias.astype(f32)[:, None, None]
    final_bias_term = jnp.sum(grad_outputs.astype(f32), axis=(0, 1))
    final_weight_term = jnp.einsum("ikd,ikc->cd", final_normed, grad_outputs, preferred_element_type=f32)
    grad_final = jnp.einsum("ikc,dc->ikd", grad_outputs, final_full, preferred_element_type=f32)
    grad_resid, grad_final_shift, grad_final_scale = modulate_back(resid, final_scale, grad_final)
    final_mod_term = jnp.stack([grad_final_shift, grad_final_scale], axis=1)

    block_sums, block_biases = [], []
    spread = [[None, None, None] for _ in range(depth)]

    def folded(source, inbox):
        own = lax.dynamic_index_in_dim(source, rank, axis=0, keepdims=False)
        return (own.astype(f32) + jnp.sum(inbox.astype(f32), axis=0)).astype(bf16)

    def fold_project(term, inbox):
        return folded(term, inbox).reshape(2, shard // 2, -1)

    def fold_attend(term, inbox):
        total = term.astype(f32) + jnp.sum(inbox.astype(f32), axis=1)
        return total.astype(bf16).reshape(2, head_cols // 2, width)

    attend_shape = (pieces_each, piece_rows, width)
    project_term = None
    for b in reversed(range(depth)):
        base, mid, attended, expanded, attention_weights, mlp_weights, attention_saved, mlp_saved = records[b]
        routed = b > 0
        tasks = []
        if project_term is not None:
            tasks = [Fold(project_term), FoldTo(attend_shape, shard, 0, grad_attend)]
        (grad_mid, mlp_sums, grad_pair, grad_expand_bias), inboxes = mlp_backward(
            b, grad_resid, mid, expanded, kept_rows, vecs, mlp_weights, mlp_saved, 4 * b + 2, tasks
        )
        mlp_term = grad_pair.reshape(ranks, shard, 2 * hidden_cols)
        waiting = []
        early = b == 0
        tasks = [Fold(mlp_term)] + ([FoldTo(attend_shape, shard, 2)] if early else [])
        if project_term is not None:
            waiting = [
                (b + 1, 0, mlp_part),
                (b + 1, 1, fold_project(project_term, inboxes[0])),
                (b + 1, 2, fold_attend(grad_attend, inboxes[1])),
            ]
        folds = len(tasks)
        tasks += [PlaneGather(part, (1, 3)) for _, _, part in waiting]
        (grad_base, attention_sums, grad_project, grad_attend, grad_project_bias), inboxes = attention_backward(
            b,
            attend_shape,
            grad_mid,
            base,
            attended,
            kept_rows,
            vecs,
            attention_weights,
            key_bias[:, :, None],
            attention_saved,
            4 * b + 3,
            tasks,
        )
        for (block, n, _), every in zip(waiting, inboxes[folds:]):
            spread[block][n] = every
        mlp_part = folded(mlp_term, inboxes[0]).reshape(2, shard // 2, -1)
        if early:
            waiting = [(b, 0, mlp_part), (b, 2, fold_attend(grad_attend, inboxes[1]))]
        project_term = grad_project.reshape(ranks, shard, 3 * head_cols)
        block_sums = [attention_sums, mlp_sums] + block_sums
        block_biases = [grad_project_bias, grad_expand_bias] + block_biases
        grad_resid = jnp.concatenate([grad_base, grad_resid[:, kept_local:]], axis=1) if routed else grad_base

    patch_bias_term = jnp.sum(grad_resid, axis=(0, 1))
    grad_embed = grad_resid.astype(bf16)
    patch_term = jnp.einsum("ikc,ikd->cd", patches, grad_embed, preferred_element_type=f32)
    grad_patches = jnp.einsum("ikd,cd->cik", grad_embed, patch_full, preferred_element_type=f32)

    edge_rows = jnp.stack([patch_bias_term, jnp.pad(final_bias_term, (0, width - patch_out))])
    tokens_out = jnp.concatenate([outputs, grad_patches], axis=0).reshape(2, (patch_out + patch_in) // 2, -1)
    tasks = [Fold(project_term, late=1)] + [PlaneGather(part, plan) for (_, _, part), plan in zip(waiting, ((0, 2), (2,)))]
    (all_mods, all_rows, all_tokens), inboxes = epilogue(
        block_sums,
        final_mod_term,
        block_biases,
        patch_term,
        final_weight_term,
        edge_rows,
        tokens_out,
        10,
        tasks,
    )
    for (block, n, _), every in zip(waiting, inboxes[1:]):
        spread[block][n] = every
    last_part = fold_project(project_term, inboxes[0])

    mod_every = all_mods.reshape(team, ranks * images, pair)
    mod_width = 3 * pair
    block_mods = jnp.stack(
        [mod_every[3 * b : 3 * b + 3].transpose(1, 0, 2).reshape(ranks * images, mod_width) for b in range(depth)]
    )
    final_mods = mod_every[3 * depth]
    grad_silu = dot(final_mods, final_adaptive, NT)
    for b in range(depth):
        grad_silu = grad_silu + dot(block_mods[b], adaptive_weight[b], NT)
    grad_silu, last = closing(
        grad_silu.reshape(ranks, images, shard), 11, [PlaneGather(last_part)]
    )
    spread[0][1] = last[0]
    grad_silu = grad_silu.transpose(1, 0, 2).reshape(images, width)
    conditioning_grad = jax.vjp(jax.nn.silu, conditioning.astype(f32))[1](grad_silu)[0]
    adaptive_weight_grad = adaptive_grad(silu_rows, block_mods)
    final_adaptive_grad = dot(silu_rows, final_mods, TN)

    def rank_part(full):
        part = full.shape[-1] // ranks
        return lax.dynamic_slice_in_dim(full, rank * part, part, axis=full.ndim - 1)

    adaptive_bias_grad = rank_part(jnp.sum(block_mods.astype(f32), axis=1))
    final_offset_grad = rank_part(jnp.sum(final_mods.astype(f32), axis=0))

    def in_order(every):
        split = every.reshape((2, team // 2) + every.shape[1:])
        return jnp.swapaxes(split, 0, 1).reshape(every.shape)

    ordered = in_order(all_tokens).reshape(team, patch_out + patch_in, images, tile_tokens)
    ordered = ordered.transpose(2, 3, 0, 1).reshape(images, sequence, patch_out + patch_in)
    tile_rows = lax.axis_index("row") * rows_tile + jnp.arange(rows_tile, dtype=jnp.int32)
    tile_cols = lax.axis_index("col") * cols_tile + jnp.arange(cols_tile, dtype=jnp.int32)
    tile_ids = (tile_rows[:, None] * grid_cols + tile_cols).reshape(-1)
    back = (kept_index[:, None, :] == tile_ids[None, :, None]).astype(f32)
    tile_out = jnp.einsum("itj,ijc->itc", back, ordered, precision=highest)
    prediction = to_planes(tile_out[..., :patch_out], PATCH, channels_out, rows_tile, cols_tile)
    latent_grad = to_planes(tile_out[..., patch_out:], PATCH, channels_in, rows_tile, cols_tile)

    expand_weight_grad, shrink_weight_grad = mlp_unpack([parts[0] for parts in spread])
    project_weight_grad = project_unpack([parts[1] for parts in spread])
    attend_weight_grad = attend_unpack([parts[2] for parts in spread], rank, shard, pieces_each, piece_rows)

    first = patch_in + patch_out
    each = -(-(first + 2 + 2 * depth) // team)
    all_sums = all_rows[:, 0, :each].reshape(-1, width)
    all_biases = in_order(all_rows[:, 1])
    sums = lax.dynamic_slice_in_dim(all_sums, rank * shard, shard, axis=1)
    token_sums = sums[first + 2 : first + 2 + 2 * depth].reshape(depth, 2, shard)
    final_bias_grad = all_sums[first + 1, :patch_out]
    rows_of = all_biases.transpose(1, 0, 2)[: 2 * depth].reshape(depth, 2, team, -1)
    expand_bias_grad = rows_of[:, 1, :, :hidden_cols].reshape(depth, -1)
    head_rows = rows_of[:, 0, :, : 3 * head_cols // HEAD_SIZE * LANES]
    head_rows = unpad_heads(head_rows.reshape(depth, team, 3, -1), 3)
    project_bias_grad = jnp.stack([head_rows[:, :, 0], head_rows[:, :, 2]], axis=1).reshape(depth, -1)

    return (
        prediction,
        latent_grad,
        conditioning_grad,
        sums[:patch_in],
        sums[first],
        adaptive_weight_grad,
        adaptive_bias_grad,
        project_weight_grad,
        rank_part(project_bias_grad),
        attend_weight_grad,
        token_sums[:, 0],
        expand_weight_grad,
        rank_part(expand_bias_grad),
        shrink_weight_grad.transpose(0, 2, 1),
        token_sums[:, 1],
        final_adaptive_grad,
        final_offset_grad,
        sums[patch_in:first].T,
        final_bias_grad,
    )


def solution(mesh):
    tokens = P("batch", None, "row", "col")
    placed = (
        tokens,
        P("batch", None),
        P("batch", None),
        P("batch"),
        P(None, "batch"),
        P("batch"),
        P(None, "batch", None),
        P(None, "batch"),
        P(None, "batch", None),
        P(None, "batch"),
        P(None, "batch", None),
        P(None, "batch"),
        P(None, "batch", None),
        P(None, "batch"),
        P(None, None, "batch"),
        P(None, "batch"),
        P("batch", None),
        P("batch"),
        P("batch", None),
        P(),
        tokens,
    )
    return jax.shard_map(
        body,
        mesh=mesh,
        in_specs=placed,
        out_specs=(tokens, tokens, P("batch", None)) + placed[4:16] + (placed[16], P("batch"), P("batch", None), P()),
        check_vma=False,
    )
```
